32 devices in a mesh: parts: 2 (over y), blk: 4 (over z), reader: 4 (over x, core), sub: 1.
Axes of the slice: x: 2, y: 2, z: 4, core: 2. Of those that a mesh axis runs over, the one named last changes fastest.
Arguments:
- images: bfloat16 [3072, 8192], P(('parts', 'blk', 'reader'), 'sub'), parts along dimension 0, may hold values from -40 to 40
- routes: int32 [3072, 2], P(('parts', 'blk', 'reader')), parts along dimension 0, may hold values from 0 to 3, all different within a row; in each aligned block of 96 rows (0 to 95, 96 to 191, ...) at most 96 rows name the same one
- projections: bfloat16 [8, 128, 8192], P(('parts', 'reader'), 'blk', 'sub'), parts along dimension 0, may hold values from -8 to 8
- noise_weights: float32 [16384], P(('parts', 'sub')), parts along dimension 0, may hold values from 0.3 to 3
Outputs:
- weighted_sums: float32 [8, 128, 8192], P(('parts', 'reader'), 'blk', 'sub'), parts along dimension 0
- normalizer: float32 [3072], P(('parts', 'blk', 'reader')), parts along dimension 0
The draws below stay inside these ranges and needn't reach their ends.
There are 2 independent parts, one for each index of `parts`. The reference program is written for one: setup_inputs(seed, part) draws one part's arguments, and reference() takes and returns one part's arrays. A program takes and returns all parts, laid end to end along the dimension named above; each array names one. Nothing has to cross between parts.
Inputs may be any that keep to these rules, and one draw needn't show every extreme that they name: `routes`: each row names 2 different class groups. In the rows of one device (aligned blocks of 96 rows) no group is named by more than 96 rows, a bound that some block reaches.
All inputs are finite; a program needn't handle non-finite values.
Results may differ from the reference program's by a relative error of at most 0.019.
Values may be sent and summed in bfloat16 or wider, within the bound.
No kernel may reach another device: no remote copies, remote signals or barrier semaphores. Data moves between devices by JAX's collectives and lax.ppermute only.
A program may use at most 64 MiB of HBM per device.

```python
import math
import jax
import jax.numpy as jnp
import numpy as np
from jax import lax

COEF = 8192
PART_DEV = 96
TOP = 2
GROUPS = 4
GREFS = 128
CAP = 96
RECV = 384
PARTICLES = 1536
N_BLK = 4
N_READER = 4


def projection_values(key):
    folded = jax.random.fold_in(key, 101)
    scale_key, vector_key = jax.random.split(folded)
    scales = jnp.exp(jax.random.uniform(scale_key, (GROUPS, GREFS, 1), jnp.float32, math.log(0.6), math.log(6.0)))
    vectors = jax.random.truncated_normal(vector_key, -4.0, 4.0, (GROUPS, GREFS, COEF), jnp.float32)
    return jnp.clip(scales * vectors * COEF ** (-0.5), -8.0, 8.0)


def draw_projections(key, part):
    return projection_values(key).astype(jnp.bfloat16)


def draw_images(key, part):
    folded = jax.random.fold_in(key, 202)
    key_list = jax.random.split(folded, 2)
    row_scale = jnp.exp(jax.random.uniform(key_list[0], (PARTICLES, 1), jnp.float32, math.log(0.3), math.log(3.0)))
    values = row_scale * jax.random.truncated_normal(key_list[1], -6.0, 6.0, (PARTICLES, COEF), jnp.float32)
    return jnp.clip(values, -40.0, 40.0).astype(jnp.bfloat16)


def deal_out(rng, own, number, rows, number_of, top, bound, slope):
    ranking = jax.random.permutation(rng, number_of)
    crowded, usual = shares(number_of, rows * top, bound, slope, True), shares(number_of, rows * top, bound, slope, False)
    places = jnp.arange(number_of)

    def named(sizes, rotation):
        used = int((sizes > 0).sum())
        fixed = max(1, used // 4)
        passed = fixed + (places - fixed + rotation * (used - fixed)) % max(1, number_of - fixed)
        return jnp.zeros((number_of,), jnp.int32).at[ranking[jnp.where(places < fixed, places, passed)]].set(jnp.asarray(sizes, jnp.int32))

    sizes = jnp.where(number % 4 == 0, named(crowded, number // 4), named(usual, number - number // 4 - 1))
    mixed = jax.random.permutation(jax.random.fold_in(own, 3), number_of)
    giver, receiver = mixed[0:number_of // 2 * 2:2], mixed[1:number_of // 2 * 2:2]
    slack = jnp.minimum(sizes[giver] - 1, bound - sizes[receiver]) // 2
    slack = jnp.where((giver == ranking[0]) | (receiver == ranking[0]) | (sizes[receiver] == 0), 0, jnp.maximum(slack, 0))
    passed = jax.random.randint(jax.random.fold_in(own, 4), (number_of // 2,), 0, 1 << 20) % (slack + 1)
    sizes = sizes.at[giver].add(-passed).at[receiver].add(passed)
    members = jnp.searchsorted(jnp.cumsum(sizes), jnp.arange(rows * top), side="right").astype(jnp.int32)
    listing = members.reshape(top, rows).T
    listing = listing[jax.random.permutation(jax.random.fold_in(own, 1), rows)]
    rotation = jax.random.randint(jax.random.fold_in(own, 2), (rows, 1), 0, top)
    return jnp.take_along_axis(listing, (jnp.arange(top)[None, :] + rotation) % top, axis=1)


def shares(amount, total, bound, skew, full):
    loads = [(1 << 20) // math.isqrt(rank ** skew) + 1 for rank in range(1, amount + 1)]
    largest = bound if full else min(bound, max(-(-total // amount), total * loads[0] // sum(loads)))
    least = 1 if total - largest >= amount - 1 else 0
    holding, spare = [largest] + [least] * (amount - 1), total - largest - least * (amount - 1)
    while spare > 0:
        movable = [i for i in range(1, amount) if holding[i] < largest] or [i for i in range(1, amount) if holding[i] < bound]
        pool, remaining = sum([loads[i] for i in movable]), spare
        for i in movable:
            extra = min(bound - holding[i], max(1, remaining * loads[i] // pool), spare)
            holding[i] = holding[i] + extra
            spare = spare - extra
    return np.array(holding)


def setup_inputs(seed: int = 0, part: int = 0) -> dict:
    keys = jax.random.split(jax.random.key(seed), 5)
    part_keys = jax.random.split(jax.random.fold_in(keys[4], part), 5)
    images = draw_images(jax.random.fold_in(jax.random.fold_in(keys[4], part), 71), part)
    routes_keys = jax.random.split(jax.random.fold_in(part_keys[1], 1), PARTICLES // PART_DEV)
    routes_turns = jax.random.permutation(jax.random.fold_in(part_keys[1], 3), PARTICLES // PART_DEV)
    routes = jax.vmap(lambda own, number: deal_out(jax.random.fold_in(part_keys[1], 2), own, number, PART_DEV, N_READER, TOP, CAP, 2))(routes_keys, routes_turns).reshape((PARTICLES, TOP))
    projections = draw_projections(jax.random.fold_in(jax.random.fold_in(keys[4], part), 71), part)
    noise_weights = jnp.clip(jnp.exp(jax.random.uniform(part_keys[3], (COEF,), jnp.float32, math.log(0.3), math.log(3.0))), 0.3, 3.0)
    return dict(images=images, routes=routes, projections=projections, noise_weights=noise_weights)


def combine_stats(row_peaks, row_totals):
    highest = jnp.max(row_peaks, axis=-1)
    spread = row_totals * jnp.exp(row_peaks - highest[..., None])
    return highest + jnp.log(jnp.sum(spread, axis=-1))


def reference(images, routes, projections, noise_weights):
    scaled = projections.astype(jnp.float32) * noise_weights[None, None, :]
    weighted = scaled.astype(jnp.bfloat16)
    penalty = 0.5 * jnp.sum(scaled * projections.astype(jnp.float32), axis=2)
    row_count = N_READER * PART_DEV
    image_rows = images.reshape(N_BLK, row_count, COEF)
    route_rows = routes.reshape(N_BLK, row_count, TOP)
    group_numbers = jnp.arange(GROUPS, dtype=jnp.int32)
    row_numbers = jnp.arange(row_count, dtype=jnp.int32)

    def one_row(running, inputs):
        block_images, block_routes = inputs

        def score_group(group_id):
            member = jnp.any(block_routes == group_id, axis=1)
            ordering = jnp.argsort(jnp.where(member, 0, 1).astype(jnp.int32), stable=True)[:RECV].astype(jnp.int32)
            chosen = block_images[ordering]
            scores = jnp.dot(chosen, weighted[group_id].T, preferred_element_type=jnp.float32) - penalty[group_id][None, :]
            row_peak = jnp.max(scores, axis=1)
            row_total = jnp.sum(jnp.exp(scores - row_peak[:, None]), axis=1)
            full_peak = jnp.zeros((row_count,), jnp.float32).at[ordering].set(row_peak)
            full_total = jnp.zeros((row_count,), jnp.float32).at[ordering].set(row_total)
            return scores, ordering, member[ordering], full_peak, full_total

        score_table, order_table, live_table, peak_table, total_table = lax.map(score_group, group_numbers)
        picked_peaks = peak_table[block_routes, row_numbers[:, None]]
        picked_totals = total_table[block_routes, row_numbers[:, None]]
        particle_norm = combine_stats(picked_peaks, picked_totals)

        def back_group(inputs):
            scores, ordering, live_slot = inputs
            slot_norm = particle_norm[ordering]
            exponent = jnp.where(live_slot[:, None], scores - slot_norm[:, None], -jnp.inf)
            posterior = jnp.exp(exponent).astype(jnp.bfloat16)
            chosen = block_images[ordering]
            partial_value = jnp.dot(posterior.T, chosen, preferred_element_type=jnp.float32)
            return partial_value.astype(jnp.bfloat16)

        partials = lax.map(back_group, (score_table, order_table, live_table))
        partials = lax.optimization_barrier(partials)
        return running + partials.astype(jnp.float32), particle_norm

    initial = jnp.zeros((GROUPS, GREFS, COEF), jnp.float32)
    total_sums, norm_rows = lax.scan(one_row, initial, (image_rows, route_rows))
    return total_sums, norm_rows.reshape(PARTICLES)
```

```python
from functools import partial

import jax
import jax.numpy as jnp
from jax import lax
from jax.experimental import pallas as pl
from jax.experimental.pallas import tpu as pltpu
from jax.sharding import PartitionSpec as P

CHUNKS = 2
VMEM_BYTES = 48 * 1024 * 1024


def swap_bit(block, axis, bit):
    size = lax.axis_size(axis)
    return lax.ppermute(block, axis, [(i, i ^ bit) for i in range(size)])


def swap_gather(block, axis):
    size = lax.axis_size(axis)
    held = {0: block}
    bit = size // 2
    while bit:
        for k in list(held):
            held[k ^ bit] = swap_bit(held[k], axis, bit)
        bit //= 2
    return [held[k] for k in range(size)]


def line_gather(block, axis):
    size = lax.axis_size(axis)
    ahead, behind = [block], [block]
    for s in range(1, size):
        ahead.append(lax.ppermute(ahead[-1], axis, [(i, i + 1) for i in range(s - 1, size - 1)]))
        behind.append(lax.ppermute(behind[-1], axis, [(i, i - 1) for i in range(1, size - s + 1)]))
    return ahead, behind


def line_scatter(parts, axis):
    size = lax.axis_size(axis)
    up = down = None
    for s in range(1, size):
        send_up, send_down = parts[s], parts[size - s]
        if s > 1:
            send_up = add_rounded(send_up, up)
            send_down = add_rounded(send_down, down)
        up = lax.ppermute(send_up, axis, [(i, i + 1) for i in range(0, s) if i + 1 < size])
        down = lax.ppermute(send_down, axis, [(i, i - 1) for i in range(size - s, size) if i > 0])
    total = parts[0].astype(jnp.float32)
    if size > 1:
        total = total + up.astype(jnp.float32) + down.astype(jnp.float32)
    return total


def add_rounded(one, other):
    return (one.astype(jnp.float32) + other.astype(jnp.float32)).astype(jnp.bfloat16)


def score_kernel(readers, members, first, place_ref, *refs):
    refs = list(refs)
    image_refs = [refs.pop(0) for _ in range(readers)]
    ahead_refs = [refs.pop(0) for _ in range(members)]
    behind_refs = [None] + [refs.pop(0) for _ in range(members - 1)]
    noise_ref = refs.pop(0)
    earlier_ref = None if first else refs.pop(0)
    score_ref, all_ref, weighted_ref, penalty_ref = refs
    rows = image_refs[0].shape[0]
    count = ahead_refs[0].shape[0]
    reader, member = place_ref[0], place_ref[1]
    for k in range(readers):
        start = pl.multiple_of((reader ^ k) * rows, rows)
        all_ref[pl.ds(start, rows), :] = image_refs[k][...]
    noise = noise_ref[...]

    def weigh(s, ref):
        block = ref[...].astype(jnp.float32)
        scaled = block * noise
        weighted_ref[pl.ds(s * count, count), :] = scaled.astype(jnp.bfloat16)
        penalty_ref[pl.ds(s * count, count), :] = 0.5 * jnp.sum(
            scaled * block, axis=1, keepdims=True
        )

    weigh(0, ahead_refs[0])
    for s in range(1, members):

        @pl.when(member >= s)
        def _(s=s):
            weigh(s, ahead_refs[s])

        @pl.when(member < s)
        def _(s=s):
            weigh(s, behind_refs[members - s])

    scores = lax.dot_general(
        weighted_ref[...],
        all_ref[...],
        (((1,), (1,)), ((), ())),
        preferred_element_type=jnp.float32,
    )
    scores = scores - penalty_ref[...]
    if not first:
        scores = scores + earlier_ref[...]
    score_ref[...] = scores


def score_chunk(place, image_blocks, ahead, behind, noise, earlier):
    readers, members = len(image_blocks), len(ahead)
    rows, width = image_blocks[0].shape
    refs = ahead[0].shape[0] * members
    operands = [*image_blocks, *ahead, *behind[1:], noise]
    if earlier is not None:
        operands.append(earlier)
    vmem = pl.BlockSpec(memory_space=pltpu.VMEM)
    return pl.pallas_call(
        partial(score_kernel, readers, members, earlier is None),
        out_shape=(
            jax.ShapeDtypeStruct((refs, readers * rows), jnp.float32),
            jax.ShapeDtypeStruct((readers * rows, width), jnp.bfloat16),
        ),
        in_specs=[pl.BlockSpec(memory_space=pltpu.SMEM)] + [vmem] * len(operands),
        out_specs=(vmem, vmem),
        scratch_shapes=[
            pltpu.VMEM((refs, width), jnp.bfloat16),
            pltpu.VMEM((refs, 1), jnp.float32),
        ],
        compiler_params=pltpu.CompilerParams(vmem_limit_bytes=VMEM_BYTES),
        cost_estimate=pl.CostEstimate(
            flops=2 * refs * readers * rows * width,
            bytes_accessed=4 * readers * rows * width,
            transcendentals=0,
        ),
        name="scores",
    )(place, *operands)


def lse_kernel(score_ref, lse_ref):
    scores = score_ref[...]
    peak = jnp.max(scores, axis=0, keepdims=True)
    total = jnp.sum(jnp.exp(scores - peak), axis=0, keepdims=True)
    lse_ref[...] = peak + jnp.log(total)


def group_lse(scores):
    return pl.pallas_call(
        lse_kernel,
        out_shape=jax.ShapeDtypeStruct((1, scores.shape[1]), jnp.float32),
        name="group_lse",
    )(scores)


def posterior_kernel(readers, place_ref, score_ref, route_ref, *refs):
    lse_refs = refs[:readers]
    norm_ref, post_ref = refs[readers:]
    reader = place_ref[0]
    routes = route_ref[...]
    kept = []
    for k in range(readers):
        named = jnp.max(jnp.where(routes == (reader ^ k), 1.0, 0.0), axis=0, keepdims=True) > 0.0
        kept.append(jnp.where(named, lse_refs[k][...], -jnp.inf))
        if k == 0:
            mine = named
    highest = kept[0]
    for value in kept[1:]:
        highest = jnp.maximum(highest, value)
    spread = jnp.exp(kept[0] - highest)
    for value in kept[1:]:
        spread = spread + jnp.exp(value - highest)
    norm = highest + jnp.log(spread)
    norm_ref[...] = norm
    exponent = jnp.where(mine, score_ref[...] - norm, -jnp.inf)
    post_ref[...] = jnp.exp(exponent).astype(jnp.bfloat16)


def posteriors(place, scores, routes, lses):
    vmem = pl.BlockSpec(memory_space=pltpu.VMEM)
    return pl.pallas_call(
        partial(posterior_kernel, len(lses)),
        out_shape=(
            jax.ShapeDtypeStruct((1, scores.shape[1]), jnp.float32),
            jax.ShapeDtypeStruct(scores.shape, jnp.bfloat16),
        ),
        in_specs=[pl.BlockSpec(memory_space=pltpu.SMEM)] + [vmem] * (2 + len(lses)),
        out_specs=(vmem, vmem),
        name="posteriors",
    )(place, scores, routes, *lses)


def sums_kernel(members, post_ref, all_ref, *out_refs):
    sums = jnp.dot(post_ref[...], all_ref[...], preferred_element_type=jnp.float32)
    count = sums.shape[0] // members
    for s in range(members):
        out_refs[s][...] = sums[s * count : (s + 1) * count].astype(out_refs[s].dtype)


def sums_chunk(members, posterior, all_images):
    refs = posterior.shape[0]
    slots, width = all_images.shape
    tile = min(width, 1024)
    block = jax.ShapeDtypeStruct((refs // members, width), jnp.bfloat16)
    return pl.pallas_call(
        partial(sums_kernel, members),
        grid=(width // tile,),
        out_shape=(block,) * members,
        in_specs=[
            pl.BlockSpec((refs, slots), lambda i: (0, 0)),
            pl.BlockSpec((slots, tile), lambda i: (0, i)),
        ],
        out_specs=(pl.BlockSpec((refs // members, tile), lambda i: (0, i)),) * members,
        compiler_params=pltpu.CompilerParams(vmem_limit_bytes=VMEM_BYTES),
        cost_estimate=pl.CostEstimate(
            flops=2 * refs * slots * width,
            bytes_accessed=2 * slots * width,
            transcendentals=0,
        ),
        name="sums",
    )(posterior, all_images)


def on_device(images, routes, projections, noise_weights):
    readers = lax.axis_size("reader")
    members = lax.axis_size("blk")
    reader = lax.axis_index("reader")
    member = lax.axis_index("blk")
    place = jnp.stack([reader, member]).astype(jnp.int32)
    rows, half_width = images.shape
    width = half_width // CHUNKS
    projections = projections[0]
    noise = noise_weights.reshape(1, half_width)

    route_blocks = jnp.stack(swap_gather(routes.T, "reader"))
    order = jnp.arange(readers, dtype=jnp.int32) ^ reader
    all_routes = route_blocks[order].transpose(1, 0, 2).reshape(routes.shape[1], readers * rows)

    pieces = [slice(q * width, (q + 1) * width) for q in range(CHUNKS)]
    lines = [line_gather(projections[:, piece], "blk") for piece in pieces]
    gathered = [swap_gather(images[:, piece], "reader") for piece in pieces]
    scores = None
    all_images = []
    for piece, (ahead, behind), blocks in zip(pieces, lines, gathered):
        scores, every = score_chunk(place, blocks, ahead, behind, noise[:, piece], scores)
        all_images.append(every)
    if lax.axis_size("sub") > 1:
        scores = lax.psum(scores, "sub")
    mine = group_lse(scores)
    lses = [mine] + [swap_bit(mine, "reader", k) for k in range(1, readers)]
    norms, posterior = posteriors(place, scores, all_routes, lses)
    normalizer = lax.dynamic_slice(norms.reshape(-1), (reader * rows,), (rows,))
    totals = [
        line_scatter(sums_chunk(members, posterior, every), "blk") for every in all_images
    ]
    return (jnp.concatenate(totals, axis=1)[None], normalizer)


def solution(mesh):
    return jax.shard_map(
        on_device,
        mesh=mesh,
        in_specs=(
            P(("parts", "blk", "reader"), "sub"),
            P(("parts", "blk", "reader"), None),
            P(("parts", "reader"), "blk", "sub"),
            P(("parts", "sub")),
        ),
        out_specs=(P(("parts", "reader"), "blk", "sub"), P(("parts", "blk", "reader"))),
        check_vma=False,
    )
```

```python
from functools import partial

import jax
import jax.numpy as jnp
from jax import lax
from jax.experimental import pallas as pl
from jax.experimental.pallas import tpu as pltpu
from jax.sharding import PartitionSpec as P

PIECES = 2
TILE = 1024
VMEM_BYTES = 48 * 1024 * 1024
SMEM_SPEC = pl.BlockSpec(memory_space=pltpu.SMEM)
VMEM_SPEC = pl.BlockSpec(memory_space=pltpu.VMEM)


def relative(member, s, members):
    if members == 4:
        return member ^ s
    return lax.rem(member + (members - s), members)


def swap_bits(block, axis, bits):
    return lax.ppermute(block, axis, [(i, i ^ bits) for i in range(lax.axis_size(axis))])


def add_rounded(one, other):
    return (one.astype(jnp.float32) + other.astype(jnp.float32)).astype(jnp.bfloat16)


def pair_scatter(parts, axis):
    member = lax.axis_index(axis)
    is_end = (member == 0) | (member == 3)
    sides = [(0, 1), (1, 0), (2, 3), (3, 2)]
    middle = [(1, 2), (2, 1), (0, 0), (3, 3)]
    for_far_end = lax.ppermute(parts[3], axis, sides)
    across_end = lax.ppermute(add_rounded(parts[2], for_far_end), axis, middle)
    for_far_middle = lax.ppermute(parts[2], axis, sides)
    across_middle = lax.ppermute(add_rounded(parts[3], for_far_middle), axis, middle)
    near = jnp.where(is_end, parts[1], add_rounded(parts[1], across_end))
    from_side = lax.ppermute(near, axis, sides)
    total = parts[0].astype(jnp.float32) + from_side.astype(jnp.float32)
    return total + jnp.where(is_end, 0.0, across_middle.astype(jnp.float32))


def line_scatter(parts, axis):
    size = lax.axis_size(axis)
    up = down = None
    for s in range(1, size):
        send_up, send_down = parts[s], parts[size - s]
        if s > 1:
            send_up = add_rounded(send_up, up)
            send_down = add_rounded(send_down, down)
        up = lax.ppermute(send_up, axis, [(i, i + 1) for i in range(0, s) if i + 1 < size])
        down = lax.ppermute(send_down, axis, [(i, i - 1) for i in range(size - s, size) if i > 0])
    total = parts[0].astype(jnp.float32)
    if size > 1:
        total = total + up.astype(jnp.float32) + down.astype(jnp.float32)
    return total


def column_lse(scores):
    peak = jnp.max(scores, axis=0, keepdims=True)
    total = jnp.sum(jnp.exp(scores - peak), axis=0, keepdims=True)
    return peak + jnp.log(total)


def score_kernel(
    members, finish, place_ref, image_ref, projection_ref, noise_ref, score_ref, lse_ref, weighted_ref
):
    step = pl.program_id(0)
    member = place_ref[1]
    count = projection_ref.shape[1]
    noise = noise_ref[...]

    @pl.when(step == 0)
    def _():
        score_ref[...] = jnp.zeros_like(score_ref)

    penalties = []
    for s in range(members):
        block = projection_ref[relative(member, s, members)].astype(jnp.float32)
        scaled = block * noise
        weighted_ref[pl.ds(s * count, count), :] = scaled.astype(jnp.bfloat16)
        penalties.append(0.5 * jnp.sum(scaled * block, axis=1, keepdims=True))
    scores = lax.dot_general(
        weighted_ref[...],
        image_ref[...],
        (((1,), (1,)), ((), ())),
        preferred_element_type=jnp.float32,
    )
    score_ref[...] += scores - jnp.concatenate(penalties, axis=0)

    @pl.when(step == pl.num_programs(0) - 1)
    def _():
        if finish:
            lse_ref[...] = column_lse(score_ref[...])


def all_scores(place, images, projections, noise, finish):
    members, count, width = projections.shape
    slots = images.shape[0]
    refs = members * count
    tile = min(TILE, width)
    return pl.pallas_call(
        partial(score_kernel, members, finish),
        grid=(width // tile,),
        out_shape=(
            jax.ShapeDtypeStruct((refs, slots), jnp.float32),
            jax.ShapeDtypeStruct((1, slots), jnp.float32),
        ),
        in_specs=[
            SMEM_SPEC,
            pl.BlockSpec((slots, tile), lambda i: (0, i)),
            pl.BlockSpec((members, count, tile), lambda i: (0, 0, i)),
            pl.BlockSpec((1, tile), lambda i: (0, i)),
        ],
        out_specs=(
            pl.BlockSpec((refs, slots), lambda i: (0, 0)),
            pl.BlockSpec((1, slots), lambda i: (0, 0)),
        ),
        scratch_shapes=[pltpu.VMEM((refs, tile), jnp.bfloat16)],
        compiler_params=pltpu.CompilerParams(vmem_limit_bytes=VMEM_BYTES),
        cost_estimate=pl.CostEstimate(
            flops=2 * refs * slots * width,
            bytes_accessed=2 * slots * width,
            transcendentals=0,
        ),
        name="scores",
    )(place, images, projections, noise)


def lse_kernel(score_ref, lse_ref):
    lse_ref[...] = column_lse(score_ref[...])


def group_lse(scores):
    return pl.pallas_call(
        lse_kernel,
        out_shape=jax.ShapeDtypeStruct((1, scores.shape[1]), jnp.float32),
        name="group_lse",
    )(scores)


def sums_kernel(readers, members, place_ref, score_ref, route_ref, *refs):
    lse_refs = refs[:readers]
    image_ref = refs[readers]
    out_refs = refs[readers + 1 : readers + 1 + members]
    norm_ref, post_ref = refs[readers + 1 + members :]

    @pl.when(pl.program_id(0) == 0)
    def _():
        reader = place_ref[0]
        routes = route_ref[...]
        kept = []
        for k in range(readers):
            hits = jnp.where(routes == (reader ^ k), 1.0, 0.0)
            named = jnp.max(hits, axis=0, keepdims=True) > 0.0
            kept.append(jnp.where(named, lse_refs[k][...], -jnp.inf))
            if k == 0:
                mine = named
        highest = kept[0]
        for value in kept[1:]:
            highest = jnp.maximum(highest, value)
        spread = jnp.exp(kept[0] - highest)
        for value in kept[1:]:
            spread = spread + jnp.exp(value - highest)
        norm = highest + jnp.log(spread)
        norm_ref[...] = norm
        exponent = jnp.where(mine, score_ref[...] - norm, -jnp.inf)
        post_ref[...] = jnp.exp(exponent).astype(jnp.bfloat16)

    sums = jnp.dot(post_ref[...], image_ref[...], preferred_element_type=jnp.float32)
    count = sums.shape[0] // members
    for s in range(members):
        out_refs[s][...] = sums[s * count : (s + 1) * count].astype(out_refs[s].dtype)


def group_sums(members, place, scores, routes, lses, images, piece, pieces):
    refs = scores.shape[0]
    slots, full = images.shape
    width = full // pieces
    tile = min(TILE, width)
    steps = width // tile
    block = jax.ShapeDtypeStruct((refs // members, width), jnp.bfloat16)
    whole = lambda i: (0, 0)
    outs = pl.pallas_call(
        partial(sums_kernel, len(lses), members),
        grid=(steps,),
        out_shape=(block,) * members + (jax.ShapeDtypeStruct((1, slots), jnp.float32),),
        in_specs=[
            SMEM_SPEC,
            pl.BlockSpec((refs, slots), whole),
            pl.BlockSpec(routes.shape, whole),
            *([pl.BlockSpec((1, slots), whole)] * len(lses)),
            pl.BlockSpec((slots, tile), lambda i: (0, piece * steps + i)),
        ],
        out_specs=(pl.BlockSpec((refs // members, tile), lambda i: (0, i)),) * members
        + (pl.BlockSpec((1, slots), whole),),
        scratch_shapes=[pltpu.VMEM((refs, slots), jnp.bfloat16)],
        compiler_params=pltpu.CompilerParams(vmem_limit_bytes=VMEM_BYTES),
        cost_estimate=pl.CostEstimate(
            flops=2 * refs * slots * width,
            bytes_accessed=2 * slots * width,
            transcendentals=0,
        ),
        name="sums",
    )(place, scores, routes, *lses, images)
    return outs[:members], outs[members]


def on_device(images, routes, projections, noise_weights):
    readers = lax.axis_size("reader")
    members = lax.axis_size("blk")
    reader = lax.axis_index("reader")
    place = jnp.stack([reader, lax.axis_index("blk")]).astype(jnp.int32)
    rows, width = images.shape
    noise = noise_weights.reshape(1, width)

    route_blocks = jnp.stack([routes.T] + [swap_bits(routes.T, "reader", k) for k in range(1, readers)])
    order = jnp.arange(readers, dtype=jnp.int32) ^ reader
    all_routes = route_blocks[order].transpose(1, 0, 2).reshape(routes.shape[1], readers * rows)

    all_images = lax.all_gather(images, "reader", axis=0, tiled=True)
    every = lax.all_gather(projections[0], "blk", axis=0)
    split = lax.axis_size("sub") > 1
    scores, mine = all_scores(place, all_images, every, noise, not split)
    if split:
        scores = lax.psum(scores, "sub")
        mine = group_lse(scores)
    lses = [mine] + [swap_bits(mine, "reader", k) for k in range(1, readers)]
    scatter = pair_scatter if members == 4 else line_scatter
    totals = []
    for piece in range(PIECES):
        parts, norms = group_sums(
            members, place, scores, all_routes, lses, all_images, piece, PIECES
        )
        totals.append(scatter(parts, "blk"))
    normalizer = lax.dynamic_slice(norms.reshape(-1), (reader * rows,), (rows,))
    return (jnp.concatenate(totals, axis=1)[None], normalizer)


def solution(mesh):
    return jax.shard_map(
        on_device,
        mesh=mesh,
        in_specs=(
            P(("parts", "blk", "reader"), "sub"),
            P(("parts", "blk", "reader"), None),
            P(("parts", "reader"), "blk", "sub"),
            P(("parts", "sub")),
        ),
        out_specs=(P(("parts", "reader"), "blk", "sub"), P(("parts", "blk", "reader"))),
        check_vma=False,
    )
```

```python
from functools import partial

import jax
import jax.numpy as jnp
from jax import lax
from jax.experimental import pallas as pl
from jax.experimental.pallas import tpu as pltpu
from jax.sharding import PartitionSpec as P

EIGHTHS = (4, 4)
FAR_PARTS = (1, 2)
TILE = 1024
VMEM_BYTES = 48 * 1024 * 1024
SMEM_SPEC = pl.BlockSpec(memory_space=pltpu.SMEM)
VMEM_SPEC = pl.BlockSpec(memory_space=pltpu.VMEM)


def swap_bits(block, axis, bits):
    return lax.ppermute(block, axis, [(i, i ^ bits) for i in range(lax.axis_size(axis))])


def add_rounded(one, other):
    return (one.astype(jnp.float32) + other.astype(jnp.float32)).astype(jnp.bfloat16)


def pair_scatter(pieces, axis):
    member = lax.axis_index(axis)
    is_end = (member == 0) | (member == 3)
    sides = [(0, 1), (1, 0), (2, 3), (3, 2)]
    middle = [(1, 2), (2, 1), (0, 0), (3, 3)]
    for_far_end = [lax.ppermute(parts[3], axis, sides) for parts in pieces]
    second = lax.optimization_barrier([parts[2] for parts in pieces])
    for_far_middle = [lax.ppermute(part, axis, sides) for part in second]
    totals = []
    for parts, part, end, mid in zip(pieces, second, for_far_end, for_far_middle):
        across_end = lax.ppermute(add_rounded(part, end), axis, middle)
        across_middle = lax.ppermute(add_rounded(parts[3], mid), axis, middle)
        near = jnp.where(is_end, parts[1], add_rounded(parts[1], across_end))
        from_side = lax.ppermute(near, axis, sides)
        total = parts[0].astype(jnp.float32) + from_side.astype(jnp.float32)
        totals.append(total + jnp.where(is_end, 0.0, across_middle.astype(jnp.float32)))
    return totals


def line_scatter(pieces, axis):
    return [line_sum(parts, axis) for parts in pieces]


def line_sum(parts, axis):
    size = lax.axis_size(axis)
    up = down = None
    for s in range(1, size):
        send_up, send_down = parts[s], parts[size - s]
        if s > 1:
            send_up = add_rounded(send_up, up)
            send_down = add_rounded(send_down, down)
        up = lax.ppermute(send_up, axis, [(i, i + 1) for i in range(0, s) if i + 1 < size])
        down = lax.ppermute(send_down, axis, [(i, i - 1) for i in range(size - s, size) if i > 0])
    total = parts[0].astype(jnp.float32)
    if size > 1:
        total = total + up.astype(jnp.float32) + down.astype(jnp.float32)
    return total


def column_lse(scores):
    peak = jnp.max(scores, axis=0, keepdims=True)
    total = jnp.sum(jnp.exp(scores - peak), axis=0, keepdims=True)
    return peak + jnp.log(total)


def place_blocks(place_ref, groups, all_ref, steps):
    rows = groups[0][0].shape[0]
    step = pl.program_id(0)
    for k, refs in enumerate(groups):
        start = pl.multiple_of((place_ref[0] ^ k) * rows, rows)
        each = steps // len(refs)
        for i, ref in enumerate(refs):
            if len(refs) == 1:
                all_ref[pl.ds(start, rows), :] = ref[...]
                continue

            @pl.when((step >= i * each) & (step < (i + 1) * each))
            def _(start=start, ref=ref):
                all_ref[pl.ds(start, rows), :] = ref[...]


def take_groups(refs, counts):
    return [[refs.pop(0) for _ in range(n)] for n in counts]


def flat(groups):
    return [one for group in groups for one in group]


def score_kernel(counts, steps, first, finish, place_ref, *refs):
    parts, pairs = counts
    refs = list(refs)
    image_refs = take_groups(refs, parts)
    pair_refs = take_groups(refs, pairs)
    noise_ref = refs.pop(0)
    earlier_ref = None if first else refs.pop(0)
    score_ref, lse_ref, all_ref, weighted_ref, penalty_ref, sum_ref = refs
    step = pl.program_id(0)
    count = pair_refs[0][0].shape[0]
    noise = noise_ref[...]

    @pl.when(step == 0)
    def _():
        sum_ref[...] = jnp.zeros_like(sum_ref)
        penalty_ref[...] = jnp.zeros_like(penalty_ref)

    place_blocks(place_ref, image_refs, all_ref, steps)

    def weigh(s, ref):
        block = ref[...].astype(jnp.float32)
        scaled = block * noise
        weighted_ref[pl.ds(s * count, count), :] = scaled.astype(jnp.bfloat16)
        penalty_ref[pl.ds(s * count, count), :] += 0.5 * jnp.sum(
            scaled * block, axis=1, keepdims=True
        )

    for s, pair in enumerate(pair_refs):
        if len(pair) == 1:
            weigh(s, pair[0])
            continue

        @pl.when(place_ref[1] == 1)
        def _(s=s, pair=pair):
            weigh(s, pair[0])

        @pl.when(place_ref[1] == 0)
        def _(s=s, pair=pair):
            weigh(s, pair[1])

    sum_ref[...] += lax.dot_general(
        all_ref[...],
        weighted_ref[...],
        (((1,), (1,)), ((), ())),
        preferred_element_type=jnp.float32,
    )

    @pl.when(step == pl.num_programs(0) - 1)
    def _():
        scores = sum_ref[...].T - penalty_ref[...]
        if not first:
            scores = scores + earlier_ref[...]
        score_ref[...] = scores
        if finish:
            lse_ref[...] = column_lse(scores)


def column_specs(groups, tile, piece):
    steps = (piece.stop - piece.start) // tile
    specs = []
    for group in groups:
        for i, array in enumerate(group):
            rows, width = array.shape
            if len(group) == 1 and width >= piece.stop:
                index = lambda j: (0, piece.start // tile + j)
            else:
                each = width // tile
                index = lambda j, i=i, each=each: (0, jnp.clip(j - i * each, 0, each - 1))
            specs.append(pl.BlockSpec((rows, tile), index))
    return specs


def score_piece(place, piece, images, pairs, noise, earlier, finish):
    tile = min(TILE, piece.stop - piece.start)
    steps = (piece.stop - piece.start) // tile
    rows = images[0][0].shape[0]
    refs = len(pairs) * pairs[0][0].shape[0]
    slots = len(images) * rows
    blocks = [*flat(images), *flat(pairs), noise]
    specs = column_specs(images, tile, piece) + [
        spec for one in flat(pairs) + [noise] for spec in column_specs([[one]], tile, piece)
    ]
    whole = pl.BlockSpec((refs, slots), lambda i: (0, 0))
    if earlier is not None:
        blocks.append(earlier)
        specs.append(whole)
    return pl.pallas_call(
        partial(
            score_kernel,
            ([len(group) for group in images], [len(pair) for pair in pairs]),
            steps,
            earlier is None,
            finish,
        ),
        grid=(steps,),
        out_shape=(
            jax.ShapeDtypeStruct((refs, slots), jnp.float32),
            jax.ShapeDtypeStruct((1, slots), jnp.float32),
        ),
        in_specs=[SMEM_SPEC, *specs],
        out_specs=(whole, pl.BlockSpec((1, slots), lambda i: (0, 0))),
        scratch_shapes=[
            pltpu.VMEM((slots, tile), jnp.bfloat16),
            pltpu.VMEM((refs, tile), jnp.bfloat16),
            pltpu.VMEM((refs, 1), jnp.float32),
            pltpu.VMEM((slots, refs), jnp.float32),
        ],
        compiler_params=pltpu.CompilerParams(vmem_limit_bytes=VMEM_BYTES),
        cost_estimate=pl.CostEstimate(
            flops=2 * refs * slots * tile * steps,
            bytes_accessed=2 * slots * tile * steps,
            transcendentals=0,
        ),
        name="scores",
    )(place, *blocks)


def lse_kernel(score_ref, lse_ref):
    lse_ref[...] = column_lse(score_ref[...])


def group_lse(scores):
    return pl.pallas_call(
        lse_kernel,
        out_shape=jax.ShapeDtypeStruct((1, scores.shape[1]), jnp.float32),
        name="group_lse",
    )(scores)


def sums_kernel(parts, steps, members, place_ref, score_ref, route_ref, *refs):
    readers = len(parts)
    refs = list(refs)
    lse_refs = [refs.pop(0) for _ in range(readers)]
    image_refs = take_groups(refs, parts)
    out_refs = [refs.pop(0) for _ in range(members)]
    norm_ref, post_ref, all_ref = refs

    @pl.when(pl.program_id(0) == 0)
    def _():
        reader = place_ref[0]
        routes = route_ref[...]
        kept = []
        for k in range(readers):
            hits = jnp.where(routes == (reader ^ k), 1.0, 0.0)
            named = jnp.max(hits, axis=0, keepdims=True) > 0.0
            kept.append(jnp.where(named, lse_refs[k][...], -jnp.inf))
            if k == 0:
                mine = named
        highest = kept[0]
        for value in kept[1:]:
            highest = jnp.maximum(highest, value)
        spread = jnp.exp(kept[0] - highest)
        for value in kept[1:]:
            spread = spread + jnp.exp(value - highest)
        norm = highest + jnp.log(spread)
        norm_ref[...] = norm
        exponent = jnp.where(mine, score_ref[...] - norm, -jnp.inf)
        post_ref[...] = jnp.exp(exponent).astype(jnp.bfloat16)

    place_blocks(place_ref, image_refs, all_ref, steps)
    sums = jnp.dot(post_ref[...], all_ref[...], preferred_element_type=jnp.float32)
    count = sums.shape[0] // members
    for s in range(members):
        out_refs[s][...] = sums[s * count : (s + 1) * count].astype(out_refs[s].dtype)


def sums_piece(members, place, scores, routes, lses, images, piece):
    refs, slots = scores.shape
    width = piece.stop - piece.start
    tile = min(TILE, width)
    block = jax.ShapeDtypeStruct((refs // members, width), jnp.bfloat16)
    whole = lambda i: (0, 0)
    outs = pl.pallas_call(
        partial(sums_kernel, [len(group) for group in images], width // tile, members),
        grid=(width // tile,),
        out_shape=(block,) * members + (jax.ShapeDtypeStruct((1, slots), jnp.float32),),
        in_specs=[
            SMEM_SPEC,
            pl.BlockSpec((refs, slots), whole),
            pl.BlockSpec(routes.shape, whole),
            *([pl.BlockSpec((1, slots), whole)] * len(lses)),
            *column_specs(images, tile, piece),
        ],
        out_specs=(pl.BlockSpec((refs // members, tile), lambda i: (0, i)),) * members
        + (pl.BlockSpec((1, slots), whole),),
        scratch_shapes=[
            pltpu.VMEM((refs, slots), jnp.bfloat16),
            pltpu.VMEM((slots, tile), jnp.bfloat16),
        ],
        compiler_params=pltpu.CompilerParams(vmem_limit_bytes=VMEM_BYTES),
        cost_estimate=pl.CostEstimate(
            flops=2 * refs * slots * width,
            bytes_accessed=2 * slots * width,
            transcendentals=0,
        ),
        name="sums",
    )(place, scores, routes, *lses, *flat(images))
    return outs[:members], outs[members]


def swap_gather(block, axis, bit):
    held = {0: block}
    while bit:
        for k in list(held):
            held[k ^ bit] = swap_bits(held[k], axis, bit)
        bit //= 2
    return [held[k] for k in range(len(held))]


def pair_gather(block, axis):
    sides = [(0, 1), (1, 0), (2, 3), (3, 2)]
    middle = [(1, 2), (2, 1), (0, 0), (3, 3)]
    side, across = lax.optimization_barrier(
        (lax.ppermute(block, axis, sides), lax.ppermute(block, axis, middle))
    )
    far, across_far = lax.optimization_barrier(
        (lax.ppermute(across, axis, sides), lax.ppermute(side, axis, middle))
    )
    end = lax.ppermute(across_far, axis, sides)
    return [[block], [side], [far, across_far], [end, across]]


def line_gather(block, axis):
    size, member = lax.axis_size(axis), lax.axis_index(axis)
    ahead, behind = [block], [block]
    for s in range(1, size):
        ahead.append(lax.ppermute(ahead[-1], axis, [(i, i + 1) for i in range(s - 1, size - 1)]))
        behind.append(lax.ppermute(behind[-1], axis, [(i, i - 1) for i in range(1, size - s + 1)]))
    blocks = [block]
    for s in range(1, size):
        blocks.append(jnp.where(member >= s, ahead[s], behind[size - s]))
    return [[one] for one in blocks]


def cut(width, eighths):
    edges = [0]
    for part in eighths:
        edges.append(edges[-1] + width * part // 8)
    return [slice(a, b) for a, b in zip(edges, edges[1:])]


def on_device(images, routes, projections, noise_weights):
    readers = lax.axis_size("reader")
    members = lax.axis_size("blk")
    reader = lax.axis_index("reader")
    member = lax.axis_index("blk")
    is_end = (member == 0) | (member == members - 1)
    place = jnp.stack([reader, is_end.astype(jnp.int32)]).astype(jnp.int32)
    rows, width = images.shape
    noise = noise_weights.reshape(1, width)
    pieces = cut(width, EIGHTHS)

    far_blocks = []
    for piece, parts in zip(pieces, FAR_PARTS):
        first = swap_bits(images[:, piece], "reader", readers // 2)
        step = first.shape[1] // parts
        cuts = [
            swap_gather(first[:, i * step : (i + 1) * step], "reader", readers // 4)
            for i in range(parts)
        ]
        far_blocks.append([[first]] + [list(group) for group in list(zip(*cuts))[1:]])
    line = (pair_gather if members == 4 else line_gather)(projections[0], "blk")
    near_blocks = [[one] for one in swap_gather(images, "reader", readers // 4)]

    route_blocks = jnp.stack([routes.T] + [swap_bits(routes.T, "reader", k) for k in range(1, readers)])
    order = jnp.arange(readers, dtype=jnp.int32) ^ reader
    all_routes = route_blocks[order].transpose(1, 0, 2).reshape(routes.shape[1], readers * rows)

    split = lax.axis_size("sub") > 1
    scores = None
    for q, piece in enumerate(pieces):
        finish = q == len(pieces) - 1 and not split
        scores, mine = score_piece(
            place, piece, near_blocks + far_blocks[q], line, noise, scores, finish
        )
    if split:
        scores = lax.psum(scores, "sub")
        mine = group_lse(scores)
    lses = [mine] + [swap_bits(mine, "reader", k) for k in range(1, readers)]
    scatter = pair_scatter if members == 4 else line_scatter
    sums = []
    for q, piece in enumerate(pieces):
        parts, norms = sums_piece(
            members, place, scores, all_routes, lses, near_blocks + far_blocks[q], piece
        )
        sums.append(parts)
    totals = scatter(sums, "blk")
    normalizer = lax.dynamic_slice(norms.reshape(-1), (reader * rows,), (rows,))
    return (jnp.concatenate(totals, axis=1)[None], normalizer)


def solution(mesh):
    return jax.shard_map(
        on_device,
        mesh=mesh,
        in_specs=(
            P(("parts", "blk", "reader"), "sub"),
            P(("parts", "blk", "reader"), None),
            P(("parts", "reader"), "blk", "sub"),
            P(("parts", "sub")),
        ),
        out_specs=(P(("parts", "reader"), "blk", "sub"), P(("parts", "blk", "reader"))),
        check_vma=False,
    )
```

```python
from functools import partial

import jax
import jax.numpy as jnp
from jax import lax
from jax.experimental import pallas as pl
from jax.experimental.pallas import tpu as pltpu
from jax.sharding import PartitionSpec as P

VMEM_BYTES = 24 * 1024 * 1024
SMEM_SPEC = pl.BlockSpec(memory_space=pltpu.SMEM)
VMEM_SPEC = pl.BlockSpec(memory_space=pltpu.VMEM)
SIDES = [(0, 1), (1, 0), (2, 3), (3, 2)]
MIDDLE = [(1, 2), (2, 1), (0, 0), (3, 3)]


def swap_bits(block, axis, bits):
    return lax.ppermute(block, axis, [(i, i ^ bits) for i in range(lax.axis_size(axis))])


def swap_gather(block, axis, bit):
    held = {0: block}
    while bit:
        for k in list(held):
            held[k ^ bit] = swap_bits(held[k], axis, bit)
        bit //= 2
    return [held[k] for k in range(len(held))]


def add_rounded(one, other):
    return (one.astype(jnp.float32) + other.astype(jnp.float32)).astype(jnp.bfloat16)


def staged_gather(block, images, near_bits, far_bit):
    rows = images.shape[0]
    third = rows // 3
    thirds = [images[i * third : (i + 1) * third] for i in range(3)]
    near = swap_gather(images, "reader", near_bits)
    side = lax.ppermute(block, "blk", SIDES)
    across = lax.ppermute(block, "blk", MIDDLE)
    first = swap_bits(thirds[0], "reader", far_bit)
    side, across, first, thirds[1] = lax.optimization_barrier((side, across, first, thirds[1]))
    far = lax.ppermute(across, "blk", SIDES)
    across_far = lax.ppermute(side, "blk", MIDDLE)
    second = swap_bits(thirds[1], "reader", far_bit)
    firsts = swap_gather(first, "reader", near_bits)
    far, across_far, second, thirds[2], near, firsts = lax.optimization_barrier(
        (far, across_far, second, thirds[2], near, firsts)
    )
    end = lax.ppermute(across_far, "blk", SIDES)
    third = swap_bits(thirds[2], "reader", far_bit)
    seconds = swap_gather(second, "reader", near_bits)
    end, third, seconds = lax.optimization_barrier((end, third, seconds))
    lasts = swap_gather(third, "reader", near_bits)
    line = [[block], [side], [far, across_far], [end, across]]
    return line, [[one] for one in near] + [list(group) for group in zip(firsts, seconds, lasts)]


def plain_gather(block, images, near_bits, far_bit):
    near = swap_gather(images, "reader", near_bits)
    far = swap_gather(swap_bits(images, "reader", far_bit), "reader", near_bits)
    return line_gather(block, "blk"), [[one] for one in near + far]


def line_gather(block, axis):
    size, member = lax.axis_size(axis), lax.axis_index(axis)
    ahead, behind = [block], [block]
    for s in range(1, size):
        ahead.append(lax.ppermute(ahead[-1], axis, [(i, i + 1) for i in range(s - 1, size - 1)]))
        behind.append(lax.ppermute(behind[-1], axis, [(i, i - 1) for i in range(1, size - s + 1)]))
    blocks = [block]
    for s in range(1, size):
        blocks.append(jnp.where(member >= s, ahead[s], behind[size - s]))
    return [[one] for one in blocks]


def pair_scatter(pieces, axis):
    member = lax.axis_index(axis)
    is_end = (member == 0) | (member == 3)
    totals, across_end = [], None
    for parts in pieces:
        for_far_end = lax.ppermute(parts[3], axis, SIDES)
        for_far_middle = lax.ppermute(parts[2], axis, SIDES)
        if across_end is not None:
            for_far_end, for_far_middle, _ = lax.optimization_barrier(
                (for_far_end, for_far_middle, across_end)
            )
        across_end = lax.ppermute(add_rounded(parts[2], for_far_end), axis, MIDDLE)
        across_middle = lax.ppermute(add_rounded(parts[3], for_far_middle), axis, MIDDLE)
        near = jnp.where(is_end, parts[1], add_rounded(parts[1], across_end))
        from_side = lax.ppermute(near, axis, SIDES)
        total = parts[0].astype(jnp.float32) + from_side.astype(jnp.float32)
        totals.append(total + jnp.where(is_end, 0.0, across_middle.astype(jnp.float32)))
    return totals


def line_scatter(pieces, axis):
    return [line_sum(parts, axis) for parts in pieces]


def line_sum(parts, axis):
    size = lax.axis_size(axis)
    up = down = None
    for s in range(1, size):
        send_up, send_down = parts[s], parts[size - s]
        if s > 1:
            send_up = add_rounded(send_up, up)
            send_down = add_rounded(send_down, down)
        up = lax.ppermute(send_up, axis, [(i, i + 1) for i in range(0, s) if i + 1 < size])
        down = lax.ppermute(send_down, axis, [(i, i - 1) for i in range(size - s, size) if i > 0])
    total = parts[0].astype(jnp.float32)
    if size > 1:
        total = total + up.astype(jnp.float32) + down.astype(jnp.float32)
    return total


def column_lse(scores):
    peak = jnp.max(scores, axis=0, keepdims=True)
    total = jnp.sum(jnp.exp(scores - peak), axis=0, keepdims=True)
    return peak + jnp.log(total)


def take_groups(refs, counts):
    return [[refs.pop(0) for _ in range(n)] for n in counts]


def flat(groups):
    return [one for group in groups for one in group]


def score_kernel(counts, piece, first, finish, place_ref, *refs):
    image_counts, pair_counts = counts
    refs = list(refs)
    image_refs = take_groups(refs, image_counts)
    pair_refs = take_groups(refs, pair_counts)
    noise_ref = refs.pop(0)
    extra_ref = refs.pop(0)
    score_ref, all_ref, small_ref, weighted_ref, penalty_ref = refs
    reader = place_ref[0]
    count = pair_refs[0][0].shape[0]
    rows = image_refs[0][0].shape[0]
    width = piece.stop - piece.start

    def columns(ref):
        return ref[:, piece] if ref.shape[1] > width else ref[...]

    for k, group in enumerate(image_refs):
        each = rows // len(group)
        for i, ref in enumerate(group):
            start = pl.multiple_of((reader ^ k) * rows + i * each, each)
            all_ref[pl.ds(start, each), :] = columns(ref)
    noise = columns(noise_ref)

    def weigh(s, ref):
        block = columns(ref).astype(jnp.float32)
        scaled = block * noise
        weighted_ref[s * count : (s + 1) * count, :] = scaled.astype(jnp.bfloat16)
        penalty_ref[s * count : (s + 1) * count, :] = 0.5 * jnp.sum(
            scaled * block, axis=1, keepdims=True
        )

    for s, pair in enumerate(pair_refs):
        if len(pair) == 1:
            weigh(s, pair[0])
            continue

        @pl.when(place_ref[1] == 1)
        def _(s=s, pair=pair):
            weigh(s, pair[0])

        @pl.when(place_ref[1] == 0)
        def _(s=s, pair=pair):
            weigh(s, pair[1])

    scores = lax.dot_general(
        weighted_ref[...],
        all_ref[...],
        (((1,), (1,)), ((), ())),
        preferred_element_type=jnp.float32,
    )
    scores = scores - penalty_ref[...]
    if first:
        routes = extra_ref[...]
        for k in range(small_ref.shape[0]):
            hits = jnp.where(routes == (reader ^ k), 1.0, 0.0)
            small_ref[k : k + 1, :] = jnp.max(hits, axis=0, keepdims=True)
    else:
        scores = scores + extra_ref[...]
    score_ref[...] = scores
    if finish:
        small_ref[...] = column_lse(scores)


def score_piece(place, piece, pairs, images, noise, routes, earlier, finish):
    width = piece.stop - piece.start
    rows = images[0][0].shape[0]
    refs = len(pairs) * pairs[0][0].shape[0]
    slots = len(images) * rows
    first = earlier is None
    operands = [*flat(images), *flat(pairs), noise, routes if first else earlier]
    return pl.pallas_call(
        partial(
            score_kernel,
            ([len(group) for group in images], [len(pair) for pair in pairs]),
            piece,
            first,
            finish,
        ),
        out_shape=(
            jax.ShapeDtypeStruct((refs, slots), jnp.float32),
            jax.ShapeDtypeStruct((slots, width), jnp.bfloat16),
            jax.ShapeDtypeStruct((len(images) if first else 1, slots), jnp.float32),
        ),
        in_specs=[SMEM_SPEC] + [VMEM_SPEC] * len(operands),
        out_specs=(VMEM_SPEC,) * 3,
        scratch_shapes=[
            pltpu.VMEM((refs, width), jnp.bfloat16),
            pltpu.VMEM((refs, 1), jnp.float32),
        ],
        compiler_params=pltpu.CompilerParams(vmem_limit_bytes=VMEM_BYTES),
        cost_estimate=pl.CostEstimate(
            flops=refs * slots * width // 8,
            bytes_accessed=slots * width // 8,
            transcendentals=0,
        ),
        name="scores",
    )(place, *operands)


def lse_kernel(score_ref, lse_ref):
    lse_ref[...] = column_lse(score_ref[...])


def group_lse(scores):
    return pl.pallas_call(
        lse_kernel,
        out_shape=jax.ShapeDtypeStruct((1, scores.shape[1]), jnp.float32),
        name="group_lse",
    )(scores)


def emit_sums(posterior, all_ref, out_refs):
    sums = jnp.dot(posterior, all_ref[...], preferred_element_type=jnp.float32)
    count = sums.shape[0] // len(out_refs)
    for s, out_ref in enumerate(out_refs):
        out_ref[...] = sums[s * count : (s + 1) * count].astype(out_ref.dtype)


def first_sums_kernel(readers, members, score_ref, mask_ref, *refs):
    lse_refs = refs[:readers]
    all_ref = refs[readers]
    out_refs = refs[readers + 1 : readers + 1 + members]
    norm_ref, post_ref = refs[readers + 1 + members :]
    kept = []
    for k in range(readers):
        kept.append(jnp.where(mask_ref[k : k + 1, :] > 0.0, lse_refs[k][...], -jnp.inf))
    highest = kept[0]
    for value in kept[1:]:
        highest = jnp.maximum(highest, value)
    spread = jnp.exp(kept[0] - highest)
    for value in kept[1:]:
        spread = spread + jnp.exp(value - highest)
    norm = highest + jnp.log(spread)
    norm_ref[...] = norm
    exponent = jnp.where(mask_ref[0:1, :] > 0.0, score_ref[...] - norm, -jnp.inf)
    posterior = jnp.exp(exponent).astype(jnp.bfloat16)
    post_ref[...] = posterior
    emit_sums(posterior, all_ref, out_refs)


def later_sums_kernel(post_ref, all_ref, *out_refs):
    emit_sums(post_ref[...], all_ref, out_refs)


def sums_call(kernel, operands, extra, members, all_images, refs):
    slots, width = all_images.shape
    block = jax.ShapeDtypeStruct((refs // members, width), jnp.bfloat16)
    outs = pl.pallas_call(
        kernel,
        out_shape=(block,) * members + tuple(extra),
        in_specs=[VMEM_SPEC] * (len(operands) + 1),
        out_specs=(VMEM_SPEC,) * (members + len(extra)),
        compiler_params=pltpu.CompilerParams(vmem_limit_bytes=VMEM_BYTES),
        cost_estimate=pl.CostEstimate(
            flops=2 * refs * slots * width,
            bytes_accessed=2 * slots * width,
            transcendentals=0,
        ),
        name="sums",
    )(*operands, all_images)
    return outs[:members], outs[members:]


def on_device(images, routes, projections, noise_weights):
    readers = lax.axis_size("reader")
    members = lax.axis_size("blk")
    reader = lax.axis_index("reader")
    member = lax.axis_index("blk")
    is_end = (member == 0) | (member == members - 1)
    place = jnp.stack([reader, is_end.astype(jnp.int32)]).astype(jnp.int32)
    rows, width = images.shape
    noise = noise_weights.reshape(1, width)
    projections = projections[0]
    half = width // 2
    pieces = [slice(0, half), slice(half, width)]
    gather = staged_gather if members == 4 and rows % 48 == 0 else plain_gather
    streams = [
        gather(projections[:, piece], images[:, piece], readers // 4, readers // 2)
        for piece in pieces
    ]

    route_blocks = jnp.stack([routes.T] + [swap_bits(routes.T, "reader", k) for k in range(1, readers)])
    order = jnp.arange(readers, dtype=jnp.int32) ^ reader
    all_routes = route_blocks[order].transpose(1, 0, 2).reshape(routes.shape[1], readers * rows)

    split = lax.axis_size("sub") > 1
    scores, first_images, masks = score_piece(
        place, pieces[0], *streams[0], noise, all_routes, None, False
    )
    scores, last_images, mine = score_piece(
        place, pieces[1], *streams[1], noise, None, scores, not split
    )
    if split:
        scores = lax.psum(scores, "sub")
        mine = group_lse(scores)
    lses = [mine] + [swap_bits(mine, "reader", k) for k in range(1, readers)]
    refs, slots = scores.shape
    first_parts, (norms, posterior) = sums_call(
        partial(first_sums_kernel, readers, members),
        (scores, masks, *lses),
        (
            jax.ShapeDtypeStruct((1, slots), jnp.float32),
            jax.ShapeDtypeStruct((refs, slots), jnp.bfloat16),
        ),
        members,
        first_images,
        refs,
    )
    last_parts, _ = sums_call(later_sums_kernel, (posterior,), (), members, last_images, refs)
    scatter = pair_scatter if members == 4 else line_scatter
    totals = scatter((first_parts, last_parts), "blk")
    normalizer = lax.dynamic_slice(norms.reshape(-1), (reader * rows,), (rows,))
    return (jnp.concatenate(totals, axis=1)[None], normalizer)


def solution(mesh):
    return jax.shard_map(
        on_device,
        mesh=mesh,
        in_specs=(
            P(("parts", "blk", "reader"), "sub"),
            P(("parts", "blk", "reader"), None),
            P(("parts", "reader"), "blk", "sub"),
            P(("parts", "sub")),
        ),
        out_specs=(P(("parts", "reader"), "blk", "sub"), P(("parts", "blk", "reader"))),
        check_vma=False,
    )
```

```python
from functools import partial

import jax
import jax.numpy as jnp
from jax import lax
from jax.experimental import pallas as pl
from jax.experimental.pallas import tpu as pltpu
from jax.sharding import PartitionSpec as P

VMEM_BYTES = 56 * 1024 * 1024
CHUNK = 2048
PARTS = 4
SMEM_SPEC = pl.BlockSpec(memory_space=pltpu.SMEM)
VMEM_SPEC = pl.BlockSpec(memory_space=pltpu.VMEM)
ANY_SPEC = pl.BlockSpec(memory_space=pl.ANY)
SIDES = [(0, 1), (1, 0), (2, 3), (3, 2)]
MIDDLE = [(1, 2), (2, 1), (0, 0), (3, 3)]


def swap_bits(block, axis, bits):
    return lax.ppermute(block, axis, [(i, i ^ bits) for i in range(lax.axis_size(axis))])


def swap_gather(block, axis, bit):
    held = {0: block}
    while bit:
        for k in list(held):
            held[k ^ bit] = swap_bits(held[k], axis, bit)
        bit //= 2
    return [held[k] for k in range(len(held))]


def add_rounded(one, other):
    return (one.astype(jnp.float32) + other.astype(jnp.float32)).astype(jnp.bfloat16)


def staged_gather(block, images, routes, near_bits, far_bit):
    near = swap_gather(images, "reader", near_bits)
    crossed = swap_bits(images, "reader", far_bit)
    side = lax.ppermute(block, "blk", SIDES)
    across = lax.ppermute(block, "blk", MIDDLE)
    side, across = lax.optimization_barrier((side, across))
    far = lax.ppermute(across, "blk", SIDES)
    across_far = lax.ppermute(side, "blk", MIDDLE)
    far, across_far, routes, near = lax.optimization_barrier((far, across_far, routes, near))
    end = lax.ppermute(across_far, "blk", SIDES)
    line = [[block], [side], [far, across_far], [end, across]]
    crossed, _ = lax.optimization_barrier((crossed, across_far))
    step = images.shape[1] // PARTS
    parts = [
        swap_gather(crossed[:, i * step : (i + 1) * step], "reader", near_bits)
        for i in range(PARTS)
    ]
    far_blocks = [[crossed]] + [list(group) for group in list(zip(*parts))[1:]]
    return line, [[one] for one in near] + far_blocks, routes


def plain_gather(block, images, routes, near_bits, far_bit):
    near = swap_gather(images, "reader", near_bits)
    far = swap_gather(swap_bits(images, "reader", far_bit), "reader", near_bits)
    return line_gather(block, "blk"), [[one] for one in near + far], routes


def line_gather(block, axis):
    size, member = lax.axis_size(axis), lax.axis_index(axis)
    ahead, behind = [block], [block]
    for s in range(1, size):
        ahead.append(lax.ppermute(ahead[-1], axis, [(i, i + 1) for i in range(s - 1, size - 1)]))
        behind.append(lax.ppermute(behind[-1], axis, [(i, i - 1) for i in range(1, size - s + 1)]))
    blocks = [block]
    for s in range(1, size):
        blocks.append(jnp.where(member >= s, ahead[s], behind[size - s]))
    return [[one] for one in blocks]


def pair_scatter(pieces, axis):
    member = lax.axis_index(axis)
    is_end = (member == 0) | (member == 3)
    totals, across_end = [], None
    for parts in pieces:
        for_far_end = lax.ppermute(parts[3], axis, SIDES)
        for_far_middle = lax.ppermute(parts[2], axis, SIDES)
        if across_end is not None:
            for_far_end, for_far_middle, _ = lax.optimization_barrier(
                (for_far_end, for_far_middle, across_end)
            )
        across_end = lax.ppermute(add_rounded(parts[2], for_far_end), axis, MIDDLE)
        across_middle = lax.ppermute(add_rounded(parts[3], for_far_middle), axis, MIDDLE)
        near = jnp.where(is_end, parts[1], add_rounded(parts[1], across_end))
        from_side = lax.ppermute(near, axis, SIDES)
        total = parts[0].astype(jnp.float32) + from_side.astype(jnp.float32)
        totals.append(total + jnp.where(is_end, 0.0, across_middle.astype(jnp.float32)))
    return totals


def line_scatter(pieces, axis):
    return [line_sum(parts, axis) for parts in pieces]


def line_sum(parts, axis):
    size = lax.axis_size(axis)
    up = down = None
    for s in range(1, size):
        send_up, send_down = parts[s], parts[size - s]
        if s > 1:
            send_up = add_rounded(send_up, up)
            send_down = add_rounded(send_down, down)
        up = lax.ppermute(send_up, axis, [(i, i + 1) for i in range(0, s) if i + 1 < size])
        down = lax.ppermute(send_down, axis, [(i, i - 1) for i in range(size - s, size) if i > 0])
    total = parts[0].astype(jnp.float32)
    if size > 1:
        total = total + up.astype(jnp.float32) + down.astype(jnp.float32)
    return total


def column_lse(scores):
    peak = jnp.max(scores, axis=0, keepdims=True)
    total = jnp.sum(jnp.exp(scores - peak), axis=0, keepdims=True)
    return peak + jnp.log(total)


def take_groups(refs, counts):
    return [[refs.pop(0) for _ in range(n)] for n in counts]


def flat(groups):
    return [one for group in groups for one in group]


def copy_images(reader, groups, all_ref, sems, piece, chunk):
    rows = groups[0][0].shape[0]
    copies = []
    for c, start in enumerate(range(piece.start, piece.stop, chunk)):
        chunk_copies = []
        for k, group in enumerate(groups):
            each = group[0].shape[1]
            ref, offset = group[start // each], start % each
            row = pl.multiple_of((reader ^ k) * rows, 16)
            chunk_copies.append(
                pltpu.make_async_copy(
                    ref.at[:, pl.ds(offset, chunk)],
                    all_ref.at[pl.ds(row, rows), pl.ds(start - piece.start, chunk)],
                    sems.at[c, k],
                )
            )
        copies.append(chunk_copies)
    return copies


def score_kernel(counts, chunk, finish, place_ref, *refs):
    image_counts, pair_counts = counts
    refs = list(refs)
    image_refs = take_groups(refs, image_counts)
    pair_refs = take_groups(refs, pair_counts)
    noise_ref, route_ref, score_ref, mask_ref, lse_ref = refs[:5]
    all_ref, line_ref, weighted_ref, image_sems, line_sems = refs[5:]
    reader, is_end = place_ref[0], place_ref[1] == 1
    count, width = pair_refs[0][0].shape
    copies = copy_images(reader, image_refs, all_ref, image_sems, slice(0, width), chunk)

    def line_copy(s, ref, c):
        columns = pl.ds(c * chunk, chunk)
        return pltpu.make_async_copy(
            ref.at[:, columns],
            line_ref.at[pl.ds(s * count, count), columns],
            line_sems.at[c, s],
        )

    for c in range(width // chunk):
        for s, pair in enumerate(pair_refs):
            if len(pair) == 1:
                line_copy(s, pair[0], c).start()
                continue

            @pl.when(is_end)
            def _(s=s, pair=pair, c=c):
                line_copy(s, pair[0], c).start()

            @pl.when(jnp.logical_not(is_end))
            def _(s=s, pair=pair, c=c):
                line_copy(s, pair[1], c).start()

        for copy in copies[c]:
            copy.start()
    routes = route_ref[...]
    for k in range(mask_ref.shape[0]):
        hits = jnp.where(routes == (reader ^ k), 1.0, 0.0)
        mask_ref[k : k + 1, :] = jnp.max(hits, axis=0, keepdims=True)
    scores = jnp.zeros(score_ref.shape, jnp.float32)
    penalty = jnp.zeros((score_ref.shape[0], 1), jnp.float32)
    for c in range(width // chunk):
        columns = slice(c * chunk, (c + 1) * chunk)
        for s, pair in enumerate(pair_refs):
            line_copy(s, pair[0], c).wait()
        block = line_ref[:, columns].astype(jnp.float32)
        scaled = block * noise_ref[:, columns]
        weighted_ref[...] = scaled.astype(jnp.bfloat16)
        penalty = penalty + 0.5 * jnp.sum(scaled * block, axis=1, keepdims=True)
        for copy in copies[c]:
            copy.wait()
        scores = scores + lax.dot_general(
            weighted_ref[...],
            all_ref[:, columns],
            (((1,), (1,)), ((), ())),
            preferred_element_type=jnp.float32,
        )
    scores = scores - penalty
    score_ref[...] = scores
    if finish:
        lse_ref[...] = column_lse(scores)


def all_scores(place, pairs, images, noise, routes, finish):
    count, width = pairs[0][0].shape
    chunk = min(CHUNK, width // PARTS)
    refs = len(pairs) * count
    slots = routes.shape[1]
    moved = [*flat(images), *flat(pairs)]
    return pl.pallas_call(
        partial(
            score_kernel,
            ([len(group) for group in images], [len(pair) for pair in pairs]),
            chunk,
            finish,
        ),
        out_shape=(
            jax.ShapeDtypeStruct((refs, slots), jnp.float32),
            jax.ShapeDtypeStruct((len(images), slots), jnp.float32),
            jax.ShapeDtypeStruct((1, slots), jnp.float32),
        ),
        in_specs=[SMEM_SPEC] + [ANY_SPEC] * len(moved) + [VMEM_SPEC] * 2,
        out_specs=(VMEM_SPEC,) * 3,
        scratch_shapes=[
            pltpu.VMEM((slots, width), jnp.bfloat16),
            pltpu.VMEM((refs, width), jnp.bfloat16),
            pltpu.VMEM((refs, chunk), jnp.bfloat16),
            pltpu.SemaphoreType.DMA((width // chunk, len(images))),
            pltpu.SemaphoreType.DMA((width // chunk, len(pairs))),
        ],
        compiler_params=pltpu.CompilerParams(vmem_limit_bytes=VMEM_BYTES),
        cost_estimate=pl.CostEstimate(
            flops=2 * refs * slots * width,
            bytes_accessed=2 * (slots + refs) * width,
            transcendentals=0,
        ),
        name="scores",
    )(place, *moved, noise, routes)


def lse_kernel(score_ref, lse_ref):
    lse_ref[...] = column_lse(score_ref[...])


def group_lse(scores):
    return pl.pallas_call(
        lse_kernel,
        out_shape=jax.ShapeDtypeStruct((1, scores.shape[1]), jnp.float32),
        name="group_lse",
    )(scores)


def sums_kernel(parts, members, piece, chunk, first, place_ref, *refs):
    refs = list(refs)
    image_refs = take_groups(refs, parts)
    if first:
        score_ref, mask_ref, *lse_refs = [refs.pop(0) for _ in range(2 + len(parts))]
    else:
        post_ref = refs.pop(0)
    out_refs = [refs.pop(0) for _ in range(members)]
    if first:
        norm_ref, post_ref = refs.pop(0), refs.pop(0)
    all_ref, sems = refs
    copies = copy_images(place_ref[0], image_refs, all_ref, sems, piece, chunk)
    for chunk_copies in copies:
        for copy in chunk_copies:
            copy.start()
    if first:
        kept = []
        for k, lse_ref in enumerate(lse_refs):
            kept.append(jnp.where(mask_ref[k : k + 1, :] > 0.0, lse_ref[...], -jnp.inf))
        highest = kept[0]
        for value in kept[1:]:
            highest = jnp.maximum(highest, value)
        spread = jnp.exp(kept[0] - highest)
        for value in kept[1:]:
            spread = spread + jnp.exp(value - highest)
        norm = highest + jnp.log(spread)
        norm_ref[...] = norm
        exponent = jnp.where(mask_ref[0:1, :] > 0.0, score_ref[...] - norm, -jnp.inf)
        post_ref[...] = jnp.exp(exponent).astype(jnp.bfloat16)
    posterior = post_ref[...]
    count = posterior.shape[0] // members
    for c, chunk_copies in enumerate(copies):
        columns = slice(c * chunk, (c + 1) * chunk)
        for copy in chunk_copies:
            copy.wait()
        sums = jnp.dot(posterior, all_ref[:, columns], preferred_element_type=jnp.float32)
        for s, out_ref in enumerate(out_refs):
            out_ref[:, columns] = sums[s * count : (s + 1) * count].astype(out_ref.dtype)


def group_sums(place, piece, images, members, operands, first):
    refs, slots = operands[0].shape
    width = piece.stop - piece.start
    chunk = min(CHUNK, images[0][0].shape[1] // PARTS) // 2
    moved = flat(images)
    block = jax.ShapeDtypeStruct((refs // members, width), jnp.bfloat16)
    extra = (
        jax.ShapeDtypeStruct((1, slots), jnp.float32),
        jax.ShapeDtypeStruct((refs, slots), jnp.bfloat16),
    )
    extra = extra if first else ()
    outs = pl.pallas_call(
        partial(sums_kernel, [len(group) for group in images], members, piece, chunk, first),
        out_shape=(block,) * members + extra,
        in_specs=[SMEM_SPEC] + [ANY_SPEC] * len(moved) + [VMEM_SPEC] * len(operands),
        out_specs=(VMEM_SPEC,) * (members + len(extra)),
        scratch_shapes=[
            pltpu.VMEM((slots, width), jnp.bfloat16),
            pltpu.SemaphoreType.DMA((width // chunk, len(images))),
        ],
        compiler_params=pltpu.CompilerParams(vmem_limit_bytes=VMEM_BYTES),
        cost_estimate=pl.CostEstimate(
            flops=2 * refs * slots * width,
            bytes_accessed=2 * slots * width,
            transcendentals=0,
        ),
        name="sums",
    )(place, *moved, *operands)
    return outs[:members], outs[members:]


def on_device(images, routes, projections, noise_weights):
    readers = lax.axis_size("reader")
    members = lax.axis_size("blk")
    reader = lax.axis_index("reader")
    member = lax.axis_index("blk")
    is_end = (member == 0) | (member == members - 1)
    place = jnp.stack([reader, is_end.astype(jnp.int32)]).astype(jnp.int32)
    rows, width = images.shape
    noise = noise_weights.reshape(1, width)

    route_blocks = jnp.stack([routes.T] + [swap_bits(routes.T, "reader", k) for k in range(1, readers)])
    order = jnp.arange(readers, dtype=jnp.int32) ^ reader
    all_routes = route_blocks[order].transpose(1, 0, 2).reshape(routes.shape[1], readers * rows)
    gather = staged_gather if members == 4 and rows % 32 == 0 else plain_gather
    line, blocks, all_routes = gather(
        projections[0], images, all_routes, readers // 4, readers // 2
    )

    split = lax.axis_size("sub") > 1
    scores, masks, mine = all_scores(place, line, blocks, noise, all_routes, not split)
    if split:
        scores = lax.psum(scores, "sub")
        mine = group_lse(scores)
    lses = [mine] + [swap_bits(mine, "reader", k) for k in range(1, readers)]
    half = width // 2
    first_parts, (norms, posterior) = group_sums(
        place, slice(0, half), blocks, members, (scores, masks, *lses), True
    )
    last_parts, _ = group_sums(place, slice(half, width), blocks, members, (posterior,), False)
    scatter = pair_scatter if members == 4 else line_scatter
    totals = scatter((first_parts, last_parts), "blk")
    normalizer = lax.dynamic_slice(norms.reshape(-1), (reader * rows,), (rows,))
    return (jnp.concatenate(totals, axis=1)[None], normalizer)


def solution(mesh):
    return jax.shard_map(
        on_device,
        mesh=mesh,
        in_specs=(
            P(("parts", "blk", "reader"), "sub"),
            P(("parts", "blk", "reader"), None),
            P(("parts", "reader"), "blk", "sub"),
            P(("parts", "sub")),
        ),
        out_specs=(P(("parts", "reader"), "blk", "sub"), P(("parts", "blk", "reader"))),
        check_vma=False,
    )
```

```python
from functools import partial

import jax
import jax.numpy as jnp
from jax import lax
from jax.experimental import pallas as pl
from jax.experimental.pallas import tpu as pltpu
from jax.sharding import PartitionSpec as P

SCORE_VMEM = 20 * 1024 * 1024
SUMS_VMEM = 12 * 1024 * 1024
PARTS = 4
SMEM_SPEC = pl.BlockSpec(memory_space=pltpu.SMEM)
VMEM_SPEC = pl.BlockSpec(memory_space=pltpu.VMEM)
ANY_SPEC = pl.BlockSpec(memory_space=pl.ANY)
SIDES = [(0, 1), (1, 0), (2, 3), (3, 2)]
MIDDLE = [(1, 2), (2, 1), (0, 0), (3, 3)]


def swap_bits(block, axis, bits):
    return lax.ppermute(block, axis, [(i, i ^ bits) for i in range(lax.axis_size(axis))])


def swap_gather(block, axis, bit):
    held = {0: block}
    while bit:
        for k in list(held):
            held[k ^ bit] = swap_bits(held[k], axis, bit)
        bit //= 2
    return [held[k] for k in range(len(held))]


def add_rounded(one, other):
    return (one.astype(jnp.float32) + other.astype(jnp.float32)).astype(jnp.bfloat16)


def staged_gather(block, images, routes, near_bits, far_bit):
    crossed = swap_bits(images, "reader", far_bit)
    side = lax.ppermute(block, "blk", SIDES)
    across = lax.ppermute(block, "blk", MIDDLE)
    side, across, near = lax.optimization_barrier((side, across, images))
    near = swap_gather(near, "reader", near_bits)
    far = lax.ppermute(across, "blk", SIDES)
    across_far = lax.ppermute(side, "blk", MIDDLE)
    far, across_far = lax.optimization_barrier((far, across_far))
    end = lax.ppermute(across_far, "blk", SIDES)
    line = [[block], [side], [far, across_far], [end, across]]
    crossed, routes, _ = lax.optimization_barrier((crossed, routes, across_far))
    step = images.shape[1] // PARTS
    parts = [
        swap_gather(crossed[:, i * step : (i + 1) * step], "reader", near_bits)
        for i in range(PARTS)
    ]
    far_blocks = [[crossed]] + [list(group) for group in list(zip(*parts))[1:]]
    return line, [[one] for one in near] + far_blocks, swap_all(routes)


def swap_all(routes):
    return [routes] + [swap_bits(routes, "reader", k) for k in range(1, lax.axis_size("reader"))]


def plain_gather(block, images, routes, near_bits, far_bit):
    near = swap_gather(images, "reader", near_bits)
    far = swap_gather(swap_bits(images, "reader", far_bit), "reader", near_bits)
    return line_gather(block, "blk"), [[one] for one in near + far], swap_all(routes)


def line_gather(block, axis):
    size, member = lax.axis_size(axis), lax.axis_index(axis)
    ahead, behind = [block], [block]
    for s in range(1, size):
        ahead.append(lax.ppermute(ahead[-1], axis, [(i, i + 1) for i in range(s - 1, size - 1)]))
        behind.append(lax.ppermute(behind[-1], axis, [(i, i - 1) for i in range(1, size - s + 1)]))
    blocks = [block]
    for s in range(1, size):
        blocks.append(jnp.where(member >= s, ahead[s], behind[size - s]))
    return [[one] for one in blocks]


def pair_scatter(pieces, axis):
    member = lax.axis_index(axis)
    is_end = (member == 0) | (member == 3)
    for_far_end = [lax.ppermute(parts[3], axis, SIDES) for parts in pieces]
    *second, for_far_end[0] = lax.optimization_barrier(
        [parts[2] for parts in pieces] + for_far_end[:1]
    )
    for_far_middle = [lax.ppermute(part, axis, SIDES) for part in second]
    totals, across_end = [], None
    for parts, part, end, middle in zip(pieces, second, for_far_end, for_far_middle):
        if across_end is not None:
            end, _ = lax.optimization_barrier((end, across_end))
        across_end = lax.ppermute(add_rounded(part, end), axis, MIDDLE)
        across_middle = lax.ppermute(add_rounded(parts[3], middle), axis, MIDDLE)
        near = jnp.where(is_end, parts[1], add_rounded(parts[1], across_end))
        from_side = lax.ppermute(near, axis, SIDES)
        total = parts[0].astype(jnp.float32) + from_side.astype(jnp.float32)
        totals.append(total + jnp.where(is_end, 0.0, across_middle.astype(jnp.float32)))
    return totals


def line_scatter(pieces, axis):
    return [line_sum(parts, axis) for parts in pieces]


def line_sum(parts, axis):
    size = lax.axis_size(axis)
    up = down = None
    for s in range(1, size):
        send_up, send_down = parts[s], parts[size - s]
        if s > 1:
            send_up = add_rounded(send_up, up)
            send_down = add_rounded(send_down, down)
        up = lax.ppermute(send_up, axis, [(i, i + 1) for i in range(0, s) if i + 1 < size])
        down = lax.ppermute(send_down, axis, [(i, i - 1) for i in range(size - s, size) if i > 0])
    total = parts[0].astype(jnp.float32)
    if size > 1:
        total = total + up.astype(jnp.float32) + down.astype(jnp.float32)
    return total


def column_lse(scores):
    peak = jnp.max(scores, axis=0, keepdims=True)
    total = jnp.sum(jnp.exp(scores - peak), axis=0, keepdims=True)
    return peak + jnp.log(total)


def take_groups(refs, counts):
    return [[refs.pop(0) for _ in range(n)] for n in counts]


def flat(groups):
    return [one for group in groups for one in group]


def score_kernel(counts, halves, finish, place_ref, *refs):
    image_counts, pair_counts = counts
    refs = list(refs)
    image_refs = take_groups(refs, image_counts)
    pair_refs = take_groups(refs, pair_counts)
    noise_ref, route_ref, score_ref, mask_ref, lse_ref, all_ref = refs[:6]
    line_ref, weighted_ref, image_sems, line_sems = refs[6:]
    reader, is_end = place_ref[0], place_ref[1] == 1
    rows = image_refs[0][0].shape[0]
    count, width = pair_refs[0][0].shape
    half = width // halves

    def line_copy(s, ref, h):
        columns = pl.ds(h * half, half)
        return pltpu.make_async_copy(
            ref.at[:, columns],
            line_ref.at[pl.ds(s * count, count), columns],
            line_sems.at[h, s],
        )

    copies = []
    for h in range(halves):
        for s, pair in enumerate(pair_refs):
            if len(pair) == 1:
                line_copy(s, pair[0], h).start()
                continue

            @pl.when(is_end)
            def _(s=s, pair=pair, h=h):
                line_copy(s, pair[0], h).start()

            @pl.when(jnp.logical_not(is_end))
            def _(s=s, pair=pair, h=h):
                line_copy(s, pair[1], h).start()

        half_copies = []
        for k, group in enumerate(image_refs):
            row = pl.multiple_of((reader ^ k) * rows, 16)
            each = min(half, group[0].shape[1])
            for start in range(h * half, (h + 1) * half, each):
                own = group[0].shape[1]
                ref = group[start // own]
                copy = pltpu.make_async_copy(
                    ref.at[:, pl.ds(start % own, each)],
                    all_ref.at[pl.ds(row, rows), pl.ds(start, each)],
                    image_sems.at[h, len(half_copies)],
                )
                copy.start()
                half_copies.append(copy)
        copies.append(half_copies)
    routes = route_ref[...]
    for k in range(mask_ref.shape[0]):
        hits = jnp.where(routes == (reader ^ k), 1.0, 0.0)
        mask_ref[k : k + 1, :] = jnp.max(hits, axis=0, keepdims=True)
    scores = None
    penalty = jnp.zeros((line_ref.shape[0], 1), jnp.float32)
    step = half // 4
    for h in range(halves):
        for s, pair in enumerate(pair_refs):
            line_copy(s, pair[0], h).wait()
        for start in range(h * half, (h + 1) * half, step):
            columns = slice(start, start + step)
            block = line_ref[:, columns].astype(jnp.float32)
            scaled = block * noise_ref[:, columns]
            weighted_ref[:, columns] = scaled.astype(jnp.bfloat16)
            penalty = penalty + 0.5 * jnp.sum(scaled * block, axis=1, keepdims=True)
        for copy in copies[h]:
            copy.wait()
        columns = slice(h * half, (h + 1) * half)
        part = lax.dot_general(
            all_ref[:, columns],
            weighted_ref[:, columns],
            (((1,), (1,)), ((), ())),
            preferred_element_type=jnp.float32,
        )
        scores = part if scores is None else scores + part
    scores = scores.T - penalty
    score_ref[...] = scores
    if finish:
        lse_ref[...] = column_lse(scores)


def all_scores(place, pairs, images, noise, routes, finish):
    count, width = pairs[0][0].shape
    halves = 2
    refs = len(pairs) * count
    slots = routes.shape[1]
    moved = [*flat(images), *flat(pairs)]
    return pl.pallas_call(
        partial(
            score_kernel,
            ([len(group) for group in images], [len(pair) for pair in pairs]),
            halves,
            finish,
        ),
        out_shape=(
            jax.ShapeDtypeStruct((refs, slots), jnp.float32),
            jax.ShapeDtypeStruct((len(images), slots), jnp.float32),
            jax.ShapeDtypeStruct((1, slots), jnp.float32),
            jax.ShapeDtypeStruct((slots, width), jnp.bfloat16),
        ),
        in_specs=[SMEM_SPEC] + [ANY_SPEC] * len(moved) + [VMEM_SPEC] * 2,
        out_specs=(VMEM_SPEC,) * 4,
        scratch_shapes=[
            pltpu.VMEM((refs, width), jnp.bfloat16),
            pltpu.VMEM((refs, width), jnp.bfloat16),
            pltpu.SemaphoreType.DMA((halves, len(flat(images)))),
            pltpu.SemaphoreType.DMA((halves, len(pairs))),
        ],
        compiler_params=pltpu.CompilerParams(vmem_limit_bytes=SCORE_VMEM),
        cost_estimate=pl.CostEstimate(
            flops=2 * refs * slots * width,
            bytes_accessed=2 * (slots + refs) * width,
            transcendentals=0,
        ),
        name="scores",
    )(place, *moved, noise, routes)


def lse_kernel(score_ref, lse_ref):
    lse_ref[...] = column_lse(score_ref[...])


def group_lse(scores):
    return pl.pallas_call(
        lse_kernel,
        out_shape=jax.ShapeDtypeStruct((1, scores.shape[1]), jnp.float32),
        name="group_lse",
    )(scores)


def emit_sums(posterior, all_ref, piece, out_refs):
    sums = jnp.dot(posterior, all_ref[:, piece], preferred_element_type=jnp.float32)
    count = sums.shape[0] // len(out_refs)
    for s, out_ref in enumerate(out_refs):
        out_ref[...] = sums[s * count : (s + 1) * count].astype(out_ref.dtype)


def first_sums_kernel(readers, members, piece, all_ref, score_ref, mask_ref, *refs):
    lse_refs = refs[:readers]
    out_refs = refs[readers : readers + members]
    norm_ref, post_ref = refs[readers + members :]
    kept = []
    for k, lse_ref in enumerate(lse_refs):
        kept.append(jnp.where(mask_ref[k : k + 1, :] > 0.0, lse_ref[...], -jnp.inf))
    highest = kept[0]
    for value in kept[1:]:
        highest = jnp.maximum(highest, value)
    spread = jnp.exp(kept[0] - highest)
    for value in kept[1:]:
        spread = spread + jnp.exp(value - highest)
    norm = highest + jnp.log(spread)
    norm_ref[...] = norm
    exponent = jnp.where(mask_ref[0:1, :] > 0.0, score_ref[...] - norm, -jnp.inf)
    posterior = jnp.exp(exponent).astype(jnp.bfloat16)
    post_ref[...] = posterior
    emit_sums(posterior, all_ref, piece, out_refs)


def later_sums_kernel(piece, all_ref, post_ref, *out_refs):
    emit_sums(post_ref[...], all_ref, piece, out_refs)


def group_sums(kernel, piece, members, all_images, operands, extra):
    refs, slots = operands[0].shape
    width = piece.stop - piece.start
    block = jax.ShapeDtypeStruct((refs // members, width), jnp.bfloat16)
    outs = pl.pallas_call(
        kernel,
        out_shape=(block,) * members + extra,
        in_specs=[VMEM_SPEC] * (1 + len(operands)),
        out_specs=(VMEM_SPEC,) * (members + len(extra)),
        compiler_params=pltpu.CompilerParams(vmem_limit_bytes=SUMS_VMEM),
        cost_estimate=pl.CostEstimate(
            flops=2 * refs * slots * width,
            bytes_accessed=2 * slots * width,
            transcendentals=0,
        ),
        name="sums",
    )(all_images, *operands)
    return outs[:members], outs[members:]


def on_device(images, routes, projections, noise_weights):
    readers = lax.axis_size("reader")
    members = lax.axis_size("blk")
    reader = lax.axis_index("reader")
    member = lax.axis_index("blk")
    is_end = (member == 0) | (member == members - 1)
    place = jnp.stack([reader, is_end.astype(jnp.int32)]).astype(jnp.int32)
    rows, width = images.shape
    noise = noise_weights.reshape(1, width)

    gather = staged_gather if members == 4 and rows % 32 == 0 else plain_gather
    line, blocks, route_blocks = gather(
        projections[0], images, routes.T, readers // 4, readers // 2
    )
    order = jnp.arange(readers, dtype=jnp.int32) ^ reader
    all_routes = jnp.stack(route_blocks)[order].transpose(1, 0, 2)
    all_routes = all_routes.reshape(routes.shape[1], readers * rows)

    split = lax.axis_size("sub") > 1
    scores, masks, mine, all_images = all_scores(
        place, line, blocks, noise, all_routes, not split
    )
    if split:
        scores = lax.psum(scores, "sub")
        mine = group_lse(scores)
    lses = [mine] + [swap_bits(mine, "reader", k) for k in range(1, readers)]
    half = width // 2
    first, last = slice(0, half), slice(half, width)
    extra = (
        jax.ShapeDtypeStruct((1, scores.shape[1]), jnp.float32),
        jax.ShapeDtypeStruct(scores.shape, jnp.bfloat16),
    )
    first_parts, (norms, posterior) = group_sums(
        partial(first_sums_kernel, readers, members, first),
        first,
        members,
        all_images,
        (scores, masks, *lses),
        extra,
    )
    last_parts, _ = group_sums(
        partial(later_sums_kernel, last), last, members, all_images, (posterior,), ()
    )
    scatter = pair_scatter if members == 4 else line_scatter
    totals = scatter((first_parts, last_parts), "blk")
    normalizer = lax.dynamic_slice(norms.reshape(-1), (reader * rows,), (rows,))
    return (jnp.concatenate(totals, axis=1)[None], normalizer)


def solution(mesh):
    return jax.shard_map(
        on_device,
        mesh=mesh,
        in_specs=(
            P(("parts", "blk", "reader"), "sub"),
            P(("parts", "blk", "reader"), None),
            P(("parts", "reader"), "blk", "sub"),
            P(("parts", "sub")),
        ),
        out_specs=(P(("parts", "reader"), "blk", "sub"), P(("parts", "blk", "reader"))),
        check_vma=False,
    )
```

```python
from functools import partial

import jax
import jax.numpy as jnp
from jax import lax
from jax.experimental import pallas as pl
from jax.experimental.pallas import tpu as pltpu
from jax.sharding import PartitionSpec as P

SCORE_VMEM = 20 * 1024 * 1024
SUMS_VMEM = 12 * 1024 * 1024
VMEM_SPEC = pl.BlockSpec(memory_space=pltpu.VMEM)
ANY_SPEC = pl.BlockSpec(memory_space=pl.ANY)
SIDES = [(0, 1), (1, 0), (2, 3), (3, 2)]
MIDDLE = [(1, 2), (2, 1), (0, 0), (3, 3)]
ENDS = [(0, 3), (3, 0), (1, 1), (2, 2)]


def swap_bits(block, axis, bits):
    return lax.ppermute(block, axis, [(i, i ^ bits) for i in range(lax.axis_size(axis))])


def swap_gather(block, axis, bit):
    held = {0: block}
    while bit:
        for k in list(held):
            held[k ^ bit] = swap_bits(held[k], axis, bit)
        bit //= 2
    return [held[k] for k in range(len(held))]


def add_rounded(one, other):
    return (one.astype(jnp.float32) + other.astype(jnp.float32)).astype(jnp.bfloat16)


def staged_gather(block, images, routes, near_bits, far_bit):
    routes = swap_all(routes)
    own, images, *routes = lax.optimization_barrier((block, images, *routes))
    crossed = swap_bits(images, "reader", far_bit)
    side = lax.ppermute(block, "blk", SIDES)
    across = lax.ppermute(block, "blk", MIDDLE)
    end = lax.ppermute(block, "blk", ENDS)
    side, across, images = lax.optimization_barrier((side, across, images))
    near = swap_gather(images, "reader", near_bits)
    far = lax.ppermute(across, "blk", SIDES)
    across_far = lax.ppermute(side, "blk", MIDDLE)
    crossed, far, across_far, end, *near = lax.optimization_barrier(
        (crossed, far, across_far, end, *near)
    )
    line = [[own], [side], [far, across_far], [end, across]]
    return line, near + swap_gather(crossed, "reader", near_bits), routes


def swap_all(routes):
    return [routes] + [swap_bits(routes, "reader", k) for k in range(1, lax.axis_size("reader"))]


def plain_gather(block, images, routes, near_bits, far_bit):
    near = swap_gather(images, "reader", near_bits)
    far = swap_gather(swap_bits(images, "reader", far_bit), "reader", near_bits)
    return line_gather(block, "blk"), near + far, swap_all(routes)


def line_gather(block, axis):
    size, member = lax.axis_size(axis), lax.axis_index(axis)
    ahead, behind = [block], [block]
    for s in range(1, size):
        ahead.append(lax.ppermute(ahead[-1], axis, [(i, i + 1) for i in range(s - 1, size - 1)]))
        behind.append(lax.ppermute(behind[-1], axis, [(i, i - 1) for i in range(1, size - s + 1)]))
    blocks = [block]
    for s in range(1, size):
        blocks.append(jnp.where(member >= s, ahead[s], behind[size - s]))
    return [[one] for one in blocks]


def pair_scatter(pieces, axis):
    member = lax.axis_index(axis)
    is_end = (member == 0) | (member == 3)
    for_far_end = [lax.ppermute(parts[3], axis, SIDES) for parts in pieces]
    *second, for_far_end[0] = lax.optimization_barrier(
        [parts[2] for parts in pieces] + for_far_end[:1]
    )
    for_far_middle = [lax.ppermute(part, axis, SIDES) for part in second]
    totals, across_end = [], None
    for parts, part, end, middle in zip(pieces, second, for_far_end, for_far_middle):
        if across_end is not None:
            end, _ = lax.optimization_barrier((end, across_end))
        across_end = lax.ppermute(add_rounded(part, end), axis, MIDDLE)
        across_middle = lax.ppermute(add_rounded(parts[3], middle), axis, MIDDLE)
        near = jnp.where(is_end, parts[1], add_rounded(parts[1], across_end))
        from_side = lax.ppermute(near, axis, SIDES)
        total = parts[0].astype(jnp.float32) + from_side.astype(jnp.float32)
        totals.append(total + jnp.where(is_end, 0.0, across_middle.astype(jnp.float32)))
    return totals


def line_scatter(pieces, axis):
    return [line_sum(parts, axis) for parts in pieces]


def line_sum(parts, axis):
    size = lax.axis_size(axis)
    up = down = None
    for s in range(1, size):
        send_up, send_down = parts[s], parts[size - s]
        if s > 1:
            send_up = add_rounded(send_up, up)
            send_down = add_rounded(send_down, down)
        up = lax.ppermute(send_up, axis, [(i, i + 1) for i in range(0, s) if i + 1 < size])
        down = lax.ppermute(send_down, axis, [(i, i - 1) for i in range(size - s, size) if i > 0])
    total = parts[0].astype(jnp.float32)
    if size > 1:
        total = total + up.astype(jnp.float32) + down.astype(jnp.float32)
    return total


def column_lse(scores):
    peak = jnp.max(scores, axis=0, keepdims=True)
    total = jnp.sum(jnp.exp(scores - peak), axis=0, keepdims=True)
    return peak + jnp.log(total)


def score_kernel(readers, pair_counts, halves, finish, *refs):
    refs = list(refs)
    image_refs = [refs.pop(0) for _ in range(readers)]
    pair_refs = [[refs.pop(0) for _ in range(n)] for n in pair_counts]
    route_refs = [refs.pop(0) for _ in range(readers)]
    noise_ref, score_ref, mask_ref, lse_ref, all_ref = refs[:5]
    line_ref, weighted_ref, image_sems, line_sems = refs[5:]
    reader, member = lax.axis_index("reader"), lax.axis_index("blk")
    is_end = (member == 0) | (member == lax.axis_size("blk") - 1)
    rows = image_refs[0].shape[0]
    count, width = pair_refs[0][0].shape
    half = width // halves

    def line_copy(s, ref, h):
        columns = pl.ds(h * half, half)
        return pltpu.make_async_copy(
            ref.at[:, columns],
            line_ref.at[pl.ds(s * count, count), columns],
            line_sems.at[h, s],
        )

    copies = []
    for h in range(halves):
        for s, pair in enumerate(pair_refs):
            if len(pair) == 1:
                line_copy(s, pair[0], h).start()
                continue

            @pl.when(is_end)
            def _(s=s, pair=pair, h=h):
                line_copy(s, pair[0], h).start()

            @pl.when(jnp.logical_not(is_end))
            def _(s=s, pair=pair, h=h):
                line_copy(s, pair[1], h).start()

        columns = pl.ds(h * half, half)
        half_copies = []
        for k, ref in enumerate(image_refs):
            row = pl.multiple_of((reader ^ k) * rows, 16)
            copy = pltpu.make_async_copy(
                ref.at[:, columns], all_ref.at[pl.ds(row, rows), columns], image_sems.at[h, k]
            )
            copy.start()
            half_copies.append(copy)
        copies.append(half_copies)
    routes = [ref[...] for ref in route_refs]
    bit = 1
    while bit < readers:
        flip = (reader & bit) > 0
        routes = [jnp.where(flip, routes[k ^ bit], one) for k, one in enumerate(routes)]
        bit *= 2
    for j, route in enumerate(routes):
        for k in range(readers):
            hits = jnp.where(route == (reader ^ k), 1.0, 0.0)
            mask_ref[k : k + 1, j * rows : (j + 1) * rows] = jnp.max(hits, axis=0, keepdims=True)
    scores = None
    penalty = jnp.zeros((line_ref.shape[0], 1), jnp.float32)
    step = half // 4
    for h in range(halves):
        for s, pair in enumerate(pair_refs):
            line_copy(s, pair[0], h).wait()
        for start in range(h * half, (h + 1) * half, step):
            columns = slice(start, start + step)
            block = line_ref[:, columns].astype(jnp.float32)
            scaled = block * noise_ref[:, columns]
            weighted_ref[:, columns] = scaled.astype(jnp.bfloat16)
            penalty = penalty + 0.5 * jnp.sum(scaled * block, axis=1, keepdims=True)
        for copy in copies[h]:
            copy.wait()
        columns = slice(h * half, (h + 1) * half)
        part = lax.dot_general(
            all_ref[:, columns],
            weighted_ref[:, columns],
            (((1,), (1,)), ((), ())),
            preferred_element_type=jnp.float32,
        )
        scores = part if scores is None else scores + part
    scores = scores.T - penalty
    score_ref[...] = scores
    if finish:
        lse_ref[...] = column_lse(scores)


def all_scores(pairs, images, noise, routes, finish):
    count, width = pairs[0][0].shape
    halves = 2
    refs = len(pairs) * count
    slots = len(images) * images[0].shape[0]
    moved = [*images, *[one for pair in pairs for one in pair]]
    return pl.pallas_call(
        partial(
            score_kernel,
            len(images),
            [len(pair) for pair in pairs],
            halves,
            finish,
        ),
        out_shape=(
            jax.ShapeDtypeStruct((refs, slots), jnp.float32),
            jax.ShapeDtypeStruct((len(images), slots), jnp.float32),
            jax.ShapeDtypeStruct((1, slots), jnp.float32),
            jax.ShapeDtypeStruct((slots, width), jnp.bfloat16),
        ),
        in_specs=[ANY_SPEC] * len(moved) + [VMEM_SPEC] * (len(routes) + 1),
        out_specs=(VMEM_SPEC,) * 4,
        scratch_shapes=[
            pltpu.VMEM((refs, width), jnp.bfloat16),
            pltpu.VMEM((refs, width), jnp.bfloat16),
            pltpu.SemaphoreType.DMA((halves, len(images))),
            pltpu.SemaphoreType.DMA((halves, len(pairs))),
        ],
        compiler_params=pltpu.CompilerParams(vmem_limit_bytes=SCORE_VMEM),
        cost_estimate=pl.CostEstimate(
            flops=2 * refs * slots * width,
            bytes_accessed=2 * (slots + refs) * width,
            transcendentals=0,
        ),
        name="scores",
    )(*moved, *routes, noise)


def lse_kernel(score_ref, lse_ref):
    lse_ref[...] = column_lse(score_ref[...])


def group_lse(scores):
    return pl.pallas_call(
        lse_kernel,
        out_shape=jax.ShapeDtypeStruct((1, scores.shape[1]), jnp.float32),
        name="group_lse",
    )(scores)


def emit_sums(posterior, all_ref, piece, out_refs):
    sums = jnp.dot(posterior, all_ref[:, piece], preferred_element_type=jnp.float32)
    count = sums.shape[0] // len(out_refs)
    for s, out_ref in enumerate(out_refs):
        out_ref[...] = sums[s * count : (s + 1) * count].astype(out_ref.dtype)


def first_sums_kernel(readers, members, piece, all_ref, score_ref, mask_ref, *refs):
    lse_refs = refs[:readers]
    out_refs = refs[readers : readers + members]
    norm_ref, post_ref = refs[readers + members :]
    kept = []
    for k, lse_ref in enumerate(lse_refs):
        kept.append(jnp.where(mask_ref[k : k + 1, :] > 0.0, lse_ref[...], -jnp.inf))
    highest = kept[0]
    for value in kept[1:]:
        highest = jnp.maximum(highest, value)
    spread = jnp.exp(kept[0] - highest)
    for value in kept[1:]:
        spread = spread + jnp.exp(value - highest)
    norm = highest + jnp.log(spread)
    norm_ref[...] = norm
    exponent = jnp.where(mask_ref[0:1, :] > 0.0, score_ref[...] - norm, -jnp.inf)
    posterior = jnp.exp(exponent).astype(jnp.bfloat16)
    post_ref[...] = posterior
    emit_sums(posterior, all_ref, piece, out_refs)


def later_sums_kernel(piece, all_ref, post_ref, *out_refs):
    emit_sums(post_ref[...], all_ref, piece, out_refs)


def group_sums(kernel, piece, members, all_images, operands, extra):
    refs, slots = operands[0].shape
    width = piece.stop - piece.start
    block = jax.ShapeDtypeStruct((refs // members, width), jnp.bfloat16)
    outs = pl.pallas_call(
        kernel,
        out_shape=(block,) * members + extra,
        in_specs=[VMEM_SPEC] * (1 + len(operands)),
        out_specs=(VMEM_SPEC,) * (members + len(extra)),
        compiler_params=pltpu.CompilerParams(vmem_limit_bytes=SUMS_VMEM),
        cost_estimate=pl.CostEstimate(
            flops=2 * refs * slots * width,
            bytes_accessed=2 * slots * width,
            transcendentals=0,
        ),
        name="sums",
    )(all_images, *operands)
    return outs[:members], outs[members:]


def on_device(images, routes, projections, noise_weights):
    readers = lax.axis_size("reader")
    members = lax.axis_size("blk")
    reader = lax.axis_index("reader")
    rows, width = images.shape
    noise = noise_weights.reshape(1, width)

    gather = staged_gather if members == 4 and rows % 32 == 0 else plain_gather
    line, blocks, route_blocks = gather(
        projections[0], images, routes.T, readers // 4, readers // 2
    )
    split = lax.axis_size("sub") > 1
    scores, masks, mine, all_images = all_scores(
        line, blocks, noise, route_blocks, not split
    )
    if split:
        scores = lax.psum(scores, "sub")
        mine = group_lse(scores)
    lses = [mine] + [swap_bits(mine, "reader", k) for k in range(1, readers)]
    half = width // 2
    first, last = slice(0, half), slice(half, width)
    extra = (
        jax.ShapeDtypeStruct((1, scores.shape[1]), jnp.float32),
        jax.ShapeDtypeStruct(scores.shape, jnp.bfloat16),
    )
    first_parts, (norms, posterior) = group_sums(
        partial(first_sums_kernel, readers, members, first),
        first,
        members,
        all_images,
        (scores, masks, *lses),
        extra,
    )
    last_parts, _ = group_sums(
        partial(later_sums_kernel, last), last, members, all_images, (posterior,), ()
    )
    scatter = pair_scatter if members == 4 else line_scatter
    totals = scatter((first_parts, last_parts), "blk")
    normalizer = lax.dynamic_slice(norms.reshape(-1), (reader * rows,), (rows,))
    return (jnp.concatenate(totals, axis=1)[None], normalizer)


def solution(mesh):
    return jax.shard_map(
        on_device,
        mesh=mesh,
        in_specs=(
            P(("parts", "blk", "reader"), "sub"),
            P(("parts", "blk", "reader"), None),
            P(("parts", "reader"), "blk", "sub"),
            P(("parts", "sub")),
        ),
        out_specs=(P(("parts", "reader"), "blk", "sub"), P(("parts", "blk", "reader"))),
        check_vma=False,
    )
```

```python
from functools import partial

import jax
import jax.numpy as jnp
from jax import lax
from jax.experimental import pallas as pl
from jax.experimental.pallas import tpu as pltpu
from jax.sharding import PartitionSpec as P

SCORE_VMEM = 20 * 1024 * 1024
SUMS_VMEM = 12 * 1024 * 1024
STEP = 1024
VMEM_SPEC = pl.BlockSpec(memory_space=pltpu.VMEM)
ANY_SPEC = pl.BlockSpec(memory_space=pl.ANY)
SIDES = [(0, 1), (1, 0), (2, 3), (3, 2)]
MIDDLE = [(1, 2), (2, 1), (0, 0), (3, 3)]
ENDS = [(0, 3), (3, 0), (1, 1), (2, 2)]


def swap_bits(block, axis, bits):
    return lax.ppermute(block, axis, [(i, i ^ bits) for i in range(lax.axis_size(axis))])


def swap_gather(block, axis, bit):
    held = {0: block}
    while bit:
        for k in list(held):
            held[k ^ bit] = swap_bits(held[k], axis, bit)
        bit //= 2
    return [held[k] for k in range(len(held))]


def add_rounded(one, other):
    return (one.astype(jnp.float32) + other.astype(jnp.float32)).astype(jnp.bfloat16)


def staged_gather(block, images, noise, routes, near_bits, far_bit):
    routes = swap_all(routes)
    far_images, *routes = lax.optimization_barrier((images, *routes))
    near = swap_gather(images, "reader", near_bits)
    crossed = swap_bits(far_images, "reader", far_bit)
    side = lax.ppermute(block, "blk", SIDES)
    across = lax.ppermute(block, "blk", MIDDLE)
    end = lax.ppermute(block, "blk", ENDS)
    side, across = lax.optimization_barrier((side, across))
    far = lax.ppermute(across, "blk", SIDES)
    across_far = lax.ppermute(side, "blk", MIDDLE)
    staged = stage([[block], [side], None, [end, across]], near, noise)
    crossed, far, across_far, *staged = lax.optimization_barrier(
        (crossed, far, across_far, *staged)
    )
    return staged, [far, across_far], swap_gather(crossed, "reader", near_bits), routes


def swap_all(routes):
    return [routes] + [swap_bits(routes, "reader", k) for k in range(1, lax.axis_size("reader"))]


def plain_gather(block, images, noise, routes, near_bits, far_bit):
    near = swap_gather(images, "reader", near_bits)
    far = swap_gather(swap_bits(images, "reader", far_bit), "reader", near_bits)
    line = line_gather(block, "blk")
    staged = stage([[one] for one in line[:2]] + [None] + [[one] for one in line[3:]], near, noise)
    return staged, [line[2]], far, swap_all(routes)


def line_gather(block, axis):
    size, member = lax.axis_size(axis), lax.axis_index(axis)
    ahead, behind = [block], [block]
    for s in range(1, size):
        ahead.append(lax.ppermute(ahead[-1], axis, [(i, i + 1) for i in range(s - 1, size - 1)]))
        behind.append(lax.ppermute(behind[-1], axis, [(i, i - 1) for i in range(1, size - s + 1)]))
    blocks = [block]
    for s in range(1, size):
        blocks.append(jnp.where(member >= s, ahead[s], behind[size - s]))
    return blocks


def pair_scatter(pieces, axis):
    member = lax.axis_index(axis)
    is_end = (member == 0) | (member == 3)
    for_far_end = [lax.ppermute(parts[3], axis, SIDES) for parts in pieces]
    *second, for_far_end[0] = lax.optimization_barrier(
        [parts[2] for parts in pieces] + for_far_end[:1]
    )
    for_far_middle = [lax.ppermute(part, axis, SIDES) for part in second]
    totals = []
    for parts, part, end, middle in zip(pieces, second, for_far_end, for_far_middle):
        across_end = lax.ppermute(add_rounded(part, end), axis, MIDDLE)
        across_middle = lax.ppermute(add_rounded(parts[3], middle), axis, MIDDLE)
        near = jnp.where(is_end, parts[1], add_rounded(parts[1], across_end))
        from_side = lax.ppermute(near, axis, SIDES)
        total = parts[0].astype(jnp.float32) + from_side.astype(jnp.float32)
        totals.append(total + jnp.where(is_end, 0.0, across_middle.astype(jnp.float32)))
    return totals


def line_scatter(pieces, axis):
    return [line_sum(parts, axis) for parts in pieces]


def line_sum(parts, axis):
    size = lax.axis_size(axis)
    up = down = None
    for s in range(1, size):
        send_up, send_down = parts[s], parts[size - s]
        if s > 1:
            send_up = add_rounded(send_up, up)
            send_down = add_rounded(send_down, down)
        up = lax.ppermute(send_up, axis, [(i, i + 1) for i in range(0, s) if i + 1 < size])
        down = lax.ppermute(send_down, axis, [(i, i - 1) for i in range(size - s, size) if i > 0])
    total = parts[0].astype(jnp.float32)
    if size > 1:
        total = total + up.astype(jnp.float32) + down.astype(jnp.float32)
    return total


def column_lse(scores):
    peak = jnp.max(scores, axis=0, keepdims=True)
    total = jnp.sum(jnp.exp(scores - peak), axis=0, keepdims=True)
    return peak + jnp.log(total)


def at_end():
    member = lax.axis_index("blk")
    return (member == 0) | (member == lax.axis_size("blk") - 1)


def either(refs, act):
    if len(refs) == 1:
        act(refs[0])
        return
    is_end = at_end()

    @pl.when(is_end)
    def _():
        act(refs[0])

    @pl.when(jnp.logical_not(is_end))
    def _():
        act(refs[1])


def weigh(block_ref, noise_ref, weighted_ref, penalty_ref, start):
    count, width = block_ref.shape
    rows = slice(start, start + count)
    penalty = jnp.zeros((count, 1), jnp.float32)
    for column in range(0, width, STEP):
        columns = slice(column, column + STEP)
        block = block_ref[:, columns].astype(jnp.float32)
        scaled = block * noise_ref[:, columns]
        weighted_ref[rows, columns] = scaled.astype(jnp.bfloat16)
        penalty = penalty + 0.5 * jnp.sum(scaled * block, axis=1, keepdims=True)
    penalty_ref[rows, :] = penalty


def stage_kernel(near_count, counts, *refs):
    refs = list(refs)
    near_refs = [refs.pop(0) for _ in range(near_count)]
    pair_refs = [[refs.pop(0) for _ in range(n)] for n in counts]
    noise_ref, weighted_ref, penalty_ref, near_ref, noise_out_ref, block_ref, near_sems, sems = refs
    rows = near_refs[0].shape[0]
    count = block_ref.shape[1]
    copies = []
    for k, ref in enumerate(near_refs):
        copy = pltpu.make_async_copy(ref, near_ref.at[pl.ds(k * rows, rows), :], near_sems.at[k])
        copy.start()
        copies.append(copy)

    def block_copy(s, ref):
        return pltpu.make_async_copy(ref, block_ref.at[s], sems.at[s])

    for s, pair in enumerate(pair_refs):
        if pair:
            either(pair, lambda ref, s=s: block_copy(s, ref).start())
    noise_out_ref[...] = noise_ref[...]
    for s, pair in enumerate(pair_refs):
        if pair:
            block_copy(s, pair[0]).wait()
            weigh(block_ref.at[s], noise_ref, weighted_ref, penalty_ref, s * count)
        else:
            weighted_ref[s * count : (s + 1) * count, :] = jnp.zeros(
                (count, weighted_ref.shape[1]), jnp.bfloat16
            )
            penalty_ref[s * count : (s + 1) * count, :] = jnp.zeros((count, 1), jnp.float32)
    for copy in copies:
        copy.wait()


def stage(pairs, near, noise):
    count, width = pairs[0][0].shape
    refs = len(pairs) * count
    moved = [*near, *[one for pair in pairs for one in pair or []]]
    return pl.pallas_call(
        partial(stage_kernel, len(near), [len(pair or []) for pair in pairs]),
        out_shape=(
            jax.ShapeDtypeStruct((refs, width), jnp.bfloat16),
            jax.ShapeDtypeStruct((refs, 1), jnp.float32),
            jax.ShapeDtypeStruct((len(near) * near[0].shape[0], width), jnp.bfloat16),
            jax.ShapeDtypeStruct((1, width), jnp.float32),
        ),
        in_specs=[ANY_SPEC] * len(moved) + [VMEM_SPEC],
        out_specs=(VMEM_SPEC,) * 4,
        scratch_shapes=[
            pltpu.VMEM((len(pairs), count, width), jnp.bfloat16),
            pltpu.SemaphoreType.DMA((len(near),)),
            pltpu.SemaphoreType.DMA((len(pairs),)),
        ],
        compiler_params=pltpu.CompilerParams(vmem_limit_bytes=SCORE_VMEM),
        cost_estimate=pl.CostEstimate(
            flops=8 * refs * width, bytes_accessed=24_000_000, transcendentals=0
        ),
        name="stage",
    )(*moved, noise)


def score_kernel(readers, last_count, finish, *refs):
    refs = list(refs)
    near_ref = refs.pop(0)
    rows = near_ref.shape[0] * 2 // readers
    far_refs = [refs.pop(0) for _ in range(readers // 2)]
    last_refs = [refs.pop(0) for _ in range(last_count)]
    staged_ref, staged_penalty_ref, noise_ref = [refs.pop(0) for _ in range(3)]
    route_refs = [refs.pop(0) for _ in range(readers)]
    score_ref, mask_ref, lse_ref, all_ref = refs[:4]
    block_ref, weighted_ref, penalty_ref, image_sems, block_sem = refs[4:]
    reader = lax.axis_index("reader")
    count, width = block_ref.shape

    def block_copy(ref):
        return pltpu.make_async_copy(ref, block_ref, block_sem)

    either(last_refs, lambda ref: block_copy(ref).start())
    copies = []
    for k in range(readers):
        row = pl.multiple_of((reader ^ k) * rows, 16)
        if k < readers // 2:
            source = near_ref.at[pl.ds(k * rows, rows), :]
        else:
            source = far_refs[k - readers // 2]
        copy = pltpu.make_async_copy(source, all_ref.at[pl.ds(row, rows), :], image_sems.at[k])
        copy.start()
        copies.append(copy)
    routes = [ref[...] for ref in route_refs]
    bit = 1
    while bit < readers:
        flip = (reader & bit) > 0
        routes = [jnp.where(flip, routes[k ^ bit], one) for k, one in enumerate(routes)]
        bit *= 2
    for j, route in enumerate(routes):
        for k in range(readers):
            hits = jnp.where(route == (reader ^ k), 1.0, 0.0)
            mask_ref[k : k + 1, j * rows : (j + 1) * rows] = jnp.max(hits, axis=0, keepdims=True)
    weighted_ref[...] = staged_ref[...]
    penalty_ref[...] = staged_penalty_ref[...]
    block_copy(last_refs[0]).wait()
    weigh(block_ref, noise_ref, weighted_ref, penalty_ref, 2 * count)
    for copy in copies:
        copy.wait()
    scores = lax.dot_general(
        all_ref[...],
        weighted_ref[...],
        (((1,), (1,)), ((), ())),
        preferred_element_type=jnp.float32,
    )
    scores = scores.T - penalty_ref[...]
    score_ref[...] = scores
    if finish:
        lse_ref[...] = column_lse(scores)


def all_scores(staged, last, far, routes, finish):
    weighted, penalty, near, noise = staged
    count, width = last[0].shape
    refs = weighted.shape[0]
    slots = 2 * near.shape[0]
    moved = [near, *far, *last]
    return pl.pallas_call(
        partial(score_kernel, len(routes), len(last), finish),
        out_shape=(
            jax.ShapeDtypeStruct((refs, slots), jnp.float32),
            jax.ShapeDtypeStruct((len(routes), slots), jnp.float32),
            jax.ShapeDtypeStruct((1, slots), jnp.float32),
            jax.ShapeDtypeStruct((slots, width), jnp.bfloat16),
        ),
        in_specs=[ANY_SPEC] * len(moved) + [VMEM_SPEC] * (3 + len(routes)),
        out_specs=(VMEM_SPEC,) * 4,
        scratch_shapes=[
            pltpu.VMEM((count, width), jnp.bfloat16),
            pltpu.VMEM((refs, width), jnp.bfloat16),
            pltpu.VMEM((refs, 1), jnp.float32),
            pltpu.SemaphoreType.DMA((len(routes),)),
            pltpu.SemaphoreType.DMA,
        ],
        compiler_params=pltpu.CompilerParams(vmem_limit_bytes=SCORE_VMEM),
        cost_estimate=pl.CostEstimate(
            flops=2 * refs * slots * width,
            bytes_accessed=2 * (slots + refs) * width,
            transcendentals=0,
        ),
        name="scores",
    )(*moved, weighted, penalty, noise, *routes)


def lse_kernel(score_ref, lse_ref):
    lse_ref[...] = column_lse(score_ref[...])


def group_lse(scores):
    return pl.pallas_call(
        lse_kernel,
        out_shape=jax.ShapeDtypeStruct((1, scores.shape[1]), jnp.float32),
        name="group_lse",
    )(scores)


def sums_kernel(readers, members, pieces, all_ref, score_ref, mask_ref, *refs):
    lse_refs, norm_ref, out_refs = refs[:readers], refs[readers], refs[readers + 1 :]
    kept = []
    for k, lse_ref in enumerate(lse_refs):
        kept.append(jnp.where(mask_ref[k : k + 1, :] > 0.0, lse_ref[...], -jnp.inf))
    highest = kept[0]
    for value in kept[1:]:
        highest = jnp.maximum(highest, value)
    spread = jnp.exp(kept[0] - highest)
    for value in kept[1:]:
        spread = spread + jnp.exp(value - highest)
    norm = highest + jnp.log(spread)
    norm_ref[...] = norm
    exponent = jnp.where(mask_ref[0:1, :] > 0.0, score_ref[...] - norm, -jnp.inf)
    posterior = jnp.exp(exponent).astype(jnp.bfloat16)
    count = posterior.shape[0] // members
    for q, piece in enumerate(pieces):
        sums = jnp.dot(posterior, all_ref[:, piece], preferred_element_type=jnp.float32)
        for s, out_ref in enumerate(out_refs[q * members : (q + 1) * members]):
            out_ref[...] = sums[s * count : (s + 1) * count].astype(out_ref.dtype)


def group_sums(members, pieces, all_images, scores, masks, lses):
    refs, slots = scores.shape
    width = all_images.shape[1]
    blocks = [
        jax.ShapeDtypeStruct((refs // members, piece.stop - piece.start), jnp.bfloat16)
        for piece in pieces
        for _ in range(members)
    ]
    norms, *outs = pl.pallas_call(
        partial(sums_kernel, len(lses), members, pieces),
        out_shape=(jax.ShapeDtypeStruct((1, slots), jnp.float32), *blocks),
        in_specs=[VMEM_SPEC] * (3 + len(lses)),
        out_specs=(VMEM_SPEC,) * (1 + len(blocks)),
        compiler_params=pltpu.CompilerParams(vmem_limit_bytes=SUMS_VMEM),
        cost_estimate=pl.CostEstimate(
            flops=2 * refs * slots * width,
            bytes_accessed=2 * slots * width,
            transcendentals=0,
        ),
        name="sums",
    )(all_images, scores, masks, *lses)
    return norms, [outs[q * members : (q + 1) * members] for q in range(len(pieces))]


def on_device(images, routes, projections, noise_weights):
    readers = lax.axis_size("reader")
    members = lax.axis_size("blk")
    reader = lax.axis_index("reader")
    rows, width = images.shape
    noise = noise_weights.reshape(1, width)

    gather = staged_gather if members == 4 and rows % 32 == 0 else plain_gather
    staged, last, far, route_blocks = gather(
        projections[0], images, noise, routes.T, readers // 4, readers // 2
    )
    split = lax.axis_size("sub") > 1
    scores, masks, mine, all_images = all_scores(staged, last, far, route_blocks, not split)
    if split:
        scores = lax.psum(scores, "sub")
        mine = group_lse(scores)
    lses = [mine] + [swap_bits(mine, "reader", k) for k in range(1, readers)]
    pieces = [slice(0, width // 2), slice(width // 2, width)]
    norms, parts = group_sums(members, pieces, all_images, scores, masks, lses)
    scatter = pair_scatter if members == 4 else line_scatter
    totals = scatter(parts, "blk")
    normalizer = lax.dynamic_slice(norms.reshape(-1), (reader * rows,), (rows,))
    return (jnp.concatenate(totals, axis=1)[None], normalizer)


def solution(mesh):
    return jax.shard_map(
        on_device,
        mesh=mesh,
        in_specs=(
            P(("parts", "blk", "reader"), "sub"),
            P(("parts", "blk", "reader"), None),
            P(("parts", "reader"), "blk", "sub"),
            P(("parts", "sub")),
        ),
        out_specs=(P(("parts", "reader"), "blk", "sub"), P(("parts", "blk", "reader"))),
        check_vma=False,
    )
```

```python
from functools import partial

import jax
import jax.numpy as jnp
from jax import lax
from jax.experimental import pallas as pl
from jax.experimental.pallas import tpu as pltpu
from jax.sharding import PartitionSpec as P

SCORE_VMEM = 20 * 1024 * 1024
SUMS_VMEM = 12 * 1024 * 1024
STEP = 1024
VMEM_SPEC = pl.BlockSpec(memory_space=pltpu.VMEM)
ANY_SPEC = pl.BlockSpec(memory_space=pl.ANY)
SIDES = [(0, 1), (1, 0), (2, 3), (3, 2)]
MIDDLE = [(1, 2), (2, 1), (0, 0), (3, 3)]


def swap_bits(block, axis, bits):
    return lax.ppermute(block, axis, [(i, i ^ bits) for i in range(lax.axis_size(axis))])


def swap_gather(block, axis, bit):
    held = {0: block}
    while bit:
        for k in list(held):
            held[k ^ bit] = swap_bits(held[k], axis, bit)
        bit //= 2
    return [held[k] for k in range(len(held))]


def add_rounded(one, other):
    return (one.astype(jnp.float32) + other.astype(jnp.float32)).astype(jnp.bfloat16)


def staged_gather(block, images, noise, routes, near_bits, far_bit):
    half = block.shape[1] // 2
    halves = [block[:, :half], block[:, half:]]
    crossed = swap_bits(images, "reader", far_bit)
    near = swap_gather(images, "reader", near_bits)
    firsts = [
        lax.optimization_barrier(
            (lax.ppermute(one, "blk", SIDES), lax.ppermute(one, "blk", MIDDLE))
        )
        for one in halves
    ]
    early = stage(
        [[[one] for one in halves], [[side] for side, _ in firsts]], near, noise
    )
    far_parts, end_parts = [], []
    for side, across in firsts:
        far = lax.ppermute(across, "blk", SIDES)
        across_far = lax.ppermute(side, "blk", MIDDLE)
        far, across_far, *early = lax.optimization_barrier((far, across_far, *early))
        end = lax.ppermute(across_far, "blk", SIDES)
        far_parts.append([far, across_far])
        end_parts.append([end, across])
    weighted, penalty, near, noise = early
    weights = stage_rest([far_parts, end_parts], weighted, penalty, noise)
    ends = [parts[0] for parts in end_parts]
    routes, crossed, *_ = lax.optimization_barrier((routes, crossed, *ends))
    return weights, near, swap_gather(crossed, "reader", near_bits), swap_all(routes)


def swap_all(routes):
    return [routes] + [swap_bits(routes, "reader", k) for k in range(1, lax.axis_size("reader"))]


def plain_gather(block, images, noise, routes, near_bits, far_bit):
    near = swap_gather(images, "reader", near_bits)
    far = swap_gather(swap_bits(images, "reader", far_bit), "reader", near_bits)
    line = [[[one]] for one in line_gather(block, "blk")]
    weighted, penalty, near, noise = stage(line[:2], near, noise)
    weights = stage_rest(line[2:], weighted, penalty, noise)
    return weights, near, far, swap_all(routes)


def line_gather(block, axis):
    size, member = lax.axis_size(axis), lax.axis_index(axis)
    ahead, behind = [block], [block]
    for s in range(1, size):
        ahead.append(lax.ppermute(ahead[-1], axis, [(i, i + 1) for i in range(s - 1, size - 1)]))
        behind.append(lax.ppermute(behind[-1], axis, [(i, i - 1) for i in range(1, size - s + 1)]))
    blocks = [block]
    for s in range(1, size):
        blocks.append(jnp.where(member >= s, ahead[s], behind[size - s]))
    return blocks


def pair_scatter(pieces, axis):
    member = lax.axis_index(axis)
    is_end = (member == 0) | (member == 3)
    for_far_end = [lax.ppermute(parts[3], axis, SIDES) for parts in pieces]
    *second, for_far_end[0] = lax.optimization_barrier(
        [parts[2] for parts in pieces] + for_far_end[:1]
    )
    for_far_middle = [lax.ppermute(part, axis, SIDES) for part in second]
    totals = []
    for parts, part, end, middle in zip(pieces, second, for_far_end, for_far_middle):
        across_end = lax.ppermute(add_rounded(part, end), axis, MIDDLE)
        across_middle = lax.ppermute(add_rounded(parts[3], middle), axis, MIDDLE)
        near = jnp.where(is_end, parts[1], add_rounded(parts[1], across_end))
        from_side = lax.ppermute(near, axis, SIDES)
        total = parts[0].astype(jnp.float32) + from_side.astype(jnp.float32)
        totals.append(total + jnp.where(is_end, 0.0, across_middle.astype(jnp.float32)))
    return totals


def line_scatter(pieces, axis):
    return [line_sum(parts, axis) for parts in pieces]


def line_sum(parts, axis):
    size = lax.axis_size(axis)
    up = down = None
    for s in range(1, size):
        send_up, send_down = parts[s], parts[size - s]
        if s > 1:
            send_up = add_rounded(send_up, up)
            send_down = add_rounded(send_down, down)
        up = lax.ppermute(send_up, axis, [(i, i + 1) for i in range(0, s) if i + 1 < size])
        down = lax.ppermute(send_down, axis, [(i, i - 1) for i in range(size - s, size) if i > 0])
    total = parts[0].astype(jnp.float32)
    if size > 1:
        total = total + up.astype(jnp.float32) + down.astype(jnp.float32)
    return total


def column_lse(scores):
    peak = jnp.max(scores, axis=0, keepdims=True)
    total = jnp.sum(jnp.exp(scores - peak), axis=0, keepdims=True)
    return peak + jnp.log(total)


def at_end():
    member = lax.axis_index("blk")
    return (member == 0) | (member == lax.axis_size("blk") - 1)


def either(refs, act):
    if len(refs) == 1:
        act(refs[0])
        return
    is_end = at_end()

    @pl.when(is_end)
    def _():
        act(refs[0])

    @pl.when(jnp.logical_not(is_end))
    def _():
        act(refs[1])


def weigh_blocks(groups, noise_ref, weighted_ref, penalty_ref, parts_ref, sems, first):
    count, width = parts_ref.shape[1:]

    def part_copy(i, ref):
        return pltpu.make_async_copy(ref, parts_ref.at[i], sems.at[i])

    parts = [part for group in groups for part in group]
    for i, part in enumerate(parts):
        either(part, lambda ref, i=i: part_copy(i, ref).start())
    i = 0
    for s, group in enumerate(groups):
        rows = slice((first + s) * count, (first + s + 1) * count)
        penalty = jnp.zeros((count, 1), jnp.float32)
        for q, part in enumerate(group):
            part_copy(i, part[0]).wait()
            for column in range(0, width, STEP):
                columns = slice(q * width + column, q * width + column + STEP)
                block = parts_ref[i, :, column : column + STEP].astype(jnp.float32)
                scaled = block * noise_ref[:, columns]
                weighted_ref[rows, columns] = scaled.astype(jnp.bfloat16)
                penalty = penalty + 0.5 * jnp.sum(scaled * block, axis=1, keepdims=True)
            i += 1
        penalty_ref[rows, :] = penalty


def take_blocks(refs, counts):
    return [[[refs.pop(0) for _ in range(n)] for n in group] for group in counts]


def block_counts(blocks):
    return [[len(part) for part in group] for group in blocks]


def flat(blocks):
    return [one for group in blocks for part in group for one in part]


def stage_kernel(near_count, counts, *refs):
    refs = list(refs)
    near_refs = [refs.pop(0) for _ in range(near_count)]
    groups = take_blocks(refs, counts)
    noise_ref, weighted_ref, penalty_ref, near_ref, noise_out_ref, parts_ref, near_sems, sems = refs
    rows = near_refs[0].shape[0]
    copies = []
    for k, ref in enumerate(near_refs):
        copy = pltpu.make_async_copy(ref, near_ref.at[pl.ds(k * rows, rows), :], near_sems.at[k])
        copy.start()
        copies.append(copy)
    noise_out_ref[...] = noise_ref[...]
    weigh_blocks(groups, noise_ref, weighted_ref, penalty_ref, parts_ref, sems, 0)
    for copy in copies:
        copy.wait()


def stage(blocks, near, noise):
    count, part_width = blocks[0][0][0].shape
    parts = sum(len(group) for group in blocks)
    width = noise.shape[1]
    refs = len(blocks) * count
    moved = [*near, *flat(blocks)]
    return pl.pallas_call(
        partial(stage_kernel, len(near), block_counts(blocks)),
        out_shape=(
            jax.ShapeDtypeStruct((refs, width), jnp.bfloat16),
            jax.ShapeDtypeStruct((refs, 1), jnp.float32),
            jax.ShapeDtypeStruct((len(near) * near[0].shape[0], width), jnp.bfloat16),
            jax.ShapeDtypeStruct((1, width), jnp.float32),
        ),
        in_specs=[ANY_SPEC] * len(moved) + [VMEM_SPEC],
        out_specs=(VMEM_SPEC,) * 4,
        scratch_shapes=[
            pltpu.VMEM((parts, count, part_width), jnp.bfloat16),
            pltpu.SemaphoreType.DMA((len(near),)),
            pltpu.SemaphoreType.DMA((parts,)),
        ],
        compiler_params=pltpu.CompilerParams(vmem_limit_bytes=SCORE_VMEM),
        cost_estimate=pl.CostEstimate(
            flops=8 * refs * width, bytes_accessed=12_000_000, transcendentals=0
        ),
        name="stage",
    )(*moved, noise)


def stage_rest_kernel(counts, *refs):
    refs = list(refs)
    groups = take_blocks(refs, counts)
    early_ref, early_penalty_ref, noise_ref, weighted_ref, penalty_ref, parts_ref, sems = refs
    done = early_ref.shape[0]
    weighted_ref[:done, :] = early_ref[...]
    penalty_ref[:done, :] = early_penalty_ref[...]
    first = done // parts_ref.shape[1]
    weigh_blocks(groups, noise_ref, weighted_ref, penalty_ref, parts_ref, sems, first)


def stage_rest(blocks, weighted, penalty, noise):
    count, part_width = blocks[0][0][0].shape
    parts = sum(len(group) for group in blocks)
    width = noise.shape[1]
    refs = len(blocks) * count + weighted.shape[0]
    moved = flat(blocks)
    return pl.pallas_call(
        partial(stage_rest_kernel, block_counts(blocks)),
        out_shape=(
            jax.ShapeDtypeStruct((refs, width), jnp.bfloat16),
            jax.ShapeDtypeStruct((refs, 1), jnp.float32),
        ),
        in_specs=[ANY_SPEC] * len(moved) + [VMEM_SPEC] * 3,
        out_specs=(VMEM_SPEC,) * 2,
        scratch_shapes=[
            pltpu.VMEM((parts, count, part_width), jnp.bfloat16),
            pltpu.SemaphoreType.DMA((parts,)),
        ],
        compiler_params=pltpu.CompilerParams(vmem_limit_bytes=SCORE_VMEM),
        cost_estimate=pl.CostEstimate(
            flops=8 * refs * width, bytes_accessed=12_000_000, transcendentals=0
        ),
        name="stage_rest",
    )(*moved, weighted, penalty, noise)


def score_kernel(readers, finish, *refs):
    refs = list(refs)
    near_ref = refs.pop(0)
    rows = near_ref.shape[0] * 2 // readers
    far_refs = [refs.pop(0) for _ in range(readers // 2)]
    weighted_ref, penalty_ref = refs.pop(0), refs.pop(0)
    route_refs = [refs.pop(0) for _ in range(readers)]
    score_ref, mask_ref, lse_ref, all_ref, image_sems = refs
    reader = lax.axis_index("reader")
    copies = []
    for k in range(readers):
        if k < readers // 2:
            source = near_ref.at[pl.ds(k * rows, rows), :]
        else:
            source = far_refs[k - readers // 2]
        row = pl.multiple_of((reader ^ k) * rows, 16)
        copy = pltpu.make_async_copy(source, all_ref.at[pl.ds(row, rows), :], image_sems.at[k])
        copy.start()
        copies.append(copy)
    routes = [ref[...] for ref in route_refs]
    bit = 1
    while bit < readers:
        flip = (reader & bit) > 0
        routes = [jnp.where(flip, routes[k ^ bit], one) for k, one in enumerate(routes)]
        bit *= 2
    for j, route in enumerate(routes):
        for k in range(readers):
            hits = jnp.where(route == (reader ^ k), 1.0, 0.0)
            mask_ref[k : k + 1, j * rows : (j + 1) * rows] = jnp.max(hits, axis=0, keepdims=True)
    for copy in copies:
        copy.wait()
    scores = lax.dot_general(
        all_ref[...],
        weighted_ref[...],
        (((1,), (1,)), ((), ())),
        preferred_element_type=jnp.float32,
    )
    scores = scores.T - penalty_ref[...]
    score_ref[...] = scores
    if finish:
        lse_ref[...] = column_lse(scores)


def all_scores(weights, near, far, routes, finish):
    weighted, penalty = weights
    refs, width = weighted.shape
    slots = 2 * near.shape[0]
    moved = [near, *far]
    return pl.pallas_call(
        partial(score_kernel, len(routes), finish),
        out_shape=(
            jax.ShapeDtypeStruct((refs, slots), jnp.float32),
            jax.ShapeDtypeStruct((len(routes), slots), jnp.float32),
            jax.ShapeDtypeStruct((1, slots), jnp.float32),
            jax.ShapeDtypeStruct((slots, width), jnp.bfloat16),
        ),
        in_specs=[ANY_SPEC] * len(moved) + [VMEM_SPEC] * (2 + len(routes)),
        out_specs=(VMEM_SPEC,) * 4,
        scratch_shapes=[pltpu.SemaphoreType.DMA((len(routes),))],
        compiler_params=pltpu.CompilerParams(vmem_limit_bytes=SCORE_VMEM),
        cost_estimate=pl.CostEstimate(
            flops=2 * refs * slots * width,
            bytes_accessed=2 * (slots + refs) * width,
            transcendentals=0,
        ),
        name="scores",
    )(*moved, weighted, penalty, *routes)


def lse_kernel(score_ref, lse_ref):
    lse_ref[...] = column_lse(score_ref[...])


def group_lse(scores):
    return pl.pallas_call(
        lse_kernel,
        out_shape=jax.ShapeDtypeStruct((1, scores.shape[1]), jnp.float32),
        name="group_lse",
    )(scores)


def sums_kernel(readers, members, pieces, all_ref, score_ref, mask_ref, *refs):
    lse_refs, norm_ref, out_refs = refs[:readers], refs[readers], refs[readers + 1 :]
    kept = []
    for k, lse_ref in enumerate(lse_refs):
        kept.append(jnp.where(mask_ref[k : k + 1, :] > 0.0, lse_ref[...], -jnp.inf))
    highest = kept[0]
    for value in kept[1:]:
        highest = jnp.maximum(highest, value)
    spread = jnp.exp(kept[0] - highest)
    for value in kept[1:]:
        spread = spread + jnp.exp(value - highest)
    norm = highest + jnp.log(spread)
    norm_ref[...] = norm
    exponent = jnp.where(mask_ref[0:1, :] > 0.0, score_ref[...] - norm, -jnp.inf)
    posterior = jnp.exp(exponent).astype(jnp.bfloat16)
    count = posterior.shape[0] // members
    for q, piece in enumerate(pieces):
        sums = jnp.dot(posterior, all_ref[:, piece], preferred_element_type=jnp.float32)
        for s, out_ref in enumerate(out_refs[q * members : (q + 1) * members]):
            out_ref[...] = sums[s * count : (s + 1) * count].astype(out_ref.dtype)


def group_sums(members, pieces, all_images, scores, masks, lses):
    refs, slots = scores.shape
    width = all_images.shape[1]
    blocks = [
        jax.ShapeDtypeStruct((refs // members, piece.stop - piece.start), jnp.bfloat16)
        for piece in pieces
        for _ in range(members)
    ]
    norms, *outs = pl.pallas_call(
        partial(sums_kernel, len(lses), members, pieces),
        out_shape=(jax.ShapeDtypeStruct((1, slots), jnp.float32), *blocks),
        in_specs=[VMEM_SPEC] * (3 + len(lses)),
        out_specs=(VMEM_SPEC,) * (1 + len(blocks)),
        compiler_params=pltpu.CompilerParams(vmem_limit_bytes=SUMS_VMEM),
        cost_estimate=pl.CostEstimate(
            flops=2 * refs * slots * width,
            bytes_accessed=2 * slots * width,
            transcendentals=0,
        ),
        name="sums",
    )(all_images, scores, masks, *lses)
    return norms, [outs[q * members : (q + 1) * members] for q in range(len(pieces))]


def on_device(images, routes, projections, noise_weights):
    readers = lax.axis_size("reader")
    members = lax.axis_size("blk")
    reader = lax.axis_index("reader")
    rows, width = images.shape
    noise = noise_weights.reshape(1, width)

    gather = staged_gather if members == 4 and rows % 32 == 0 and readers > 1 else plain_gather
    weights, near, far, route_blocks = gather(
        projections[0], images, noise, routes.T, readers // 4, readers // 2
    )
    split = lax.axis_size("sub") > 1
    scores, masks, mine, all_images = all_scores(weights, near, far, route_blocks, not split)
    if split:
        scores = lax.psum(scores, "sub")
        mine = group_lse(scores)
    lses = [mine] + [swap_bits(mine, "reader", k) for k in range(1, readers)]
    pieces = [slice(0, width // 2), slice(width // 2, width)]
    norms, parts = group_sums(members, pieces, all_images, scores, masks, lses)
    scatter = pair_scatter if members == 4 else line_scatter
    totals = scatter(parts, "blk")
    normalizer = lax.dynamic_slice(norms.reshape(-1), (reader * rows,), (rows,))
    return (jnp.concatenate(totals, axis=1)[None], normalizer)


def solution(mesh):
    return jax.shard_map(
        on_device,
        mesh=mesh,
        in_specs=(
            P(("parts", "blk", "reader"), "sub"),
            P(("parts", "blk", "reader"), None),
            P(("parts", "reader"), "blk", "sub"),
            P(("parts", "sub")),
        ),
        out_specs=(P(("parts", "reader"), "blk", "sub"), P(("parts", "blk", "reader"))),
        check_vma=False,
    )
```

```python
from functools import partial

import jax
import jax.numpy as jnp
from jax import lax
from jax.experimental import pallas as pl
from jax.experimental.pallas import tpu as pltpu
from jax.sharding import PartitionSpec as P

SCORE_VMEM = 20 * 1024 * 1024
SUMS_VMEM = 12 * 1024 * 1024
STEP = 1024
VMEM_SPEC = pl.BlockSpec(memory_space=pltpu.VMEM)
ANY_SPEC = pl.BlockSpec(memory_space=pl.ANY)
SIDES = [(0, 1), (1, 0), (2, 3), (3, 2)]
MIDDLE = [(1, 2), (2, 1)]


def swap_bits(block, axis, bits):
    return lax.ppermute(block, axis, [(i, i ^ bits) for i in range(lax.axis_size(axis))])


def swap_gather(block, axis, bit):
    held = {0: block}
    while bit:
        for k in list(held):
            held[k ^ bit] = swap_bits(held[k], axis, bit)
        bit //= 2
    return [held[k] for k in range(len(held))]


def add_rounded(one, other):
    return (one.astype(jnp.float32) + other.astype(jnp.float32)).astype(jnp.bfloat16)


def staged_gather(block, images, noise, routes, near_bits, far_bit):
    cut = block.shape[1] // 16 * 9
    cuts = [block[:, :cut], block[:, cut:]]
    crossed = swap_bits(images, "reader", far_bit)
    near = swap_gather(images, "reader", near_bits)
    firsts = [
        lax.optimization_barrier(
            (lax.ppermute(one, "blk", SIDES), lax.ppermute(one, "blk", MIDDLE))
        )
        for one in cuts
    ]
    early = stage(
        [[[one] for one in cuts], [[side] for side, _ in firsts]], near, noise
    )
    far_parts, end_parts = [], []
    for side, across in firsts:
        far = lax.ppermute(across, "blk", SIDES)
        across_far = lax.ppermute(side, "blk", MIDDLE)
        far, across_far, *early = lax.optimization_barrier((far, across_far, *early))
        end = lax.ppermute(across_far, "blk", SIDES)
        far_parts.append([far, across_far])
        end_parts.append([end, across])
    weighted, penalty, near, noise = early
    weights = stage_rest([far_parts, end_parts], weighted, penalty, noise)
    ends = [parts[0] for parts in end_parts]
    routes, crossed, *_ = lax.optimization_barrier((routes, crossed, *ends))
    return weights, near, swap_gather(crossed, "reader", near_bits), swap_all(routes)


def swap_all(routes):
    return [routes] + [swap_bits(routes, "reader", k) for k in range(1, lax.axis_size("reader"))]


def plain_gather(block, images, noise, routes, near_bits, far_bit):
    near = swap_gather(images, "reader", near_bits)
    far = swap_gather(swap_bits(images, "reader", far_bit), "reader", near_bits)
    line = [[[one]] for one in line_gather(block, "blk")]
    weighted, penalty, near, noise = stage(line[:2], near, noise)
    weights = stage_rest(line[2:], weighted, penalty, noise)
    return weights, near, far, swap_all(routes)


def line_gather(block, axis):
    size, member = lax.axis_size(axis), lax.axis_index(axis)
    ahead, behind = [block], [block]
    for s in range(1, size):
        ahead.append(lax.ppermute(ahead[-1], axis, [(i, i + 1) for i in range(s - 1, size - 1)]))
        behind.append(lax.ppermute(behind[-1], axis, [(i, i - 1) for i in range(1, size - s + 1)]))
    blocks = [block]
    for s in range(1, size):
        blocks.append(jnp.where(member >= s, ahead[s], behind[size - s]))
    return blocks


def pair_scatter(pieces, axis):
    member = lax.axis_index(axis)
    is_end = (member == 0) | (member == 3)
    for_far_end = [lax.ppermute(parts[3], axis, SIDES) for parts in pieces]
    *second, for_far_end[0] = lax.optimization_barrier(
        [parts[2] for parts in pieces] + for_far_end[:1]
    )
    for_far_middle = [lax.ppermute(part, axis, SIDES) for part in second]
    totals = []
    for parts, part, end, middle in zip(pieces, second, for_far_end, for_far_middle):
        across_end = lax.ppermute(add_rounded(part, end), axis, MIDDLE)
        across_middle = lax.ppermute(add_rounded(parts[3], middle), axis, MIDDLE)
        near = jnp.where(is_end, parts[1], add_rounded(parts[1], across_end))
        from_side = lax.ppermute(near, axis, SIDES)
        total = parts[0].astype(jnp.float32) + from_side.astype(jnp.float32)
        totals.append(total + jnp.where(is_end, 0.0, across_middle.astype(jnp.float32)))
    return beside(totals)


def beside_kernel(count, *refs):
    out_ref, sems = refs[count:]
    copies, stop = [], out_ref.shape[1]
    for i, ref in enumerate(refs[:count]):
        start = stop - ref.shape[1]
        copies.append(pltpu.make_async_copy(ref, out_ref.at[:, start:stop], sems.at[i]))
        copies[-1].start()
        stop = start
    for copy in copies:
        copy.wait()


def beside(pieces):
    width = sum(piece.shape[1] for piece in pieces)
    return pl.pallas_call(
        partial(beside_kernel, len(pieces)),
        out_shape=jax.ShapeDtypeStruct((pieces[0].shape[0], width), pieces[0].dtype),
        in_specs=[VMEM_SPEC] * len(pieces),
        out_specs=ANY_SPEC,
        scratch_shapes=[pltpu.SemaphoreType.DMA((len(pieces),))],
        compiler_params=pltpu.CompilerParams(vmem_limit_bytes=SUMS_VMEM),
        name="beside",
    )(*pieces[::-1])


def line_scatter(pieces, axis):
    return jnp.concatenate([line_sum(parts, axis) for parts in pieces], axis=1)


def line_sum(parts, axis):
    size = lax.axis_size(axis)
    up = down = None
    for s in range(1, size):
        send_up, send_down = parts[s], parts[size - s]
        if s > 1:
            send_up = add_rounded(send_up, up)
            send_down = add_rounded(send_down, down)
        up = lax.ppermute(send_up, axis, [(i, i + 1) for i in range(0, s) if i + 1 < size])
        down = lax.ppermute(send_down, axis, [(i, i - 1) for i in range(size - s, size) if i > 0])
    total = parts[0].astype(jnp.float32)
    if size > 1:
        total = total + up.astype(jnp.float32) + down.astype(jnp.float32)
    return total


def column_lse(scores):
    peak = jnp.max(scores, axis=0, keepdims=True)
    total = jnp.sum(jnp.exp(scores - peak), axis=0, keepdims=True)
    return peak + jnp.log(total)


def at_end():
    member = lax.axis_index("blk")
    return (member == 0) | (member == lax.axis_size("blk") - 1)


def either(refs, act):
    if len(refs) == 1:
        act(refs[0])
        return
    is_end = at_end()

    @pl.when(is_end)
    def _():
        act(refs[0])

    @pl.when(jnp.logical_not(is_end))
    def _():
        act(refs[1])


def weigh_blocks(groups, noise_ref, weighted_ref, penalty_ref, block_ref, sems, first):
    count = block_ref.shape[1]
    parts = []
    for s, group in enumerate(groups):
        start = 0
        for refs in group:
            stop = start + refs[0].shape[1]
            parts.append((s, slice(start, stop), refs))
            start = stop

    def part_copy(i, ref):
        s, columns, _ = parts[i]
        return pltpu.make_async_copy(ref, block_ref.at[s, :, columns], sems.at[i])

    for i, (_, _, refs) in enumerate(parts):
        either(refs, lambda ref, i=i: part_copy(i, ref).start())
    for s in range(len(groups)):
        rows = slice((first + s) * count, (first + s + 1) * count)
        penalty = jnp.zeros((count, 1), jnp.float32)
        for i, (t, columns, refs) in enumerate(parts):
            if t != s:
                continue
            part_copy(i, refs[0]).wait()
            for start in range(columns.start, columns.stop, STEP):
                piece = slice(start, min(start + STEP, columns.stop))
                block = block_ref[s, :, piece].astype(jnp.float32)
                scaled = block * noise_ref[:, piece]
                weighted_ref[rows, piece] = scaled.astype(jnp.bfloat16)
                penalty = penalty + 0.5 * jnp.sum(scaled * block, axis=1, keepdims=True)
        penalty_ref[rows, :] = penalty


def take_blocks(refs, counts):
    return [[[refs.pop(0) for _ in range(n)] for n in group] for group in counts]


def block_counts(blocks):
    return [[len(part) for part in group] for group in blocks]


def flat(blocks):
    return [one for group in blocks for part in group for one in part]


def stage_kernel(near_count, counts, *refs):
    refs = list(refs)
    near_refs = [refs.pop(0) for _ in range(near_count)]
    groups = take_blocks(refs, counts)
    noise_ref, weighted_ref, penalty_ref, near_ref, noise_out_ref, block_ref, near_sems, sems = refs
    rows = near_refs[0].shape[0]
    copies = []
    for k, ref in enumerate(near_refs):
        copy = pltpu.make_async_copy(ref, near_ref.at[pl.ds(k * rows, rows), :], near_sems.at[k])
        copy.start()
        copies.append(copy)
    noise_out_ref[...] = noise_ref[...]
    weigh_blocks(groups, noise_ref, weighted_ref, penalty_ref, block_ref, sems, 0)
    for copy in copies:
        copy.wait()


def stage(blocks, near, noise):
    count = blocks[0][0][0].shape[0]
    parts = sum(len(group) for group in blocks)
    width = noise.shape[1]
    refs = len(blocks) * count
    moved = [*near, *flat(blocks)]
    return pl.pallas_call(
        partial(stage_kernel, len(near), block_counts(blocks)),
        out_shape=(
            jax.ShapeDtypeStruct((refs, width), jnp.bfloat16),
            jax.ShapeDtypeStruct((refs, 1), jnp.float32),
            jax.ShapeDtypeStruct((len(near) * near[0].shape[0], width), jnp.bfloat16),
            jax.ShapeDtypeStruct((1, width), jnp.float32),
        ),
        in_specs=[ANY_SPEC] * len(moved) + [VMEM_SPEC],
        out_specs=(VMEM_SPEC,) * 4,
        scratch_shapes=[
            pltpu.VMEM((len(blocks), count, width), jnp.bfloat16),
            pltpu.SemaphoreType.DMA((len(near),)),
            pltpu.SemaphoreType.DMA((parts,)),
        ],
        compiler_params=pltpu.CompilerParams(vmem_limit_bytes=SCORE_VMEM),
        cost_estimate=pl.CostEstimate(
            flops=8 * refs * width, bytes_accessed=12_000_000, transcendentals=0
        ),
        name="stage",
    )(*moved, noise)


def stage_rest_kernel(counts, *refs):
    refs = list(refs)
    groups = take_blocks(refs, counts)
    early_ref, early_penalty_ref, noise_ref, weighted_ref, penalty_ref, block_ref, sems = refs
    done = early_ref.shape[0]
    weighted_ref[:done, :] = early_ref[...]
    penalty_ref[:done, :] = early_penalty_ref[...]
    first = done // block_ref.shape[1]
    weigh_blocks(groups, noise_ref, weighted_ref, penalty_ref, block_ref, sems, first)


def stage_rest(blocks, weighted, penalty, noise):
    count = blocks[0][0][0].shape[0]
    parts = sum(len(group) for group in blocks)
    width = noise.shape[1]
    refs = len(blocks) * count + weighted.shape[0]
    moved = flat(blocks)
    return pl.pallas_call(
        partial(stage_rest_kernel, block_counts(blocks)),
        out_shape=(
            jax.ShapeDtypeStruct((refs, width), jnp.bfloat16),
            jax.ShapeDtypeStruct((refs, 1), jnp.float32),
        ),
        in_specs=[ANY_SPEC] * len(moved) + [VMEM_SPEC] * 3,
        out_specs=(VMEM_SPEC,) * 2,
        scratch_shapes=[
            pltpu.VMEM((len(blocks), count, width), jnp.bfloat16),
            pltpu.SemaphoreType.DMA((parts,)),
        ],
        compiler_params=pltpu.CompilerParams(vmem_limit_bytes=SCORE_VMEM),
        cost_estimate=pl.CostEstimate(
            flops=8 * refs * width, bytes_accessed=12_000_000, transcendentals=0
        ),
        name="stage_rest",
    )(*moved, weighted, penalty, noise)


def score_kernel(readers, finish, *refs):
    refs = list(refs)
    near_ref = refs.pop(0)
    rows = near_ref.shape[0] * 2 // readers
    far_refs = [refs.pop(0) for _ in range(readers // 2)]
    weighted_ref, penalty_ref = refs.pop(0), refs.pop(0)
    route_refs = [refs.pop(0) for _ in range(readers)]
    score_ref, mask_ref, lse_ref, all_ref, image_sems = refs
    reader = lax.axis_index("reader")
    copies = []
    for k in range(readers):
        if k < readers // 2:
            source = near_ref.at[pl.ds(k * rows, rows), :]
        else:
            source = far_refs[k - readers // 2]
        row = pl.multiple_of((reader ^ k) * rows, 16)
        copy = pltpu.make_async_copy(source, all_ref.at[pl.ds(row, rows), :], image_sems.at[k])
        copy.start()
        copies.append(copy)
    routes = [ref[...] for ref in route_refs]
    bit = 1
    while bit < readers:
        flip = (reader & bit) > 0
        routes = [jnp.where(flip, routes[k ^ bit], one) for k, one in enumerate(routes)]
        bit *= 2
    for j, route in enumerate(routes):
        for k in range(readers):
            hits = jnp.where(route == (reader ^ k), 1.0, 0.0)
            mask_ref[k : k + 1, j * rows : (j + 1) * rows] = jnp.max(hits, axis=0, keepdims=True)
    for copy in copies:
        copy.wait()
    scores = lax.dot_general(
        all_ref[...],
        weighted_ref[...],
        (((1,), (1,)), ((), ())),
        preferred_element_type=jnp.float32,
    )
    scores = scores.T - penalty_ref[...]
    score_ref[...] = scores
    if finish:
        lse_ref[...] = column_lse(scores)


def all_scores(weights, near, far, routes, finish):
    weighted, penalty = weights
    refs, width = weighted.shape
    slots = 2 * near.shape[0]
    moved = [near, *far]
    return pl.pallas_call(
        partial(score_kernel, len(routes), finish),
        out_shape=(
            jax.ShapeDtypeStruct((refs, slots), jnp.float32),
            jax.ShapeDtypeStruct((len(routes), slots), jnp.float32),
            jax.ShapeDtypeStruct((1, slots), jnp.float32),
            jax.ShapeDtypeStruct((slots, width), jnp.bfloat16),
        ),
        in_specs=[ANY_SPEC] * len(moved) + [VMEM_SPEC] * (2 + len(routes)),
        out_specs=(VMEM_SPEC,) * 4,
        scratch_shapes=[pltpu.SemaphoreType.DMA((len(routes),))],
        compiler_params=pltpu.CompilerParams(vmem_limit_bytes=SCORE_VMEM),
        cost_estimate=pl.CostEstimate(
            flops=2 * refs * slots * width,
            bytes_accessed=2 * (slots + refs) * width,
            transcendentals=0,
        ),
        name="scores",
    )(*moved, weighted, penalty, *routes)


def lse_kernel(score_ref, lse_ref):
    lse_ref[...] = column_lse(score_ref[...])


def group_lse(scores):
    return pl.pallas_call(
        lse_kernel,
        out_shape=jax.ShapeDtypeStruct((1, scores.shape[1]), jnp.float32),
        name="group_lse",
    )(scores)


def sums_kernel(readers, members, pieces, all_ref, score_ref, mask_ref, *refs):
    lse_refs, norm_ref, out_refs = refs[:readers], refs[readers], refs[readers + 1 :]
    kept = []
    for k, lse_ref in enumerate(lse_refs):
        kept.append(jnp.where(mask_ref[k : k + 1, :] > 0.0, lse_ref[...], -jnp.inf))
    highest = kept[0]
    for value in kept[1:]:
        highest = jnp.maximum(highest, value)
    spread = jnp.exp(kept[0] - highest)
    for value in kept[1:]:
        spread = spread + jnp.exp(value - highest)
    norm = highest + jnp.log(spread)
    norm_ref[...] = norm
    exponent = jnp.where(mask_ref[0:1, :] > 0.0, score_ref[...] - norm, -jnp.inf)
    posterior = jnp.exp(exponent).astype(jnp.bfloat16)
    count = posterior.shape[0] // members
    for q, piece in enumerate(pieces):
        sums = jnp.dot(posterior, all_ref[:, piece], preferred_element_type=jnp.float32)
        for s, out_ref in enumerate(out_refs[q * members : (q + 1) * members]):
            out_ref[...] = sums[s * count : (s + 1) * count].astype(out_ref.dtype)


def group_sums(members, pieces, all_images, scores, masks, lses):
    refs, slots = scores.shape
    width = all_images.shape[1]
    blocks = [
        jax.ShapeDtypeStruct((refs // members, piece.stop - piece.start), jnp.bfloat16)
        for piece in pieces
        for _ in range(members)
    ]
    norms, *outs = pl.pallas_call(
        partial(sums_kernel, len(lses), members, pieces),
        out_shape=(jax.ShapeDtypeStruct((1, slots), jnp.float32), *blocks),
        in_specs=[VMEM_SPEC] * (3 + len(lses)),
        out_specs=(VMEM_SPEC,) * (1 + len(blocks)),
        compiler_params=pltpu.CompilerParams(vmem_limit_bytes=SUMS_VMEM),
        cost_estimate=pl.CostEstimate(
            flops=2 * refs * slots * width,
            bytes_accessed=2 * slots * width,
            transcendentals=0,
        ),
        name="sums",
    )(all_images, scores, masks, *lses)
    return norms, [outs[q * members : (q + 1) * members] for q in range(len(pieces))]


def on_device(images, routes, projections, noise_weights):
    readers = lax.axis_size("reader")
    members = lax.axis_size("blk")
    reader = lax.axis_index("reader")
    rows, width = images.shape
    noise = noise_weights.reshape(1, width)

    gather = staged_gather if members == 4 and rows % 32 == 0 and readers > 1 else plain_gather
    weights, near, far, route_blocks = gather(
        projections[0], images, noise, routes.T, readers // 4, readers // 2
    )
    split = lax.axis_size("sub") > 1
    scores, masks, mine, all_images = all_scores(weights, near, far, route_blocks, not split)
    if split:
        scores = lax.psum(scores, "sub")
        mine = group_lse(scores)
    lses = [mine] + [swap_bits(mine, "reader", k) for k in range(1, readers)]
    pieces = [slice(0, width // 2), slice(width // 2, width)]
    norms, parts = group_sums(members, pieces, all_images, scores, masks, lses)
    scatter = pair_scatter if members == 4 else line_scatter
    total = scatter(parts, "blk")
    normalizer = lax.dynamic_slice(norms.reshape(-1), (reader * rows,), (rows,))
    return (total[None], normalizer)


def solution(mesh):
    return jax.shard_map(
        on_device,
        mesh=mesh,
        in_specs=(
            P(("parts", "blk", "reader"), "sub"),
            P(("parts", "blk", "reader"), None),
            P(("parts", "reader"), "blk", "sub"),
            P(("parts", "sub")),
        ),
        out_specs=(P(("parts", "reader"), "blk", "sub"), P(("parts", "blk", "reader"))),
        check_vma=False,
    )
```

```python
from functools import partial

import jax
import jax.numpy as jnp
from jax import lax
from jax.experimental import pallas as pl
from jax.experimental.pallas import tpu as pltpu
from jax.sharding import PartitionSpec as P

SCORE_VMEM = 20 * 1024 * 1024
SUMS_VMEM = 12 * 1024 * 1024
STEP = 1024
VMEM_SPEC = pl.BlockSpec(memory_space=pltpu.VMEM)
ANY_SPEC = pl.BlockSpec(memory_space=pl.ANY)
SIDES = [(0, 1), (1, 0), (2, 3), (3, 2)]
MIDDLE = [(1, 2), (2, 1)]


def swap_bits(block, axis, bits):
    return lax.ppermute(block, axis, [(i, i ^ bits) for i in range(lax.axis_size(axis))])


def swap_gather(block, axis, bit):
    held = {0: block}
    while bit:
        for k in list(held):
            held[k ^ bit] = swap_bits(held[k], axis, bit)
        bit //= 2
    return [held[k] for k in range(len(held))]


def add_rounded(one, other):
    return (one.astype(jnp.float32) + other.astype(jnp.float32)).astype(jnp.bfloat16)


def staged_gather(block, images, noise, routes, near_bits, far_bit):
    cut = block.shape[1] // 16 * 9
    cuts = [block[:, :cut], block[:, cut:]]
    crossed = swap_bits(images, "reader", far_bit)
    near = swap_gather(images, "reader", near_bits)
    firsts = [
        lax.optimization_barrier(
            (lax.ppermute(one, "blk", SIDES), lax.ppermute(one, "blk", MIDDLE))
        )
        for one in cuts
    ]
    early = stage(
        [[[one] for one in cuts], [[side] for side, _ in firsts]], near, noise
    )
    far_parts, end_parts = [], []
    for side, across in firsts:
        far = lax.ppermute(across, "blk", SIDES)
        across_far = lax.ppermute(side, "blk", MIDDLE)
        far, across_far, *early = lax.optimization_barrier((far, across_far, *early))
        end = lax.ppermute(across_far, "blk", SIDES)
        far_parts.append([far, across_far])
        end_parts.append([end, across])
    weighted, penalty, near, noise = early
    weights = stage_rest([far_parts, end_parts], weighted, penalty, noise)
    ends = [parts[0] for parts in end_parts]
    routes, crossed, *_ = lax.optimization_barrier((routes, crossed, *ends))
    far = [[one] for one in swap_gather(crossed, "reader", near_bits)]
    return weights, near, far, swap_all(routes)


def swap_all(routes):
    return [routes] + [swap_bits(routes, "reader", k) for k in range(1, lax.axis_size("reader"))]


def plain_gather(block, images, noise, routes, near_bits, far_bit):
    near = swap_gather(images, "reader", near_bits)
    far = swap_gather(swap_bits(images, "reader", far_bit), "reader", near_bits)
    line = [[[one]] for one in line_gather(block, "blk")]
    weighted, penalty, near, noise = stage(line[:2], near, noise)
    weights = stage_rest(line[2:], weighted, penalty, noise)
    return weights, near, [[one] for one in far], swap_all(routes)


def line_gather(block, axis):
    size, member = lax.axis_size(axis), lax.axis_index(axis)
    ahead, behind = [block], [block]
    for s in range(1, size):
        ahead.append(lax.ppermute(ahead[-1], axis, [(i, i + 1) for i in range(s - 1, size - 1)]))
        behind.append(lax.ppermute(behind[-1], axis, [(i, i - 1) for i in range(1, size - s + 1)]))
    blocks = [block]
    for s in range(1, size):
        blocks.append(jnp.where(member >= s, ahead[s], behind[size - s]))
    return blocks


def pair_scatter(pieces, axis):
    member = lax.axis_index(axis)
    is_end = (member == 0) | (member == 3)
    for_far_end = [lax.ppermute(parts[3], axis, SIDES) for parts in pieces]
    *second, for_far_end[0] = lax.optimization_barrier(
        [parts[2] for parts in pieces] + for_far_end[:1]
    )
    for_far_middle = [lax.ppermute(part, axis, SIDES) for part in second]
    totals = []
    for parts, part, end, middle in zip(pieces, second, for_far_end, for_far_middle):
        across_end = lax.ppermute(add_rounded(part, end), axis, MIDDLE)
        across_middle = lax.ppermute(add_rounded(parts[3], middle), axis, MIDDLE)
        near = jnp.where(is_end, parts[1], add_rounded(parts[1], across_end))
        from_side = lax.ppermute(near, axis, SIDES)
        total = parts[0].astype(jnp.float32) + from_side.astype(jnp.float32)
        totals.append(total + jnp.where(is_end, 0.0, across_middle.astype(jnp.float32)))
    return beside(totals)


def beside_kernel(count, *refs):
    out_ref, sems = refs[count:]
    copies, stop = [], out_ref.shape[1]
    for i, ref in enumerate(refs[:count]):
        start = stop - ref.shape[1]
        copies.append(pltpu.make_async_copy(ref, out_ref.at[:, start:stop], sems.at[i]))
        copies[-1].start()
        stop = start
    for copy in copies:
        copy.wait()


def beside(pieces):
    width = sum(piece.shape[1] for piece in pieces)
    return pl.pallas_call(
        partial(beside_kernel, len(pieces)),
        out_shape=jax.ShapeDtypeStruct((pieces[0].shape[0], width), pieces[0].dtype),
        in_specs=[VMEM_SPEC] * len(pieces),
        out_specs=ANY_SPEC,
        scratch_shapes=[pltpu.SemaphoreType.DMA((len(pieces),))],
        compiler_params=pltpu.CompilerParams(vmem_limit_bytes=SUMS_VMEM),
        name="beside",
    )(*pieces[::-1])


def line_scatter(pieces, axis):
    return jnp.concatenate([line_sum(parts, axis) for parts in pieces], axis=1)


def line_sum(parts, axis):
    size = lax.axis_size(axis)
    up = down = None
    for s in range(1, size):
        send_up, send_down = parts[s], parts[size - s]
        if s > 1:
            send_up = add_rounded(send_up, up)
            send_down = add_rounded(send_down, down)
        up = lax.ppermute(send_up, axis, [(i, i + 1) for i in range(0, s) if i + 1 < size])
        down = lax.ppermute(send_down, axis, [(i, i - 1) for i in range(size - s, size) if i > 0])
    total = parts[0].astype(jnp.float32)
    if size > 1:
        total = total + up.astype(jnp.float32) + down.astype(jnp.float32)
    return total


def column_lse(scores):
    peak = jnp.max(scores, axis=0, keepdims=True)
    total = jnp.sum(jnp.exp(scores - peak), axis=0, keepdims=True)
    return peak + jnp.log(total)


def at_end():
    member = lax.axis_index("blk")
    return (member == 0) | (member == lax.axis_size("blk") - 1)


def either(refs, act):
    if len(refs) == 1:
        act(refs[0])
        return
    is_end = at_end()

    @pl.when(is_end)
    def _():
        act(refs[0])

    @pl.when(jnp.logical_not(is_end))
    def _():
        act(refs[1])


def weigh_blocks(groups, noise_ref, weighted_ref, penalty_ref, block_ref, sems, first):
    count = block_ref.shape[1]
    parts = []
    for s, group in enumerate(groups):
        start = 0
        for refs in group:
            stop = start + refs[0].shape[1]
            parts.append((s, slice(start, stop), refs))
            start = stop

    def part_copy(i, ref):
        s, columns, _ = parts[i]
        return pltpu.make_async_copy(ref, block_ref.at[s, :, columns], sems.at[i])

    for i, (_, _, refs) in enumerate(parts):
        either(refs, lambda ref, i=i: part_copy(i, ref).start())
    for s in range(len(groups)):
        rows = slice((first + s) * count, (first + s + 1) * count)
        penalty = jnp.zeros((count, 1), jnp.float32)
        for i, (t, columns, refs) in enumerate(parts):
            if t != s:
                continue
            part_copy(i, refs[0]).wait()
            for start in range(columns.start, columns.stop, STEP):
                piece = slice(start, min(start + STEP, columns.stop))
                block = block_ref[s, :, piece].astype(jnp.float32)
                scaled = block * noise_ref[:, piece]
                weighted_ref[rows, piece] = scaled.astype(jnp.bfloat16)
                penalty = penalty + 0.5 * jnp.sum(scaled * block, axis=1, keepdims=True)
        penalty_ref[rows, :] = penalty


def take_blocks(refs, counts):
    return [[[refs.pop(0) for _ in range(n)] for n in group] for group in counts]


def block_counts(blocks):
    return [[len(part) for part in group] for group in blocks]


def flat(blocks):
    return [one for group in blocks for part in group for one in part]


def stage_kernel(near_count, counts, *refs):
    refs = list(refs)
    near_refs = [refs.pop(0) for _ in range(near_count)]
    groups = take_blocks(refs, counts)
    noise_ref, weighted_ref, penalty_ref, near_ref, noise_out_ref, block_ref, near_sems, sems = refs
    rows = near_refs[0].shape[0]
    copies = []
    for k, ref in enumerate(near_refs):
        copy = pltpu.make_async_copy(ref, near_ref.at[pl.ds(k * rows, rows), :], near_sems.at[k])
        copy.start()
        copies.append(copy)
    noise_out_ref[...] = noise_ref[...]
    weigh_blocks(groups, noise_ref, weighted_ref, penalty_ref, block_ref, sems, 0)
    for copy in copies:
        copy.wait()


def stage(blocks, near, noise):
    count = blocks[0][0][0].shape[0]
    parts = sum(len(group) for group in blocks)
    width = noise.shape[1]
    refs = len(blocks) * count
    moved = [*near, *flat(blocks)]
    return pl.pallas_call(
        partial(stage_kernel, len(near), block_counts(blocks)),
        out_shape=(
            jax.ShapeDtypeStruct((refs, width), jnp.bfloat16),
            jax.ShapeDtypeStruct((refs, 1), jnp.float32),
            jax.ShapeDtypeStruct((len(near) * near[0].shape[0], width), jnp.bfloat16),
            jax.ShapeDtypeStruct((1, width), jnp.float32),
        ),
        in_specs=[ANY_SPEC] * len(moved) + [VMEM_SPEC],
        out_specs=(VMEM_SPEC,) * 4,
        scratch_shapes=[
            pltpu.VMEM((len(blocks), count, width), jnp.bfloat16),
            pltpu.SemaphoreType.DMA((len(near),)),
            pltpu.SemaphoreType.DMA((parts,)),
        ],
        compiler_params=pltpu.CompilerParams(vmem_limit_bytes=SCORE_VMEM),
        cost_estimate=pl.CostEstimate(
            flops=8 * refs * width, bytes_accessed=12_000_000, transcendentals=0
        ),
        name="stage",
    )(*moved, noise)


def stage_rest_kernel(counts, *refs):
    refs = list(refs)
    groups = take_blocks(refs, counts)
    early_ref, early_penalty_ref, noise_ref, turned_ref, penalty_ref = refs[:5]
    weighted_ref, block_ref, sems = refs[5:]
    done = early_ref.shape[0]
    weighted_ref[:done, :] = early_ref[...]
    penalty_ref[:done, :] = early_penalty_ref[...]
    first = done // block_ref.shape[1]
    weigh_blocks(groups, noise_ref, weighted_ref, penalty_ref, block_ref, sems, first)
    width = weighted_ref.shape[1]
    for start in range(0, width, STEP):
        piece = slice(start, min(start + STEP, width))
        turned_ref[piece, :] = weighted_ref[:, piece].T


def stage_rest(blocks, weighted, penalty, noise):
    count = blocks[0][0][0].shape[0]
    parts = sum(len(group) for group in blocks)
    width = noise.shape[1]
    refs = len(blocks) * count + weighted.shape[0]
    moved = flat(blocks)
    return pl.pallas_call(
        partial(stage_rest_kernel, block_counts(blocks)),
        out_shape=(
            jax.ShapeDtypeStruct((width, refs), jnp.bfloat16),
            jax.ShapeDtypeStruct((refs, 1), jnp.float32),
        ),
        in_specs=[ANY_SPEC] * len(moved) + [VMEM_SPEC] * 3,
        out_specs=(VMEM_SPEC,) * 2,
        scratch_shapes=[
            pltpu.VMEM((refs, width), jnp.bfloat16),
            pltpu.VMEM((len(blocks), count, width), jnp.bfloat16),
            pltpu.SemaphoreType.DMA((parts,)),
        ],
        compiler_params=pltpu.CompilerParams(vmem_limit_bytes=SCORE_VMEM),
        cost_estimate=pl.CostEstimate(
            flops=8 * refs * width, bytes_accessed=12_000_000, transcendentals=0
        ),
        name="stage_rest",
    )(*moved, weighted, penalty, noise)


def score_kernel(readers, far_counts, finish, *refs):
    refs = list(refs)
    near_ref = refs.pop(0)
    rows = near_ref.shape[0] * 2 // readers
    far_refs = [[refs.pop(0) for _ in range(n)] for n in far_counts]
    weighted_ref, penalty_ref = refs.pop(0), refs.pop(0)
    route_refs = [refs.pop(0) for _ in range(readers)]
    score_ref, mask_ref, lse_ref, all_ref, image_sems = refs
    reader = lax.axis_index("reader")
    copies = []
    for k in range(readers):
        if k < readers // 2:
            sources = [near_ref.at[pl.ds(k * rows, rows), :]]
        else:
            sources = far_refs[k - readers // 2]
        row, start = pl.multiple_of((reader ^ k) * rows, 16), 0
        for source in sources:
            columns = pl.ds(start, source.shape[1])
            copy = pltpu.make_async_copy(
                source, all_ref.at[pl.ds(row, rows), columns], image_sems.at[len(copies)]
            )
            copy.start()
            copies.append(copy)
            start += source.shape[1]
    routes = [ref[...] for ref in route_refs]
    bit = 1
    while bit < readers:
        flip = (reader & bit) > 0
        routes = [jnp.where(flip, routes[k ^ bit], one) for k, one in enumerate(routes)]
        bit *= 2
    for j, route in enumerate(routes):
        for k in range(readers):
            hits = jnp.where(route == (reader ^ k), 1.0, 0.0)
            mask_ref[k : k + 1, j * rows : (j + 1) * rows] = jnp.max(hits, axis=0, keepdims=True)
    for copy in copies:
        copy.wait()
    scores = jnp.dot(all_ref[...], weighted_ref[...], preferred_element_type=jnp.float32)
    scores = scores.T - penalty_ref[...]
    score_ref[...] = scores
    if finish:
        lse_ref[...] = column_lse(scores)


def all_scores(weights, near, far, routes, finish):
    weighted, penalty = weights
    width, refs = weighted.shape
    slots = 2 * near.shape[0]
    moved = [near, *[one for group in far for one in group]]
    return pl.pallas_call(
        partial(score_kernel, len(routes), [len(group) for group in far], finish),
        out_shape=(
            jax.ShapeDtypeStruct((refs, slots), jnp.float32),
            jax.ShapeDtypeStruct((len(routes), slots), jnp.float32),
            jax.ShapeDtypeStruct((1, slots), jnp.float32),
            jax.ShapeDtypeStruct((slots, width), jnp.bfloat16),
        ),
        in_specs=[ANY_SPEC] * len(moved) + [VMEM_SPEC] * (2 + len(routes)),
        out_specs=(VMEM_SPEC,) * 4,
        scratch_shapes=[pltpu.SemaphoreType.DMA((len(moved) + len(routes),))],
        compiler_params=pltpu.CompilerParams(vmem_limit_bytes=SCORE_VMEM),
        cost_estimate=pl.CostEstimate(
            flops=2 * refs * slots * width,
            bytes_accessed=2 * (slots + refs) * width,
            transcendentals=0,
        ),
        name="scores",
    )(*moved, weighted, penalty, *routes)


def lse_kernel(score_ref, lse_ref):
    lse_ref[...] = column_lse(score_ref[...])


def group_lse(scores):
    return pl.pallas_call(
        lse_kernel,
        out_shape=jax.ShapeDtypeStruct((1, scores.shape[1]), jnp.float32),
        name="group_lse",
    )(scores)


def sums_kernel(readers, members, pieces, all_ref, score_ref, mask_ref, *refs):
    lse_refs, norm_ref, out_refs = refs[:readers], refs[readers], refs[readers + 1 :]
    kept = []
    for k, lse_ref in enumerate(lse_refs):
        kept.append(jnp.where(mask_ref[k : k + 1, :] > 0.0, lse_ref[...], -jnp.inf))
    highest = kept[0]
    for value in kept[1:]:
        highest = jnp.maximum(highest, value)
    spread = jnp.exp(kept[0] - highest)
    for value in kept[1:]:
        spread = spread + jnp.exp(value - highest)
    norm = highest + jnp.log(spread)
    norm_ref[...] = norm
    exponent = jnp.where(mask_ref[0:1, :] > 0.0, score_ref[...] - norm, -jnp.inf)
    posterior = jnp.exp(exponent).astype(jnp.bfloat16)
    count = posterior.shape[0] // members
    for q, piece in enumerate(pieces):
        sums = jnp.dot(posterior, all_ref[:, piece], preferred_element_type=jnp.float32)
        for s, out_ref in enumerate(out_refs[q * members : (q + 1) * members]):
            out_ref[...] = sums[s * count : (s + 1) * count].astype(out_ref.dtype)


def group_sums(members, pieces, all_images, scores, masks, lses):
    refs, slots = scores.shape
    width = all_images.shape[1]
    blocks = [
        jax.ShapeDtypeStruct((refs // members, piece.stop - piece.start), jnp.bfloat16)
        for piece in pieces
        for _ in range(members)
    ]
    norms, *outs = pl.pallas_call(
        partial(sums_kernel, len(lses), members, pieces),
        out_shape=(jax.ShapeDtypeStruct((1, slots), jnp.float32), *blocks),
        in_specs=[VMEM_SPEC] * (3 + len(lses)),
        out_specs=(VMEM_SPEC,) * (1 + len(blocks)),
        compiler_params=pltpu.CompilerParams(vmem_limit_bytes=SUMS_VMEM),
        cost_estimate=pl.CostEstimate(
            flops=2 * refs * slots * width,
            bytes_accessed=2 * slots * width,
            transcendentals=0,
        ),
        name="sums",
    )(all_images, scores, masks, *lses)
    return norms, [outs[q * members : (q + 1) * members] for q in range(len(pieces))]


def on_device(images, routes, projections, noise_weights):
    readers = lax.axis_size("reader")
    members = lax.axis_size("blk")
    reader = lax.axis_index("reader")
    rows, width = images.shape
    noise = noise_weights.reshape(1, width)

    gather = staged_gather if members == 4 and rows % 16 == 0 and readers > 1 else plain_gather
    weights, near, far, route_blocks = gather(
        projections[0], images, noise, routes.T, readers // 4, readers // 2
    )
    split = lax.axis_size("sub") > 1
    scores, masks, mine, all_images = all_scores(weights, near, far, route_blocks, not split)
    if split:
        scores = lax.psum(scores, "sub")
        mine = group_lse(scores)
    lses = [mine] + [swap_bits(mine, "reader", k) for k in range(1, readers)]
    pieces = [slice(0, width // 2), slice(width // 2, width)]
    norms, parts = group_sums(members, pieces, all_images, scores, masks, lses)
    scatter = pair_scatter if members == 4 else line_scatter
    total = scatter(parts, "blk")
    normalizer = lax.dynamic_slice(norms.reshape(-1), (reader * rows,), (rows,))
    return (total[None], normalizer)


def solution(mesh):
    return jax.shard_map(
        on_device,
        mesh=mesh,
        in_specs=(
            P(("parts", "blk", "reader"), "sub"),
            P(("parts", "blk", "reader"), None),
            P(("parts", "reader"), "blk", "sub"),
            P(("parts", "sub")),
        ),
        out_specs=(P(("parts", "reader"), "blk", "sub"), P(("parts", "blk", "reader"))),
        check_vma=False,
    )
```

```python
from functools import partial

import jax
import jax.numpy as jnp
from jax import lax
from jax.experimental import pallas as pl
from jax.experimental.pallas import tpu as pltpu
from jax.sharding import PartitionSpec as P

SCORE_VMEM = 20 * 1024 * 1024
SUMS_VMEM = 12 * 1024 * 1024
STEP = 1024
VMEM_SPEC = pl.BlockSpec(memory_space=pltpu.VMEM)
ANY_SPEC = pl.BlockSpec(memory_space=pl.ANY)
SIDES = [(0, 1), (1, 0), (2, 3), (3, 2)]
MIDDLE = [(1, 2), (2, 1)]


def swap_bits(block, axis, bits):
    return lax.ppermute(block, axis, [(i, i ^ bits) for i in range(lax.axis_size(axis))])


def swap_gather(block, axis, bit):
    held = {0: block}
    while bit:
        for k in list(held):
            held[k ^ bit] = swap_bits(held[k], axis, bit)
        bit //= 2
    return [held[k] for k in range(len(held))]


def add_rounded(one, other):
    return (one.astype(jnp.float32) + other.astype(jnp.float32)).astype(jnp.bfloat16)


def staged_gather(block, images, noise, routes, near_bits, far_bit):
    cut = block.shape[1] // 16 * 9
    cuts = [block[:, :cut], block[:, cut:]]
    crossed = swap_bits(images, "reader", far_bit)
    near = swap_gather(images, "reader", near_bits)
    firsts = [
        lax.optimization_barrier(
            (lax.ppermute(one, "blk", SIDES), lax.ppermute(one, "blk", MIDDLE))
        )
        for one in cuts
    ]
    early = stage(
        [[[one] for one in cuts], [[side] for side, _ in firsts]], near, noise
    )
    far_parts, end_parts = [], []
    for side, across in firsts:
        far = lax.ppermute(across, "blk", SIDES)
        across_far = lax.ppermute(side, "blk", MIDDLE)
        far, across_far, *early = lax.optimization_barrier((far, across_far, *early))
        end = lax.ppermute(across_far, "blk", SIDES)
        far_parts.append([far, across_far])
        end_parts.append([end, across])
    weighted, penalty, near, noise = early
    ends = [parts[0] for parts in end_parts]
    routes, crossed, *_ = lax.optimization_barrier((routes, crossed, *ends))
    far = swap_gather(crossed, "reader", near_bits)
    weights = stage_rest([far_parts, end_parts], near, crossed, weighted, penalty, noise)
    return weights, far[1:], swap_all(routes)


def swap_all(routes):
    return [routes] + [swap_bits(routes, "reader", k) for k in range(1, lax.axis_size("reader"))]


def plain_gather(block, images, noise, routes, near_bits, far_bit):
    near = swap_gather(images, "reader", near_bits)
    far = swap_gather(swap_bits(images, "reader", far_bit), "reader", near_bits)
    line = [[[one]] for one in line_gather(block, "blk")]
    weighted, penalty, near, noise = stage(line[:2], near, noise)
    weights = stage_rest(line[2:], near, far[0], weighted, penalty, noise)
    return weights, far[1:], swap_all(routes)


def line_gather(block, axis):
    size, member = lax.axis_size(axis), lax.axis_index(axis)
    ahead, behind = [block], [block]
    for s in range(1, size):
        ahead.append(lax.ppermute(ahead[-1], axis, [(i, i + 1) for i in range(s - 1, size - 1)]))
        behind.append(lax.ppermute(behind[-1], axis, [(i, i - 1) for i in range(1, size - s + 1)]))
    blocks = [block]
    for s in range(1, size):
        blocks.append(jnp.where(member >= s, ahead[s], behind[size - s]))
    return blocks


def pair_scatter(pieces, axis):
    member = lax.axis_index(axis)
    is_end = (member == 0) | (member == 3)
    for_far_end = [lax.ppermute(parts[3], axis, SIDES) for parts in pieces]
    *second, for_far_end[0] = lax.optimization_barrier(
        [parts[2] for parts in pieces] + for_far_end[:1]
    )
    for_far_middle = [lax.ppermute(part, axis, SIDES) for part in second]
    totals = []
    for parts, part, end, middle in zip(pieces, second, for_far_end, for_far_middle):
        across_end = lax.ppermute(add_rounded(part, end), axis, MIDDLE)
        across_middle = lax.ppermute(add_rounded(parts[3], middle), axis, MIDDLE)
        near = jnp.where(is_end, parts[1], add_rounded(parts[1], across_end))
        from_side = lax.ppermute(near, axis, SIDES)
        total = parts[0].astype(jnp.float32) + from_side.astype(jnp.float32)
        totals.append(total + jnp.where(is_end, 0.0, across_middle.astype(jnp.float32)))
    return beside(totals)


def beside_kernel(count, *refs):
    out_ref, sems = refs[count:]
    copies, stop = [], out_ref.shape[1]
    for i, ref in enumerate(refs[:count]):
        start = stop - ref.shape[1]
        copies.append(pltpu.make_async_copy(ref, out_ref.at[:, start:stop], sems.at[i]))
        copies[-1].start()
        stop = start
    for copy in copies:
        copy.wait()


def beside(pieces):
    width = sum(piece.shape[1] for piece in pieces)
    return pl.pallas_call(
        partial(beside_kernel, len(pieces)),
        out_shape=jax.ShapeDtypeStruct((pieces[0].shape[0], width), pieces[0].dtype),
        in_specs=[VMEM_SPEC] * len(pieces),
        out_specs=ANY_SPEC,
        scratch_shapes=[pltpu.SemaphoreType.DMA((len(pieces),))],
        compiler_params=pltpu.CompilerParams(vmem_limit_bytes=SUMS_VMEM),
        name="beside",
    )(*pieces[::-1])


def line_scatter(pieces, axis):
    return jnp.concatenate([line_sum(parts, axis) for parts in pieces], axis=1)


def line_sum(parts, axis):
    size = lax.axis_size(axis)
    up = down = None
    for s in range(1, size):
        send_up, send_down = parts[s], parts[size - s]
        if s > 1:
            send_up = add_rounded(send_up, up)
            send_down = add_rounded(send_down, down)
        up = lax.ppermute(send_up, axis, [(i, i + 1) for i in range(0, s) if i + 1 < size])
        down = lax.ppermute(send_down, axis, [(i, i - 1) for i in range(size - s, size) if i > 0])
    total = parts[0].astype(jnp.float32)
    if size > 1:
        total = total + up.astype(jnp.float32) + down.astype(jnp.float32)
    return total


def column_lse(scores):
    peak = jnp.max(scores, axis=0, keepdims=True)
    total = jnp.sum(jnp.exp(scores - peak), axis=0, keepdims=True)
    return peak + jnp.log(total)


def at_end():
    member = lax.axis_index("blk")
    return (member == 0) | (member == lax.axis_size("blk") - 1)


def either(refs, act):
    if len(refs) == 1:
        act(refs[0])
        return
    is_end = at_end()

    @pl.when(is_end)
    def _():
        act(refs[0])

    @pl.when(jnp.logical_not(is_end))
    def _():
        act(refs[1])


def weigh_blocks(groups, noise_ref, weighted_ref, penalty_ref, block_ref, sems, first):
    count = block_ref.shape[1]
    parts = []
    for s, group in enumerate(groups):
        start = 0
        for refs in group:
            stop = start + refs[0].shape[1]
            parts.append((s, slice(start, stop), refs))
            start = stop

    def part_copy(i, ref):
        s, columns, _ = parts[i]
        return pltpu.make_async_copy(ref, block_ref.at[s, :, columns], sems.at[i])

    for i, (_, _, refs) in enumerate(parts):
        either(refs, lambda ref, i=i: part_copy(i, ref).start())
    for s in range(len(groups)):
        rows = slice((first + s) * count, (first + s + 1) * count)
        penalty = jnp.zeros((count, 1), jnp.float32)
        for i, (t, columns, refs) in enumerate(parts):
            if t != s:
                continue
            part_copy(i, refs[0]).wait()
            for start in range(columns.start, columns.stop, STEP):
                piece = slice(start, min(start + STEP, columns.stop))
                block = block_ref[s, :, piece].astype(jnp.float32)
                scaled = block * noise_ref[:, piece]
                weighted_ref[rows, piece] = scaled.astype(jnp.bfloat16)
                penalty = penalty + 0.5 * jnp.sum(scaled * block, axis=1, keepdims=True)
        penalty_ref[rows, :] = penalty


def take_blocks(refs, counts):
    return [[[refs.pop(0) for _ in range(n)] for n in group] for group in counts]


def block_counts(blocks):
    return [[len(part) for part in group] for group in blocks]


def flat(blocks):
    return [one for group in blocks for part in group for one in part]


def stage_kernel(near_count, counts, *refs):
    refs = list(refs)
    near_refs = [refs.pop(0) for _ in range(near_count)]
    groups = take_blocks(refs, counts)
    noise_ref, weighted_ref, penalty_ref, near_ref, noise_out_ref, block_ref, near_sems, sems = refs
    rows = near_refs[0].shape[0]
    copies = []
    for k, ref in enumerate(near_refs):
        copy = pltpu.make_async_copy(ref, near_ref.at[pl.ds(k * rows, rows), :], near_sems.at[k])
        copy.start()
        copies.append(copy)
    noise_out_ref[...] = noise_ref[...]
    weigh_blocks(groups, noise_ref, weighted_ref, penalty_ref, block_ref, sems, 0)
    for copy in copies:
        copy.wait()


def stage(blocks, near, noise):
    count = blocks[0][0][0].shape[0]
    parts = sum(len(group) for group in blocks)
    width = noise.shape[1]
    refs = len(blocks) * count
    moved = [*near, *flat(blocks)]
    return pl.pallas_call(
        partial(stage_kernel, len(near), block_counts(blocks)),
        out_shape=(
            jax.ShapeDtypeStruct((refs, width), jnp.bfloat16),
            jax.ShapeDtypeStruct((refs, 1), jnp.float32),
            jax.ShapeDtypeStruct((len(near) * near[0].shape[0], width), jnp.bfloat16),
            jax.ShapeDtypeStruct((1, width), jnp.float32),
        ),
        in_specs=[ANY_SPEC] * len(moved) + [VMEM_SPEC],
        out_specs=(VMEM_SPEC,) * 4,
        scratch_shapes=[
            pltpu.VMEM((len(blocks), count, width), jnp.bfloat16),
            pltpu.SemaphoreType.DMA((len(near),)),
            pltpu.SemaphoreType.DMA((parts,)),
        ],
        compiler_params=pltpu.CompilerParams(vmem_limit_bytes=SCORE_VMEM),
        cost_estimate=pl.CostEstimate(
            flops=8 * refs * width, bytes_accessed=12_000_000, transcendentals=0
        ),
        name="stage",
    )(*moved, noise)


def image_copies(groups, rows, all_ref, sems):
    reader = lax.axis_index("reader")
    copies = []
    for k, source in groups:
        row = pl.multiple_of((reader ^ k) * rows, 16)
        copies.append(
            pltpu.make_async_copy(source, all_ref.at[pl.ds(row, rows), :], sems.at[len(copies)])
        )
    return copies


def stage_rest_kernel(readers, counts, *refs):
    refs = list(refs)
    groups = take_blocks(refs, counts)
    near_ref, far_ref = refs.pop(0), refs.pop(0)
    early_ref, early_penalty_ref, noise_ref, turned_ref, penalty_ref, all_ref = refs[:6]
    weighted_ref, block_ref, sems, image_sems = refs[6:]
    rows = far_ref.shape[0]
    sources = [(k, near_ref.at[pl.ds(k * rows, rows), :]) for k in range(readers // 2)]
    copies = image_copies(sources + [(readers // 2, far_ref)], rows, all_ref, image_sems)
    for copy in copies:
        copy.start()
    done = early_ref.shape[0]
    weighted_ref[:done, :] = early_ref[...]
    penalty_ref[:done, :] = early_penalty_ref[...]
    first = done // block_ref.shape[1]
    weigh_blocks(groups, noise_ref, weighted_ref, penalty_ref, block_ref, sems, first)
    width = weighted_ref.shape[1]
    for start in range(0, width, STEP):
        piece = slice(start, min(start + STEP, width))
        turned_ref[piece, :] = weighted_ref[:, piece].T
    for copy in copies:
        copy.wait()


def stage_rest(blocks, near, crossed, weighted, penalty, noise):
    count = blocks[0][0][0].shape[0]
    parts = sum(len(group) for group in blocks)
    width = noise.shape[1]
    refs = len(blocks) * count + weighted.shape[0]
    readers = 2 * near.shape[0] // crossed.shape[0]
    moved = [*flat(blocks), near, crossed]
    return pl.pallas_call(
        partial(stage_rest_kernel, readers, block_counts(blocks)),
        out_shape=(
            jax.ShapeDtypeStruct((width, refs), jnp.bfloat16),
            jax.ShapeDtypeStruct((refs, 1), jnp.float32),
            jax.ShapeDtypeStruct((2 * near.shape[0], width), jnp.bfloat16),
        ),
        in_specs=[ANY_SPEC] * len(moved) + [VMEM_SPEC] * 3,
        out_specs=(VMEM_SPEC,) * 3,
        scratch_shapes=[
            pltpu.VMEM((refs, width), jnp.bfloat16),
            pltpu.VMEM((len(blocks), count, width), jnp.bfloat16),
            pltpu.SemaphoreType.DMA((parts,)),
            pltpu.SemaphoreType.DMA((readers // 2 + 1,)),
        ],
        compiler_params=pltpu.CompilerParams(vmem_limit_bytes=SCORE_VMEM),
        cost_estimate=pl.CostEstimate(
            flops=8 * refs * width, bytes_accessed=12_000_000, transcendentals=0
        ),
        name="stage_rest",
    )(*moved, weighted, penalty, noise)


def score_kernel(readers, finish, *refs):
    refs = list(refs)
    far_refs = [refs.pop(0) for _ in range(readers // 2 - 1)]
    weighted_ref, penalty_ref, _ = refs.pop(0), refs.pop(0), refs.pop(0)
    route_refs = [refs.pop(0) for _ in range(readers)]
    score_ref, mask_ref, lse_ref, all_ref, image_sems = refs
    reader = lax.axis_index("reader")
    rows = route_refs[0].shape[1]
    sources = [(readers // 2 + 1 + i, ref) for i, ref in enumerate(far_refs)]
    copies = image_copies(sources, rows, all_ref, image_sems)
    for copy in copies:
        copy.start()
    routes = [ref[...] for ref in route_refs]
    bit = 1
    while bit < readers:
        flip = (reader & bit) > 0
        routes = [jnp.where(flip, routes[k ^ bit], one) for k, one in enumerate(routes)]
        bit *= 2
    for j, route in enumerate(routes):
        for k in range(readers):
            hits = jnp.where(route == (reader ^ k), 1.0, 0.0)
            mask_ref[k : k + 1, j * rows : (j + 1) * rows] = jnp.max(hits, axis=0, keepdims=True)
    for copy in copies:
        copy.wait()
    scores = jnp.dot(all_ref[...], weighted_ref[...], preferred_element_type=jnp.float32)
    scores = scores.T - penalty_ref[...]
    score_ref[...] = scores
    if finish:
        lse_ref[...] = column_lse(scores)


def all_scores(weights, far, routes, finish):
    weighted, penalty, images = weights
    width, refs = weighted.shape
    slots = images.shape[0]
    return pl.pallas_call(
        partial(score_kernel, len(routes), finish),
        out_shape=(
            jax.ShapeDtypeStruct((refs, slots), jnp.float32),
            jax.ShapeDtypeStruct((len(routes), slots), jnp.float32),
            jax.ShapeDtypeStruct((1, slots), jnp.float32),
            jax.ShapeDtypeStruct((slots, width), jnp.bfloat16),
        ),
        in_specs=[ANY_SPEC] * len(far) + [VMEM_SPEC] * (3 + len(routes)),
        out_specs=(VMEM_SPEC,) * 4,
        scratch_shapes=[pltpu.SemaphoreType.DMA((len(far),))],
        input_output_aliases={len(far) + 2: 3},
        compiler_params=pltpu.CompilerParams(vmem_limit_bytes=SCORE_VMEM),
        cost_estimate=pl.CostEstimate(
            flops=2 * refs * slots * width,
            bytes_accessed=2 * (slots + refs) * width,
            transcendentals=0,
        ),
        name="scores",
    )(*far, weighted, penalty, images, *routes)


def lse_kernel(score_ref, lse_ref):
    lse_ref[...] = column_lse(score_ref[...])


def group_lse(scores):
    return pl.pallas_call(
        lse_kernel,
        out_shape=jax.ShapeDtypeStruct((1, scores.shape[1]), jnp.float32),
        name="group_lse",
    )(scores)


def sums_kernel(readers, members, pieces, all_ref, score_ref, mask_ref, *refs):
    lse_refs, norm_ref, out_refs = refs[:readers], refs[readers], refs[readers + 1 :]
    kept = []
    for k, lse_ref in enumerate(lse_refs):
        kept.append(jnp.where(mask_ref[k : k + 1, :] > 0.0, lse_ref[...], -jnp.inf))
    highest = kept[0]
    for value in kept[1:]:
        highest = jnp.maximum(highest, value)
    spread = jnp.exp(kept[0] - highest)
    for value in kept[1:]:
        spread = spread + jnp.exp(value - highest)
    norm = highest + jnp.log(spread)
    norm_ref[...] = norm
    exponent = jnp.where(mask_ref[0:1, :] > 0.0, score_ref[...] - norm, -jnp.inf)
    posterior = jnp.exp(exponent).astype(jnp.bfloat16)
    count = posterior.shape[0] // members
    for q, piece in enumerate(pieces):
        sums = jnp.dot(posterior, all_ref[:, piece], preferred_element_type=jnp.float32)
        for s, out_ref in enumerate(out_refs[q * members : (q + 1) * members]):
            out_ref[...] = sums[s * count : (s + 1) * count].astype(out_ref.dtype)


def group_sums(members, pieces, all_images, scores, masks, lses):
    refs, slots = scores.shape
    width = all_images.shape[1]
    blocks = [
        jax.ShapeDtypeStruct((refs // members, piece.stop - piece.start), jnp.bfloat16)
        for piece in pieces
        for _ in range(members)
    ]
    norms, *outs = pl.pallas_call(
        partial(sums_kernel, len(lses), members, pieces),
        out_shape=(jax.ShapeDtypeStruct((1, slots), jnp.float32), *blocks),
        in_specs=[VMEM_SPEC] * (3 + len(lses)),
        out_specs=(VMEM_SPEC,) * (1 + len(blocks)),
        compiler_params=pltpu.CompilerParams(vmem_limit_bytes=SUMS_VMEM),
        cost_estimate=pl.CostEstimate(
            flops=2 * refs * slots * width,
            bytes_accessed=2 * slots * width,
            transcendentals=0,
        ),
        name="sums",
    )(all_images, scores, masks, *lses)
    return norms, [outs[q * members : (q + 1) * members] for q in range(len(pieces))]


def on_device(images, routes, projections, noise_weights):
    readers = lax.axis_size("reader")
    members = lax.axis_size("blk")
    reader = lax.axis_index("reader")
    rows, width = images.shape
    noise = noise_weights.reshape(1, width)

    gather = staged_gather if members == 4 and rows % 16 == 0 and readers > 1 else plain_gather
    weights, far, route_blocks = gather(
        projections[0], images, noise, routes.T, readers // 4, readers // 2
    )
    split = lax.axis_size("sub") > 1
    scores, masks, mine, all_images = all_scores(weights, far, route_blocks, not split)
    if split:
        scores = lax.psum(scores, "sub")
        mine = group_lse(scores)
    lses = [mine] + [swap_bits(mine, "reader", k) for k in range(1, readers)]
    pieces = [slice(0, width // 2), slice(width // 2, width)]
    norms, parts = group_sums(members, pieces, all_images, scores, masks, lses)
    scatter = pair_scatter if members == 4 else line_scatter
    total = scatter(parts, "blk")
    normalizer = lax.dynamic_slice(norms.reshape(-1), (reader * rows,), (rows,))
    return (total[None], normalizer)


def solution(mesh):
    return jax.shard_map(
        on_device,
        mesh=mesh,
        in_specs=(
            P(("parts", "blk", "reader"), "sub"),
            P(("parts", "blk", "reader"), None),
            P(("parts", "reader"), "blk", "sub"),
            P(("parts", "sub")),
        ),
        out_specs=(P(("parts", "reader"), "blk", "sub"), P(("parts", "blk", "reader"))),
        check_vma=False,
    )
```

```python
from functools import partial

import jax
import jax.numpy as jnp
from jax import lax
from jax.experimental import pallas as pl
from jax.experimental.pallas import tpu as pltpu
from jax.sharding import PartitionSpec as P

SCORE_VMEM = 20 * 1024 * 1024
SUMS_VMEM = 12 * 1024 * 1024
STEP = 1024
VMEM_SPEC = pl.BlockSpec(memory_space=pltpu.VMEM)
ANY_SPEC = pl.BlockSpec(memory_space=pl.ANY)
SIDES = [(0, 1), (1, 0), (2, 3), (3, 2)]
MIDDLE = [(1, 2), (2, 1)]


def swap_bits(block, axis, bits):
    return lax.ppermute(block, axis, [(i, i ^ bits) for i in range(lax.axis_size(axis))])


def swap_gather(block, axis, bit):
    held = {0: block}
    while bit:
        for k in list(held):
            held[k ^ bit] = swap_bits(held[k], axis, bit)
        bit //= 2
    return [held[k] for k in range(len(held))]


def add_rounded(one, other):
    return (one.astype(jnp.float32) + other.astype(jnp.float32)).astype(jnp.bfloat16)


def staged_gather(block, images, noise, routes, near_bits, far_bit):
    cut = block.shape[1] // 16 * 9
    cuts = [block[:, :cut], block[:, cut:]]
    crossed = swap_bits(images, "reader", far_bit)
    near = swap_gather(images, "reader", near_bits)
    firsts = [
        lax.optimization_barrier(
            (lax.ppermute(one, "blk", SIDES), lax.ppermute(one, "blk", MIDDLE))
        )
        for one in cuts
    ]
    early = stage(
        [[[one] for one in cuts], [[side] for side, _ in firsts]], near, noise
    )
    far_parts, end_parts = [], []
    for side, across in firsts:
        far = lax.ppermute(across, "blk", SIDES)
        across_far = lax.ppermute(side, "blk", MIDDLE)
        far, across_far, *early = lax.optimization_barrier((far, across_far, *early))
        end = lax.ppermute(across_far, "blk", SIDES)
        far_parts.append([far, across_far])
        end_parts.append([end, across])
    weighted, penalty, near, noise = early
    weights = stage_rest([far_parts, end_parts], weighted, penalty, noise)
    ends = [parts[0] for parts in end_parts]
    routes, crossed, *_ = lax.optimization_barrier((routes, crossed, *ends))
    return weights, near, swap_gather(crossed, "reader", near_bits), swap_all(routes)


def swap_all(routes):
    return [routes] + [swap_bits(routes, "reader", k) for k in range(1, lax.axis_size("reader"))]


def plain_gather(block, images, noise, routes, near_bits, far_bit):
    near = swap_gather(images, "reader", near_bits)
    far = swap_gather(swap_bits(images, "reader", far_bit), "reader", near_bits)
    line = [[[one]] for one in line_gather(block, "blk")]
    weighted, penalty, near, noise = stage(line[:2], near, noise)
    weights = stage_rest(line[2:], weighted, penalty, noise)
    return weights, near, far, swap_all(routes)


def line_gather(block, axis):
    size, member = lax.axis_size(axis), lax.axis_index(axis)
    ahead, behind = [block], [block]
    for s in range(1, size):
        ahead.append(lax.ppermute(ahead[-1], axis, [(i, i + 1) for i in range(s - 1, size - 1)]))
        behind.append(lax.ppermute(behind[-1], axis, [(i, i - 1) for i in range(1, size - s + 1)]))
    blocks = [block]
    for s in range(1, size):
        blocks.append(jnp.where(member >= s, ahead[s], behind[size - s]))
    return blocks


def pair_scatter(pieces, axis):
    member = lax.axis_index(axis)
    is_end = (member == 0) | (member == 3)
    for_far_end = [lax.ppermute(parts[3], axis, SIDES) for parts in pieces]
    *second, for_far_end[0] = lax.optimization_barrier(
        [parts[2] for parts in pieces] + for_far_end[:1]
    )
    for_far_middle = [lax.ppermute(part, axis, SIDES) for part in second]
    totals = []
    for parts, part, end, middle in zip(pieces, second, for_far_end, for_far_middle):
        across_end = lax.ppermute(add_rounded(part, end), axis, MIDDLE)
        across_middle = lax.ppermute(add_rounded(parts[3], middle), axis, MIDDLE)
        near = jnp.where(is_end, parts[1], add_rounded(parts[1], across_end))
        from_side = lax.ppermute(near, axis, SIDES)
        total = parts[0].astype(jnp.float32) + from_side.astype(jnp.float32)
        totals.append(total + jnp.where(is_end, 0.0, across_middle.astype(jnp.float32)))
    return beside(totals)


def beside_kernel(count, *refs):
    out_ref, sems = refs[count:]
    copies, stop = [], out_ref.shape[1]
    for i, ref in enumerate(refs[:count]):
        start = stop - ref.shape[1]
        copies.append(pltpu.make_async_copy(ref, out_ref.at[:, start:stop], sems.at[i]))
        copies[-1].start()
        stop = start
    for copy in copies:
        copy.wait()


def beside(pieces):
    width = sum(piece.shape[1] for piece in pieces)
    return pl.pallas_call(
        partial(beside_kernel, len(pieces)),
        out_shape=jax.ShapeDtypeStruct((pieces[0].shape[0], width), pieces[0].dtype),
        in_specs=[VMEM_SPEC] * len(pieces),
        out_specs=ANY_SPEC,
        scratch_shapes=[pltpu.SemaphoreType.DMA((len(pieces),))],
        compiler_params=pltpu.CompilerParams(vmem_limit_bytes=SUMS_VMEM),
        name="beside",
    )(*pieces[::-1])


def line_scatter(pieces, axis):
    return jnp.concatenate([line_sum(parts, axis) for parts in pieces], axis=1)


def line_sum(parts, axis):
    size = lax.axis_size(axis)
    up = down = None
    for s in range(1, size):
        send_up, send_down = parts[s], parts[size - s]
        if s > 1:
            send_up = add_rounded(send_up, up)
            send_down = add_rounded(send_down, down)
        up = lax.ppermute(send_up, axis, [(i, i + 1) for i in range(0, s) if i + 1 < size])
        down = lax.ppermute(send_down, axis, [(i, i - 1) for i in range(size - s, size) if i > 0])
    total = parts[0].astype(jnp.float32)
    if size > 1:
        total = total + up.astype(jnp.float32) + down.astype(jnp.float32)
    return total


def column_lse(scores):
    peak = jnp.max(scores, axis=0, keepdims=True)
    total = jnp.sum(jnp.exp(scores - peak), axis=0, keepdims=True)
    return peak + jnp.log(total)


def at_end():
    member = lax.axis_index("blk")
    return (member == 0) | (member == lax.axis_size("blk") - 1)


def either(refs, act):
    if len(refs) == 1:
        act(refs[0])
        return
    is_end = at_end()

    @pl.when(is_end)
    def _():
        act(refs[0])

    @pl.when(jnp.logical_not(is_end))
    def _():
        act(refs[1])


def weigh_blocks(groups, noise_ref, weighted_ref, penalty_ref, block_ref, sems, first):
    count = block_ref.shape[1]
    parts = []
    for s, group in enumerate(groups):
        start = 0
        for refs in group:
            stop = start + refs[0].shape[1]
            parts.append((s, slice(start, stop), refs))
            start = stop

    def part_copy(i, ref):
        s, columns, _ = parts[i]
        return pltpu.make_async_copy(ref, block_ref.at[s, :, columns], sems.at[i])

    for i, (_, _, refs) in enumerate(parts):
        either(refs, lambda ref, i=i: part_copy(i, ref).start())
    for s in range(len(groups)):
        rows = slice((first + s) * count, (first + s + 1) * count)
        penalty = jnp.zeros((count, 1), jnp.float32)
        for i, (t, columns, refs) in enumerate(parts):
            if t != s:
                continue
            part_copy(i, refs[0]).wait()
            for start in range(columns.start, columns.stop, STEP):
                piece = slice(start, min(start + STEP, columns.stop))
                block = block_ref[s, :, piece].astype(jnp.float32)
                scaled = block * noise_ref[:, piece]
                weighted_ref[rows, piece] = scaled.astype(jnp.bfloat16)
                penalty = penalty + 0.5 * jnp.sum(scaled * block, axis=1, keepdims=True)
        penalty_ref[rows, :] = penalty


def take_blocks(refs, counts):
    return [[[refs.pop(0) for _ in range(n)] for n in group] for group in counts]


def block_counts(blocks):
    return [[len(part) for part in group] for group in blocks]


def flat(blocks):
    return [one for group in blocks for part in group for one in part]


def stage_kernel(near_count, counts, *refs):
    refs = list(refs)
    near_refs = [refs.pop(0) for _ in range(near_count)]
    groups = take_blocks(refs, counts)
    noise_ref, weighted_ref, penalty_ref, near_ref, noise_out_ref, block_ref, near_sems, sems = refs
    rows = near_refs[0].shape[0]
    copies = []
    for k, ref in enumerate(near_refs):
        copy = pltpu.make_async_copy(ref, near_ref.at[pl.ds(k * rows, rows), :], near_sems.at[k])
        copy.start()
        copies.append(copy)
    noise_out_ref[...] = noise_ref[...]
    weigh_blocks(groups, noise_ref, weighted_ref, penalty_ref, block_ref, sems, 0)
    for copy in copies:
        copy.wait()


def stage(blocks, near, noise):
    count = blocks[0][0][0].shape[0]
    parts = sum(len(group) for group in blocks)
    width = noise.shape[1]
    refs = len(blocks) * count
    moved = [*near, *flat(blocks)]
    return pl.pallas_call(
        partial(stage_kernel, len(near), block_counts(blocks)),
        out_shape=(
            jax.ShapeDtypeStruct((refs, width), jnp.bfloat16),
            jax.ShapeDtypeStruct((refs, 1), jnp.float32),
            jax.ShapeDtypeStruct((len(near) * near[0].shape[0], width), jnp.bfloat16),
            jax.ShapeDtypeStruct((1, width), jnp.float32),
        ),
        in_specs=[ANY_SPEC] * len(moved) + [VMEM_SPEC],
        out_specs=(VMEM_SPEC,) * 4,
        scratch_shapes=[
            pltpu.VMEM((len(blocks), count, width), jnp.bfloat16),
            pltpu.SemaphoreType.DMA((len(near),)),
            pltpu.SemaphoreType.DMA((parts,)),
        ],
        compiler_params=pltpu.CompilerParams(vmem_limit_bytes=SCORE_VMEM),
        cost_estimate=pl.CostEstimate(
            flops=8 * refs * width, bytes_accessed=12_000_000, transcendentals=0
        ),
        name="stage",
    )(*moved, noise)


def stage_rest_kernel(counts, *refs):
    refs = list(refs)
    groups = take_blocks(refs, counts)
    early_ref, early_penalty_ref, noise_ref, weighted_ref, penalty_ref, block_ref, sems = refs
    done = early_ref.shape[0]
    weighted_ref[:done, :] = early_ref[...]
    penalty_ref[:done, :] = early_penalty_ref[...]
    first = done // block_ref.shape[1]
    weigh_blocks(groups, noise_ref, weighted_ref, penalty_ref, block_ref, sems, first)


def stage_rest(blocks, weighted, penalty, noise):
    count = blocks[0][0][0].shape[0]
    parts = sum(len(group) for group in blocks)
    width = noise.shape[1]
    refs = len(blocks) * count + weighted.shape[0]
    moved = flat(blocks)
    return pl.pallas_call(
        partial(stage_rest_kernel, block_counts(blocks)),
        out_shape=(
            jax.ShapeDtypeStruct((refs, width), jnp.bfloat16),
            jax.ShapeDtypeStruct((refs, 1), jnp.float32),
        ),
        in_specs=[ANY_SPEC] * len(moved) + [VMEM_SPEC] * 3,
        out_specs=(VMEM_SPEC,) * 2,
        scratch_shapes=[
            pltpu.VMEM((len(blocks), count, width), jnp.bfloat16),
            pltpu.SemaphoreType.DMA((parts,)),
        ],
        compiler_params=pltpu.CompilerParams(vmem_limit_bytes=SCORE_VMEM),
        cost_estimate=pl.CostEstimate(
            flops=8 * refs * width, bytes_accessed=12_000_000, transcendentals=0
        ),
        name="stage_rest",
    )(*moved, weighted, penalty, noise)


def score_kernel(readers, finish, *refs):
    refs = list(refs)
    near_ref = refs.pop(0)
    rows = near_ref.shape[0] * 2 // readers
    far_refs = [refs.pop(0) for _ in range(readers // 2)]
    weighted_ref, penalty_ref = refs.pop(0), refs.pop(0)
    route_refs = [refs.pop(0) for _ in range(readers)]
    score_ref, mask_ref, lse_ref, all_ref, image_sems = refs
    reader = lax.axis_index("reader")
    copies = []
    for k in range(readers):
        if k < readers // 2:
            source = near_ref.at[pl.ds(k * rows, rows), :]
        else:
            source = far_refs[k - readers // 2]
        row = pl.multiple_of((reader ^ k) * rows, 16)
        copy = pltpu.make_async_copy(source, all_ref.at[pl.ds(row, rows), :], image_sems.at[k])
        copy.start()
        copies.append(copy)
    routes = [ref[...] for ref in route_refs]
    bit = 1
    while bit < readers:
        flip = (reader & bit) > 0
        routes = [jnp.where(flip, routes[k ^ bit], one) for k, one in enumerate(routes)]
        bit *= 2
    for j, route in enumerate(routes):
        for k in range(readers):
            hits = jnp.where(route == (reader ^ k), 1.0, 0.0)
            mask_ref[k : k + 1, j * rows : (j + 1) * rows] = jnp.max(hits, axis=0, keepdims=True)
    for copy in copies:
        copy.wait()
    scores = lax.dot_general(
        all_ref[...],
        weighted_ref[...],
        (((1,), (1,)), ((), ())),
        preferred_element_type=jnp.float32,
    )
    scores = scores.T - penalty_ref[...]
    score_ref[...] = scores
    if finish:
        lse_ref[...] = column_lse(scores)


def all_scores(weights, near, far, routes, finish):
    weighted, penalty = weights
    refs, width = weighted.shape
    slots = 2 * near.shape[0]
    moved = [near, *far]
    return pl.pallas_call(
        partial(score_kernel, len(routes), finish),
        out_shape=(
            jax.ShapeDtypeStruct((refs, slots), jnp.float32),
            jax.ShapeDtypeStruct((len(routes), slots), jnp.float32),
            jax.ShapeDtypeStruct((1, slots), jnp.float32),
            jax.ShapeDtypeStruct((slots, width), jnp.bfloat16),
        ),
        in_specs=[ANY_SPEC] * len(moved) + [VMEM_SPEC] * (2 + len(routes)),
        out_specs=(VMEM_SPEC,) * 4,
        scratch_shapes=[pltpu.SemaphoreType.DMA((len(routes),))],
        compiler_params=pltpu.CompilerParams(vmem_limit_bytes=SCORE_VMEM),
        cost_estimate=pl.CostEstimate(
            flops=2 * refs * slots * width,
            bytes_accessed=2 * (slots + refs) * width,
            transcendentals=0,
        ),
        name="scores",
    )(*moved, weighted, penalty, *routes)


def lse_kernel(score_ref, lse_ref):
    lse_ref[...] = column_lse(score_ref[...])


def group_lse(scores):
    return pl.pallas_call(
        lse_kernel,
        out_shape=jax.ShapeDtypeStruct((1, scores.shape[1]), jnp.float32),
        name="group_lse",
    )(scores)


def emit_sums(posterior, all_ref, piece, out_refs):
    sums = jnp.dot(posterior, all_ref[:, piece], preferred_element_type=jnp.float32)
    count = sums.shape[0] // len(out_refs)
    for s, out_ref in enumerate(out_refs):
        out_ref[...] = sums[s * count : (s + 1) * count].astype(out_ref.dtype)


def first_sums_kernel(readers, piece, all_ref, score_ref, mask_ref, *refs):
    lse_refs, norm_ref, post_ref = refs[:readers], refs[readers], refs[readers + 1]
    kept = []
    for k, lse_ref in enumerate(lse_refs):
        kept.append(jnp.where(mask_ref[k : k + 1, :] > 0.0, lse_ref[...], -jnp.inf))
    highest = kept[0]
    for value in kept[1:]:
        highest = jnp.maximum(highest, value)
    spread = jnp.exp(kept[0] - highest)
    for value in kept[1:]:
        spread = spread + jnp.exp(value - highest)
    norm = highest + jnp.log(spread)
    norm_ref[...] = norm
    exponent = jnp.where(mask_ref[0:1, :] > 0.0, score_ref[...] - norm, -jnp.inf)
    posterior = jnp.exp(exponent).astype(jnp.bfloat16)
    post_ref[...] = posterior
    emit_sums(posterior, all_ref, piece, refs[readers + 2 :])


def later_sums_kernel(piece, all_ref, post_ref, *out_refs):
    emit_sums(post_ref[...], all_ref, piece, out_refs)


def group_sums(kernel, piece, members, all_images, operands, extra):
    refs, slots = operands[0].shape
    width = piece.stop - piece.start
    block = jax.ShapeDtypeStruct((refs // members, width), jnp.bfloat16)
    outs = pl.pallas_call(
        kernel,
        out_shape=tuple(extra) + (block,) * members,
        in_specs=[VMEM_SPEC] * (1 + len(operands)),
        out_specs=(VMEM_SPEC,) * (len(extra) + members),
        compiler_params=pltpu.CompilerParams(vmem_limit_bytes=SUMS_VMEM),
        cost_estimate=pl.CostEstimate(
            flops=2 * refs * slots * width,
            bytes_accessed=2 * slots * width,
            transcendentals=0,
        ),
        name="sums",
    )(all_images, *operands)
    return outs[: len(extra)], outs[len(extra) :]


def on_device(images, routes, projections, noise_weights):
    readers = lax.axis_size("reader")
    members = lax.axis_size("blk")
    reader = lax.axis_index("reader")
    rows, width = images.shape
    noise = noise_weights.reshape(1, width)

    gather = staged_gather if members == 4 and rows % 32 == 0 and readers > 1 else plain_gather
    weights, near, far, route_blocks = gather(
        projections[0], images, noise, routes.T, readers // 4, readers // 2
    )
    split = lax.axis_size("sub") > 1
    scores, masks, mine, all_images = all_scores(weights, near, far, route_blocks, not split)
    if split:
        scores = lax.psum(scores, "sub")
        mine = group_lse(scores)
    lses = [mine] + [swap_bits(mine, "reader", k) for k in range(1, readers)]
    pieces = [slice(0, width // 2), slice(width // 2, width)]
    extra = (
        jax.ShapeDtypeStruct((1, scores.shape[1]), jnp.float32),
        jax.ShapeDtypeStruct(scores.shape, jnp.bfloat16),
    )
    (norms, posterior), first = group_sums(
        partial(first_sums_kernel, readers, pieces[0]),
        pieces[0],
        members,
        all_images,
        (scores, masks, *lses),
        extra,
    )
    _, last = group_sums(
        partial(later_sums_kernel, pieces[1]), pieces[1], members, all_images, (posterior,), ()
    )
    parts = [first, last]
    scatter = pair_scatter if members == 4 else line_scatter
    total = scatter(parts, "blk")
    normalizer = lax.dynamic_slice(norms.reshape(-1), (reader * rows,), (rows,))
    return (total[None], normalizer)


def solution(mesh):
    return jax.shard_map(
        on_device,
        mesh=mesh,
        in_specs=(
            P(("parts", "blk", "reader"), "sub"),
            P(("parts", "blk", "reader"), None),
            P(("parts", "reader"), "blk", "sub"),
            P(("parts", "sub")),
        ),
        out_specs=(P(("parts", "reader"), "blk", "sub"), P(("parts", "blk", "reader"))),
        check_vma=False,
    )
```

```python
from functools import partial

import jax
import jax.numpy as jnp
from jax import lax
from jax.experimental import pallas as pl
from jax.experimental.pallas import tpu as pltpu
from jax.sharding import PartitionSpec as P

SCORE_VMEM = 20 * 1024 * 1024
SUMS_VMEM = 12 * 1024 * 1024
STEP = 1024
VMEM_SPEC = pl.BlockSpec(memory_space=pltpu.VMEM)
ANY_SPEC = pl.BlockSpec(memory_space=pl.ANY)
SIDES = [(0, 1), (1, 0), (2, 3), (3, 2)]
MIDDLE = [(1, 2), (2, 1)]


def swap_bits(block, axis, bits):
    return lax.ppermute(block, axis, [(i, i ^ bits) for i in range(lax.axis_size(axis))])


def swap_gather(block, axis, bit):
    held = {0: block}
    while bit:
        for k in list(held):
            held[k ^ bit] = swap_bits(held[k], axis, bit)
        bit //= 2
    return [held[k] for k in range(len(held))]


def add_rounded(one, other):
    return (one.astype(jnp.float32) + other.astype(jnp.float32)).astype(jnp.bfloat16)


def staged_gather(block, images, noise, routes, near_bits, far_bit):
    cut = block.shape[1] // 16 * 9
    cuts = [block[:, :cut], block[:, cut:]]
    crossed = swap_bits(images, "reader", far_bit)
    near = swap_gather(images, "reader", near_bits)
    near_routes = swap_gather(routes, "reader", near_bits)
    firsts = [
        lax.optimization_barrier(
            (lax.ppermute(one, "blk", SIDES), lax.ppermute(one, "blk", MIDDLE))
        )
        for one in cuts
    ]
    early = stage(
        [[[one] for one in cuts], [[side] for side, _ in firsts]], near, noise, near_routes
    )
    far_parts, end_parts = [], []
    for side, across in firsts:
        far = lax.ppermute(across, "blk", SIDES)
        across_far = lax.ppermute(side, "blk", MIDDLE)
        far, across_far, *early = lax.optimization_barrier((far, across_far, *early))
        end = lax.ppermute(across_far, "blk", SIDES)
        far_parts.append([far, across_far])
        end_parts.append([end, across])
    weighted, penalty, near, noise, routes = early
    ends = [parts[0] for parts in end_parts]
    far_routes, crossed, *_ = lax.optimization_barrier((routes, crossed, *ends))
    far_routes = swap_bits(far_routes, "reader", far_bit)
    far = swap_gather(crossed, "reader", near_bits)
    staged = stage_rest([far_parts, end_parts], near, crossed, weighted, penalty, noise)
    return staged, far[1:], (routes, far_routes)


def plain_gather(block, images, noise, routes, near_bits, far_bit):
    near = swap_gather(images, "reader", near_bits)
    near_routes = swap_gather(routes, "reader", near_bits)
    far = swap_gather(swap_bits(images, "reader", far_bit), "reader", near_bits)
    line = [[[one]] for one in line_gather(block, "blk")]
    weighted, penalty, near, noise, routes = stage(line[:2], near, noise, near_routes)
    staged = stage_rest(line[2:], near, far[0], weighted, penalty, noise)
    return staged, far[1:], (routes, swap_bits(routes, "reader", far_bit))


def line_gather(block, axis):
    size, member = lax.axis_size(axis), lax.axis_index(axis)
    ahead, behind = [block], [block]
    for s in range(1, size):
        ahead.append(lax.ppermute(ahead[-1], axis, [(i, i + 1) for i in range(s - 1, size - 1)]))
        behind.append(lax.ppermute(behind[-1], axis, [(i, i - 1) for i in range(1, size - s + 1)]))
    blocks = [block]
    for s in range(1, size):
        blocks.append(jnp.where(member >= s, ahead[s], behind[size - s]))
    return blocks


def pair_scatter(pieces, axis):
    member = lax.axis_index(axis)
    is_end = (member == 0) | (member == 3)
    for_far_end = [lax.ppermute(parts[3], axis, SIDES) for parts in pieces]
    *second, for_far_end[0] = lax.optimization_barrier(
        [parts[2] for parts in pieces] + for_far_end[:1]
    )
    for_far_middle = [lax.ppermute(part, axis, SIDES) for part in second]
    totals = []
    for parts, part, end, middle in zip(pieces, second, for_far_end, for_far_middle):
        across_end = lax.ppermute(add_rounded(part, end), axis, MIDDLE)
        across_middle = lax.ppermute(add_rounded(parts[3], middle), axis, MIDDLE)
        near = jnp.where(is_end, parts[1], add_rounded(parts[1], across_end))
        from_side = lax.ppermute(near, axis, SIDES)
        total = parts[0].astype(jnp.float32) + from_side.astype(jnp.float32)
        totals.append(total + jnp.where(is_end, 0.0, across_middle.astype(jnp.float32)))
    return beside(totals)


def beside_kernel(count, *refs):
    out_ref, sems = refs[count:]
    copies, stop = [], out_ref.shape[1]
    for i, ref in enumerate(refs[:count]):
        start = stop - ref.shape[1]
        copies.append(pltpu.make_async_copy(ref, out_ref.at[:, start:stop], sems.at[i]))
        copies[-1].start()
        stop = start
    for copy in copies:
        copy.wait()


def beside(pieces):
    width = sum(piece.shape[1] for piece in pieces)
    return pl.pallas_call(
        partial(beside_kernel, len(pieces)),
        out_shape=jax.ShapeDtypeStruct((pieces[0].shape[0], width), pieces[0].dtype),
        in_specs=[VMEM_SPEC] * len(pieces),
        out_specs=ANY_SPEC,
        scratch_shapes=[pltpu.SemaphoreType.DMA((len(pieces),))],
        compiler_params=pltpu.CompilerParams(vmem_limit_bytes=SUMS_VMEM),
        name="beside",
    )(*pieces[::-1])


def line_scatter(pieces, axis):
    return jnp.concatenate([line_sum(parts, axis) for parts in pieces], axis=1)


def line_sum(parts, axis):
    size = lax.axis_size(axis)
    up = down = None
    for s in range(1, size):
        send_up, send_down = parts[s], parts[size - s]
        if s > 1:
            send_up = add_rounded(send_up, up)
            send_down = add_rounded(send_down, down)
        up = lax.ppermute(send_up, axis, [(i, i + 1) for i in range(0, s) if i + 1 < size])
        down = lax.ppermute(send_down, axis, [(i, i - 1) for i in range(size - s, size) if i > 0])
    total = parts[0].astype(jnp.float32)
    if size > 1:
        total = total + up.astype(jnp.float32) + down.astype(jnp.float32)
    return total


def column_lse(scores):
    peak = jnp.max(scores, axis=0, keepdims=True)
    total = jnp.sum(jnp.exp(scores - peak), axis=0, keepdims=True)
    return peak + jnp.log(total)


def at_end():
    member = lax.axis_index("blk")
    return (member == 0) | (member == lax.axis_size("blk") - 1)


def either(refs, act):
    if len(refs) == 1:
        act(refs[0])
        return
    is_end = at_end()

    @pl.when(is_end)
    def _():
        act(refs[0])

    @pl.when(jnp.logical_not(is_end))
    def _():
        act(refs[1])


def weigh_blocks(groups, noise_ref, weighted_ref, penalty_ref, block_ref, sems, first):
    count = block_ref.shape[1]
    parts = []
    for s, group in enumerate(groups):
        start = 0
        for refs in group:
            stop = start + refs[0].shape[1]
            parts.append((s, slice(start, stop), refs))
            start = stop

    def part_copy(i, ref):
        s, columns, _ = parts[i]
        return pltpu.make_async_copy(ref, block_ref.at[s, :, columns], sems.at[i])

    for i, (_, _, refs) in enumerate(parts):
        either(refs, lambda ref, i=i: part_copy(i, ref).start())
    for s in range(len(groups)):
        rows = slice((first + s) * count, (first + s + 1) * count)
        penalty = jnp.zeros((count, 1), jnp.float32)
        for i, (t, columns, refs) in enumerate(parts):
            if t != s:
                continue
            part_copy(i, refs[0]).wait()
            for start in range(columns.start, columns.stop, STEP):
                piece = slice(start, min(start + STEP, columns.stop))
                block = block_ref[s, :, piece].astype(jnp.float32)
                scaled = block * noise_ref[:, piece]
                weighted_ref[rows, piece] = scaled.astype(jnp.bfloat16)
                penalty = penalty + 0.5 * jnp.sum(scaled * block, axis=1, keepdims=True)
        penalty_ref[rows, :] = penalty


def take_blocks(refs, counts):
    return [[[refs.pop(0) for _ in range(n)] for n in group] for group in counts]


def block_counts(blocks):
    return [[len(part) for part in group] for group in blocks]


def flat(blocks):
    return [one for group in blocks for part in group for one in part]


def stage_kernel(near_count, counts, *refs):
    refs = list(refs)
    near_refs = [refs.pop(0) for _ in range(near_count)]
    groups = take_blocks(refs, counts)
    route_refs = [refs.pop(0) for _ in range(near_count)]
    noise_ref, weighted_ref, penalty_ref, near_ref, noise_out_ref, route_ref = refs[:6]
    block_ref, near_sems, sems = refs[6:]
    rows = near_refs[0].shape[0]
    top = route_refs[0].shape[0]
    for k, ref in enumerate(route_refs):
        route_ref[k * top : (k + 1) * top, :] = ref[...]
    copies = []
    for k, ref in enumerate(near_refs):
        copy = pltpu.make_async_copy(ref, near_ref.at[pl.ds(k * rows, rows), :], near_sems.at[k])
        copy.start()
        copies.append(copy)
    noise_out_ref[...] = noise_ref[...]
    weigh_blocks(groups, noise_ref, weighted_ref, penalty_ref, block_ref, sems, 0)
    for copy in copies:
        copy.wait()


def stage(blocks, near, noise, routes):
    count = blocks[0][0][0].shape[0]
    parts = sum(len(group) for group in blocks)
    width = noise.shape[1]
    refs = len(blocks) * count
    rows = near[0].shape[0]
    moved = [*near, *flat(blocks)]
    return pl.pallas_call(
        partial(stage_kernel, len(near), block_counts(blocks)),
        out_shape=(
            jax.ShapeDtypeStruct((refs, width), jnp.bfloat16),
            jax.ShapeDtypeStruct((refs, 1), jnp.float32),
            jax.ShapeDtypeStruct((len(near) * near[0].shape[0], width), jnp.bfloat16),
            jax.ShapeDtypeStruct((1, width), jnp.float32),
            jax.ShapeDtypeStruct((len(routes) * routes[0].shape[0], rows), jnp.int32),
        ),
        in_specs=[ANY_SPEC] * len(moved) + [VMEM_SPEC] * (len(routes) + 1),
        out_specs=(VMEM_SPEC,) * 5,
        scratch_shapes=[
            pltpu.VMEM((len(blocks), count, width), jnp.bfloat16),
            pltpu.SemaphoreType.DMA((len(near),)),
            pltpu.SemaphoreType.DMA((parts,)),
        ],
        compiler_params=pltpu.CompilerParams(vmem_limit_bytes=SCORE_VMEM),
        cost_estimate=pl.CostEstimate(
            flops=8 * refs * width, bytes_accessed=12_000_000, transcendentals=0
        ),
        name="stage",
    )(*moved, *routes, noise)


def place_images(k, source, all_ref, sem):
    rows = source.shape[0]
    row = pl.multiple_of((lax.axis_index("reader") ^ k) * rows, 16)
    return pltpu.make_async_copy(source, all_ref.at[pl.ds(row, rows), :], sem), pl.ds(row, rows)


def stage_rest_kernel(readers, counts, *refs):
    refs = list(refs)
    groups = take_blocks(refs, counts)
    near_ref, far_ref, early_ref, early_penalty_ref, noise_ref = [refs.pop(0) for _ in range(5)]
    turned_ref, penalty_ref, all_ref, product_ref = refs[:4]
    weighted_ref, block_ref, sems, image_sems = refs[4:]
    rows = far_ref.shape[0]
    half = readers // 2
    sources = [near_ref.at[pl.ds(k * rows, rows), :] for k in range(half)] + [far_ref]
    placed = [place_images(k, one, all_ref, image_sems.at[k]) for k, one in enumerate(sources)]
    for copy, _ in placed:
        copy.start()
    done = early_ref.shape[0]
    weighted_ref[:done, :] = early_ref[...]
    penalty_ref[:done, :] = early_penalty_ref[...]
    first = done // block_ref.shape[1]
    weigh_blocks(groups, noise_ref, weighted_ref, penalty_ref, block_ref, sems, first)
    width = weighted_ref.shape[1]
    for start in range(0, width, STEP):
        piece = slice(start, min(start + STEP, width))
        turned_ref[piece, :] = weighted_ref[:, piece].T
    products = jnp.dot(near_ref[...], turned_ref[...], preferred_element_type=jnp.float32)
    for k in range(half):
        product_ref[placed[k][1], :] = products[k * rows : (k + 1) * rows]
    product_ref[placed[half][1], :] = jnp.dot(
        far_ref[...], turned_ref[...], preferred_element_type=jnp.float32
    )
    for copy, _ in placed:
        copy.wait()


def stage_rest(blocks, near, crossed, weighted, penalty, noise):
    count = blocks[0][0][0].shape[0]
    parts = sum(len(group) for group in blocks)
    width = noise.shape[1]
    refs = len(blocks) * count + weighted.shape[0]
    slots = 2 * near.shape[0]
    readers = slots // crossed.shape[0]
    moved = flat(blocks)
    return pl.pallas_call(
        partial(stage_rest_kernel, readers, block_counts(blocks)),
        out_shape=(
            jax.ShapeDtypeStruct((width, refs), jnp.bfloat16),
            jax.ShapeDtypeStruct((refs, 1), jnp.float32),
            jax.ShapeDtypeStruct((slots, width), jnp.bfloat16),
            jax.ShapeDtypeStruct((slots, refs), jnp.float32),
        ),
        in_specs=[ANY_SPEC] * len(moved) + [VMEM_SPEC] * 5,
        out_specs=(VMEM_SPEC,) * 4,
        scratch_shapes=[
            pltpu.VMEM((refs, width), jnp.bfloat16),
            pltpu.VMEM((len(blocks), count, width), jnp.bfloat16),
            pltpu.SemaphoreType.DMA((parts,)),
            pltpu.SemaphoreType.DMA((readers // 2 + 1,)),
        ],
        compiler_params=pltpu.CompilerParams(vmem_limit_bytes=SCORE_VMEM),
        cost_estimate=pl.CostEstimate(
            flops=8 * refs * width, bytes_accessed=12_000_000, transcendentals=0
        ),
        name="stage_rest",
    )(*moved, near, crossed, weighted, penalty, noise)


def score_kernel(readers, finish, *refs):
    refs = list(refs)
    half = readers // 2
    far_refs = [refs.pop(0) for _ in range(half - 1)]
    turned_ref, penalty_ref, _, product_ref, near_route_ref, far_route_ref = refs[:6]
    score_ref, mask_ref, lse_ref, all_ref, sum_ref, image_sems = refs[6:]
    reader = lax.axis_index("reader")
    placed = [
        place_images(half + 1 + i, ref, all_ref, image_sems.at[i])
        for i, ref in enumerate(far_refs)
    ]
    for copy, _ in placed:
        copy.start()
    sum_ref[...] = product_ref[...]
    for (_, place), ref in zip(placed, far_refs):
        sum_ref[place, :] = jnp.dot(
            ref[...], turned_ref[...], preferred_element_type=jnp.float32
        )
    top, rows = near_route_ref.shape[0] // half, near_route_ref.shape[1]
    routes = [ref[k * top : (k + 1) * top, :] for ref in (near_route_ref, far_route_ref) for k in range(half)]
    bit = 1
    while bit < readers:
        flip = (reader & bit) > 0
        routes = [jnp.where(flip, routes[k ^ bit], one) for k, one in enumerate(routes)]
        bit *= 2
    for j, route in enumerate(routes):
        for k in range(readers):
            hits = jnp.where(route == (reader ^ k), 1.0, 0.0)
            mask_ref[k : k + 1, j * rows : (j + 1) * rows] = jnp.max(hits, axis=0, keepdims=True)
    scores = sum_ref[...].T - penalty_ref[...]
    score_ref[...] = scores
    if finish:
        lse_ref[...] = column_lse(scores)
    for copy, _ in placed:
        copy.wait()


def all_scores(staged, far, routes, finish):
    turned, penalty, images, products = staged
    width, refs = turned.shape
    slots, rows = images.shape[0], far[0].shape[0]
    readers = slots // rows
    return pl.pallas_call(
        partial(score_kernel, readers, finish),
        out_shape=(
            jax.ShapeDtypeStruct((refs, slots), jnp.float32),
            jax.ShapeDtypeStruct((readers, slots), jnp.float32),
            jax.ShapeDtypeStruct((1, slots), jnp.float32),
            jax.ShapeDtypeStruct((slots, width), jnp.bfloat16),
        ),
        in_specs=[VMEM_SPEC] * (len(far) + 6),
        out_specs=(VMEM_SPEC,) * 4,
        scratch_shapes=[
            pltpu.VMEM((slots, refs), jnp.float32),
            pltpu.SemaphoreType.DMA((len(far),)),
        ],
        input_output_aliases={len(far) + 2: 3},
        compiler_params=pltpu.CompilerParams(vmem_limit_bytes=SCORE_VMEM),
        cost_estimate=pl.CostEstimate(
            flops=2 * refs * slots * width,
            bytes_accessed=2 * (slots + refs) * width,
            transcendentals=0,
        ),
        name="scores",
    )(*far, turned, penalty, images, products, *routes)


def lse_kernel(score_ref, lse_ref):
    lse_ref[...] = column_lse(score_ref[...])


def group_lse(scores):
    return pl.pallas_call(
        lse_kernel,
        out_shape=jax.ShapeDtypeStruct((1, scores.shape[1]), jnp.float32),
        name="group_lse",
    )(scores)


def emit_sums(posterior, all_ref, piece, out_refs):
    sums = jnp.dot(posterior, all_ref[:, piece], preferred_element_type=jnp.float32)
    count = sums.shape[0] // len(out_refs)
    for s, out_ref in enumerate(out_refs):
        out_ref[...] = sums[s * count : (s + 1) * count].astype(out_ref.dtype)


def first_sums_kernel(readers, piece, all_ref, score_ref, mask_ref, *refs):
    lse_refs, norm_ref, post_ref = refs[:readers], refs[readers], refs[readers + 1]
    kept = []
    for k, lse_ref in enumerate(lse_refs):
        kept.append(jnp.where(mask_ref[k : k + 1, :] > 0.0, lse_ref[...], -jnp.inf))
    highest = kept[0]
    for value in kept[1:]:
        highest = jnp.maximum(highest, value)
    spread = jnp.exp(kept[0] - highest)
    for value in kept[1:]:
        spread = spread + jnp.exp(value - highest)
    norm = highest + jnp.log(spread)
    norm_ref[...] = norm
    exponent = jnp.where(mask_ref[0:1, :] > 0.0, score_ref[...] - norm, -jnp.inf)
    posterior = jnp.exp(exponent).astype(jnp.bfloat16)
    post_ref[...] = posterior
    emit_sums(posterior, all_ref, piece, refs[readers + 2 :])


def later_sums_kernel(piece, all_ref, post_ref, *out_refs):
    emit_sums(post_ref[...], all_ref, piece, out_refs)


def group_sums(kernel, piece, members, all_images, operands, extra):
    refs, slots = operands[0].shape
    width = piece.stop - piece.start
    block = jax.ShapeDtypeStruct((refs // members, width), jnp.bfloat16)
    outs = pl.pallas_call(
        kernel,
        out_shape=tuple(extra) + (block,) * members,
        in_specs=[VMEM_SPEC] * (1 + len(operands)),
        out_specs=(VMEM_SPEC,) * (len(extra) + members),
        compiler_params=pltpu.CompilerParams(vmem_limit_bytes=SUMS_VMEM),
        cost_estimate=pl.CostEstimate(
            flops=2 * refs * slots * width,
            bytes_accessed=2 * slots * width,
            transcendentals=0,
        ),
        name="sums",
    )(all_images, *operands)
    return outs[: len(extra)], outs[len(extra) :]


def on_device(images, routes, projections, noise_weights):
    readers = lax.axis_size("reader")
    members = lax.axis_size("blk")
    reader = lax.axis_index("reader")
    rows, width = images.shape
    noise = noise_weights.reshape(1, width)

    gather = staged_gather if members == 4 and rows % 32 == 0 and readers > 1 else plain_gather
    staged, far, all_routes = gather(
        projections[0], images, noise, routes.T, readers // 4, readers // 2
    )
    split = lax.axis_size("sub") > 1
    scores, masks, mine, all_images = all_scores(staged, far, all_routes, not split)
    if split:
        scores = lax.psum(scores, "sub")
        mine = group_lse(scores)
    lses = [mine] + [swap_bits(mine, "reader", k) for k in range(1, readers)]
    pieces = [slice(0, width // 2), slice(width // 2, width)]
    extra = (
        jax.ShapeDtypeStruct((1, scores.shape[1]), jnp.float32),
        jax.ShapeDtypeStruct(scores.shape, jnp.bfloat16),
    )
    (norms, posterior), first = group_sums(
        partial(first_sums_kernel, readers, pieces[0]),
        pieces[0],
        members,
        all_images,
        (scores, masks, *lses),
        extra,
    )
    _, last = group_sums(
        partial(later_sums_kernel, pieces[1]), pieces[1], members, all_images, (posterior,), ()
    )
    parts = [first, last]
    scatter = pair_scatter if members == 4 else line_scatter
    total = scatter(parts, "blk")
    normalizer = lax.dynamic_slice(norms.reshape(-1), (reader * rows,), (rows,))
    return (total[None], normalizer)


def solution(mesh):
    return jax.shard_map(
        on_device,
        mesh=mesh,
        in_specs=(
            P(("parts", "blk", "reader"), "sub"),
            P(("parts", "blk", "reader"), None),
            P(("parts", "reader"), "blk", "sub"),
            P(("parts", "sub")),
        ),
        out_specs=(P(("parts", "reader"), "blk", "sub"), P(("parts", "blk", "reader"))),
        check_vma=False,
    )
```

```python
from functools import partial

import jax
import jax.numpy as jnp
from jax import lax
from jax.experimental import pallas as pl
from jax.experimental.pallas import tpu as pltpu
from jax.sharding import PartitionSpec as P

SCORE_VMEM = 20 * 1024 * 1024
SUMS_VMEM = 12 * 1024 * 1024
STEP = 1024
VMEM_SPEC = pl.BlockSpec(memory_space=pltpu.VMEM)
ANY_SPEC = pl.BlockSpec(memory_space=pl.ANY)
SIDES = [(0, 1), (1, 0), (2, 3), (3, 2)]
MIDDLE = [(1, 2), (2, 1)]


def swap_bits(block, axis, bits):
    return lax.ppermute(block, axis, [(i, i ^ bits) for i in range(lax.axis_size(axis))])


def swap_gather(block, axis, bit):
    held = {0: block}
    while bit:
        for k in list(held):
            held[k ^ bit] = swap_bits(held[k], axis, bit)
        bit //= 2
    return [held[k] for k in range(len(held))]


def add_rounded(one, other):
    return (one.astype(jnp.float32) + other.astype(jnp.float32)).astype(jnp.bfloat16)


def staged_gather(block, images, noise, routes, near_bits, far_bit):
    cut = block.shape[1] // 16 * 9
    cuts = [block[:, :cut], block[:, cut:]]
    crossed = swap_bits(images, "reader", far_bit)
    near = swap_gather(images, "reader", near_bits)
    firsts = [
        lax.optimization_barrier(
            (lax.ppermute(one, "blk", SIDES), lax.ppermute(one, "blk", MIDDLE))
        )
        for one in cuts
    ]
    early = stage(
        [[[one] for one in cuts], [[side] for side, _ in firsts]], near, noise
    )
    far_parts, end_parts = [], []
    for side, across in firsts:
        far = lax.ppermute(across, "blk", SIDES)
        side, *_ = lax.optimization_barrier((side, *near))
        across_far = lax.ppermute(side, "blk", MIDDLE)
        far, across_far, *early = lax.optimization_barrier((far, across_far, *early))
        end = lax.ppermute(across_far, "blk", SIDES)
        far_parts.append([far, across_far])
        end_parts.append([end, across])
    weighted, penalty, staged_near, noise = early
    ends = [parts[0] for parts in end_parts]
    routes, crossed, *_ = lax.optimization_barrier((routes, crossed, *ends))
    far = swap_gather(crossed, "reader", near_bits)
    staged = stage_rest([far_parts, end_parts], staged_near, crossed, weighted, penalty, noise)
    return staged, far[1:], swap_all(routes)


def swap_all(routes):
    return [routes] + [swap_bits(routes, "reader", k) for k in range(1, lax.axis_size("reader"))]


def plain_gather(block, images, noise, routes, near_bits, far_bit):
    near = swap_gather(images, "reader", near_bits)
    far = swap_gather(swap_bits(images, "reader", far_bit), "reader", near_bits)
    line = [[[one]] for one in line_gather(block, "blk")]
    weighted, penalty, near, noise = stage(line[:2], near, noise)
    staged = stage_rest(line[2:], near, far[0], weighted, penalty, noise)
    return staged, far[1:], swap_all(routes)


def line_gather(block, axis):
    size, member = lax.axis_size(axis), lax.axis_index(axis)
    ahead, behind = [block], [block]
    for s in range(1, size):
        ahead.append(lax.ppermute(ahead[-1], axis, [(i, i + 1) for i in range(s - 1, size - 1)]))
        behind.append(lax.ppermute(behind[-1], axis, [(i, i - 1) for i in range(1, size - s + 1)]))
    blocks = [block]
    for s in range(1, size):
        blocks.append(jnp.where(member >= s, ahead[s], behind[size - s]))
    return blocks


def pair_scatter(pieces, axis):
    member = lax.axis_index(axis)
    is_end = (member == 0) | (member == 3)
    for_far_end = [lax.ppermute(parts[3], axis, SIDES) for parts in pieces]
    *second, for_far_end[0] = lax.optimization_barrier(
        [parts[2] for parts in pieces] + for_far_end[:1]
    )
    for_far_middle = [lax.ppermute(part, axis, SIDES) for part in second]
    totals = []
    for parts, part, end, middle in zip(pieces, second, for_far_end, for_far_middle):
        across_end = lax.ppermute(add_rounded(part, end), axis, MIDDLE)
        across_middle = lax.ppermute(add_rounded(parts[3], middle), axis, MIDDLE)
        near = jnp.where(is_end, parts[1], add_rounded(parts[1], across_end))
        from_side = lax.ppermute(near, axis, SIDES)
        total = parts[0].astype(jnp.float32) + from_side.astype(jnp.float32)
        totals.append(total + jnp.where(is_end, 0.0, across_middle.astype(jnp.float32)))
    return beside(totals)


def beside_kernel(count, *refs):
    out_ref, sems = refs[count:]
    copies, stop = [], out_ref.shape[1]
    for i, ref in enumerate(refs[:count]):
        start = stop - ref.shape[1]
        copies.append(pltpu.make_async_copy(ref, out_ref.at[:, start:stop], sems.at[i]))
        copies[-1].start()
        stop = start
    for copy in copies:
        copy.wait()


def beside(pieces):
    width = sum(piece.shape[1] for piece in pieces)
    return pl.pallas_call(
        partial(beside_kernel, len(pieces)),
        out_shape=jax.ShapeDtypeStruct((pieces[0].shape[0], width), pieces[0].dtype),
        in_specs=[VMEM_SPEC] * len(pieces),
        out_specs=ANY_SPEC,
        scratch_shapes=[pltpu.SemaphoreType.DMA((len(pieces),))],
        compiler_params=pltpu.CompilerParams(vmem_limit_bytes=SUMS_VMEM),
        name="beside",
    )(*pieces[::-1])


def line_scatter(pieces, axis):
    return jnp.concatenate([line_sum(parts, axis) for parts in pieces], axis=1)


def line_sum(parts, axis):
    size = lax.axis_size(axis)
    up = down = None
    for s in range(1, size):
        send_up, send_down = parts[s], parts[size - s]
        if s > 1:
            send_up = add_rounded(send_up, up)
            send_down = add_rounded(send_down, down)
        up = lax.ppermute(send_up, axis, [(i, i + 1) for i in range(0, s) if i + 1 < size])
        down = lax.ppermute(send_down, axis, [(i, i - 1) for i in range(size - s, size) if i > 0])
    total = parts[0].astype(jnp.float32)
    if size > 1:
        total = total + up.astype(jnp.float32) + down.astype(jnp.float32)
    return total


def column_lse(scores):
    peak = jnp.max(scores, axis=0, keepdims=True)
    total = jnp.sum(jnp.exp(scores - peak), axis=0, keepdims=True)
    return peak + jnp.log(total)


def at_end():
    member = lax.axis_index("blk")
    return (member == 0) | (member == lax.axis_size("blk") - 1)


def either(refs, act):
    if len(refs) == 1:
        act(refs[0])
        return
    is_end = at_end()

    @pl.when(is_end)
    def _():
        act(refs[0])

    @pl.when(jnp.logical_not(is_end))
    def _():
        act(refs[1])


def weigh_blocks(groups, noise_ref, weighted_ref, penalty_ref, block_ref, sems, first):
    count = block_ref.shape[1]
    parts = []
    for s, group in enumerate(groups):
        start = 0
        for refs in group:
            stop = start + refs[0].shape[1]
            parts.append((s, slice(start, stop), refs))
            start = stop

    def part_copy(i, ref):
        s, columns, _ = parts[i]
        return pltpu.make_async_copy(ref, block_ref.at[s, :, columns], sems.at[i])

    for i, (_, _, refs) in enumerate(parts):
        either(refs, lambda ref, i=i: part_copy(i, ref).start())
    for s in range(len(groups)):
        rows = slice((first + s) * count, (first + s + 1) * count)
        penalty = jnp.zeros((count, 1), jnp.float32)
        for i, (t, columns, refs) in enumerate(parts):
            if t != s:
                continue
            part_copy(i, refs[0]).wait()
            for start in range(columns.start, columns.stop, STEP):
                piece = slice(start, min(start + STEP, columns.stop))
                block = block_ref[s, :, piece].astype(jnp.float32)
                scaled = block * noise_ref[:, piece]
                weighted_ref[rows, piece] = scaled.astype(jnp.bfloat16)
                penalty = penalty + 0.5 * jnp.sum(scaled * block, axis=1, keepdims=True)
        penalty_ref[rows, :] = penalty


def take_blocks(refs, counts):
    return [[[refs.pop(0) for _ in range(n)] for n in group] for group in counts]


def block_counts(blocks):
    return [[len(part) for part in group] for group in blocks]


def flat(blocks):
    return [one for group in blocks for part in group for one in part]


def stage_kernel(near_count, counts, *refs):
    refs = list(refs)
    near_refs = [refs.pop(0) for _ in range(near_count)]
    groups = take_blocks(refs, counts)
    noise_ref, weighted_ref, penalty_ref, near_ref, noise_out_ref, block_ref, near_sems, sems = refs
    rows = near_refs[0].shape[0]
    copies = []
    for k, ref in enumerate(near_refs):
        copy = pltpu.make_async_copy(ref, near_ref.at[pl.ds(k * rows, rows), :], near_sems.at[k])
        copy.start()
        copies.append(copy)
    noise_out_ref[...] = noise_ref[...]
    weigh_blocks(groups, noise_ref, weighted_ref, penalty_ref, block_ref, sems, 0)
    for copy in copies:
        copy.wait()


def stage(blocks, near, noise):
    count = blocks[0][0][0].shape[0]
    parts = sum(len(group) for group in blocks)
    width = noise.shape[1]
    refs = len(blocks) * count
    moved = [*near, *flat(blocks)]
    return pl.pallas_call(
        partial(stage_kernel, len(near), block_counts(blocks)),
        out_shape=(
            jax.ShapeDtypeStruct((refs, width), jnp.bfloat16),
            jax.ShapeDtypeStruct((refs, 1), jnp.float32),
            jax.ShapeDtypeStruct((len(near) * near[0].shape[0], width), jnp.bfloat16),
            jax.ShapeDtypeStruct((1, width), jnp.float32),
        ),
        in_specs=[ANY_SPEC] * len(moved) + [VMEM_SPEC],
        out_specs=(VMEM_SPEC,) * 4,
        scratch_shapes=[
            pltpu.VMEM((len(blocks), count, width), jnp.bfloat16),
            pltpu.SemaphoreType.DMA((len(near),)),
            pltpu.SemaphoreType.DMA((parts,)),
        ],
        compiler_params=pltpu.CompilerParams(vmem_limit_bytes=SCORE_VMEM),
        cost_estimate=pl.CostEstimate(
            flops=8 * refs * width, bytes_accessed=12_000_000, transcendentals=0
        ),
        name="stage",
    )(*moved, noise)


def place_images(k, source, all_ref, sem):
    rows = source.shape[0]
    row = pl.multiple_of((lax.axis_index("reader") ^ k) * rows, 16)
    return pltpu.make_async_copy(source, all_ref.at[pl.ds(row, rows), :], sem), pl.ds(row, rows)


def stage_rest_kernel(readers, counts, *refs):
    refs = list(refs)
    groups = take_blocks(refs, counts)
    near_ref, far_ref, early_ref, early_penalty_ref, noise_ref = [refs.pop(0) for _ in range(5)]
    turned_ref, penalty_ref, all_ref, product_ref = refs[:4]
    weighted_ref, block_ref, sems, image_sems = refs[4:]
    rows = far_ref.shape[0]
    half = readers // 2
    sources = [near_ref.at[pl.ds(k * rows, rows), :] for k in range(half)] + [far_ref]
    placed = [place_images(k, one, all_ref, image_sems.at[k]) for k, one in enumerate(sources)]
    for copy, _ in placed:
        copy.start()
    done = early_ref.shape[0]
    weighted_ref[:done, :] = early_ref[...]
    penalty_ref[:done, :] = early_penalty_ref[...]
    first = done // block_ref.shape[1]
    weigh_blocks(groups, noise_ref, weighted_ref, penalty_ref, block_ref, sems, first)
    width = weighted_ref.shape[1]
    for start in range(0, width, STEP):
        piece = slice(start, min(start + STEP, width))
        turned_ref[piece, :] = weighted_ref[:, piece].T
    products = jnp.dot(near_ref[...], turned_ref[...], preferred_element_type=jnp.float32)
    for k in range(half):
        product_ref[placed[k][1], :] = products[k * rows : (k + 1) * rows]
    product_ref[placed[half][1], :] = jnp.dot(
        far_ref[...], turned_ref[...], preferred_element_type=jnp.float32
    )
    for copy, _ in placed:
        copy.wait()


def stage_rest(blocks, near, crossed, weighted, penalty, noise):
    count = blocks[0][0][0].shape[0]
    parts = sum(len(group) for group in blocks)
    width = noise.shape[1]
    refs = len(blocks) * count + weighted.shape[0]
    slots = 2 * near.shape[0]
    readers = slots // crossed.shape[0]
    moved = flat(blocks)
    return pl.pallas_call(
        partial(stage_rest_kernel, readers, block_counts(blocks)),
        out_shape=(
            jax.ShapeDtypeStruct((width, refs), jnp.bfloat16),
            jax.ShapeDtypeStruct((refs, 1), jnp.float32),
            jax.ShapeDtypeStruct((slots, width), jnp.bfloat16),
            jax.ShapeDtypeStruct((slots, refs), jnp.float32),
        ),
        in_specs=[ANY_SPEC] * len(moved) + [VMEM_SPEC] * 5,
        out_specs=(VMEM_SPEC,) * 4,
        scratch_shapes=[
            pltpu.VMEM((refs, width), jnp.bfloat16),
            pltpu.VMEM((len(blocks), count, width), jnp.bfloat16),
            pltpu.SemaphoreType.DMA((parts,)),
            pltpu.SemaphoreType.DMA((readers // 2 + 1,)),
        ],
        compiler_params=pltpu.CompilerParams(vmem_limit_bytes=SCORE_VMEM),
        cost_estimate=pl.CostEstimate(
            flops=8 * refs * width, bytes_accessed=12_000_000, transcendentals=0
        ),
        name="stage_rest",
    )(*moved, near, crossed, weighted, penalty, noise)


def score_kernel(readers, finish, *refs):
    refs = list(refs)
    half = readers // 2
    far_refs = [refs.pop(0) for _ in range(half - 1)]
    turned_ref, penalty_ref, _, product_ref = [refs.pop(0) for _ in range(4)]
    route_refs = [refs.pop(0) for _ in range(readers)]
    score_ref, mask_ref, lse_ref, all_ref, sum_ref, image_sems = refs
    reader = lax.axis_index("reader")
    placed = [
        place_images(half + 1 + i, ref, all_ref, image_sems.at[i])
        for i, ref in enumerate(far_refs)
    ]
    for copy, _ in placed:
        copy.start()
    sum_ref[...] = product_ref[...]
    for (_, place), ref in zip(placed, far_refs):
        sum_ref[place, :] = jnp.dot(
            ref[...], turned_ref[...], preferred_element_type=jnp.float32
        )
    rows = route_refs[0].shape[1]
    routes = [ref[...] for ref in route_refs]
    bit = 1
    while bit < readers:
        flip = (reader & bit) > 0
        routes = [jnp.where(flip, routes[k ^ bit], one) for k, one in enumerate(routes)]
        bit *= 2
    for j, route in enumerate(routes):
        for k in range(readers):
            hits = jnp.where(route == (reader ^ k), 1.0, 0.0)
            mask_ref[k : k + 1, j * rows : (j + 1) * rows] = jnp.max(hits, axis=0, keepdims=True)
    scores = sum_ref[...].T - penalty_ref[...]
    score_ref[...] = scores
    if finish:
        lse_ref[...] = column_lse(scores)
    for copy, _ in placed:
        copy.wait()


def all_scores(staged, far, routes, finish):
    turned, penalty, images, products = staged
    width, refs = turned.shape
    slots, rows = images.shape[0], far[0].shape[0]
    readers = slots // rows
    return pl.pallas_call(
        partial(score_kernel, readers, finish),
        out_shape=(
            jax.ShapeDtypeStruct((refs, slots), jnp.float32),
            jax.ShapeDtypeStruct((readers, slots), jnp.float32),
            jax.ShapeDtypeStruct((1, slots), jnp.float32),
            jax.ShapeDtypeStruct((slots, width), jnp.bfloat16),
        ),
        in_specs=[VMEM_SPEC] * (len(far) + 4 + len(routes)),
        out_specs=(VMEM_SPEC,) * 4,
        scratch_shapes=[
            pltpu.VMEM((slots, refs), jnp.float32),
            pltpu.SemaphoreType.DMA((len(far),)),
        ],
        input_output_aliases={len(far) + 2: 3},
        compiler_params=pltpu.CompilerParams(vmem_limit_bytes=SCORE_VMEM),
        cost_estimate=pl.CostEstimate(
            flops=2 * refs * slots * width,
            bytes_accessed=2 * (slots + refs) * width,
            transcendentals=0,
        ),
        name="scores",
    )(*far, turned, penalty, images, products, *routes)


def lse_kernel(score_ref, lse_ref):
    lse_ref[...] = column_lse(score_ref[...])


def group_lse(scores):
    return pl.pallas_call(
        lse_kernel,
        out_shape=jax.ShapeDtypeStruct((1, scores.shape[1]), jnp.float32),
        name="group_lse",
    )(scores)


def emit_sums(posterior, all_ref, piece, out_refs):
    sums = jnp.dot(posterior, all_ref[:, piece], preferred_element_type=jnp.float32)
    count = sums.shape[0] // len(out_refs)
    for s, out_ref in enumerate(out_refs):
        out_ref[...] = sums[s * count : (s + 1) * count].astype(out_ref.dtype)


def first_sums_kernel(readers, piece, all_ref, score_ref, mask_ref, *refs):
    lse_refs, norm_ref, post_ref = refs[:readers], refs[readers], refs[readers + 1]
    kept = []
    for k, lse_ref in enumerate(lse_refs):
        kept.append(jnp.where(mask_ref[k : k + 1, :] > 0.0, lse_ref[...], -jnp.inf))
    highest = kept[0]
    for value in kept[1:]:
        highest = jnp.maximum(highest, value)
    spread = jnp.exp(kept[0] - highest)
    for value in kept[1:]:
        spread = spread + jnp.exp(value - highest)
    norm = highest + jnp.log(spread)
    norm_ref[...] = norm
    exponent = jnp.where(mask_ref[0:1, :] > 0.0, score_ref[...] - norm, -jnp.inf)
    posterior = jnp.exp(exponent).astype(jnp.bfloat16)
    post_ref[...] = posterior
    emit_sums(posterior, all_ref, piece, refs[readers + 2 :])


def later_sums_kernel(piece, all_ref, post_ref, *out_refs):
    emit_sums(post_ref[...], all_ref, piece, out_refs)


def group_sums(kernel, piece, members, all_images, operands, extra):
    refs, slots = operands[0].shape
    width = piece.stop - piece.start
    block = jax.ShapeDtypeStruct((refs // members, width), jnp.bfloat16)
    outs = pl.pallas_call(
        kernel,
        out_shape=tuple(extra) + (block,) * members,
        in_specs=[VMEM_SPEC] * (1 + len(operands)),
        out_specs=(VMEM_SPEC,) * (len(extra) + members),
        compiler_params=pltpu.CompilerParams(vmem_limit_bytes=SUMS_VMEM),
        cost_estimate=pl.CostEstimate(
            flops=2 * refs * slots * width,
            bytes_accessed=2 * slots * width,
            transcendentals=0,
        ),
        name="sums",
    )(all_images, *operands)
    return outs[: len(extra)], outs[len(extra) :]


def on_device(images, routes, projections, noise_weights):
    readers = lax.axis_size("reader")
    members = lax.axis_size("blk")
    reader = lax.axis_index("reader")
    rows, width = images.shape
    noise = noise_weights.reshape(1, width)

    gather = staged_gather if members == 4 and rows % 32 == 0 and readers > 1 else plain_gather
    staged, far, all_routes = gather(
        projections[0], images, noise, routes.T, readers // 4, readers // 2
    )
    split = lax.axis_size("sub") > 1
    scores, masks, mine, all_images = all_scores(staged, far, all_routes, not split)
    if split:
        scores = lax.psum(scores, "sub")
        mine = group_lse(scores)
    lses = [mine] + [swap_bits(mine, "reader", k) for k in range(1, readers)]
    pieces = [slice(0, width // 2), slice(width // 2, width)]
    extra = (
        jax.ShapeDtypeStruct((1, scores.shape[1]), jnp.float32),
        jax.ShapeDtypeStruct(scores.shape, jnp.bfloat16),
    )
    (norms, posterior), first = group_sums(
        partial(first_sums_kernel, readers, pieces[0]),
        pieces[0],
        members,
        all_images,
        (scores, masks, *lses),
        extra,
    )
    _, last = group_sums(
        partial(later_sums_kernel, pieces[1]), pieces[1], members, all_images, (posterior,), ()
    )
    parts = [first, last]
    scatter = pair_scatter if members == 4 else line_scatter
    total = scatter(parts, "blk")
    normalizer = lax.dynamic_slice(norms.reshape(-1), (reader * rows,), (rows,))
    return (total[None], normalizer)


def solution(mesh):
    return jax.shard_map(
        on_device,
        mesh=mesh,
        in_specs=(
            P(("parts", "blk", "reader"), "sub"),
            P(("parts", "blk", "reader"), None),
            P(("parts", "reader"), "blk", "sub"),
            P(("parts", "sub")),
        ),
        out_specs=(P(("parts", "reader"), "blk", "sub"), P(("parts", "blk", "reader"))),
        check_vma=False,
    )
```

```python
from functools import partial

import jax
import jax.numpy as jnp
from jax import lax
from jax.experimental import pallas as pl
from jax.experimental.pallas import tpu as pltpu
from jax.sharding import PartitionSpec as P

SCORE_VMEM = 20 * 1024 * 1024
SUMS_VMEM = 12 * 1024 * 1024
STEP = 1024
VMEM_SPEC = pl.BlockSpec(memory_space=pltpu.VMEM)
ANY_SPEC = pl.BlockSpec(memory_space=pl.ANY)
SIDES = [(0, 1), (1, 0), (2, 3), (3, 2)]
MIDDLE = [(1, 2), (2, 1)]


def swap_bits(block, axis, bits):
    return lax.ppermute(block, axis, [(i, i ^ bits) for i in range(lax.axis_size(axis))])


def swap_gather(block, axis, bit):
    held = {0: block}
    while bit:
        for k in list(held):
            held[k ^ bit] = swap_bits(held[k], axis, bit)
        bit //= 2
    return [held[k] for k in range(len(held))]


def add_rounded(one, other):
    return (one.astype(jnp.float32) + other.astype(jnp.float32)).astype(jnp.bfloat16)


def staged_gather(block, images, noise, routes, near_bits, far_bit):
    cut = block.shape[1] // 16 * 9
    cuts = [block[:, :cut], block[:, cut:]]
    crossed = swap_bits(images, "reader", far_bit)
    near = swap_gather(images, "reader", near_bits)
    firsts = [
        lax.optimization_barrier(
            (lax.ppermute(one, "blk", SIDES), lax.ppermute(one, "blk", MIDDLE))
        )
        for one in cuts
    ]
    early = stage(
        [[[one] for one in cuts], [[side] for side, _ in firsts]], near, noise
    )
    far_parts, end_parts = [], []
    for last, (side, across) in enumerate(firsts):
        far = lax.ppermute(across, "blk", SIDES)
        side, *_ = lax.optimization_barrier((side, *near))
        across_far = lax.ppermute(side, "blk", MIDDLE)
        if last:
            far, across_far, *early = lax.optimization_barrier((far, across_far, *early))
        else:
            far, across_far = lax.optimization_barrier((far, across_far))
        end = lax.ppermute(across_far, "blk", SIDES)
        far_parts.append([far, across_far])
        end_parts.append([end, across])
    weighted, penalty, staged_near, noise = early
    ends = [parts[0] for parts in end_parts]
    routes, crossed = lax.optimization_barrier((routes, crossed))
    routes = swap_all(routes)
    crossed, *rest = lax.optimization_barrier((crossed, *routes, *ends))
    routes = rest[: len(routes)]
    far = swap_gather(crossed, "reader", near_bits)
    staged = stage_rest([far_parts, end_parts], staged_near, crossed, weighted, penalty, noise)
    return staged, far[1:], routes


def swap_all(routes):
    return [routes] + [swap_bits(routes, "reader", k) for k in range(1, lax.axis_size("reader"))]


def plain_gather(block, images, noise, routes, near_bits, far_bit):
    near = swap_gather(images, "reader", near_bits)
    far = swap_gather(swap_bits(images, "reader", far_bit), "reader", near_bits)
    line = [[[one]] for one in line_gather(block, "blk")]
    weighted, penalty, near, noise = stage(line[:2], near, noise)
    staged = stage_rest(line[2:], near, far[0], weighted, penalty, noise)
    return staged, far[1:], swap_all(routes)


def line_gather(block, axis):
    size, member = lax.axis_size(axis), lax.axis_index(axis)
    ahead, behind = [block], [block]
    for s in range(1, size):
        ahead.append(lax.ppermute(ahead[-1], axis, [(i, i + 1) for i in range(s - 1, size - 1)]))
        behind.append(lax.ppermute(behind[-1], axis, [(i, i - 1) for i in range(1, size - s + 1)]))
    blocks = [block]
    for s in range(1, size):
        blocks.append(jnp.where(member >= s, ahead[s], behind[size - s]))
    return blocks


def pair_scatter(pieces, axis):
    member = lax.axis_index(axis)
    is_end = (member == 0) | (member == 3)
    for_far_end = [lax.ppermute(parts[3], axis, SIDES) for parts in pieces]
    *second, for_far_end[0] = lax.optimization_barrier(
        [parts[2] for parts in pieces] + for_far_end[:1]
    )
    for_far_middle = [lax.ppermute(part, axis, SIDES) for part in second]
    totals = []
    for parts, part, end, middle in zip(pieces, second, for_far_end, for_far_middle):
        across_end = lax.ppermute(add_rounded(part, end), axis, MIDDLE)
        across_middle = lax.ppermute(add_rounded(parts[3], middle), axis, MIDDLE)
        near = jnp.where(is_end, parts[1], add_rounded(parts[1], across_end))
        from_side = lax.ppermute(near, axis, SIDES)
        total = parts[0].astype(jnp.float32) + from_side.astype(jnp.float32)
        totals.append(total + jnp.where(is_end, 0.0, across_middle.astype(jnp.float32)))
    return beside(totals)


def beside_kernel(count, *refs):
    out_ref, sems = refs[count:]
    copies, stop = [], out_ref.shape[1]
    for i, ref in enumerate(refs[:count]):
        start = stop - ref.shape[1]
        copies.append(pltpu.make_async_copy(ref, out_ref.at[:, start:stop], sems.at[i]))
        copies[-1].start()
        stop = start
    for copy in copies:
        copy.wait()


def beside(pieces):
    width = sum(piece.shape[1] for piece in pieces)
    return pl.pallas_call(
        partial(beside_kernel, len(pieces)),
        out_shape=jax.ShapeDtypeStruct((pieces[0].shape[0], width), pieces[0].dtype),
        in_specs=[VMEM_SPEC] * len(pieces),
        out_specs=ANY_SPEC,
        scratch_shapes=[pltpu.SemaphoreType.DMA((len(pieces),))],
        compiler_params=pltpu.CompilerParams(vmem_limit_bytes=SUMS_VMEM),
        name="beside",
    )(*pieces[::-1])


def line_scatter(pieces, axis):
    return jnp.concatenate([line_sum(parts, axis) for parts in pieces], axis=1)


def line_sum(parts, axis):
    size = lax.axis_size(axis)
    up = down = None
    for s in range(1, size):
        send_up, send_down = parts[s], parts[size - s]
        if s > 1:
            send_up = add_rounded(send_up, up)
            send_down = add_rounded(send_down, down)
        up = lax.ppermute(send_up, axis, [(i, i + 1) for i in range(0, s) if i + 1 < size])
        down = lax.ppermute(send_down, axis, [(i, i - 1) for i in range(size - s, size) if i > 0])
    total = parts[0].astype(jnp.float32)
    if size > 1:
        total = total + up.astype(jnp.float32) + down.astype(jnp.float32)
    return total


def column_lse(scores):
    peak = jnp.max(scores, axis=0, keepdims=True)
    total = jnp.sum(jnp.exp(scores - peak), axis=0, keepdims=True)
    return peak + jnp.log(total)


def at_end():
    member = lax.axis_index("blk")
    return (member == 0) | (member == lax.axis_size("blk") - 1)


def either(refs, act):
    if len(refs) == 1:
        act(refs[0])
        return
    is_end = at_end()

    @pl.when(is_end)
    def _():
        act(refs[0])

    @pl.when(jnp.logical_not(is_end))
    def _():
        act(refs[1])


def weigh_blocks(groups, noise_ref, weighted_ref, penalty_ref, block_ref, sems, first):
    count = block_ref.shape[1]
    parts = []
    for s, group in enumerate(groups):
        start = 0
        for refs in group:
            stop = start + refs[0].shape[1]
            parts.append((s, slice(start, stop), refs))
            start = stop

    def part_copy(i, ref):
        s, columns, _ = parts[i]
        return pltpu.make_async_copy(ref, block_ref.at[s, :, columns], sems.at[i])

    for i, (_, _, refs) in enumerate(parts):
        either(refs, lambda ref, i=i: part_copy(i, ref).start())
    for s in range(len(groups)):
        rows = slice((first + s) * count, (first + s + 1) * count)
        penalty = jnp.zeros((count, 1), jnp.float32)
        for i, (t, columns, refs) in enumerate(parts):
            if t != s:
                continue
            part_copy(i, refs[0]).wait()
            for start in range(columns.start, columns.stop, STEP):
                piece = slice(start, min(start + STEP, columns.stop))
                block = block_ref[s, :, piece].astype(jnp.float32)
                scaled = block * noise_ref[:, piece]
                weighted_ref[rows, piece] = scaled.astype(jnp.bfloat16)
                penalty = penalty + 0.5 * jnp.sum(scaled * block, axis=1, keepdims=True)
        penalty_ref[rows, :] = penalty


def take_blocks(refs, counts):
    return [[[refs.pop(0) for _ in range(n)] for n in group] for group in counts]


def block_counts(blocks):
    return [[len(part) for part in group] for group in blocks]


def flat(blocks):
    return [one for group in blocks for part in group for one in part]


def stage_kernel(near_count, counts, *refs):
    refs = list(refs)
    near_refs = [refs.pop(0) for _ in range(near_count)]
    groups = take_blocks(refs, counts)
    noise_ref, weighted_ref, penalty_ref, near_ref, noise_out_ref, block_ref, near_sems, sems = refs
    rows = near_refs[0].shape[0]
    copies = []
    for k, ref in enumerate(near_refs):
        copy = pltpu.make_async_copy(ref, near_ref.at[pl.ds(k * rows, rows), :], near_sems.at[k])
        copy.start()
        copies.append(copy)
    noise_out_ref[...] = noise_ref[...]
    weigh_blocks(groups, noise_ref, weighted_ref, penalty_ref, block_ref, sems, 0)
    for copy in copies:
        copy.wait()


def stage(blocks, near, noise):
    count = blocks[0][0][0].shape[0]
    parts = sum(len(group) for group in blocks)
    width = noise.shape[1]
    refs = len(blocks) * count
    moved = [*near, *flat(blocks)]
    return pl.pallas_call(
        partial(stage_kernel, len(near), block_counts(blocks)),
        out_shape=(
            jax.ShapeDtypeStruct((refs, width), jnp.bfloat16),
            jax.ShapeDtypeStruct((refs, 1), jnp.float32),
            jax.ShapeDtypeStruct((len(near) * near[0].shape[0], width), jnp.bfloat16),
            jax.ShapeDtypeStruct((1, width), jnp.float32),
        ),
        in_specs=[ANY_SPEC] * len(moved) + [VMEM_SPEC],
        out_specs=(VMEM_SPEC,) * 4,
        scratch_shapes=[
            pltpu.VMEM((len(blocks), count, width), jnp.bfloat16),
            pltpu.SemaphoreType.DMA((len(near),)),
            pltpu.SemaphoreType.DMA((parts,)),
        ],
        compiler_params=pltpu.CompilerParams(vmem_limit_bytes=SCORE_VMEM),
        cost_estimate=pl.CostEstimate(
            flops=8 * refs * width, bytes_accessed=12_000_000, transcendentals=0
        ),
        name="stage",
    )(*moved, noise)


def place_images(k, source, all_ref, sem):
    rows = source.shape[0]
    row = pl.multiple_of((lax.axis_index("reader") ^ k) * rows, 16)
    return pltpu.make_async_copy(source, all_ref.at[pl.ds(row, rows), :], sem), pl.ds(row, rows)


def stage_rest_kernel(readers, counts, *refs):
    refs = list(refs)
    groups = take_blocks(refs, counts)
    near_ref, far_ref, early_ref, early_penalty_ref, noise_ref = [refs.pop(0) for _ in range(5)]
    turned_ref, penalty_ref, all_ref, product_ref = refs[:4]
    weighted_ref, block_ref, sems, image_sems = refs[4:]
    rows = far_ref.shape[0]
    half = readers // 2
    sources = [near_ref.at[pl.ds(k * rows, rows), :] for k in range(half)] + [far_ref]
    placed = [place_images(k, one, all_ref, image_sems.at[k]) for k, one in enumerate(sources)]
    for copy, _ in placed:
        copy.start()
    done = early_ref.shape[0]
    weighted_ref[:done, :] = early_ref[...]
    penalty_ref[:done, :] = early_penalty_ref[...]
    first = done // block_ref.shape[1]
    weigh_blocks(groups, noise_ref, weighted_ref, penalty_ref, block_ref, sems, first)
    width = weighted_ref.shape[1]
    for start in range(0, width, STEP):
        piece = slice(start, min(start + STEP, width))
        turned_ref[piece, :] = weighted_ref[:, piece].T
    products = jnp.dot(near_ref[...], turned_ref[...], preferred_element_type=jnp.float32)
    for k in range(half):
        product_ref[placed[k][1], :] = products[k * rows : (k + 1) * rows]
    product_ref[placed[half][1], :] = jnp.dot(
        far_ref[...], turned_ref[...], preferred_element_type=jnp.float32
    )
    for copy, _ in placed:
        copy.wait()


def stage_rest(blocks, near, crossed, weighted, penalty, noise):
    count = blocks[0][0][0].shape[0]
    parts = sum(len(group) for group in blocks)
    width = noise.shape[1]
    refs = len(blocks) * count + weighted.shape[0]
    slots = 2 * near.shape[0]
    readers = slots // crossed.shape[0]
    moved = flat(blocks)
    return pl.pallas_call(
        partial(stage_rest_kernel, readers, block_counts(blocks)),
        out_shape=(
            jax.ShapeDtypeStruct((width, refs), jnp.bfloat16),
            jax.ShapeDtypeStruct((refs, 1), jnp.float32),
            jax.ShapeDtypeStruct((slots, width), jnp.bfloat16),
            jax.ShapeDtypeStruct((slots, refs), jnp.float32),
        ),
        in_specs=[ANY_SPEC] * len(moved) + [VMEM_SPEC] * 5,
        out_specs=(VMEM_SPEC,) * 4,
        scratch_shapes=[
            pltpu.VMEM((refs, width), jnp.bfloat16),
            pltpu.VMEM((len(blocks), count, width), jnp.bfloat16),
            pltpu.SemaphoreType.DMA((parts,)),
            pltpu.SemaphoreType.DMA((readers // 2 + 1,)),
        ],
        compiler_params=pltpu.CompilerParams(vmem_limit_bytes=SCORE_VMEM),
        cost_estimate=pl.CostEstimate(
            flops=8 * refs * width, bytes_accessed=12_000_000, transcendentals=0
        ),
        name="stage_rest",
    )(*moved, near, crossed, weighted, penalty, noise)


def score_kernel(readers, finish, *refs):
    refs = list(refs)
    half = readers // 2
    far_refs = [refs.pop(0) for _ in range(half - 1)]
    turned_ref, penalty_ref, _, product_ref = [refs.pop(0) for _ in range(4)]
    route_refs = [refs.pop(0) for _ in range(readers)]
    score_ref, mask_ref, lse_ref, all_ref, sum_ref, image_sems = refs
    reader = lax.axis_index("reader")
    placed = [
        place_images(half + 1 + i, ref, all_ref, image_sems.at[i])
        for i, ref in enumerate(far_refs)
    ]
    for copy, _ in placed:
        copy.start()
    sum_ref[...] = product_ref[...]
    for (_, place), ref in zip(placed, far_refs):
        sum_ref[place, :] = jnp.dot(
            ref[...], turned_ref[...], preferred_element_type=jnp.float32
        )
    rows = route_refs[0].shape[1]
    routes = [ref[...] for ref in route_refs]
    bit = 1
    while bit < readers:
        flip = (reader & bit) > 0
        routes = [jnp.where(flip, routes[k ^ bit], one) for k, one in enumerate(routes)]
        bit *= 2
    for j, route in enumerate(routes):
        for k in range(readers):
            hits = jnp.where(route == (reader ^ k), 1.0, 0.0)
            mask_ref[k : k + 1, j * rows : (j + 1) * rows] = jnp.max(hits, axis=0, keepdims=True)
    scores = sum_ref[...].T - penalty_ref[...]
    score_ref[...] = scores
    if finish:
        lse_ref[...] = column_lse(scores)
    for copy, _ in placed:
        copy.wait()


def all_scores(staged, far, routes, finish):
    turned, penalty, images, products = staged
    width, refs = turned.shape
    slots, rows = images.shape[0], far[0].shape[0]
    readers = slots // rows
    return pl.pallas_call(
        partial(score_kernel, readers, finish),
        out_shape=(
            jax.ShapeDtypeStruct((refs, slots), jnp.float32),
            jax.ShapeDtypeStruct((readers, slots), jnp.float32),
            jax.ShapeDtypeStruct((1, slots), jnp.float32),
            jax.ShapeDtypeStruct((slots, width), jnp.bfloat16),
        ),
        in_specs=[VMEM_SPEC] * (len(far) + 4 + len(routes)),
        out_specs=(VMEM_SPEC,) * 4,
        scratch_shapes=[
            pltpu.VMEM((slots, refs), jnp.float32),
            pltpu.SemaphoreType.DMA((len(far),)),
        ],
        input_output_aliases={len(far) + 2: 3},
        compiler_params=pltpu.CompilerParams(vmem_limit_bytes=SCORE_VMEM),
        cost_estimate=pl.CostEstimate(
            flops=2 * refs * slots * width,
            bytes_accessed=2 * (slots + refs) * width,
            transcendentals=0,
        ),
        name="scores",
    )(*far, turned, penalty, images, products, *routes)


def lse_kernel(score_ref, lse_ref):
    lse_ref[...] = column_lse(score_ref[...])


def group_lse(scores):
    return pl.pallas_call(
        lse_kernel,
        out_shape=jax.ShapeDtypeStruct((1, scores.shape[1]), jnp.float32),
        name="group_lse",
    )(scores)


def emit_sums(posterior, all_ref, piece, out_refs):
    sums = jnp.dot(posterior, all_ref[:, piece], preferred_element_type=jnp.float32)
    count = sums.shape[0] // len(out_refs)
    for s, out_ref in enumerate(out_refs):
        out_ref[...] = sums[s * count : (s + 1) * count].astype(out_ref.dtype)


def first_sums_kernel(readers, piece, all_ref, score_ref, mask_ref, *refs):
    lse_refs, norm_ref, post_ref = refs[:readers], refs[readers], refs[readers + 1]
    kept = []
    for k, lse_ref in enumerate(lse_refs):
        kept.append(jnp.where(mask_ref[k : k + 1, :] > 0.0, lse_ref[...], -jnp.inf))
    highest = kept[0]
    for value in kept[1:]:
        highest = jnp.maximum(highest, value)
    spread = jnp.exp(kept[0] - highest)
    for value in kept[1:]:
        spread = spread + jnp.exp(value - highest)
    norm = highest + jnp.log(spread)
    norm_ref[...] = norm
    exponent = jnp.where(mask_ref[0:1, :] > 0.0, score_ref[...] - norm, -jnp.inf)
    posterior = jnp.exp(exponent).astype(jnp.bfloat16)
    post_ref[...] = posterior
    emit_sums(posterior, all_ref, piece, refs[readers + 2 :])


def later_sums_kernel(piece, all_ref, post_ref, *out_refs):
    emit_sums(post_ref[...], all_ref, piece, out_refs)


def group_sums(kernel, piece, members, all_images, operands, extra):
    refs, slots = operands[0].shape
    width = piece.stop - piece.start
    block = jax.ShapeDtypeStruct((refs // members, width), jnp.bfloat16)
    outs = pl.pallas_call(
        kernel,
        out_shape=tuple(extra) + (block,) * members,
        in_specs=[VMEM_SPEC] * (1 + len(operands)),
        out_specs=(VMEM_SPEC,) * (len(extra) + members),
        compiler_params=pltpu.CompilerParams(vmem_limit_bytes=SUMS_VMEM),
        cost_estimate=pl.CostEstimate(
            flops=2 * refs * slots * width,
            bytes_accessed=2 * slots * width,
            transcendentals=0,
        ),
        name="sums",
    )(all_images, *operands)
    return outs[: len(extra)], outs[len(extra) :]


def on_device(images, routes, projections, noise_weights):
    readers = lax.axis_size("reader")
    members = lax.axis_size("blk")
    reader = lax.axis_index("reader")
    rows, width = images.shape
    noise = noise_weights.reshape(1, width)

    gather = staged_gather if members == 4 and rows % 32 == 0 and readers > 1 else plain_gather
    staged, far, all_routes = gather(
        projections[0], images, noise, routes.T, readers // 4, readers // 2
    )
    split = lax.axis_size("sub") > 1
    scores, masks, mine, all_images = all_scores(staged, far, all_routes, not split)
    if split:
        scores = lax.psum(scores, "sub")
        mine = group_lse(scores)
    lses = [mine] + [swap_bits(mine, "reader", k) for k in range(1, readers)]
    pieces = [slice(0, width // 2), slice(width // 2, width)]
    extra = (
        jax.ShapeDtypeStruct((1, scores.shape[1]), jnp.float32),
        jax.ShapeDtypeStruct(scores.shape, jnp.bfloat16),
    )
    (norms, posterior), first = group_sums(
        partial(first_sums_kernel, readers, pieces[0]),
        pieces[0],
        members,
        all_images,
        (scores, masks, *lses),
        extra,
    )
    _, last = group_sums(
        partial(later_sums_kernel, pieces[1]), pieces[1], members, all_images, (posterior,), ()
    )
    parts = [first, last]
    scatter = pair_scatter if members == 4 else line_scatter
    total = scatter(parts, "blk")
    normalizer = lax.dynamic_slice(norms.reshape(-1), (reader * rows,), (rows,))
    return (total[None], normalizer)


def solution(mesh):
    return jax.shard_map(
        on_device,
        mesh=mesh,
        in_specs=(
            P(("parts", "blk", "reader"), "sub"),
            P(("parts", "blk", "reader"), None),
            P(("parts", "reader"), "blk", "sub"),
            P(("parts", "sub")),
        ),
        out_specs=(P(("parts", "reader"), "blk", "sub"), P(("parts", "blk", "reader"))),
        check_vma=False,
    )
```

```python
from functools import partial

import jax
import jax.numpy as jnp
from jax import lax
from jax.experimental import pallas as pl
from jax.experimental.pallas import tpu as pltpu
from jax.sharding import PartitionSpec as P

SCORE_VMEM = 20 * 1024 * 1024
SUMS_VMEM = 12 * 1024 * 1024
STEP = 1024
VMEM_SPEC = pl.BlockSpec(memory_space=pltpu.VMEM)
ANY_SPEC = pl.BlockSpec(memory_space=pl.ANY)
SIDES = [(0, 1), (1, 0), (2, 3), (3, 2)]
MIDDLE = [(1, 2), (2, 1)]


def swap_bits(block, axis, bits):
    return lax.ppermute(block, axis, [(i, i ^ bits) for i in range(lax.axis_size(axis))])


def swap_gather(block, axis, bit):
    held = {0: block}
    while bit:
        for k in list(held):
            held[k ^ bit] = swap_bits(held[k], axis, bit)
        bit //= 2
    return [held[k] for k in range(len(held))]


def add_rounded(one, other):
    return (one.astype(jnp.float32) + other.astype(jnp.float32)).astype(jnp.bfloat16)


def staged_gather(block, images, noise, routes, near_bits, far_bit):
    cut = block.shape[1] // 16 * 9
    cuts = [block[:, :cut], block[:, cut:]]
    crossed = swap_bits(images, "reader", far_bit)
    near = swap_gather(images, "reader", near_bits)
    firsts = [
        lax.optimization_barrier(
            (lax.ppermute(one, "blk", SIDES), lax.ppermute(one, "blk", MIDDLE))
        )
        for one in cuts
    ]
    far_parts, end_parts = [], []
    for last, (side, across) in enumerate(firsts):
        far = lax.ppermute(across, "blk", SIDES)
        side, *_ = lax.optimization_barrier((side, *near))
        across_far = lax.ppermute(side, "blk", MIDDLE)
        if last:
            far, across_far, *early = lax.optimization_barrier((far, across_far, *early))
        else:
            far, across_far, routes = lax.optimization_barrier((far, across_far, routes))
            blocks = [[[one] for one in cuts], [[one] for one, _ in firsts]]
            early = stage(blocks, near, noise, swap_gather(routes, "reader", near_bits))
        end = lax.ppermute(across_far, "blk", SIDES)
        far_parts.append([far, across_far])
        end_parts.append([end, across])
    weighted, penalty, staged_near, noise, routes = early
    ends = [parts[0] for parts in end_parts]
    far_routes, crossed = lax.optimization_barrier((routes, crossed))
    far_routes = swap_bits(far_routes, "reader", far_bit)
    crossed, far_routes, *_ = lax.optimization_barrier((crossed, far_routes, *ends))
    far = swap_gather(crossed, "reader", near_bits)
    staged = stage_rest([far_parts, end_parts], staged_near, crossed, weighted, penalty, noise)
    return staged, far[1:], (routes, far_routes)


def plain_gather(block, images, noise, routes, near_bits, far_bit):
    near = swap_gather(images, "reader", near_bits)
    near_routes = swap_gather(routes, "reader", near_bits)
    far = swap_gather(swap_bits(images, "reader", far_bit), "reader", near_bits)
    line = [[[one]] for one in line_gather(block, "blk")]
    weighted, penalty, near, noise, routes = stage(line[:2], near, noise, near_routes)
    staged = stage_rest(line[2:], near, far[0], weighted, penalty, noise)
    return staged, far[1:], (routes, swap_bits(routes, "reader", far_bit))


def line_gather(block, axis):
    size, member = lax.axis_size(axis), lax.axis_index(axis)
    ahead, behind = [block], [block]
    for s in range(1, size):
        ahead.append(lax.ppermute(ahead[-1], axis, [(i, i + 1) for i in range(s - 1, size - 1)]))
        behind.append(lax.ppermute(behind[-1], axis, [(i, i - 1) for i in range(1, size - s + 1)]))
    blocks = [block]
    for s in range(1, size):
        blocks.append(jnp.where(member >= s, ahead[s], behind[size - s]))
    return blocks


def pair_scatter(pieces, axis):
    member = lax.axis_index(axis)
    is_end = (member == 0) | (member == 3)
    for_far_end = [lax.ppermute(parts[3], axis, SIDES) for parts in pieces]
    *second, for_far_end[0] = lax.optimization_barrier(
        [parts[2] for parts in pieces] + for_far_end[:1]
    )
    for_far_middle = [lax.ppermute(part, axis, SIDES) for part in second]
    totals = []
    for parts, part, end, middle in zip(pieces, second, for_far_end, for_far_middle):
        across_end = lax.ppermute(add_rounded(part, end), axis, MIDDLE)
        across_middle = lax.ppermute(add_rounded(parts[3], middle), axis, MIDDLE)
        near = jnp.where(is_end, parts[1], add_rounded(parts[1], across_end))
        from_side = lax.ppermute(near, axis, SIDES)
        total = parts[0].astype(jnp.float32) + from_side.astype(jnp.float32)
        totals.append(total + jnp.where(is_end, 0.0, across_middle.astype(jnp.float32)))
    return beside(totals)


def beside_kernel(count, *refs):
    out_ref, sems = refs[count:]
    copies, stop = [], out_ref.shape[1]
    for i, ref in enumerate(refs[:count]):
        start = stop - ref.shape[1]
        copies.append(pltpu.make_async_copy(ref, out_ref.at[:, start:stop], sems.at[i]))
        copies[-1].start()
        stop = start
    for copy in copies:
        copy.wait()


def beside(pieces):
    width = sum(piece.shape[1] for piece in pieces)
    return pl.pallas_call(
        partial(beside_kernel, len(pieces)),
        out_shape=jax.ShapeDtypeStruct((pieces[0].shape[0], width), pieces[0].dtype),
        in_specs=[VMEM_SPEC] * len(pieces),
        out_specs=ANY_SPEC,
        scratch_shapes=[pltpu.SemaphoreType.DMA((len(pieces),))],
        compiler_params=pltpu.CompilerParams(vmem_limit_bytes=SUMS_VMEM),
        name="beside",
    )(*pieces[::-1])


def line_scatter(pieces, axis):
    return jnp.concatenate([line_sum(parts, axis) for parts in pieces], axis=1)


def line_sum(parts, axis):
    size = lax.axis_size(axis)
    up = down = None
    for s in range(1, size):
        send_up, send_down = parts[s], parts[size - s]
        if s > 1:
            send_up = add_rounded(send_up, up)
            send_down = add_rounded(send_down, down)
        up = lax.ppermute(send_up, axis, [(i, i + 1) for i in range(0, s) if i + 1 < size])
        down = lax.ppermute(send_down, axis, [(i, i - 1) for i in range(size - s, size) if i > 0])
    total = parts[0].astype(jnp.float32)
    if size > 1:
        total = total + up.astype(jnp.float32) + down.astype(jnp.float32)
    return total


def column_lse(scores):
    peak = jnp.max(scores, axis=0, keepdims=True)
    total = jnp.sum(jnp.exp(scores - peak), axis=0, keepdims=True)
    return peak + jnp.log(total)


def at_end():
    member = lax.axis_index("blk")
    return (member == 0) | (member == lax.axis_size("blk") - 1)


def either(refs, act):
    if len(refs) == 1:
        act(refs[0])
        return
    is_end = at_end()

    @pl.when(is_end)
    def _():
        act(refs[0])

    @pl.when(jnp.logical_not(is_end))
    def _():
        act(refs[1])


def weigh_blocks(groups, noise_ref, weighted_ref, penalty_ref, block_ref, sems, first):
    count = block_ref.shape[1]
    parts = []
    for s, group in enumerate(groups):
        start = 0
        for refs in group:
            stop = start + refs[0].shape[1]
            parts.append((s, slice(start, stop), refs))
            start = stop

    def part_copy(i, ref):
        s, columns, _ = parts[i]
        return pltpu.make_async_copy(ref, block_ref.at[s, :, columns], sems.at[i])

    for i, (_, _, refs) in enumerate(parts):
        either(refs, lambda ref, i=i: part_copy(i, ref).start())
    for s in range(len(groups)):
        rows = slice((first + s) * count, (first + s + 1) * count)
        penalty = jnp.zeros((count, 1), jnp.float32)
        for i, (t, columns, refs) in enumerate(parts):
            if t != s:
                continue
            part_copy(i, refs[0]).wait()
            for start in range(columns.start, columns.stop, STEP):
                piece = slice(start, min(start + STEP, columns.stop))
                block = block_ref[s, :, piece].astype(jnp.float32)
                scaled = block * noise_ref[:, piece]
                weighted_ref[rows, piece] = scaled.astype(jnp.bfloat16)
                penalty = penalty + 0.5 * jnp.sum(scaled * block, axis=1, keepdims=True)
        penalty_ref[rows, :] = penalty


def take_blocks(refs, counts):
    return [[[refs.pop(0) for _ in range(n)] for n in group] for group in counts]


def block_counts(blocks):
    return [[len(part) for part in group] for group in blocks]


def flat(blocks):
    return [one for group in blocks for part in group for one in part]


def stage_kernel(near_count, counts, *refs):
    refs = list(refs)
    near_refs = [refs.pop(0) for _ in range(near_count)]
    groups = take_blocks(refs, counts)
    route_refs = [refs.pop(0) for _ in range(near_count)]
    noise_ref, weighted_ref, penalty_ref, near_ref, noise_out_ref, route_ref = refs[:6]
    block_ref, near_sems, sems = refs[6:]
    rows = near_refs[0].shape[0]
    top = route_refs[0].shape[0]
    for k, ref in enumerate(route_refs):
        route_ref[k * top : (k + 1) * top, :] = ref[...]
    copies = []
    for k, ref in enumerate(near_refs):
        copy = pltpu.make_async_copy(ref, near_ref.at[pl.ds(k * rows, rows), :], near_sems.at[k])
        copy.start()
        copies.append(copy)
    noise_out_ref[...] = noise_ref[...]
    weigh_blocks(groups, noise_ref, weighted_ref, penalty_ref, block_ref, sems, 0)
    for copy in copies:
        copy.wait()


def stage(blocks, near, noise, routes):
    count = blocks[0][0][0].shape[0]
    parts = sum(len(group) for group in blocks)
    width = noise.shape[1]
    refs = len(blocks) * count
    rows = near[0].shape[0]
    moved = [*near, *flat(blocks)]
    return pl.pallas_call(
        partial(stage_kernel, len(near), block_counts(blocks)),
        out_shape=(
            jax.ShapeDtypeStruct((refs, width), jnp.bfloat16),
            jax.ShapeDtypeStruct((refs, 1), jnp.float32),
            jax.ShapeDtypeStruct((len(near) * near[0].shape[0], width), jnp.bfloat16),
            jax.ShapeDtypeStruct((1, width), jnp.float32),
            jax.ShapeDtypeStruct((len(routes) * routes[0].shape[0], rows), jnp.int32),
        ),
        in_specs=[ANY_SPEC] * len(moved) + [VMEM_SPEC] * (len(routes) + 1),
        out_specs=(VMEM_SPEC,) * 5,
        scratch_shapes=[
            pltpu.VMEM((len(blocks), count, width), jnp.bfloat16),
            pltpu.SemaphoreType.DMA((len(near),)),
            pltpu.SemaphoreType.DMA((parts,)),
        ],
        compiler_params=pltpu.CompilerParams(vmem_limit_bytes=SCORE_VMEM),
        cost_estimate=pl.CostEstimate(
            flops=8 * refs * width, bytes_accessed=12_000_000, transcendentals=0
        ),
        name="stage",
    )(*moved, *routes, noise)


def place_images(k, source, all_ref, sem):
    rows = source.shape[0]
    row = pl.multiple_of((lax.axis_index("reader") ^ k) * rows, 16)
    return pltpu.make_async_copy(source, all_ref.at[pl.ds(row, rows), :], sem), pl.ds(row, rows)


def stage_rest_kernel(readers, counts, *refs):
    refs = list(refs)
    groups = take_blocks(refs, counts)
    near_ref, far_ref, early_ref, early_penalty_ref, noise_ref = [refs.pop(0) for _ in range(5)]
    turned_ref, penalty_ref, all_ref, product_ref = refs[:4]
    weighted_ref, block_ref, sems, image_sems = refs[4:]
    rows = far_ref.shape[0]
    half = readers // 2
    sources = [near_ref.at[pl.ds(k * rows, rows), :] for k in range(half)] + [far_ref]
    placed = [place_images(k, one, all_ref, image_sems.at[k]) for k, one in enumerate(sources)]
    for copy, _ in placed:
        copy.start()
    done = early_ref.shape[0]
    weighted_ref[:done, :] = early_ref[...]
    penalty_ref[:done, :] = early_penalty_ref[...]
    first = done // block_ref.shape[1]
    weigh_blocks(groups, noise_ref, weighted_ref, penalty_ref, block_ref, sems, first)
    width = weighted_ref.shape[1]
    for start in range(0, width, STEP):
        piece = slice(start, min(start + STEP, width))
        turned_ref[piece, :] = weighted_ref[:, piece].T
    products = jnp.dot(near_ref[...], turned_ref[...], preferred_element_type=jnp.float32)
    for k in range(half):
        product_ref[placed[k][1], :] = products[k * rows : (k + 1) * rows]
    product_ref[placed[half][1], :] = jnp.dot(
        far_ref[...], turned_ref[...], preferred_element_type=jnp.float32
    )
    for copy, _ in placed:
        copy.wait()


def stage_rest(blocks, near, crossed, weighted, penalty, noise):
    count = blocks[0][0][0].shape[0]
    parts = sum(len(group) for group in blocks)
    width = noise.shape[1]
    refs = len(blocks) * count + weighted.shape[0]
    slots = 2 * near.shape[0]
    readers = slots // crossed.shape[0]
    moved = flat(blocks)
    return pl.pallas_call(
        partial(stage_rest_kernel, readers, block_counts(blocks)),
        out_shape=(
            jax.ShapeDtypeStruct((width, refs), jnp.bfloat16),
            jax.ShapeDtypeStruct((refs, 1), jnp.float32),
            jax.ShapeDtypeStruct((slots, width), jnp.bfloat16),
            jax.ShapeDtypeStruct((slots, refs), jnp.float32),
        ),
        in_specs=[ANY_SPEC] * len(moved) + [VMEM_SPEC] * 5,
        out_specs=(VMEM_SPEC,) * 4,
        scratch_shapes=[
            pltpu.VMEM((refs, width), jnp.bfloat16),
            pltpu.VMEM((len(blocks), count, width), jnp.bfloat16),
            pltpu.SemaphoreType.DMA((parts,)),
            pltpu.SemaphoreType.DMA((readers // 2 + 1,)),
        ],
        compiler_params=pltpu.CompilerParams(vmem_limit_bytes=SCORE_VMEM),
        cost_estimate=pl.CostEstimate(
            flops=8 * refs * width, bytes_accessed=12_000_000, transcendentals=0
        ),
        name="stage_rest",
    )(*moved, near, crossed, weighted, penalty, noise)


def score_kernel(readers, finish, *refs):
    refs = list(refs)
    half = readers // 2
    far_refs = [refs.pop(0) for _ in range(half - 1)]
    turned_ref, penalty_ref, _, product_ref = [refs.pop(0) for _ in range(4)]
    near_route_ref, far_route_ref = refs.pop(0), refs.pop(0)
    score_ref, mask_ref, lse_ref, all_ref, sum_ref, image_sems = refs
    reader = lax.axis_index("reader")
    placed = [
        place_images(half + 1 + i, ref, all_ref, image_sems.at[i])
        for i, ref in enumerate(far_refs)
    ]
    for copy, _ in placed:
        copy.start()
    sum_ref[...] = product_ref[...]
    for (_, place), ref in zip(placed, far_refs):
        sum_ref[place, :] = jnp.dot(
            ref[...], turned_ref[...], preferred_element_type=jnp.float32
        )
    top, rows = near_route_ref.shape[0] // half, near_route_ref.shape[1]
    routes = [near_route_ref[k * top : (k + 1) * top, :] for k in range(half)]
    routes += [far_route_ref[k * top : (k + 1) * top, :] for k in range(half)]
    bit = 1
    while bit < readers:
        flip = (reader & bit) > 0
        routes = [jnp.where(flip, routes[k ^ bit], one) for k, one in enumerate(routes)]
        bit *= 2
    for j, route in enumerate(routes):
        for k in range(readers):
            hits = jnp.where(route == (reader ^ k), 1.0, 0.0)
            mask_ref[k : k + 1, j * rows : (j + 1) * rows] = jnp.max(hits, axis=0, keepdims=True)
    scores = sum_ref[...].T - penalty_ref[...]
    score_ref[...] = scores
    if finish:
        lse_ref[...] = column_lse(scores)
    for copy, _ in placed:
        copy.wait()


def all_scores(staged, far, routes, finish):
    turned, penalty, images, products = staged
    width, refs = turned.shape
    slots, rows = images.shape[0], far[0].shape[0]
    readers = slots // rows
    return pl.pallas_call(
        partial(score_kernel, readers, finish),
        out_shape=(
            jax.ShapeDtypeStruct((refs, slots), jnp.float32),
            jax.ShapeDtypeStruct((readers, slots), jnp.float32),
            jax.ShapeDtypeStruct((1, slots), jnp.float32),
            jax.ShapeDtypeStruct((slots, width), jnp.bfloat16),
        ),
        in_specs=[VMEM_SPEC] * (len(far) + 4 + len(routes)),
        out_specs=(VMEM_SPEC,) * 4,
        scratch_shapes=[
            pltpu.VMEM((slots, refs), jnp.float32),
            pltpu.SemaphoreType.DMA((len(far),)),
        ],
        input_output_aliases={len(far) + 2: 3},
        compiler_params=pltpu.CompilerParams(vmem_limit_bytes=SCORE_VMEM),
        cost_estimate=pl.CostEstimate(
            flops=2 * refs * slots * width,
            bytes_accessed=2 * (slots + refs) * width,
            transcendentals=0,
        ),
        name="scores",
    )(*far, turned, penalty, images, products, *routes)


def lse_kernel(score_ref, lse_ref):
    lse_ref[...] = column_lse(score_ref[...])


def group_lse(scores):
    return pl.pallas_call(
        lse_kernel,
        out_shape=jax.ShapeDtypeStruct((1, scores.shape[1]), jnp.float32),
        name="group_lse",
    )(scores)


def emit_sums(posterior, all_ref, piece, out_refs):
    sums = jnp.dot(posterior, all_ref[:, piece], preferred_element_type=jnp.float32)
    count = sums.shape[0] // len(out_refs)
    for s, out_ref in enumerate(out_refs):
        out_ref[...] = sums[s * count : (s + 1) * count].astype(out_ref.dtype)


def first_sums_kernel(readers, piece, all_ref, score_ref, mask_ref, *refs):
    lse_refs, norm_ref, post_ref = refs[:readers], refs[readers], refs[readers + 1]
    kept = []
    for k, lse_ref in enumerate(lse_refs):
        kept.append(jnp.where(mask_ref[k : k + 1, :] > 0.0, lse_ref[...], -jnp.inf))
    highest = kept[0]
    for value in kept[1:]:
        highest = jnp.maximum(highest, value)
    spread = jnp.exp(kept[0] - highest)
    for value in kept[1:]:
        spread = spread + jnp.exp(value - highest)
    norm = highest + jnp.log(spread)
    norm_ref[...] = norm
    exponent = jnp.where(mask_ref[0:1, :] > 0.0, score_ref[...] - norm, -jnp.inf)
    posterior = jnp.exp(exponent).astype(jnp.bfloat16)
    post_ref[...] = posterior
    emit_sums(posterior, all_ref, piece, refs[readers + 2 :])


def later_sums_kernel(piece, all_ref, post_ref, *out_refs):
    emit_sums(post_ref[...], all_ref, piece, out_refs)


def group_sums(kernel, piece, members, all_images, operands, extra):
    refs, slots = operands[0].shape
    width = piece.stop - piece.start
    block = jax.ShapeDtypeStruct((refs // members, width), jnp.bfloat16)
    outs = pl.pallas_call(
        kernel,
        out_shape=tuple(extra) + (block,) * members,
        in_specs=[VMEM_SPEC] * (1 + len(operands)),
        out_specs=(VMEM_SPEC,) * (len(extra) + members),
        compiler_params=pltpu.CompilerParams(vmem_limit_bytes=SUMS_VMEM),
        cost_estimate=pl.CostEstimate(
            flops=2 * refs * slots * width,
            bytes_accessed=2 * slots * width,
            transcendentals=0,
        ),
        name="sums",
    )(all_images, *operands)
    return outs[: len(extra)], outs[len(extra) :]


def on_device(images, routes, projections, noise_weights):
    readers = lax.axis_size("reader")
    members = lax.axis_size("blk")
    reader = lax.axis_index("reader")
    rows, width = images.shape
    noise = noise_weights.reshape(1, width)

    gather = staged_gather if members == 4 and rows % 32 == 0 and readers > 1 else plain_gather
    staged, far, all_routes = gather(
        projections[0], images, noise, routes.T, readers // 4, readers // 2
    )
    split = lax.axis_size("sub") > 1
    scores, masks, mine, all_images = all_scores(staged, far, all_routes, not split)
    if split:
        scores = lax.psum(scores, "sub")
        mine = group_lse(scores)
    lses = [mine] + [swap_bits(mine, "reader", k) for k in range(1, readers)]
    pieces = [slice(0, width // 2), slice(width // 2, width)]
    extra = (
        jax.ShapeDtypeStruct((1, scores.shape[1]), jnp.float32),
        jax.ShapeDtypeStruct(scores.shape, jnp.bfloat16),
    )
    (norms, posterior), first = group_sums(
        partial(first_sums_kernel, readers, pieces[0]),
        pieces[0],
        members,
        all_images,
        (scores, masks, *lses),
        extra,
    )
    _, last = group_sums(
        partial(later_sums_kernel, pieces[1]), pieces[1], members, all_images, (posterior,), ()
    )
    parts = [first, last]
    scatter = pair_scatter if members == 4 else line_scatter
    total = scatter(parts, "blk")
    normalizer = lax.dynamic_slice(norms.reshape(-1), (reader * rows,), (rows,))
    return (total[None], normalizer)


def solution(mesh):
    return jax.shard_map(
        on_device,
        mesh=mesh,
        in_specs=(
            P(("parts", "blk", "reader"), "sub"),
            P(("parts", "blk", "reader"), None),
            P(("parts", "reader"), "blk", "sub"),
            P(("parts", "sub")),
        ),
        out_specs=(P(("parts", "reader"), "blk", "sub"), P(("parts", "blk", "reader"))),
        check_vma=False,
    )
```

```python
from functools import partial

import jax
import jax.numpy as jnp
from jax import lax
from jax.experimental import pallas as pl
from jax.experimental.pallas import tpu as pltpu
from jax.sharding import PartitionSpec as P

SCORE_VMEM = 20 * 1024 * 1024
SUMS_VMEM = 12 * 1024 * 1024
STEP = 1024
VMEM_SPEC = pl.BlockSpec(memory_space=pltpu.VMEM)
ANY_SPEC = pl.BlockSpec(memory_space=pl.ANY)
SIDES = [(0, 1), (1, 0), (2, 3), (3, 2)]
MIDDLE = [(1, 2), (2, 1)]


def swap_bits(block, axis, bits):
    return lax.ppermute(block, axis, [(i, i ^ bits) for i in range(lax.axis_size(axis))])


def swap_gather(block, axis, bit):
    held = {0: block}
    while bit:
        for k in list(held):
            held[k ^ bit] = swap_bits(held[k], axis, bit)
        bit //= 2
    return [held[k] for k in range(len(held))]


def add_rounded(one, other):
    return (one.astype(jnp.float32) + other.astype(jnp.float32)).astype(jnp.bfloat16)


def staged_gather(block, images, noise, routes, near_bits, far_bit):
    cut = block.shape[1] // 16 * 9
    cuts = [block[:, :cut], block[:, cut:]]
    crossed = swap_bits(images, "reader", far_bit)
    near = swap_gather(images, "reader", near_bits)
    firsts = [
        lax.optimization_barrier(
            (lax.ppermute(one, "blk", SIDES), lax.ppermute(one, "blk", MIDDLE))
        )
        for one in cuts
    ]
    far_parts, end_parts = [], []
    for side, across in firsts:
        far = lax.ppermute(across, "blk", SIDES)
        side, *_ = lax.optimization_barrier((side, *near))
        across_far = lax.ppermute(side, "blk", MIDDLE)
        far, across_far, routes = lax.optimization_barrier((far, across_far, routes))
        end = lax.ppermute(across_far, "blk", SIDES)
        far_parts.append([far, across_far])
        end_parts.append([end, across])
    blocks = [[[one] for one in cuts], [[one] for one, _ in firsts]]
    early = stage(blocks, near, noise, swap_gather(routes, "reader", near_bits))
    weighted, penalty, staged_near, noise, routes = early
    ends = [parts[0] for parts in end_parts]
    far_routes, crossed = lax.optimization_barrier((routes, crossed))
    far_routes = swap_bits(far_routes, "reader", far_bit)
    crossed, far_routes, *_ = lax.optimization_barrier((crossed, far_routes, *ends))
    far = swap_gather(crossed, "reader", near_bits)
    staged = stage_rest([far_parts, end_parts], staged_near, crossed, weighted, penalty, noise)
    return staged, far[1:], (routes, far_routes)


def plain_gather(block, images, noise, routes, near_bits, far_bit):
    near = swap_gather(images, "reader", near_bits)
    near_routes = swap_gather(routes, "reader", near_bits)
    far = swap_gather(swap_bits(images, "reader", far_bit), "reader", near_bits)
    line = [[[one]] for one in line_gather(block, "blk")]
    weighted, penalty, near, noise, routes = stage(line[:2], near, noise, near_routes)
    staged = stage_rest(line[2:], near, far[0], weighted, penalty, noise)
    return staged, far[1:], (routes, swap_bits(routes, "reader", far_bit))


def line_gather(block, axis):
    size, member = lax.axis_size(axis), lax.axis_index(axis)
    ahead, behind = [block], [block]
    for s in range(1, size):
        ahead.append(lax.ppermute(ahead[-1], axis, [(i, i + 1) for i in range(s - 1, size - 1)]))
        behind.append(lax.ppermute(behind[-1], axis, [(i, i - 1) for i in range(1, size - s + 1)]))
    blocks = [block]
    for s in range(1, size):
        blocks.append(jnp.where(member >= s, ahead[s], behind[size - s]))
    return blocks


def pair_scatter(pieces, axis):
    member = lax.axis_index(axis)
    is_end = (member == 0) | (member == 3)
    for_far_end = [lax.ppermute(parts[3], axis, SIDES) for parts in pieces]
    *second, for_far_end[0] = lax.optimization_barrier(
        [parts[2] for parts in pieces] + for_far_end[:1]
    )
    for_far_middle = [lax.ppermute(part, axis, SIDES) for part in second]
    totals = []
    for parts, part, end, middle in zip(pieces, second, for_far_end, for_far_middle):
        across_end = lax.ppermute(add_rounded(part, end), axis, MIDDLE)
        across_middle = lax.ppermute(add_rounded(parts[3], middle), axis, MIDDLE)
        near = jnp.where(is_end, parts[1], add_rounded(parts[1], across_end))
        from_side = lax.ppermute(near, axis, SIDES)
        total = parts[0].astype(jnp.float32) + from_side.astype(jnp.float32)
        totals.append(total + jnp.where(is_end, 0.0, across_middle.astype(jnp.float32)))
    return beside(totals)


def beside_kernel(count, *refs):
    out_ref, sems = refs[count:]
    copies, stop = [], out_ref.shape[1]
    for i, ref in enumerate(refs[:count]):
        start = stop - ref.shape[1]
        copies.append(pltpu.make_async_copy(ref, out_ref.at[:, start:stop], sems.at[i]))
        copies[-1].start()
        stop = start
    for copy in copies:
        copy.wait()


def beside(pieces):
    width = sum(piece.shape[1] for piece in pieces)
    return pl.pallas_call(
        partial(beside_kernel, len(pieces)),
        out_shape=jax.ShapeDtypeStruct((pieces[0].shape[0], width), pieces[0].dtype),
        in_specs=[VMEM_SPEC] * len(pieces),
        out_specs=ANY_SPEC,
        scratch_shapes=[pltpu.SemaphoreType.DMA((len(pieces),))],
        compiler_params=pltpu.CompilerParams(vmem_limit_bytes=SUMS_VMEM),
        name="beside",
    )(*pieces[::-1])


def line_scatter(pieces, axis):
    return jnp.concatenate([line_sum(parts, axis) for parts in pieces], axis=1)


def line_sum(parts, axis):
    size = lax.axis_size(axis)
    up = down = None
    for s in range(1, size):
        send_up, send_down = parts[s], parts[size - s]
        if s > 1:
            send_up = add_rounded(send_up, up)
            send_down = add_rounded(send_down, down)
        up = lax.ppermute(send_up, axis, [(i, i + 1) for i in range(0, s) if i + 1 < size])
        down = lax.ppermute(send_down, axis, [(i, i - 1) for i in range(size - s, size) if i > 0])
    total = parts[0].astype(jnp.float32)
    if size > 1:
        total = total + up.astype(jnp.float32) + down.astype(jnp.float32)
    return total


def column_lse(scores):
    peak = jnp.max(scores, axis=0, keepdims=True)
    total = jnp.sum(jnp.exp(scores - peak), axis=0, keepdims=True)
    return peak + jnp.log(total)


def at_end():
    member = lax.axis_index("blk")
    return (member == 0) | (member == lax.axis_size("blk") - 1)


def either(refs, act):
    if len(refs) == 1:
        act(refs[0])
        return
    is_end = at_end()

    @pl.when(is_end)
    def _():
        act(refs[0])

    @pl.when(jnp.logical_not(is_end))
    def _():
        act(refs[1])


def weigh_blocks(groups, noise_ref, weighted_ref, penalty_ref, block_ref, sems, first):
    count = block_ref.shape[1]
    parts = []
    for s, group in enumerate(groups):
        start = 0
        for refs in group:
            stop = start + refs[0].shape[1]
            parts.append((s, slice(start, stop), refs))
            start = stop

    def part_copy(i, ref):
        s, columns, _ = parts[i]
        return pltpu.make_async_copy(ref, block_ref.at[s, :, columns], sems.at[i])

    for i, (_, _, refs) in enumerate(parts):
        either(refs, lambda ref, i=i: part_copy(i, ref).start())
    for s in range(len(groups)):
        rows = slice((first + s) * count, (first + s + 1) * count)
        penalty = jnp.zeros((count, 1), jnp.float32)
        for i, (t, columns, refs) in enumerate(parts):
            if t != s:
                continue
            part_copy(i, refs[0]).wait()
            for start in range(columns.start, columns.stop, STEP):
                piece = slice(start, min(start + STEP, columns.stop))
                block = block_ref[s, :, piece].astype(jnp.float32)
                scaled = block * noise_ref[:, piece]
                weighted_ref[rows, piece] = scaled.astype(jnp.bfloat16)
                penalty = penalty + 0.5 * jnp.sum(scaled * block, axis=1, keepdims=True)
        penalty_ref[rows, :] = penalty


def take_blocks(refs, counts):
    return [[[refs.pop(0) for _ in range(n)] for n in group] for group in counts]


def block_counts(blocks):
    return [[len(part) for part in group] for group in blocks]


def flat(blocks):
    return [one for group in blocks for part in group for one in part]


def stage_kernel(near_count, counts, *refs):
    refs = list(refs)
    near_refs = [refs.pop(0) for _ in range(near_count)]
    groups = take_blocks(refs, counts)
    route_refs = [refs.pop(0) for _ in range(near_count)]
    noise_ref, weighted_ref, penalty_ref, near_ref, noise_out_ref, route_ref = refs[:6]
    block_ref, near_sems, sems = refs[6:]
    rows = near_refs[0].shape[0]
    top = route_refs[0].shape[0]
    for k, ref in enumerate(route_refs):
        route_ref[k * top : (k + 1) * top, :] = ref[...]
    copies = []
    for k, ref in enumerate(near_refs):
        copy = pltpu.make_async_copy(ref, near_ref.at[pl.ds(k * rows, rows), :], near_sems.at[k])
        copy.start()
        copies.append(copy)
    noise_out_ref[...] = noise_ref[...]
    weigh_blocks(groups, noise_ref, weighted_ref, penalty_ref, block_ref, sems, 0)
    for copy in copies:
        copy.wait()


def stage(blocks, near, noise, routes):
    count = blocks[0][0][0].shape[0]
    parts = sum(len(group) for group in blocks)
    width = noise.shape[1]
    refs = len(blocks) * count
    rows = near[0].shape[0]
    moved = [*near, *flat(blocks)]
    return pl.pallas_call(
        partial(stage_kernel, len(near), block_counts(blocks)),
        out_shape=(
            jax.ShapeDtypeStruct((refs, width), jnp.bfloat16),
            jax.ShapeDtypeStruct((refs, 1), jnp.float32),
            jax.ShapeDtypeStruct((len(near) * near[0].shape[0], width), jnp.bfloat16),
            jax.ShapeDtypeStruct((1, width), jnp.float32),
            jax.ShapeDtypeStruct((len(routes) * routes[0].shape[0], rows), jnp.int32),
        ),
        in_specs=[ANY_SPEC] * len(moved) + [VMEM_SPEC] * (len(routes) + 1),
        out_specs=(VMEM_SPEC,) * 5,
        scratch_shapes=[
            pltpu.VMEM((len(blocks), count, width), jnp.bfloat16),
            pltpu.SemaphoreType.DMA((len(near),)),
            pltpu.SemaphoreType.DMA((parts,)),
        ],
        compiler_params=pltpu.CompilerParams(vmem_limit_bytes=SCORE_VMEM),
        cost_estimate=pl.CostEstimate(
            flops=8 * refs * width, bytes_accessed=12_000_000, transcendentals=0
        ),
        name="stage",
    )(*moved, *routes, noise)


def place_images(k, source, all_ref, sem):
    rows = source.shape[0]
    row = pl.multiple_of((lax.axis_index("reader") ^ k) * rows, 16)
    return pltpu.make_async_copy(source, all_ref.at[pl.ds(row, rows), :], sem), pl.ds(row, rows)


def stage_rest_kernel(readers, counts, *refs):
    refs = list(refs)
    groups = take_blocks(refs, counts)
    near_ref, far_ref, early_ref, early_penalty_ref, noise_ref = [refs.pop(0) for _ in range(5)]
    turned_ref, penalty_ref, all_ref, product_ref = refs[:4]
    weighted_ref, block_ref, sems, image_sems = refs[4:]
    rows = far_ref.shape[0]
    half = readers // 2
    sources = [near_ref.at[pl.ds(k * rows, rows), :] for k in range(half)] + [far_ref]
    placed = [place_images(k, one, all_ref, image_sems.at[k]) for k, one in enumerate(sources)]
    for copy, _ in placed:
        copy.start()
    done = early_ref.shape[0]
    weighted_ref[:done, :] = early_ref[...]
    penalty_ref[:done, :] = early_penalty_ref[...]
    first = done // block_ref.shape[1]
    weigh_blocks(groups, noise_ref, weighted_ref, penalty_ref, block_ref, sems, first)
    width = weighted_ref.shape[1]
    for start in range(0, width, STEP):
        piece = slice(start, min(start + STEP, width))
        turned_ref[piece, :] = weighted_ref[:, piece].T
    products = jnp.dot(near_ref[...], turned_ref[...], preferred_element_type=jnp.float32)
    for k in range(half):
        product_ref[placed[k][1], :] = products[k * rows : (k + 1) * rows]
    product_ref[placed[half][1], :] = jnp.dot(
        far_ref[...], turned_ref[...], preferred_element_type=jnp.float32
    )
    for copy, _ in placed:
        copy.wait()


def stage_rest(blocks, near, crossed, weighted, penalty, noise):
    count = blocks[0][0][0].shape[0]
    parts = sum(len(group) for group in blocks)
    width = noise.shape[1]
    refs = len(blocks) * count + weighted.shape[0]
    slots = 2 * near.shape[0]
    readers = slots // crossed.shape[0]
    moved = flat(blocks)
    return pl.pallas_call(
        partial(stage_rest_kernel, readers, block_counts(blocks)),
        out_shape=(
            jax.ShapeDtypeStruct((width, refs), jnp.bfloat16),
            jax.ShapeDtypeStruct((refs, 1), jnp.float32),
            jax.ShapeDtypeStruct((slots, width), jnp.bfloat16),
            jax.ShapeDtypeStruct((slots, refs), jnp.float32),
        ),
        in_specs=[ANY_SPEC] * len(moved) + [VMEM_SPEC] * 5,
        out_specs=(VMEM_SPEC,) * 4,
        scratch_shapes=[
            pltpu.VMEM((refs, width), jnp.bfloat16),
            pltpu.VMEM((len(blocks), count, width), jnp.bfloat16),
            pltpu.SemaphoreType.DMA((parts,)),
            pltpu.SemaphoreType.DMA((readers // 2 + 1,)),
        ],
        compiler_params=pltpu.CompilerParams(vmem_limit_bytes=SCORE_VMEM),
        cost_estimate=pl.CostEstimate(
            flops=8 * refs * width, bytes_accessed=12_000_000, transcendentals=0
        ),
        name="stage_rest",
    )(*moved, near, crossed, weighted, penalty, noise)


def score_kernel(readers, finish, *refs):
    refs = list(refs)
    half = readers // 2
    far_refs = [refs.pop(0) for _ in range(half - 1)]
    turned_ref, penalty_ref, _, product_ref = [refs.pop(0) for _ in range(4)]
    near_route_ref, far_route_ref = refs.pop(0), refs.pop(0)
    score_ref, mask_ref, lse_ref, all_ref, sum_ref, image_sems = refs
    reader = lax.axis_index("reader")
    placed = [
        place_images(half + 1 + i, ref, all_ref, image_sems.at[i])
        for i, ref in enumerate(far_refs)
    ]
    for copy, _ in placed:
        copy.start()
    sum_ref[...] = product_ref[...]
    for (_, place), ref in zip(placed, far_refs):
        sum_ref[place, :] = jnp.dot(
            ref[...], turned_ref[...], preferred_element_type=jnp.float32
        )
    top, rows = near_route_ref.shape[0] // half, near_route_ref.shape[1]
    routes = [near_route_ref[k * top : (k + 1) * top, :] for k in range(half)]
    routes += [far_route_ref[k * top : (k + 1) * top, :] for k in range(half)]
    bit = 1
    while bit < readers:
        flip = (reader & bit) > 0
        routes = [jnp.where(flip, routes[k ^ bit], one) for k, one in enumerate(routes)]
        bit *= 2
    for j, route in enumerate(routes):
        for k in range(readers):
            hits = jnp.where(route == (reader ^ k), 1.0, 0.0)
            mask_ref[k : k + 1, j * rows : (j + 1) * rows] = jnp.max(hits, axis=0, keepdims=True)
    scores = sum_ref[...].T - penalty_ref[...]
    score_ref[...] = scores
    if finish:
        lse_ref[...] = column_lse(scores)
    for copy, _ in placed:
        copy.wait()


def all_scores(staged, far, routes, finish):
    turned, penalty, images, products = staged
    width, refs = turned.shape
    slots, rows = images.shape[0], far[0].shape[0]
    readers = slots // rows
    return pl.pallas_call(
        partial(score_kernel, readers, finish),
        out_shape=(
            jax.ShapeDtypeStruct((refs, slots), jnp.float32),
            jax.ShapeDtypeStruct((readers, slots), jnp.float32),
            jax.ShapeDtypeStruct((1, slots), jnp.float32),
            jax.ShapeDtypeStruct((slots, width), jnp.bfloat16),
        ),
        in_specs=[VMEM_SPEC] * (len(far) + 4 + len(routes)),
        out_specs=(VMEM_SPEC,) * 4,
        scratch_shapes=[
            pltpu.VMEM((slots, refs), jnp.float32),
            pltpu.SemaphoreType.DMA((len(far),)),
        ],
        input_output_aliases={len(far) + 2: 3},
        compiler_params=pltpu.CompilerParams(vmem_limit_bytes=SCORE_VMEM),
        cost_estimate=pl.CostEstimate(
            flops=2 * refs * slots * width,
            bytes_accessed=2 * (slots + refs) * width,
            transcendentals=0,
        ),
        name="scores",
    )(*far, turned, penalty, images, products, *routes)


def lse_kernel(score_ref, lse_ref):
    lse_ref[...] = column_lse(score_ref[...])


def group_lse(scores):
    return pl.pallas_call(
        lse_kernel,
        out_shape=jax.ShapeDtypeStruct((1, scores.shape[1]), jnp.float32),
        name="group_lse",
    )(scores)


def emit_sums(posterior, all_ref, piece, out_refs):
    sums = jnp.dot(posterior, all_ref[:, piece], preferred_element_type=jnp.float32)
    count = sums.shape[0] // len(out_refs)
    for s, out_ref in enumerate(out_refs):
        out_ref[...] = sums[s * count : (s + 1) * count].astype(out_ref.dtype)


def first_sums_kernel(readers, piece, all_ref, score_ref, mask_ref, *refs):
    lse_refs, norm_ref, post_ref = refs[:readers], refs[readers], refs[readers + 1]
    kept = []
    for k, lse_ref in enumerate(lse_refs):
        kept.append(jnp.where(mask_ref[k : k + 1, :] > 0.0, lse_ref[...], -jnp.inf))
    highest = kept[0]
    for value in kept[1:]:
        highest = jnp.maximum(highest, value)
    spread = jnp.exp(kept[0] - highest)
    for value in kept[1:]:
        spread = spread + jnp.exp(value - highest)
    norm = highest + jnp.log(spread)
    norm_ref[...] = norm
    exponent = jnp.where(mask_ref[0:1, :] > 0.0, score_ref[...] - norm, -jnp.inf)
    posterior = jnp.exp(exponent).astype(jnp.bfloat16)
    post_ref[...] = posterior
    emit_sums(posterior, all_ref, piece, refs[readers + 2 :])


def later_sums_kernel(piece, all_ref, post_ref, *out_refs):
    emit_sums(post_ref[...], all_ref, piece, out_refs)


def group_sums(kernel, piece, members, all_images, operands, extra):
    refs, slots = operands[0].shape
    width = piece.stop - piece.start
    block = jax.ShapeDtypeStruct((refs // members, width), jnp.bfloat16)
    outs = pl.pallas_call(
        kernel,
        out_shape=tuple(extra) + (block,) * members,
        in_specs=[VMEM_SPEC] * (1 + len(operands)),
        out_specs=(VMEM_SPEC,) * (len(extra) + members),
        compiler_params=pltpu.CompilerParams(vmem_limit_bytes=SUMS_VMEM),
        cost_estimate=pl.CostEstimate(
            flops=2 * refs * slots * width,
            bytes_accessed=2 * slots * width,
            transcendentals=0,
        ),
        name="sums",
    )(all_images, *operands)
    return outs[: len(extra)], outs[len(extra) :]


def on_device(images, routes, projections, noise_weights):
    readers = lax.axis_size("reader")
    members = lax.axis_size("blk")
    reader = lax.axis_index("reader")
    rows, width = images.shape
    noise = noise_weights.reshape(1, width)

    gather = staged_gather if members == 4 and rows % 32 == 0 and readers > 1 else plain_gather
    staged, far, all_routes = gather(
        projections[0], images, noise, routes.T, readers // 4, readers // 2
    )
    split = lax.axis_size("sub") > 1
    scores, masks, mine, all_images = all_scores(staged, far, all_routes, not split)
    if split:
        scores = lax.psum(scores, "sub")
        mine = group_lse(scores)
    lses = [mine] + [swap_bits(mine, "reader", k) for k in range(1, readers)]
    pieces = [slice(0, width // 2), slice(width // 2, width)]
    extra = (
        jax.ShapeDtypeStruct((1, scores.shape[1]), jnp.float32),
        jax.ShapeDtypeStruct(scores.shape, jnp.bfloat16),
    )
    (norms, posterior), first = group_sums(
        partial(first_sums_kernel, readers, pieces[0]),
        pieces[0],
        members,
        all_images,
        (scores, masks, *lses),
        extra,
    )
    _, last = group_sums(
        partial(later_sums_kernel, pieces[1]), pieces[1], members, all_images, (posterior,), ()
    )
    parts = [first, last]
    scatter = pair_scatter if members == 4 else line_scatter
    total = scatter(parts, "blk")
    normalizer = lax.dynamic_slice(norms.reshape(-1), (reader * rows,), (rows,))
    return (total[None], normalizer)


def solution(mesh):
    return jax.shard_map(
        on_device,
        mesh=mesh,
        in_specs=(
            P(("parts", "blk", "reader"), "sub"),
            P(("parts", "blk", "reader"), None),
            P(("parts", "reader"), "blk", "sub"),
            P(("parts", "sub")),
        ),
        out_specs=(P(("parts", "reader"), "blk", "sub"), P(("parts", "blk", "reader"))),
        check_vma=False,
    )
```

```python
from functools import partial

import jax
import jax.numpy as jnp
from jax import lax
from jax.experimental import pallas as pl
from jax.experimental.pallas import tpu as pltpu
from jax.sharding import PartitionSpec as P

SCORE_VMEM = 20 * 1024 * 1024
SUMS_VMEM = 12 * 1024 * 1024
STEP = 1024
VMEM_SPEC = pl.BlockSpec(memory_space=pltpu.VMEM)
ANY_SPEC = pl.BlockSpec(memory_space=pl.ANY)
SIDES = [(0, 1), (1, 0), (2, 3), (3, 2)]
MIDDLE = [(1, 2), (2, 1)]


def swap_bits(block, axis, bits):
    return lax.ppermute(block, axis, [(i, i ^ bits) for i in range(lax.axis_size(axis))])


def swap_gather(block, axis, bit):
    held = {0: block}
    while bit:
        for k in list(held):
            held[k ^ bit] = swap_bits(held[k], axis, bit)
        bit //= 2
    return [held[k] for k in range(len(held))]


def add_rounded(one, other):
    return (one.astype(jnp.float32) + other.astype(jnp.float32)).astype(jnp.bfloat16)


def staged_gather(block, images, noise, near_bits, far_bit):
    cut = block.shape[1] // 16 * 9
    cuts = [block[:, :cut], block[:, cut:]]
    crossed = swap_bits(images, "reader", far_bit)
    near = swap_gather(images, "reader", near_bits)
    firsts = [
        lax.optimization_barrier(
            (lax.ppermute(one, "blk", SIDES), lax.ppermute(one, "blk", MIDDLE))
        )
        for one in cuts
    ]
    early = stage(
        [[[one] for one in cuts], [[side] for side, _ in firsts]], near, noise
    )
    far_parts, end_parts = [], []
    for last, (side, across) in enumerate(firsts):
        far = lax.ppermute(across, "blk", SIDES)
        side, *_ = lax.optimization_barrier((side, *near))
        across_far = lax.ppermute(side, "blk", MIDDLE)
        if last:
            far, across_far, *early = lax.optimization_barrier((far, across_far, *early))
        else:
            far, across_far = lax.optimization_barrier((far, across_far))
        end = lax.ppermute(across_far, "blk", SIDES)
        far_parts.append([far, across_far])
        end_parts.append([end, across])
    weighted, penalty, staged_near, noise = early
    ends = [parts[0] for parts in end_parts]
    crossed, *_ = lax.optimization_barrier((crossed, *ends))
    far = swap_gather(crossed, "reader", near_bits)
    staged = stage_rest([far_parts, end_parts], staged_near, crossed, weighted, penalty, noise)
    return staged, far[1:]


def plain_gather(block, images, noise, near_bits, far_bit):
    near = swap_gather(images, "reader", near_bits)
    far = swap_gather(swap_bits(images, "reader", far_bit), "reader", near_bits)
    line = [[[one]] for one in line_gather(block, "blk")]
    weighted, penalty, near, noise = stage(line[:2], near, noise)
    staged = stage_rest(line[2:], near, far[0], weighted, penalty, noise)
    return staged, far[1:]


def line_gather(block, axis):
    size, member = lax.axis_size(axis), lax.axis_index(axis)
    ahead, behind = [block], [block]
    for s in range(1, size):
        ahead.append(lax.ppermute(ahead[-1], axis, [(i, i + 1) for i in range(s - 1, size - 1)]))
        behind.append(lax.ppermute(behind[-1], axis, [(i, i - 1) for i in range(1, size - s + 1)]))
    blocks = [block]
    for s in range(1, size):
        blocks.append(jnp.where(member >= s, ahead[s], behind[size - s]))
    return blocks


def pair_scatter(pieces, axis):
    member = lax.axis_index(axis)
    is_end = (member == 0) | (member == 3)
    for_far_end = [lax.ppermute(parts[3], axis, SIDES) for parts in pieces]
    *second, for_far_end[0] = lax.optimization_barrier(
        [parts[2] for parts in pieces] + for_far_end[:1]
    )
    for_far_middle = [lax.ppermute(part, axis, SIDES) for part in second]
    totals = []
    for parts, part, end, middle in zip(pieces, second, for_far_end, for_far_middle):
        across_end = lax.ppermute(add_rounded(part, end), axis, MIDDLE)
        across_middle = lax.ppermute(add_rounded(parts[3], middle), axis, MIDDLE)
        near = jnp.where(is_end, parts[1], add_rounded(parts[1], across_end))
        from_side = lax.ppermute(near, axis, SIDES)
        total = parts[0].astype(jnp.float32) + from_side.astype(jnp.float32)
        totals.append(total + jnp.where(is_end, 0.0, across_middle.astype(jnp.float32)))
    return beside(totals)


def beside_kernel(count, *refs):
    out_ref, sems = refs[count:]
    copies, stop = [], out_ref.shape[1]
    for i, ref in enumerate(refs[:count]):
        start = stop - ref.shape[1]
        copies.append(pltpu.make_async_copy(ref, out_ref.at[:, start:stop], sems.at[i]))
        copies[-1].start()
        stop = start
    for copy in copies:
        copy.wait()


def beside(pieces):
    width = sum(piece.shape[1] for piece in pieces)
    return pl.pallas_call(
        partial(beside_kernel, len(pieces)),
        out_shape=jax.ShapeDtypeStruct((pieces[0].shape[0], width), pieces[0].dtype),
        in_specs=[VMEM_SPEC] * len(pieces),
        out_specs=ANY_SPEC,
        scratch_shapes=[pltpu.SemaphoreType.DMA((len(pieces),))],
        compiler_params=pltpu.CompilerParams(vmem_limit_bytes=SUMS_VMEM),
        name="beside",
    )(*pieces[::-1])


def line_scatter(pieces, axis):
    return jnp.concatenate([line_sum(parts, axis) for parts in pieces], axis=1)


def line_sum(parts, axis):
    size = lax.axis_size(axis)
    up = down = None
    for s in range(1, size):
        send_up, send_down = parts[s], parts[size - s]
        if s > 1:
            send_up = add_rounded(send_up, up)
            send_down = add_rounded(send_down, down)
        up = lax.ppermute(send_up, axis, [(i, i + 1) for i in range(0, s) if i + 1 < size])
        down = lax.ppermute(send_down, axis, [(i, i - 1) for i in range(size - s, size) if i > 0])
    total = parts[0].astype(jnp.float32)
    if size > 1:
        total = total + up.astype(jnp.float32) + down.astype(jnp.float32)
    return total


def column_lse(scores):
    peak = jnp.max(scores, axis=0, keepdims=True)
    total = jnp.sum(jnp.exp(scores - peak), axis=0, keepdims=True)
    return peak + jnp.log(total)


def at_end():
    member = lax.axis_index("blk")
    return (member == 0) | (member == lax.axis_size("blk") - 1)


def either(refs, act):
    if len(refs) == 1:
        act(refs[0])
        return
    is_end = at_end()

    @pl.when(is_end)
    def _():
        act(refs[0])

    @pl.when(jnp.logical_not(is_end))
    def _():
        act(refs[1])


def weigh_blocks(groups, noise_ref, weighted_ref, penalty_ref, block_ref, sems, first):
    count = block_ref.shape[1]
    parts = []
    for s, group in enumerate(groups):
        start = 0
        for refs in group:
            stop = start + refs[0].shape[1]
            parts.append((s, slice(start, stop), refs))
            start = stop

    def part_copy(i, ref):
        s, columns, _ = parts[i]
        return pltpu.make_async_copy(ref, block_ref.at[s, :, columns], sems.at[i])

    for i, (_, _, refs) in enumerate(parts):
        either(refs, lambda ref, i=i: part_copy(i, ref).start())
    for s in range(len(groups)):
        rows = slice((first + s) * count, (first + s + 1) * count)
        penalty = jnp.zeros((count, 1), jnp.float32)
        for i, (t, columns, refs) in enumerate(parts):
            if t != s:
                continue
            part_copy(i, refs[0]).wait()
            for start in range(columns.start, columns.stop, STEP):
                piece = slice(start, min(start + STEP, columns.stop))
                block = block_ref[s, :, piece].astype(jnp.float32)
                scaled = block * noise_ref[:, piece]
                weighted_ref[rows, piece] = scaled.astype(jnp.bfloat16)
                penalty = penalty + 0.5 * jnp.sum(scaled * block, axis=1, keepdims=True)
        penalty_ref[rows, :] = penalty


def take_blocks(refs, counts):
    return [[[refs.pop(0) for _ in range(n)] for n in group] for group in counts]


def block_counts(blocks):
    return [[len(part) for part in group] for group in blocks]


def flat(blocks):
    return [one for group in blocks for part in group for one in part]


def stage_kernel(near_count, counts, *refs):
    refs = list(refs)
    near_refs = [refs.pop(0) for _ in range(near_count)]
    groups = take_blocks(refs, counts)
    noise_ref, weighted_ref, penalty_ref, near_ref, noise_out_ref, block_ref, near_sems, sems = refs
    rows = near_refs[0].shape[0]
    copies = []
    for k, ref in enumerate(near_refs):
        copy = pltpu.make_async_copy(ref, near_ref.at[pl.ds(k * rows, rows), :], near_sems.at[k])
        copy.start()
        copies.append(copy)
    noise_out_ref[...] = noise_ref[...]
    weigh_blocks(groups, noise_ref, weighted_ref, penalty_ref, block_ref, sems, 0)
    for copy in copies:
        copy.wait()


def stage(blocks, near, noise):
    count = blocks[0][0][0].shape[0]
    parts = sum(len(group) for group in blocks)
    width = noise.shape[1]
    refs = len(blocks) * count
    moved = [*near, *flat(blocks)]
    return pl.pallas_call(
        partial(stage_kernel, len(near), block_counts(blocks)),
        out_shape=(
            jax.ShapeDtypeStruct((refs, width), jnp.bfloat16),
            jax.ShapeDtypeStruct((refs, 1), jnp.float32),
            jax.ShapeDtypeStruct((len(near) * near[0].shape[0], width), jnp.bfloat16),
            jax.ShapeDtypeStruct((1, width), jnp.float32),
        ),
        in_specs=[ANY_SPEC] * len(moved) + [VMEM_SPEC],
        out_specs=(VMEM_SPEC,) * 4,
        scratch_shapes=[
            pltpu.VMEM((len(blocks), count, width), jnp.bfloat16),
            pltpu.SemaphoreType.DMA((len(near),)),
            pltpu.SemaphoreType.DMA((parts,)),
        ],
        compiler_params=pltpu.CompilerParams(vmem_limit_bytes=SCORE_VMEM),
        cost_estimate=pl.CostEstimate(
            flops=8 * refs * width, bytes_accessed=12_000_000, transcendentals=0
        ),
        name="stage",
    )(*moved, noise)


def place_images(k, source, all_ref, sem):
    rows = source.shape[0]
    row = pl.multiple_of((lax.axis_index("reader") ^ k) * rows, 16)
    return pltpu.make_async_copy(source, all_ref.at[pl.ds(row, rows), :], sem), pl.ds(row, rows)


def stage_rest_kernel(readers, counts, *refs):
    refs = list(refs)
    groups = take_blocks(refs, counts)
    near_ref, far_ref, early_ref, early_penalty_ref, noise_ref = [refs.pop(0) for _ in range(5)]
    turned_ref, penalty_ref, all_ref, product_ref = refs[:4]
    weighted_ref, block_ref, sems, image_sems = refs[4:]
    rows = far_ref.shape[0]
    half = readers // 2
    sources = [near_ref.at[pl.ds(k * rows, rows), :] for k in range(half)] + [far_ref]
    placed = [place_images(k, one, all_ref, image_sems.at[k]) for k, one in enumerate(sources)]
    for copy, _ in placed:
        copy.start()
    done = early_ref.shape[0]
    weighted_ref[:done, :] = early_ref[...]
    penalty_ref[:done, :] = early_penalty_ref[...]
    first = done // block_ref.shape[1]
    weigh_blocks(groups, noise_ref, weighted_ref, penalty_ref, block_ref, sems, first)
    width = weighted_ref.shape[1]
    for start in range(0, width, STEP):
        piece = slice(start, min(start + STEP, width))
        turned_ref[piece, :] = weighted_ref[:, piece].T
    products = jnp.dot(near_ref[...], turned_ref[...], preferred_element_type=jnp.float32)
    for k in range(half):
        product_ref[placed[k][1], :] = products[k * rows : (k + 1) * rows]
    product_ref[placed[half][1], :] = jnp.dot(
        far_ref[...], turned_ref[...], preferred_element_type=jnp.float32
    )
    for copy, _ in placed:
        copy.wait()


def stage_rest(blocks, near, crossed, weighted, penalty, noise):
    count = blocks[0][0][0].shape[0]
    parts = sum(len(group) for group in blocks)
    width = noise.shape[1]
    refs = len(blocks) * count + weighted.shape[0]
    slots = 2 * near.shape[0]
    readers = slots // crossed.shape[0]
    moved = flat(blocks)
    return pl.pallas_call(
        partial(stage_rest_kernel, readers, block_counts(blocks)),
        out_shape=(
            jax.ShapeDtypeStruct((width, refs), jnp.bfloat16),
            jax.ShapeDtypeStruct((refs, 1), jnp.float32),
            jax.ShapeDtypeStruct((slots, width), jnp.bfloat16),
            jax.ShapeDtypeStruct((slots, refs), jnp.float32),
        ),
        in_specs=[ANY_SPEC] * len(moved) + [VMEM_SPEC] * 5,
        out_specs=(VMEM_SPEC,) * 4,
        scratch_shapes=[
            pltpu.VMEM((refs, width), jnp.bfloat16),
            pltpu.VMEM((len(blocks), count, width), jnp.bfloat16),
            pltpu.SemaphoreType.DMA((parts,)),
            pltpu.SemaphoreType.DMA((readers // 2 + 1,)),
        ],
        compiler_params=pltpu.CompilerParams(vmem_limit_bytes=SCORE_VMEM),
        cost_estimate=pl.CostEstimate(
            flops=8 * refs * width, bytes_accessed=12_000_000, transcendentals=0
        ),
        name="stage_rest",
    )(*moved, near, crossed, weighted, penalty, noise)


def write_packet(packet_ref, scores, route_ref):
    top, rows = route_ref.shape
    packet_ref[0:1, :] = column_lse(scores)
    packet_ref[1:2, :] = jnp.zeros((1, packet_ref.shape[1]), jnp.float32)
    for t in range(top):
        packet_ref[1:2, t * rows : (t + 1) * rows] = route_ref[t : t + 1, :].astype(jnp.float32)


def score_kernel(readers, finish, *refs):
    refs = list(refs)
    half = readers // 2
    far_refs = [refs.pop(0) for _ in range(half - 1)]
    turned_ref, penalty_ref, _, product_ref, route_ref = refs[:5]
    score_ref, packet_ref, all_ref, sum_ref, image_sems = refs[5:]
    placed = [
        place_images(half + 1 + i, ref, all_ref, image_sems.at[i])
        for i, ref in enumerate(far_refs)
    ]
    for copy, _ in placed:
        copy.start()
    sum_ref[...] = product_ref[...]
    for (_, place), ref in zip(placed, far_refs):
        sum_ref[place, :] = jnp.dot(
            ref[...], turned_ref[...], preferred_element_type=jnp.float32
        )
    scores = sum_ref[...].T - penalty_ref[...]
    score_ref[...] = scores
    if finish:
        write_packet(packet_ref, scores, route_ref)
    for copy, _ in placed:
        copy.wait()


def all_scores(staged, far, routes, finish):
    turned, penalty, images, products = staged
    width, refs = turned.shape
    slots, rows = images.shape[0], far[0].shape[0]
    return pl.pallas_call(
        partial(score_kernel, slots // rows, finish),
        out_shape=(
            jax.ShapeDtypeStruct((refs, slots), jnp.float32),
            jax.ShapeDtypeStruct((2, slots), jnp.float32),
            jax.ShapeDtypeStruct((slots, width), jnp.bfloat16),
        ),
        in_specs=[VMEM_SPEC] * (len(far) + 5),
        out_specs=(VMEM_SPEC,) * 3,
        scratch_shapes=[
            pltpu.VMEM((slots, refs), jnp.float32),
            pltpu.SemaphoreType.DMA((len(far),)),
        ],
        input_output_aliases={len(far) + 2: 2},
        compiler_params=pltpu.CompilerParams(vmem_limit_bytes=SCORE_VMEM),
        cost_estimate=pl.CostEstimate(
            flops=2 * refs * slots * width,
            bytes_accessed=2 * (slots + refs) * width,
            transcendentals=0,
        ),
        name="scores",
    )(*far, turned, penalty, images, products, routes)


def packet_kernel(score_ref, route_ref, packet_ref):
    write_packet(packet_ref, score_ref[...], route_ref)


def make_packet(scores, routes):
    return pl.pallas_call(
        packet_kernel,
        out_shape=jax.ShapeDtypeStruct((2, scores.shape[1]), jnp.float32),
        name="packet",
    )(scores, routes)


def write_masks(packets, rows, top, mask_ref):
    reader = lax.axis_index("reader")
    readers = len(packets)
    for t in range(top):
        routes = [ref[1:2, t * rows : (t + 1) * rows] for ref in packets]
        bit = 1
        while bit < readers:
            flip = (reader & bit) > 0
            routes = [jnp.where(flip, routes[k ^ bit], one) for k, one in enumerate(routes)]
            bit *= 2
        for j, route in enumerate(routes):
            columns = slice(j * rows, (j + 1) * rows)
            for k in range(readers):
                hits = jnp.where(route == (reader ^ k).astype(jnp.float32), 1.0, 0.0)
                if t:
                    hits = jnp.maximum(hits, mask_ref[k : k + 1, columns])
                mask_ref[k : k + 1, columns] = hits


def emit_sums(posterior, all_ref, piece, out_refs):
    sums = jnp.dot(posterior, all_ref[:, piece], preferred_element_type=jnp.float32)
    count = sums.shape[0] // len(out_refs)
    for s, out_ref in enumerate(out_refs):
        out_ref[...] = sums[s * count : (s + 1) * count].astype(out_ref.dtype)


def first_sums_kernel(readers, top, piece, all_ref, score_ref, *refs):
    refs = list(refs)
    packets = [refs.pop(0) for _ in range(readers)]
    mask_ref = refs.pop()
    norm_ref, post_ref, *out_refs = refs
    write_masks(packets, packets[0].shape[1] // readers, top, mask_ref)
    kept = []
    for k, packet in enumerate(packets):
        kept.append(jnp.where(mask_ref[k : k + 1, :] > 0.0, packet[0:1, :], -jnp.inf))
    highest = kept[0]
    for value in kept[1:]:
        highest = jnp.maximum(highest, value)
    spread = jnp.exp(kept[0] - highest)
    for value in kept[1:]:
        spread = spread + jnp.exp(value - highest)
    norm = highest + jnp.log(spread)
    norm_ref[...] = norm
    exponent = jnp.where(mask_ref[0:1, :] > 0.0, score_ref[...] - norm, -jnp.inf)
    posterior = jnp.exp(exponent).astype(jnp.bfloat16)
    post_ref[...] = posterior
    emit_sums(posterior, all_ref, piece, out_refs)


def later_sums_kernel(piece, all_ref, post_ref, *out_refs):
    emit_sums(post_ref[...], all_ref, piece, out_refs)


def group_sums(kernel, piece, members, all_images, operands, extra, scratch=()):
    refs, slots = operands[0].shape
    width = piece.stop - piece.start
    block = jax.ShapeDtypeStruct((refs // members, width), jnp.bfloat16)
    outs = pl.pallas_call(
        kernel,
        out_shape=tuple(extra) + (block,) * members,
        in_specs=[VMEM_SPEC] * (1 + len(operands)),
        out_specs=(VMEM_SPEC,) * (len(extra) + members),
        scratch_shapes=scratch,
        compiler_params=pltpu.CompilerParams(vmem_limit_bytes=SUMS_VMEM),
        cost_estimate=pl.CostEstimate(
            flops=2 * refs * slots * width,
            bytes_accessed=2 * slots * width,
            transcendentals=0,
        ),
        name="sums",
    )(all_images, *operands)
    return outs[: len(extra)], outs[len(extra) :]


def on_device(images, routes, projections, noise_weights):
    readers = lax.axis_size("reader")
    members = lax.axis_size("blk")
    reader = lax.axis_index("reader")
    rows, width = images.shape
    noise = noise_weights.reshape(1, width)

    gather = staged_gather if members == 4 and rows % 32 == 0 and readers > 1 else plain_gather
    staged, far = gather(projections[0], images, noise, readers // 4, readers // 2)
    split = lax.axis_size("sub") > 1
    scores, mine, all_images = all_scores(staged, far, routes.T, not split)
    if split:
        scores = lax.psum(scores, "sub")
        mine = make_packet(scores, routes.T)
    packets = [mine] + [swap_bits(mine, "reader", k) for k in range(1, readers)]
    pieces = [slice(0, width // 2), slice(width // 2, width)]
    extra = (
        jax.ShapeDtypeStruct((1, scores.shape[1]), jnp.float32),
        jax.ShapeDtypeStruct(scores.shape, jnp.bfloat16),
    )
    (norms, posterior), first = group_sums(
        partial(first_sums_kernel, readers, routes.shape[1], pieces[0]),
        pieces[0],
        members,
        all_images,
        (scores, *packets),
        extra,
        (pltpu.VMEM((readers, scores.shape[1]), jnp.float32),),
    )
    _, last = group_sums(
        partial(later_sums_kernel, pieces[1]), pieces[1], members, all_images, (posterior,), ()
    )
    parts = [first, last]
    scatter = pair_scatter if members == 4 else line_scatter
    total = scatter(parts, "blk")
    normalizer = lax.dynamic_slice(norms.reshape(-1), (reader * rows,), (rows,))
    return (total[None], normalizer)


def solution(mesh):
    return jax.shard_map(
        on_device,
        mesh=mesh,
        in_specs=(
            P(("parts", "blk", "reader"), "sub"),
            P(("parts", "blk", "reader"), None),
            P(("parts", "reader"), "blk", "sub"),
            P(("parts", "sub")),
        ),
        out_specs=(P(("parts", "reader"), "blk", "sub"), P(("parts", "blk", "reader"))),
        check_vma=False,
    )
```

```python
from functools import partial

import jax
import jax.numpy as jnp
from jax import lax
from jax.experimental import pallas as pl
from jax.experimental.pallas import tpu as pltpu
from jax.sharding import PartitionSpec as P

SCORE_VMEM = 20 * 1024 * 1024
SUMS_VMEM = 12 * 1024 * 1024
STEP = 1024
VMEM_SPEC = pl.BlockSpec(memory_space=pltpu.VMEM)
ANY_SPEC = pl.BlockSpec(memory_space=pl.ANY)
SIDES = [(0, 1), (1, 0), (2, 3), (3, 2)]
MIDDLE = [(1, 2), (2, 1)]


def swap_bits(block, axis, bits):
    return lax.ppermute(block, axis, [(i, i ^ bits) for i in range(lax.axis_size(axis))])


def swap_gather(block, axis, bit):
    held = {0: block}
    while bit:
        for k in list(held):
            held[k ^ bit] = swap_bits(held[k], axis, bit)
        bit //= 2
    return [held[k] for k in range(len(held))]


def add_rounded(one, other):
    return (one.astype(jnp.float32) + other.astype(jnp.float32)).astype(jnp.bfloat16)


def staged_gather(block, images, noise, near_bits, far_bit):
    cut = block.shape[1] // 16 * 9
    cuts = [block[:, :cut], block[:, cut:]]
    crossed = swap_bits(images, "reader", far_bit)
    near = swap_gather(images, "reader", near_bits)
    firsts = [
        lax.optimization_barrier(
            (lax.ppermute(one, "blk", SIDES), lax.ppermute(one, "blk", MIDDLE))
        )
        for one in cuts
    ]
    early = stage(
        [[[one] for one in cuts], [[side] for side, _ in firsts]], near, noise
    )
    far_parts, end_parts = [], []
    for last, (side, across) in enumerate(firsts):
        far = lax.ppermute(across, "blk", SIDES)
        side, *_ = lax.optimization_barrier((side, *near))
        across_far = lax.ppermute(side, "blk", MIDDLE)
        if last:
            far, across_far, *early = lax.optimization_barrier((far, across_far, *early))
        else:
            far, across_far = lax.optimization_barrier((far, across_far))
        end = lax.ppermute(across_far, "blk", SIDES)
        far_parts.append([far, across_far])
        end_parts.append([end, across])
    weighted, penalty, staged_near, noise = early
    ends = [parts[0] for parts in end_parts]
    crossed, *_ = lax.optimization_barrier((crossed, *ends))
    far = swap_gather(crossed, "reader", near_bits)
    staged = stage_rest([far_parts, end_parts], staged_near, crossed, weighted, penalty, noise)
    return staged, far[1:]


def plain_gather(block, images, noise, near_bits, far_bit):
    near = swap_gather(images, "reader", near_bits)
    far = swap_gather(swap_bits(images, "reader", far_bit), "reader", near_bits)
    line = [[[one]] for one in line_gather(block, "blk")]
    weighted, penalty, near, noise = stage(line[:2], near, noise)
    staged = stage_rest(line[2:], near, far[0], weighted, penalty, noise)
    return staged, far[1:]


def line_gather(block, axis):
    size, member = lax.axis_size(axis), lax.axis_index(axis)
    ahead, behind = [block], [block]
    for s in range(1, size):
        ahead.append(lax.ppermute(ahead[-1], axis, [(i, i + 1) for i in range(s - 1, size - 1)]))
        behind.append(lax.ppermute(behind[-1], axis, [(i, i - 1) for i in range(1, size - s + 1)]))
    blocks = [block]
    for s in range(1, size):
        blocks.append(jnp.where(member >= s, ahead[s], behind[size - s]))
    return blocks


def pair_scatter(pieces, axis):
    member = lax.axis_index(axis)
    is_end = (member == 0) | (member == 3)
    for_far_end = [lax.ppermute(parts[3], axis, SIDES) for parts in pieces]
    *second, for_far_end[0] = lax.optimization_barrier(
        [parts[2] for parts in pieces] + for_far_end[:1]
    )
    for_far_middle = [lax.ppermute(part, axis, SIDES) for part in second]
    totals = []
    for parts, part, end, middle in zip(pieces, second, for_far_end, for_far_middle):
        across_end = lax.ppermute(add_rounded(part, end), axis, MIDDLE)
        across_middle = lax.ppermute(add_rounded(parts[3], middle), axis, MIDDLE)
        near = jnp.where(is_end, parts[1], add_rounded(parts[1], across_end))
        from_side = lax.ppermute(near, axis, SIDES)
        total = parts[0].astype(jnp.float32) + from_side.astype(jnp.float32)
        totals.append(total + jnp.where(is_end, 0.0, across_middle.astype(jnp.float32)))
    return beside(totals)


def beside_kernel(count, *refs):
    out_ref, sems = refs[count:]
    copies, stop = [], out_ref.shape[1]
    for i, ref in enumerate(refs[:count]):
        start = stop - ref.shape[1]
        copies.append(pltpu.make_async_copy(ref, out_ref.at[:, start:stop], sems.at[i]))
        copies[-1].start()
        stop = start
    for copy in copies:
        copy.wait()


def beside(pieces):
    width = sum(piece.shape[1] for piece in pieces)
    return pl.pallas_call(
        partial(beside_kernel, len(pieces)),
        out_shape=jax.ShapeDtypeStruct((pieces[0].shape[0], width), pieces[0].dtype),
        in_specs=[VMEM_SPEC] * len(pieces),
        out_specs=ANY_SPEC,
        scratch_shapes=[pltpu.SemaphoreType.DMA((len(pieces),))],
        compiler_params=pltpu.CompilerParams(vmem_limit_bytes=SUMS_VMEM),
        name="beside",
    )(*pieces[::-1])


def line_scatter(pieces, axis):
    return jnp.concatenate([line_sum(parts, axis) for parts in pieces], axis=1)


def line_sum(parts, axis):
    size = lax.axis_size(axis)
    up = down = None
    for s in range(1, size):
        send_up, send_down = parts[s], parts[size - s]
        if s > 1:
            send_up = add_rounded(send_up, up)
            send_down = add_rounded(send_down, down)
        up = lax.ppermute(send_up, axis, [(i, i + 1) for i in range(0, s) if i + 1 < size])
        down = lax.ppermute(send_down, axis, [(i, i - 1) for i in range(size - s, size) if i > 0])
    total = parts[0].astype(jnp.float32)
    if size > 1:
        total = total + up.astype(jnp.float32) + down.astype(jnp.float32)
    return total


def column_lse(scores):
    peak = jnp.max(scores, axis=0, keepdims=True)
    total = jnp.sum(jnp.exp(scores - peak), axis=0, keepdims=True)
    return peak + jnp.log(total)


def at_end():
    member = lax.axis_index("blk")
    return (member == 0) | (member == lax.axis_size("blk") - 1)


def either(refs, act):
    if len(refs) == 1:
        act(refs[0])
        return
    is_end = at_end()

    @pl.when(is_end)
    def _():
        act(refs[0])

    @pl.when(jnp.logical_not(is_end))
    def _():
        act(refs[1])


def weigh_blocks(groups, noise_ref, weighted_ref, penalty_ref, block_ref, sems, first):
    count = block_ref.shape[1]
    parts = []
    for s, group in enumerate(groups):
        start = 0
        for refs in group:
            stop = start + refs[0].shape[1]
            parts.append((s, slice(start, stop), refs))
            start = stop

    def part_copy(i, ref):
        s, columns, _ = parts[i]
        return pltpu.make_async_copy(ref, block_ref.at[s, :, columns], sems.at[i])

    for i, (_, _, refs) in enumerate(parts):
        either(refs, lambda ref, i=i: part_copy(i, ref).start())
    for s in range(len(groups)):
        rows = slice((first + s) * count, (first + s + 1) * count)
        penalty = jnp.zeros((count, 1), jnp.float32)
        for i, (t, columns, refs) in enumerate(parts):
            if t != s:
                continue
            part_copy(i, refs[0]).wait()
            for start in range(columns.start, columns.stop, STEP):
                piece = slice(start, min(start + STEP, columns.stop))
                block = block_ref[s, :, piece].astype(jnp.float32)
                scaled = block * noise_ref[:, piece]
                weighted_ref[rows, piece] = scaled.astype(jnp.bfloat16)
                penalty = penalty + 0.5 * jnp.sum(scaled * block, axis=1, keepdims=True)
        penalty_ref[rows, :] = penalty


def take_blocks(refs, counts):
    return [[[refs.pop(0) for _ in range(n)] for n in group] for group in counts]


def block_counts(blocks):
    return [[len(part) for part in group] for group in blocks]


def flat(blocks):
    return [one for group in blocks for part in group for one in part]


def stage_kernel(near_count, counts, *refs):
    refs = list(refs)
    near_refs = [refs.pop(0) for _ in range(near_count)]
    groups = take_blocks(refs, counts)
    noise_ref, weighted_ref, penalty_ref, near_ref, noise_out_ref, block_ref, near_sems, sems = refs
    rows = near_refs[0].shape[0]
    copies = []
    for k, ref in enumerate(near_refs):
        copy = pltpu.make_async_copy(ref, near_ref.at[pl.ds(k * rows, rows), :], near_sems.at[k])
        copy.start()
        copies.append(copy)
    noise_out_ref[...] = noise_ref[...]
    weigh_blocks(groups, noise_ref, weighted_ref, penalty_ref, block_ref, sems, 0)
    for copy in copies:
        copy.wait()


def stage(blocks, near, noise):
    count = blocks[0][0][0].shape[0]
    parts = sum(len(group) for group in blocks)
    width = noise.shape[1]
    refs = len(blocks) * count
    moved = [*near, *flat(blocks)]
    return pl.pallas_call(
        partial(stage_kernel, len(near), block_counts(blocks)),
        out_shape=(
            jax.ShapeDtypeStruct((refs, width), jnp.bfloat16),
            jax.ShapeDtypeStruct((refs, 1), jnp.float32),
            jax.ShapeDtypeStruct((len(near) * near[0].shape[0], width), jnp.bfloat16),
            jax.ShapeDtypeStruct((1, width), jnp.float32),
        ),
        in_specs=[ANY_SPEC] * len(moved) + [VMEM_SPEC],
        out_specs=(VMEM_SPEC,) * 4,
        scratch_shapes=[
            pltpu.VMEM((len(blocks), count, width), jnp.bfloat16),
            pltpu.SemaphoreType.DMA((len(near),)),
            pltpu.SemaphoreType.DMA((parts,)),
        ],
        compiler_params=pltpu.CompilerParams(vmem_limit_bytes=SCORE_VMEM),
        cost_estimate=pl.CostEstimate(
            flops=8 * refs * width, bytes_accessed=12_000_000, transcendentals=0
        ),
        name="stage",
    )(*moved, noise)


def place_images(k, source, all_ref, sem):
    rows = source.shape[0]
    row = pl.multiple_of((lax.axis_index("reader") ^ k) * rows, 16)
    return pltpu.make_async_copy(source, all_ref.at[pl.ds(row, rows), :], sem), pl.ds(row, rows)


def stage_rest_kernel(readers, counts, *refs):
    refs = list(refs)
    groups = take_blocks(refs, counts)
    near_ref, far_ref, early_ref, early_penalty_ref, noise_ref = [refs.pop(0) for _ in range(5)]
    turned_ref, penalty_ref, all_ref, product_ref = refs[:4]
    weighted_ref, block_ref, sems, image_sems = refs[4:]
    rows = far_ref.shape[0]
    half = readers // 2
    sources = [near_ref.at[pl.ds(k * rows, rows), :] for k in range(half)] + [far_ref]
    placed = [place_images(k, one, all_ref, image_sems.at[k]) for k, one in enumerate(sources)]
    for copy, _ in placed:
        copy.start()
    done = early_ref.shape[0]
    weighted_ref[:done, :] = early_ref[...]
    penalty_ref[:done, :] = early_penalty_ref[...]
    first = done // block_ref.shape[1]
    weigh_blocks(groups, noise_ref, weighted_ref, penalty_ref, block_ref, sems, first)
    width = weighted_ref.shape[1]
    for start in range(0, width, STEP):
        piece = slice(start, min(start + STEP, width))
        turned_ref[piece, :] = weighted_ref[:, piece].T
    products = jnp.dot(near_ref[...], turned_ref[...], preferred_element_type=jnp.float32)
    for k in range(half):
        product_ref[placed[k][1], :] = products[k * rows : (k + 1) * rows]
    product_ref[placed[half][1], :] = jnp.dot(
        far_ref[...], turned_ref[...], preferred_element_type=jnp.float32
    )
    for copy, _ in placed:
        copy.wait()


def stage_rest(blocks, near, crossed, weighted, penalty, noise):
    count = blocks[0][0][0].shape[0]
    parts = sum(len(group) for group in blocks)
    width = noise.shape[1]
    refs = len(blocks) * count + weighted.shape[0]
    slots = 2 * near.shape[0]
    readers = slots // crossed.shape[0]
    moved = flat(blocks)
    return pl.pallas_call(
        partial(stage_rest_kernel, readers, block_counts(blocks)),
        out_shape=(
            jax.ShapeDtypeStruct((width, refs), jnp.bfloat16),
            jax.ShapeDtypeStruct((refs, 1), jnp.float32),
            jax.ShapeDtypeStruct((slots, width), jnp.bfloat16),
            jax.ShapeDtypeStruct((slots, refs), jnp.float32),
        ),
        in_specs=[ANY_SPEC] * len(moved) + [VMEM_SPEC] * 5,
        out_specs=(VMEM_SPEC,) * 4,
        scratch_shapes=[
            pltpu.VMEM((refs, width), jnp.bfloat16),
            pltpu.VMEM((len(blocks), count, width), jnp.bfloat16),
            pltpu.SemaphoreType.DMA((parts,)),
            pltpu.SemaphoreType.DMA((readers // 2 + 1,)),
        ],
        compiler_params=pltpu.CompilerParams(vmem_limit_bytes=SCORE_VMEM),
        cost_estimate=pl.CostEstimate(
            flops=8 * refs * width, bytes_accessed=12_000_000, transcendentals=0
        ),
        name="stage_rest",
    )(*moved, near, crossed, weighted, penalty, noise)


def write_packet(packet_ref, scores, route_ref):
    top, rows = route_ref.shape
    packet_ref[0:1, :] = column_lse(scores)
    packet_ref[1:2, :] = jnp.zeros((1, packet_ref.shape[1]), jnp.float32)
    for t in range(top):
        packet_ref[1:2, t * rows : (t + 1) * rows] = route_ref[t : t + 1, :].astype(jnp.float32)


def score_kernel(readers, finish, *refs):
    refs = list(refs)
    half = readers // 2
    far_refs = [refs.pop(0) for _ in range(half - 1)]
    turned_ref, penalty_ref, _, product_ref, route_ref = refs[:5]
    score_ref, packet_ref, all_ref, sum_ref, image_sems = refs[5:]
    placed = [
        place_images(half + 1 + i, ref, all_ref, image_sems.at[i])
        for i, ref in enumerate(far_refs)
    ]
    for copy, _ in placed:
        copy.start()
    sum_ref[...] = product_ref[...]
    for (_, place), ref in zip(placed, far_refs):
        sum_ref[place, :] = jnp.dot(
            ref[...], turned_ref[...], preferred_element_type=jnp.float32
        )
    scores = sum_ref[...].T - penalty_ref[...]
    score_ref[...] = scores
    if finish:
        write_packet(packet_ref, scores, route_ref)
    for copy, _ in placed:
        copy.wait()


def all_scores(staged, far, routes, finish):
    turned, penalty, images, products = staged
    width, refs = turned.shape
    slots, rows = images.shape[0], far[0].shape[0]
    return pl.pallas_call(
        partial(score_kernel, slots // rows, finish),
        out_shape=(
            jax.ShapeDtypeStruct((refs, slots), jnp.float32),
            jax.ShapeDtypeStruct((2, slots), jnp.float32),
            jax.ShapeDtypeStruct((slots, width), jnp.bfloat16),
        ),
        in_specs=[VMEM_SPEC] * (len(far) + 5),
        out_specs=(VMEM_SPEC,) * 3,
        scratch_shapes=[
            pltpu.VMEM((slots, refs), jnp.float32),
            pltpu.SemaphoreType.DMA((len(far),)),
        ],
        input_output_aliases={len(far) + 2: 2},
        compiler_params=pltpu.CompilerParams(vmem_limit_bytes=SCORE_VMEM),
        cost_estimate=pl.CostEstimate(
            flops=2 * refs * slots * width,
            bytes_accessed=2 * (slots + refs) * width,
            transcendentals=0,
        ),
        name="scores",
    )(*far, turned, penalty, images, products, routes)


def packet_kernel(score_ref, route_ref, packet_ref):
    write_packet(packet_ref, score_ref[...], route_ref)


def make_packet(scores, routes):
    return pl.pallas_call(
        packet_kernel,
        out_shape=jax.ShapeDtypeStruct((2, scores.shape[1]), jnp.float32),
        name="packet",
    )(scores, routes)


def write_routes(packets, rows, route_ref):
    reader = lax.axis_index("reader")
    readers = len(packets)
    for t in range(route_ref.shape[0]):
        routes = [ref[1:2, t * rows : (t + 1) * rows] for ref in packets]
        bit = 1
        while bit < readers:
            flip = (reader & bit) > 0
            routes = [jnp.where(flip, routes[k ^ bit], one) for k, one in enumerate(routes)]
            bit *= 2
        for j, route in enumerate(routes):
            route_ref[t : t + 1, j * rows : (j + 1) * rows] = route


def emit_sums(posterior, all_ref, piece, out_refs):
    sums = jnp.dot(posterior, all_ref[:, piece], preferred_element_type=jnp.float32)
    count = sums.shape[0] // len(out_refs)
    for s, out_ref in enumerate(out_refs):
        out_ref[...] = sums[s * count : (s + 1) * count].astype(out_ref.dtype)


def first_sums_kernel(readers, piece, all_ref, score_ref, *refs):
    refs = list(refs)
    packets = [refs.pop(0) for _ in range(readers)]
    route_ref = refs.pop()
    norm_ref, post_ref, *out_refs = refs
    write_routes(packets, packets[0].shape[1] // readers, route_ref)
    routes = route_ref[...]
    kept, mine = [], None
    for k, packet in enumerate(packets):
        group = (lax.axis_index("reader") ^ k).astype(jnp.float32)
        hits = jnp.where(routes == group, 1.0, 0.0)
        named = jnp.max(hits, axis=0, keepdims=True) > 0.0
        kept.append(jnp.where(named, packet[0:1, :], -jnp.inf))
        mine = named if k == 0 else mine
    highest = kept[0]
    for value in kept[1:]:
        highest = jnp.maximum(highest, value)
    spread = jnp.exp(kept[0] - highest)
    for value in kept[1:]:
        spread = spread + jnp.exp(value - highest)
    norm = highest + jnp.log(spread)
    norm_ref[...] = norm
    exponent = jnp.where(mine, score_ref[...] - norm, -jnp.inf)
    posterior = jnp.exp(exponent).astype(jnp.bfloat16)
    post_ref[...] = posterior
    emit_sums(posterior, all_ref, piece, out_refs)


def later_sums_kernel(piece, all_ref, post_ref, *out_refs):
    emit_sums(post_ref[...], all_ref, piece, out_refs)


def group_sums(kernel, piece, members, all_images, operands, extra, scratch=()):
    refs, slots = operands[0].shape
    width = piece.stop - piece.start
    block = jax.ShapeDtypeStruct((refs // members, width), jnp.bfloat16)
    outs = pl.pallas_call(
        kernel,
        out_shape=tuple(extra) + (block,) * members,
        in_specs=[VMEM_SPEC] * (1 + len(operands)),
        out_specs=(VMEM_SPEC,) * (len(extra) + members),
        scratch_shapes=scratch,
        compiler_params=pltpu.CompilerParams(vmem_limit_bytes=SUMS_VMEM),
        cost_estimate=pl.CostEstimate(
            flops=2 * refs * slots * width,
            bytes_accessed=2 * slots * width,
            transcendentals=0,
        ),
        name="sums",
    )(all_images, *operands)
    return outs[: len(extra)], outs[len(extra) :]


def on_device(images, routes, projections, noise_weights):
    readers = lax.axis_size("reader")
    members = lax.axis_size("blk")
    reader = lax.axis_index("reader")
    rows, width = images.shape
    noise = noise_weights.reshape(1, width)

    gather = staged_gather if members == 4 and rows % 32 == 0 and readers > 1 else plain_gather
    staged, far = gather(projections[0], images, noise, readers // 4, readers // 2)
    split = lax.axis_size("sub") > 1
    scores, mine, all_images = all_scores(staged, far, routes.T, not split)
    if split:
        scores = lax.psum(scores, "sub")
        mine = make_packet(scores, routes.T)
    packets = [mine] + [swap_bits(mine, "reader", k) for k in range(1, readers)]
    pieces = [slice(0, width // 2), slice(width // 2, width)]
    extra = (
        jax.ShapeDtypeStruct((1, scores.shape[1]), jnp.float32),
        jax.ShapeDtypeStruct(scores.shape, jnp.bfloat16),
    )
    (norms, posterior), first = group_sums(
        partial(first_sums_kernel, readers, pieces[0]),
        pieces[0],
        members,
        all_images,
        (scores, *packets),
        extra,
        (pltpu.VMEM((routes.shape[1], scores.shape[1]), jnp.float32),),
    )
    _, last = group_sums(
        partial(later_sums_kernel, pieces[1]), pieces[1], members, all_images, (posterior,), ()
    )
    parts = [first, last]
    scatter = pair_scatter if members == 4 else line_scatter
    total = scatter(parts, "blk")
    normalizer = lax.dynamic_slice(norms.reshape(-1), (reader * rows,), (rows,))
    return (total[None], normalizer)


def solution(mesh):
    return jax.shard_map(
        on_device,
        mesh=mesh,
        in_specs=(
            P(("parts", "blk", "reader"), "sub"),
            P(("parts", "blk", "reader"), None),
            P(("parts", "reader"), "blk", "sub"),
            P(("parts", "sub")),
        ),
        out_specs=(P(("parts", "reader"), "blk", "sub"), P(("parts", "blk", "reader"))),
        check_vma=False,
    )
```

```python
from functools import partial

import jax
import jax.numpy as jnp
from jax import lax
from jax.experimental import pallas as pl
from jax.experimental.pallas import tpu as pltpu
from jax.sharding import PartitionSpec as P

SCORE_VMEM = 20 * 1024 * 1024
SUMS_VMEM = 12 * 1024 * 1024
STEP = 1024
VMEM_SPEC = pl.BlockSpec(memory_space=pltpu.VMEM)
ANY_SPEC = pl.BlockSpec(memory_space=pl.ANY)
SIDES = [(0, 1), (1, 0), (2, 3), (3, 2)]
MIDDLE = [(1, 2), (2, 1)]
OUTWARD = [(1, 0), (2, 3)]


def swap_bits(block, axis, bits):
    return lax.ppermute(block, axis, [(i, i ^ bits) for i in range(lax.axis_size(axis))])


def swap_gather(block, axis, bit):
    held = {0: block}
    while bit:
        for k in list(held):
            held[k ^ bit] = swap_bits(held[k], axis, bit)
        bit //= 2
    return [held[k] for k in range(len(held))]


def add_rounded(one, other):
    return (one.astype(jnp.float32) + other.astype(jnp.float32)).astype(jnp.bfloat16)


def staged_gather(block, images, noise, near_bits, far_bit):
    cut = block.shape[1] // 16 * 9
    cuts = [block[:, :cut], block[:, cut:]]
    crossed = swap_bits(images, "reader", far_bit)
    near = swap_gather(images, "reader", near_bits)
    firsts = [
        lax.optimization_barrier(
            (lax.ppermute(one, "blk", SIDES), lax.ppermute(one, "blk", MIDDLE))
        )
        for one in cuts
    ]
    early = stage(
        [[[one] for one in cuts], [[side] for side, _ in firsts]], near, noise
    )
    far_parts, end_parts = [], []
    for last, (side, across) in enumerate(firsts):
        far = lax.ppermute(across, "blk", SIDES)
        side, *_ = lax.optimization_barrier((side, *near))
        across_far = lax.ppermute(side, "blk", MIDDLE)
        if last:
            far, across_far, *early = lax.optimization_barrier((far, across_far, *early))
        else:
            far, across_far = lax.optimization_barrier((far, across_far))
        end = lax.ppermute(across_far, "blk", OUTWARD)
        far_parts.append([far, across_far])
        end_parts.append([end, across])
    weighted, penalty, staged_near, noise = early
    ends = [parts[0] for parts in end_parts]
    crossed, *_ = lax.optimization_barrier((crossed, *ends))
    far = swap_gather(crossed, "reader", near_bits)
    staged = stage_rest([far_parts, end_parts], staged_near, crossed, weighted, penalty, noise)
    return staged, far[1:]


def plain_gather(block, images, noise, near_bits, far_bit):
    near = swap_gather(images, "reader", near_bits)
    far = swap_gather(swap_bits(images, "reader", far_bit), "reader", near_bits)
    line = [[[one]] for one in line_gather(block, "blk")]
    weighted, penalty, near, noise = stage(line[:2], near, noise)
    staged = stage_rest(line[2:], near, far[0], weighted, penalty, noise)
    return staged, far[1:]


def line_gather(block, axis):
    size, member = lax.axis_size(axis), lax.axis_index(axis)
    ahead, behind = [block], [block]
    for s in range(1, size):
        ahead.append(lax.ppermute(ahead[-1], axis, [(i, i + 1) for i in range(s - 1, size - 1)]))
        behind.append(lax.ppermute(behind[-1], axis, [(i, i - 1) for i in range(1, size - s + 1)]))
    blocks = [block]
    for s in range(1, size):
        blocks.append(jnp.where(member >= s, ahead[s], behind[size - s]))
    return blocks


def pair_scatter(pieces, axis):
    member = lax.axis_index(axis)
    is_end = (member == 0) | (member == 3)
    for_far_end = [lax.ppermute(parts[3], axis, SIDES) for parts in pieces]
    *second, for_far_end[0] = lax.optimization_barrier(
        [parts[2] for parts in pieces] + for_far_end[:1]
    )
    for_far_middle = [lax.ppermute(part, axis, SIDES) for part in second]
    totals = []
    for parts, part, end, middle in zip(pieces, second, for_far_end, for_far_middle):
        across_end = lax.ppermute(add_rounded(part, end), axis, MIDDLE)
        across_middle = lax.ppermute(add_rounded(parts[3], middle), axis, MIDDLE)
        near = jnp.where(is_end, parts[1], add_rounded(parts[1], across_end))
        from_side = lax.ppermute(near, axis, SIDES)
        total = parts[0].astype(jnp.float32) + from_side.astype(jnp.float32)
        totals.append(total + jnp.where(is_end, 0.0, across_middle.astype(jnp.float32)))
    return beside(totals)


def beside_kernel(count, *refs):
    out_ref, sems = refs[count:]
    copies, stop = [], out_ref.shape[1]
    for i, ref in enumerate(refs[:count]):
        start = stop - ref.shape[1]
        for j, row in enumerate(range(0, ref.shape[0], 8)):
            rows = slice(row, row + 8)
            copies.append(
                pltpu.make_async_copy(ref.at[rows], out_ref.at[rows, start:stop], sems.at[i, j])
            )
            copies[-1].start()
        stop = start
    for copy in copies:
        copy.wait()


def beside(pieces):
    width = sum(piece.shape[1] for piece in pieces)
    return pl.pallas_call(
        partial(beside_kernel, len(pieces)),
        out_shape=jax.ShapeDtypeStruct((pieces[0].shape[0], width), pieces[0].dtype),
        in_specs=[VMEM_SPEC] * len(pieces),
        out_specs=ANY_SPEC,
        scratch_shapes=[pltpu.SemaphoreType.DMA((len(pieces), pieces[0].shape[0] // 8))],
        compiler_params=pltpu.CompilerParams(vmem_limit_bytes=SUMS_VMEM),
        name="beside",
    )(*pieces[::-1])


def line_scatter(pieces, axis):
    return jnp.concatenate([line_sum(parts, axis) for parts in pieces], axis=1)


def line_sum(parts, axis):
    size = lax.axis_size(axis)
    up = down = None
    for s in range(1, size):
        send_up, send_down = parts[s], parts[size - s]
        if s > 1:
            send_up = add_rounded(send_up, up)
            send_down = add_rounded(send_down, down)
        up = lax.ppermute(send_up, axis, [(i, i + 1) for i in range(0, s) if i + 1 < size])
        down = lax.ppermute(send_down, axis, [(i, i - 1) for i in range(size - s, size) if i > 0])
    total = parts[0].astype(jnp.float32)
    if size > 1:
        total = total + up.astype(jnp.float32) + down.astype(jnp.float32)
    return total


def column_lse(scores):
    peak = jnp.max(scores, axis=0, keepdims=True)
    total = jnp.sum(jnp.exp(scores - peak), axis=0, keepdims=True)
    return peak + jnp.log(total)


def at_end():
    member = lax.axis_index("blk")
    return (member == 0) | (member == lax.axis_size("blk") - 1)


def either(refs, act):
    if len(refs) == 1:
        act(refs[0])
        return
    is_end = at_end()

    @pl.when(is_end)
    def _():
        act(refs[0])

    @pl.when(jnp.logical_not(is_end))
    def _():
        act(refs[1])


def weigh_blocks(groups, noise_ref, weighted_ref, penalty_ref, block_ref, sems, first):
    count = block_ref.shape[1]
    parts = []
    for s, group in enumerate(groups):
        start = 0
        for refs in group:
            stop = start + refs[0].shape[1]
            parts.append((s, slice(start, stop), refs))
            start = stop

    def part_copy(i, ref):
        s, columns, _ = parts[i]
        return pltpu.make_async_copy(ref, block_ref.at[s, :, columns], sems.at[i])

    for i, (_, _, refs) in enumerate(parts):
        either(refs, lambda ref, i=i: part_copy(i, ref).start())
    for s in range(len(groups)):
        rows = slice((first + s) * count, (first + s + 1) * count)
        penalty = jnp.zeros((count, 1), jnp.float32)
        for i, (t, columns, refs) in enumerate(parts):
            if t != s:
                continue
            part_copy(i, refs[0]).wait()
            for start in range(columns.start, columns.stop, STEP):
                piece = slice(start, min(start + STEP, columns.stop))
                block = block_ref[s, :, piece].astype(jnp.float32)
                scaled = block * noise_ref[:, piece]
                weighted_ref[rows, piece] = scaled.astype(jnp.bfloat16)
                penalty = penalty + 0.5 * jnp.sum(scaled * block, axis=1, keepdims=True)
        penalty_ref[rows, :] = penalty


def take_blocks(refs, counts):
    return [[[refs.pop(0) for _ in range(n)] for n in group] for group in counts]


def block_counts(blocks):
    return [[len(part) for part in group] for group in blocks]


def flat(blocks):
    return [one for group in blocks for part in group for one in part]


def stage_kernel(near_count, counts, *refs):
    refs = list(refs)
    near_refs = [refs.pop(0) for _ in range(near_count)]
    groups = take_blocks(refs, counts)
    noise_ref, weighted_ref, penalty_ref, near_ref, noise_out_ref, block_ref, near_sems, sems = refs
    rows = near_refs[0].shape[0]
    copies = []
    for k, ref in enumerate(near_refs):
        copy = pltpu.make_async_copy(ref, near_ref.at[pl.ds(k * rows, rows), :], near_sems.at[k])
        copy.start()
        copies.append(copy)
    noise_out_ref[...] = noise_ref[...]
    weigh_blocks(groups, noise_ref, weighted_ref, penalty_ref, block_ref, sems, 0)
    for copy in copies:
        copy.wait()


def stage(blocks, near, noise):
    count = blocks[0][0][0].shape[0]
    parts = sum(len(group) for group in blocks)
    width = noise.shape[1]
    refs = len(blocks) * count
    moved = [*near, *flat(blocks)]
    return pl.pallas_call(
        partial(stage_kernel, len(near), block_counts(blocks)),
        out_shape=(
            jax.ShapeDtypeStruct((refs, width), jnp.bfloat16),
            jax.ShapeDtypeStruct((refs, 1), jnp.float32),
            jax.ShapeDtypeStruct((len(near) * near[0].shape[0], width), jnp.bfloat16),
            jax.ShapeDtypeStruct((1, width), jnp.float32),
        ),
        in_specs=[ANY_SPEC] * len(moved) + [VMEM_SPEC],
        out_specs=(VMEM_SPEC,) * 4,
        scratch_shapes=[
            pltpu.VMEM((len(blocks), count, width), jnp.bfloat16),
            pltpu.SemaphoreType.DMA((len(near),)),
            pltpu.SemaphoreType.DMA((parts,)),
        ],
        compiler_params=pltpu.CompilerParams(vmem_limit_bytes=SCORE_VMEM),
        cost_estimate=pl.CostEstimate(
            flops=8 * refs * width, bytes_accessed=12_000_000, transcendentals=0
        ),
        name="stage",
    )(*moved, noise)


def place_images(k, source, all_ref, sem):
    rows = source.shape[0]
    row = pl.multiple_of((lax.axis_index("reader") ^ k) * rows, 16)
    return pltpu.make_async_copy(source, all_ref.at[pl.ds(row, rows), :], sem), pl.ds(row, rows)


def stage_rest_kernel(readers, counts, *refs):
    refs = list(refs)
    groups = take_blocks(refs, counts)
    near_ref, far_ref, early_ref, early_penalty_ref, noise_ref = [refs.pop(0) for _ in range(5)]
    turned_ref, penalty_ref, all_ref, product_ref = refs[:4]
    weighted_ref, block_ref, sems, image_sems = refs[4:]
    rows = far_ref.shape[0]
    half = readers // 2
    sources = [near_ref.at[pl.ds(k * rows, rows), :] for k in range(half)] + [far_ref]
    placed = [place_images(k, one, all_ref, image_sems.at[k]) for k, one in enumerate(sources)]
    for copy, _ in placed:
        copy.start()
    done = early_ref.shape[0]
    weighted_ref[:done, :] = early_ref[...]
    penalty_ref[:done, :] = early_penalty_ref[...]
    first = done // block_ref.shape[1]
    weigh_blocks(groups, noise_ref, weighted_ref, penalty_ref, block_ref, sems, first)
    width = weighted_ref.shape[1]
    for start in range(0, width, STEP):
        piece = slice(start, min(start + STEP, width))
        turned_ref[piece, :] = weighted_ref[:, piece].T
    products = jnp.dot(near_ref[...], turned_ref[...], preferred_element_type=jnp.float32)
    for k in range(half):
        product_ref[placed[k][1], :] = products[k * rows : (k + 1) * rows]
    product_ref[placed[half][1], :] = jnp.dot(
        far_ref[...], turned_ref[...], preferred_element_type=jnp.float32
    )
    for copy, _ in placed:
        copy.wait()


def stage_rest(blocks, near, crossed, weighted, penalty, noise):
    count = blocks[0][0][0].shape[0]
    parts = sum(len(group) for group in blocks)
    width = noise.shape[1]
    refs = len(blocks) * count + weighted.shape[0]
    slots = 2 * near.shape[0]
    readers = slots // crossed.shape[0]
    moved = flat(blocks)
    return pl.pallas_call(
        partial(stage_rest_kernel, readers, block_counts(blocks)),
        out_shape=(
            jax.ShapeDtypeStruct((width, refs), jnp.bfloat16),
            jax.ShapeDtypeStruct((refs, 1), jnp.float32),
            jax.ShapeDtypeStruct((slots, width), jnp.bfloat16),
            jax.ShapeDtypeStruct((slots, refs), jnp.float32),
        ),
        in_specs=[ANY_SPEC] * len(moved) + [VMEM_SPEC] * 5,
        out_specs=(VMEM_SPEC,) * 4,
        scratch_shapes=[
            pltpu.VMEM((refs, width), jnp.bfloat16),
            pltpu.VMEM((len(blocks), count, width), jnp.bfloat16),
            pltpu.SemaphoreType.DMA((parts,)),
            pltpu.SemaphoreType.DMA((readers // 2 + 1,)),
        ],
        compiler_params=pltpu.CompilerParams(vmem_limit_bytes=SCORE_VMEM),
        cost_estimate=pl.CostEstimate(
            flops=8 * refs * width, bytes_accessed=12_000_000, transcendentals=0
        ),
        name="stage_rest",
    )(*moved, near, crossed, weighted, penalty, noise)


def write_packet(packet_ref, scores, route_ref):
    top, rows = route_ref.shape
    packet_ref[0:1, :] = column_lse(scores)
    packet_ref[1:2, :] = jnp.zeros((1, packet_ref.shape[1]), jnp.float32)
    for t in range(top):
        packet_ref[1:2, t * rows : (t + 1) * rows] = route_ref[t : t + 1, :].astype(jnp.float32)


def score_kernel(readers, finish, *refs):
    refs = list(refs)
    half = readers // 2
    far_refs = [refs.pop(0) for _ in range(half - 1)]
    turned_ref, penalty_ref, _, product_ref, route_ref = refs[:5]
    score_ref, packet_ref, all_ref, sum_ref, image_sems = refs[5:]
    placed = [
        place_images(half + 1 + i, ref, all_ref, image_sems.at[i])
        for i, ref in enumerate(far_refs)
    ]
    for copy, _ in placed:
        copy.start()
    sum_ref[...] = product_ref[...]
    for (_, place), ref in zip(placed, far_refs):
        sum_ref[place, :] = jnp.dot(
            ref[...], turned_ref[...], preferred_element_type=jnp.float32
        )
    scores = sum_ref[...].T - penalty_ref[...]
    score_ref[...] = scores
    if finish:
        write_packet(packet_ref, scores, route_ref)
    for copy, _ in placed:
        copy.wait()


def all_scores(staged, far, routes, finish):
    turned, penalty, images, products = staged
    width, refs = turned.shape
    slots, rows = images.shape[0], far[0].shape[0]
    return pl.pallas_call(
        partial(score_kernel, slots // rows, finish),
        out_shape=(
            jax.ShapeDtypeStruct((refs, slots), jnp.float32),
            jax.ShapeDtypeStruct((2, slots), jnp.float32),
            jax.ShapeDtypeStruct((slots, width), jnp.bfloat16),
        ),
        in_specs=[VMEM_SPEC] * (len(far) + 5),
        out_specs=(VMEM_SPEC,) * 3,
        scratch_shapes=[
            pltpu.VMEM((slots, refs), jnp.float32),
            pltpu.SemaphoreType.DMA((len(far),)),
        ],
        input_output_aliases={len(far) + 2: 2},
        compiler_params=pltpu.CompilerParams(vmem_limit_bytes=SCORE_VMEM),
        cost_estimate=pl.CostEstimate(
            flops=2 * refs * slots * width,
            bytes_accessed=2 * (slots + refs) * width,
            transcendentals=0,
        ),
        name="scores",
    )(*far, turned, penalty, images, products, routes)


def packet_kernel(score_ref, route_ref, packet_ref):
    write_packet(packet_ref, score_ref[...], route_ref)


def make_packet(scores, routes):
    return pl.pallas_call(
        packet_kernel,
        out_shape=jax.ShapeDtypeStruct((2, scores.shape[1]), jnp.float32),
        name="packet",
    )(scores, routes)


def write_routes(packets, rows, route_ref):
    reader = lax.axis_index("reader")
    readers = len(packets)
    for t in range(route_ref.shape[0]):
        routes = [ref[1:2, t * rows : (t + 1) * rows] for ref in packets]
        bit = 1
        while bit < readers:
            flip = (reader & bit) > 0
            routes = [jnp.where(flip, routes[k ^ bit], one) for k, one in enumerate(routes)]
            bit *= 2
        for j, route in enumerate(routes):
            route_ref[t : t + 1, j * rows : (j + 1) * rows] = route


def emit_sums(posterior, all_ref, piece, out_refs):
    sums = jnp.dot(posterior, all_ref[:, piece], preferred_element_type=jnp.float32)
    count = sums.shape[0] // len(out_refs)
    for s, out_ref in enumerate(out_refs):
        out_ref[...] = sums[s * count : (s + 1) * count].astype(out_ref.dtype)


def first_sums_kernel(readers, piece, all_ref, score_ref, *refs):
    refs = list(refs)
    packets = [refs.pop(0) for _ in range(readers)]
    route_ref = refs.pop()
    norm_ref, post_ref, *out_refs = refs
    write_routes(packets, packets[0].shape[1] // readers, route_ref)
    routes = route_ref[...]
    kept, mine = [], None
    for k, packet in enumerate(packets):
        group = (lax.axis_index("reader") ^ k).astype(jnp.float32)
        hits = jnp.where(routes == group, 1.0, 0.0)
        named = jnp.max(hits, axis=0, keepdims=True) > 0.0
        kept.append(jnp.where(named, packet[0:1, :], -jnp.inf))
        mine = named if k == 0 else mine
    highest = kept[0]
    for value in kept[1:]:
        highest = jnp.maximum(highest, value)
    spread = jnp.exp(kept[0] - highest)
    for value in kept[1:]:
        spread = spread + jnp.exp(value - highest)
    norm = highest + jnp.log(spread)
    norm_ref[...] = norm
    exponent = jnp.where(mine, score_ref[...] - norm, -jnp.inf)
    posterior = jnp.exp(exponent).astype(jnp.bfloat16)
    post_ref[...] = posterior
    emit_sums(posterior, all_ref, piece, out_refs)


def later_sums_kernel(piece, all_ref, post_ref, *out_refs):
    emit_sums(post_ref[...], all_ref, piece, out_refs)


def group_sums(kernel, piece, members, all_images, operands, extra, scratch=()):
    refs, slots = operands[0].shape
    width = piece.stop - piece.start
    block = jax.ShapeDtypeStruct((refs // members, width), jnp.bfloat16)
    outs = pl.pallas_call(
        kernel,
        out_shape=tuple(extra) + (block,) * members,
        in_specs=[VMEM_SPEC] * (1 + len(operands)),
        out_specs=(VMEM_SPEC,) * (len(extra) + members),
        scratch_shapes=scratch,
        compiler_params=pltpu.CompilerParams(vmem_limit_bytes=SUMS_VMEM),
        cost_estimate=pl.CostEstimate(
            flops=2 * refs * slots * width,
            bytes_accessed=2 * slots * width,
            transcendentals=0,
        ),
        name="sums",
    )(all_images, *operands)
    return outs[: len(extra)], outs[len(extra) :]


def on_device(images, routes, projections, noise_weights):
    readers = lax.axis_size("reader")
    members = lax.axis_size("blk")
    reader = lax.axis_index("reader")
    rows, width = images.shape
    noise = noise_weights.reshape(1, width)

    gather = staged_gather if members == 4 and rows % 32 == 0 and readers > 1 else plain_gather
    staged, far = gather(projections[0], images, noise, readers // 4, readers // 2)
    split = lax.axis_size("sub") > 1
    scores, mine, all_images = all_scores(staged, far, routes.T, not split)
    if split:
        scores = lax.psum(scores, "sub")
        mine = make_packet(scores, routes.T)
    packets = [mine] + [swap_bits(mine, "reader", k) for k in range(1, readers)]
    pieces = [slice(0, width // 2), slice(width // 2, width)]
    extra = (
        jax.ShapeDtypeStruct((1, scores.shape[1]), jnp.float32),
        jax.ShapeDtypeStruct(scores.shape, jnp.bfloat16),
    )
    (norms, posterior), first = group_sums(
        partial(first_sums_kernel, readers, pieces[0]),
        pieces[0],
        members,
        all_images,
        (scores, *packets),
        extra,
        (pltpu.VMEM((routes.shape[1], scores.shape[1]), jnp.float32),),
    )
    _, last = group_sums(
        partial(later_sums_kernel, pieces[1]), pieces[1], members, all_images, (posterior,), ()
    )
    parts = [first, last]
    scatter = pair_scatter if members == 4 else line_scatter
    total = scatter(parts, "blk")
    normalizer = lax.dynamic_slice(norms.reshape(-1), (reader * rows,), (rows,))
    return (total[None], normalizer)


def solution(mesh):
    return jax.shard_map(
        on_device,
        mesh=mesh,
        in_specs=(
            P(("parts", "blk", "reader"), "sub"),
            P(("parts", "blk", "reader"), None),
            P(("parts", "reader"), "blk", "sub"),
            P(("parts", "sub")),
        ),
        out_specs=(P(("parts", "reader"), "blk", "sub"), P(("parts", "blk", "reader"))),
        check_vma=False,
    )
```

```python
from functools import partial

import jax
import jax.numpy as jnp
from jax import lax
from jax.experimental import pallas as pl
from jax.experimental.pallas import tpu as pltpu
from jax.sharding import PartitionSpec as P

SCORE_VMEM = 20 * 1024 * 1024
SUMS_VMEM = 12 * 1024 * 1024
STEP = 1024
VMEM_SPEC = pl.BlockSpec(memory_space=pltpu.VMEM)
ANY_SPEC = pl.BlockSpec(memory_space=pl.ANY)
SIDES = [(0, 1), (1, 0), (2, 3), (3, 2)]
MIDDLE = [(1, 2), (2, 1)]
OUTWARD = [(1, 0), (2, 3)]


def swap_bits(block, axis, bits):
    return lax.ppermute(block, axis, [(i, i ^ bits) for i in range(lax.axis_size(axis))])


def swap_gather(block, axis, bit):
    held = {0: block}
    while bit:
        for k in list(held):
            held[k ^ bit] = swap_bits(held[k], axis, bit)
        bit //= 2
    return [held[k] for k in range(len(held))]


def add_rounded(one, other):
    return (one.astype(jnp.float32) + other.astype(jnp.float32)).astype(jnp.bfloat16)


def staged_gather(block, images, noise, near_bits, far_bit):
    cut = block.shape[1] // 16 * 9
    cuts = [block[:, :cut], block[:, cut:]]
    crossed = swap_bits(images, "reader", far_bit)
    near = swap_gather(images, "reader", near_bits)
    firsts = [
        lax.optimization_barrier(
            (lax.ppermute(one, "blk", SIDES), lax.ppermute(one, "blk", MIDDLE))
        )
        for one in cuts
    ]
    early = stage(
        [[[one] for one in cuts], [[side] for side, _ in firsts]], near, noise
    )
    far_parts, end_parts = [], []
    for last, (side, across) in enumerate(firsts):
        far = lax.ppermute(across, "blk", SIDES)
        side, *_ = lax.optimization_barrier((side, *near))
        across_far = lax.ppermute(side, "blk", MIDDLE)
        if last:
            far, across_far, *early = lax.optimization_barrier((far, across_far, *early))
        else:
            far, across_far = lax.optimization_barrier((far, across_far))
        end = lax.ppermute(across_far, "blk", OUTWARD if last else SIDES)
        far_parts.append([far, across_far])
        end_parts.append([end, across])
    weighted, penalty, staged_near, noise = early
    ends = [parts[0] for parts in end_parts]
    crossed, *_ = lax.optimization_barrier((crossed, *ends))
    far = swap_gather(crossed, "reader", near_bits)
    staged = stage_rest([far_parts, end_parts], staged_near, crossed, weighted, penalty, noise)
    return staged, far[1:]


def plain_gather(block, images, noise, near_bits, far_bit):
    near = swap_gather(images, "reader", near_bits)
    far = swap_gather(swap_bits(images, "reader", far_bit), "reader", near_bits)
    line = [[[one]] for one in line_gather(block, "blk")]
    weighted, penalty, near, noise = stage(line[:2], near, noise)
    staged = stage_rest(line[2:], near, far[0], weighted, penalty, noise)
    return staged, far[1:]


def line_gather(block, axis):
    size, member = lax.axis_size(axis), lax.axis_index(axis)
    ahead, behind = [block], [block]
    for s in range(1, size):
        ahead.append(lax.ppermute(ahead[-1], axis, [(i, i + 1) for i in range(s - 1, size - 1)]))
        behind.append(lax.ppermute(behind[-1], axis, [(i, i - 1) for i in range(1, size - s + 1)]))
    blocks = [block]
    for s in range(1, size):
        blocks.append(jnp.where(member >= s, ahead[s], behind[size - s]))
    return blocks


def pair_scatter(pieces, axis):
    member = lax.axis_index(axis)
    is_end = (member == 0) | (member == 3)
    for_far_end = [lax.ppermute(parts[3], axis, SIDES) for parts in pieces]
    *second, for_far_end[0] = lax.optimization_barrier(
        [parts[2] for parts in pieces] + for_far_end[:1]
    )
    for_far_middle = [lax.ppermute(part, axis, SIDES) for part in second]
    totals = []
    for parts, part, end, middle in zip(pieces, second, for_far_end, for_far_middle):
        across_end = lax.ppermute(add_rounded(part, end), axis, MIDDLE)
        across_middle = lax.ppermute(add_rounded(parts[3], middle), axis, MIDDLE)
        near = jnp.where(is_end, parts[1], add_rounded(parts[1], across_end))
        from_side = lax.ppermute(near, axis, SIDES)
        total = parts[0].astype(jnp.float32) + from_side.astype(jnp.float32)
        totals.append(total + jnp.where(is_end, 0.0, across_middle.astype(jnp.float32)))
    return beside(totals)


def beside_kernel(count, *refs):
    out_ref, sems = refs[count:]
    copies, stop = [], out_ref.shape[1]
    for i, ref in enumerate(refs[:count]):
        start = stop - ref.shape[1]
        copies.append(pltpu.make_async_copy(ref, out_ref.at[:, start:stop], sems.at[i]))
        copies[-1].start()
        stop = start
    for copy in copies:
        copy.wait()


def beside(pieces):
    width = sum(piece.shape[1] for piece in pieces)
    return pl.pallas_call(
        partial(beside_kernel, len(pieces)),
        out_shape=jax.ShapeDtypeStruct((pieces[0].shape[0], width), pieces[0].dtype),
        in_specs=[VMEM_SPEC] * len(pieces),
        out_specs=ANY_SPEC,
        scratch_shapes=[pltpu.SemaphoreType.DMA((len(pieces),))],
        compiler_params=pltpu.CompilerParams(vmem_limit_bytes=SUMS_VMEM),
        name="beside",
    )(*pieces[::-1])


def line_scatter(pieces, axis):
    return jnp.concatenate([line_sum(parts, axis) for parts in pieces], axis=1)


def line_sum(parts, axis):
    size = lax.axis_size(axis)
    up = down = None
    for s in range(1, size):
        send_up, send_down = parts[s], parts[size - s]
        if s > 1:
            send_up = add_rounded(send_up, up)
            send_down = add_rounded(send_down, down)
        up = lax.ppermute(send_up, axis, [(i, i + 1) for i in range(0, s) if i + 1 < size])
        down = lax.ppermute(send_down, axis, [(i, i - 1) for i in range(size - s, size) if i > 0])
    total = parts[0].astype(jnp.float32)
    if size > 1:
        total = total + up.astype(jnp.float32) + down.astype(jnp.float32)
    return total


def column_lse(scores):
    peak = jnp.max(scores, axis=0, keepdims=True)
    total = jnp.sum(jnp.exp(scores - peak), axis=0, keepdims=True)
    return peak + jnp.log(total)


def at_end():
    member = lax.axis_index("blk")
    return (member == 0) | (member == lax.axis_size("blk") - 1)


def either(refs, act):
    if len(refs) == 1:
        act(refs[0])
        return
    is_end = at_end()

    @pl.when(is_end)
    def _():
        act(refs[0])

    @pl.when(jnp.logical_not(is_end))
    def _():
        act(refs[1])


def weigh_blocks(groups, noise_ref, weighted_ref, penalty_ref, block_ref, sems, first):
    count = block_ref.shape[1]
    parts = []
    for s, group in enumerate(groups):
        start = 0
        for refs in group:
            stop = start + refs[0].shape[1]
            parts.append((s, slice(start, stop), refs))
            start = stop

    def part_copy(i, ref):
        s, columns, _ = parts[i]
        return pltpu.make_async_copy(ref, block_ref.at[s, :, columns], sems.at[i])

    for i, (_, _, refs) in enumerate(parts):
        either(refs, lambda ref, i=i: part_copy(i, ref).start())
    for s in range(len(groups)):
        rows = slice((first + s) * count, (first + s + 1) * count)
        penalty = jnp.zeros((count, 1), jnp.float32)
        for i, (t, columns, refs) in enumerate(parts):
            if t != s:
                continue
            part_copy(i, refs[0]).wait()
            for start in range(columns.start, columns.stop, STEP):
                piece = slice(start, min(start + STEP, columns.stop))
                block = block_ref[s, :, piece].astype(jnp.float32)
                scaled = block * noise_ref[:, piece]
                weighted_ref[rows, piece] = scaled.astype(jnp.bfloat16)
                penalty = penalty + 0.5 * jnp.sum(scaled * block, axis=1, keepdims=True)
        penalty_ref[rows, :] = penalty


def take_blocks(refs, counts):
    return [[[refs.pop(0) for _ in range(n)] for n in group] for group in counts]


def block_counts(blocks):
    return [[len(part) for part in group] for group in blocks]


def flat(blocks):
    return [one for group in blocks for part in group for one in part]


def stage_kernel(near_count, counts, *refs):
    refs = list(refs)
    near_refs = [refs.pop(0) for _ in range(near_count)]
    groups = take_blocks(refs, counts)
    noise_ref, weighted_ref, penalty_ref, near_ref, noise_out_ref, block_ref, near_sems, sems = refs
    rows = near_refs[0].shape[0]
    copies = []
    for k, ref in enumerate(near_refs):
        copy = pltpu.make_async_copy(ref, near_ref.at[pl.ds(k * rows, rows), :], near_sems.at[k])
        copy.start()
        copies.append(copy)
    noise_out_ref[...] = noise_ref[...]
    weigh_blocks(groups, noise_ref, weighted_ref, penalty_ref, block_ref, sems, 0)
    for copy in copies:
        copy.wait()


def stage(blocks, near, noise):
    count = blocks[0][0][0].shape[0]
    parts = sum(len(group) for group in blocks)
    width = noise.shape[1]
    refs = len(blocks) * count
    moved = [*near, *flat(blocks)]
    return pl.pallas_call(
        partial(stage_kernel, len(near), block_counts(blocks)),
        out_shape=(
            jax.ShapeDtypeStruct((refs, width), jnp.bfloat16),
            jax.ShapeDtypeStruct((refs, 1), jnp.float32),
            jax.ShapeDtypeStruct((len(near) * near[0].shape[0], width), jnp.bfloat16),
            jax.ShapeDtypeStruct((1, width), jnp.float32),
        ),
        in_specs=[ANY_SPEC] * len(moved) + [VMEM_SPEC],
        out_specs=(VMEM_SPEC,) * 4,
        scratch_shapes=[
            pltpu.VMEM((len(blocks), count, width), jnp.bfloat16),
            pltpu.SemaphoreType.DMA((len(near),)),
            pltpu.SemaphoreType.DMA((parts,)),
        ],
        compiler_params=pltpu.CompilerParams(vmem_limit_bytes=SCORE_VMEM),
        cost_estimate=pl.CostEstimate(
            flops=8 * refs * width, bytes_accessed=12_000_000, transcendentals=0
        ),
        name="stage",
    )(*moved, noise)


def place_images(k, source, all_ref, sem):
    rows = source.shape[0]
    row = pl.multiple_of((lax.axis_index("reader") ^ k) * rows, 16)
    return pltpu.make_async_copy(source, all_ref.at[pl.ds(row, rows), :], sem), pl.ds(row, rows)


def stage_rest_kernel(readers, counts, *refs):
    refs = list(refs)
    groups = take_blocks(refs, counts)
    near_ref, far_ref, early_ref, early_penalty_ref, noise_ref = [refs.pop(0) for _ in range(5)]
    turned_ref, penalty_ref, all_ref, product_ref = refs[:4]
    weighted_ref, block_ref, sems, image_sems = refs[4:]
    rows = far_ref.shape[0]
    half = readers // 2
    sources = [near_ref.at[pl.ds(k * rows, rows), :] for k in range(half)] + [far_ref]
    placed = [place_images(k, one, all_ref, image_sems.at[k]) for k, one in enumerate(sources)]
    for copy, _ in placed:
        copy.start()
    done = early_ref.shape[0]
    weighted_ref[:done, :] = early_ref[...]
    penalty_ref[:done, :] = early_penalty_ref[...]
    first = done // block_ref.shape[1]
    weigh_blocks(groups, noise_ref, weighted_ref, penalty_ref, block_ref, sems, first)
    width = weighted_ref.shape[1]
    for start in range(0, width, STEP):
        piece = slice(start, min(start + STEP, width))
        turned_ref[piece, :] = weighted_ref[:, piece].T
    products = jnp.dot(near_ref[...], turned_ref[...], preferred_element_type=jnp.float32)
    for k in range(half):
        product_ref[placed[k][1], :] = products[k * rows : (k + 1) * rows]
    product_ref[placed[half][1], :] = jnp.dot(
        far_ref[...], turned_ref[...], preferred_element_type=jnp.float32
    )
    for copy, _ in placed:
        copy.wait()


def stage_rest(blocks, near, crossed, weighted, penalty, noise):
    count = blocks[0][0][0].shape[0]
    parts = sum(len(group) for group in blocks)
    width = noise.shape[1]
    refs = len(blocks) * count + weighted.shape[0]
    slots = 2 * near.shape[0]
    readers = slots // crossed.shape[0]
    moved = flat(blocks)
    return pl.pallas_call(
        partial(stage_rest_kernel, readers, block_counts(blocks)),
        out_shape=(
            jax.ShapeDtypeStruct((width, refs), jnp.bfloat16),
            jax.ShapeDtypeStruct((refs, 1), jnp.float32),
            jax.ShapeDtypeStruct((slots, width), jnp.bfloat16),
            jax.ShapeDtypeStruct((slots, refs), jnp.float32),
        ),
        in_specs=[ANY_SPEC] * len(moved) + [VMEM_SPEC] * 5,
        out_specs=(VMEM_SPEC,) * 4,
        scratch_shapes=[
            pltpu.VMEM((refs, width), jnp.bfloat16),
            pltpu.VMEM((len(blocks), count, width), jnp.bfloat16),
            pltpu.SemaphoreType.DMA((parts,)),
            pltpu.SemaphoreType.DMA((readers // 2 + 1,)),
        ],
        compiler_params=pltpu.CompilerParams(vmem_limit_bytes=SCORE_VMEM),
        cost_estimate=pl.CostEstimate(
            flops=8 * refs * width, bytes_accessed=12_000_000, transcendentals=0
        ),
        name="stage_rest",
    )(*moved, near, crossed, weighted, penalty, noise)


def write_packet(packet_ref, scores, route_ref):
    top, rows = route_ref.shape
    packet_ref[0:1, :] = column_lse(scores)
    packet_ref[1:2, :] = jnp.zeros((1, packet_ref.shape[1]), jnp.float32)
    for t in range(top):
        packet_ref[1:2, t * rows : (t + 1) * rows] = route_ref[t : t + 1, :].astype(jnp.float32)


def score_kernel(readers, finish, *refs):
    refs = list(refs)
    half = readers // 2
    far_refs = [refs.pop(0) for _ in range(half - 1)]
    turned_ref, penalty_ref, _, product_ref, route_ref = refs[:5]
    score_ref, packet_ref, all_ref, sum_ref, image_sems = refs[5:]
    placed = [
        place_images(half + 1 + i, ref, all_ref, image_sems.at[i])
        for i, ref in enumerate(far_refs)
    ]
    for copy, _ in placed:
        copy.start()
    sum_ref[...] = product_ref[...]
    for (_, place), ref in zip(placed, far_refs):
        sum_ref[place, :] = jnp.dot(
            ref[...], turned_ref[...], preferred_element_type=jnp.float32
        )
    scores = sum_ref[...].T - penalty_ref[...]
    score_ref[...] = scores
    if finish:
        write_packet(packet_ref, scores, route_ref)
    for copy, _ in placed:
        copy.wait()


def all_scores(staged, far, routes, finish):
    turned, penalty, images, products = staged
    width, refs = turned.shape
    slots, rows = images.shape[0], far[0].shape[0]
    return pl.pallas_call(
        partial(score_kernel, slots // rows, finish),
        out_shape=(
            jax.ShapeDtypeStruct((refs, slots), jnp.float32),
            jax.ShapeDtypeStruct((2, slots), jnp.float32),
            jax.ShapeDtypeStruct((slots, width), jnp.bfloat16),
        ),
        in_specs=[VMEM_SPEC] * (len(far) + 5),
        out_specs=(VMEM_SPEC,) * 3,
        scratch_shapes=[
            pltpu.VMEM((slots, refs), jnp.float32),
            pltpu.SemaphoreType.DMA((len(far),)),
        ],
        input_output_aliases={len(far) + 2: 2},
        compiler_params=pltpu.CompilerParams(vmem_limit_bytes=SCORE_VMEM),
        cost_estimate=pl.CostEstimate(
            flops=2 * refs * slots * width,
            bytes_accessed=2 * (slots + refs) * width,
            transcendentals=0,
        ),
        name="scores",
    )(*far, turned, penalty, images, products, routes)


def packet_kernel(score_ref, route_ref, packet_ref):
    write_packet(packet_ref, score_ref[...], route_ref)


def make_packet(scores, routes):
    return pl.pallas_call(
        packet_kernel,
        out_shape=jax.ShapeDtypeStruct((2, scores.shape[1]), jnp.float32),
        name="packet",
    )(scores, routes)


def write_routes(packets, rows, route_ref):
    reader = lax.axis_index("reader")
    readers = len(packets)
    for t in range(route_ref.shape[0]):
        routes = [ref[1:2, t * rows : (t + 1) * rows] for ref in packets]
        bit = 1
        while bit < readers:
            flip = (reader & bit) > 0
            routes = [jnp.where(flip, routes[k ^ bit], one) for k, one in enumerate(routes)]
            bit *= 2
        for j, route in enumerate(routes):
            route_ref[t : t + 1, j * rows : (j + 1) * rows] = route


def emit_sums(posterior, all_ref, piece, out_refs):
    sums = jnp.dot(posterior, all_ref[:, piece], preferred_element_type=jnp.float32)
    count = sums.shape[0] // len(out_refs)
    for s, out_ref in enumerate(out_refs):
        out_ref[...] = sums[s * count : (s + 1) * count].astype(out_ref.dtype)


def first_sums_kernel(readers, piece, all_ref, score_ref, *refs):
    refs = list(refs)
    packets = [refs.pop(0) for _ in range(readers)]
    route_ref = refs.pop()
    norm_ref, post_ref, *out_refs = refs
    write_routes(packets, packets[0].shape[1] // readers, route_ref)
    routes = route_ref[...]
    kept, mine = [], None
    for k, packet in enumerate(packets):
        group = (lax.axis_index("reader") ^ k).astype(jnp.float32)
        hits = jnp.where(routes == group, 1.0, 0.0)
        named = jnp.max(hits, axis=0, keepdims=True) > 0.0
        kept.append(jnp.where(named, packet[0:1, :], -jnp.inf))
        mine = named if k == 0 else mine
    highest = kept[0]
    for value in kept[1:]:
        highest = jnp.maximum(highest, value)
    spread = jnp.exp(kept[0] - highest)
    for value in kept[1:]:
        spread = spread + jnp.exp(value - highest)
    norm = highest + jnp.log(spread)
    norm_ref[...] = norm
    exponent = jnp.where(mine, score_ref[...] - norm, -jnp.inf)
    posterior = jnp.exp(exponent).astype(jnp.bfloat16)
    post_ref[...] = posterior
    emit_sums(posterior, all_ref, piece, out_refs)


def later_sums_kernel(piece, all_ref, post_ref, *out_refs):
    emit_sums(post_ref[...], all_ref, piece, out_refs)


def group_sums(kernel, piece, members, all_images, operands, extra, scratch=()):
    refs, slots = operands[0].shape
    width = piece.stop - piece.start
    block = jax.ShapeDtypeStruct((refs // members, width), jnp.bfloat16)
    outs = pl.pallas_call(
        kernel,
        out_shape=tuple(extra) + (block,) * members,
        in_specs=[VMEM_SPEC] * (1 + len(operands)),
        out_specs=(VMEM_SPEC,) * (len(extra) + members),
        scratch_shapes=scratch,
        compiler_params=pltpu.CompilerParams(vmem_limit_bytes=SUMS_VMEM),
        cost_estimate=pl.CostEstimate(
            flops=2 * refs * slots * width,
            bytes_accessed=2 * slots * width,
            transcendentals=0,
        ),
        name="sums",
    )(all_images, *operands)
    return outs[: len(extra)], outs[len(extra) :]


def on_device(images, routes, projections, noise_weights):
    readers = lax.axis_size("reader")
    members = lax.axis_size("blk")
    reader = lax.axis_index("reader")
    rows, width = images.shape
    noise = noise_weights.reshape(1, width)

    gather = staged_gather if members == 4 and rows % 32 == 0 and readers > 1 else plain_gather
    staged, far = gather(projections[0], images, noise, readers // 4, readers // 2)
    split = lax.axis_size("sub") > 1
    scores, mine, all_images = all_scores(staged, far, routes.T, not split)
    if split:
        scores = lax.psum(scores, "sub")
        mine = make_packet(scores, routes.T)
    packets = [mine] + [swap_bits(mine, "reader", k) for k in range(1, readers)]
    pieces = [slice(0, width // 2), slice(width // 2, width)]
    extra = (
        jax.ShapeDtypeStruct((1, scores.shape[1]), jnp.float32),
        jax.ShapeDtypeStruct(scores.shape, jnp.bfloat16),
    )
    (norms, posterior), first = group_sums(
        partial(first_sums_kernel, readers, pieces[0]),
        pieces[0],
        members,
        all_images,
        (scores, *packets),
        extra,
        (pltpu.VMEM((routes.shape[1], scores.shape[1]), jnp.float32),),
    )
    _, last = group_sums(
        partial(later_sums_kernel, pieces[1]), pieces[1], members, all_images, (posterior,), ()
    )
    parts = [first, last]
    scatter = pair_scatter if members == 4 else line_scatter
    total = scatter(parts, "blk")
    normalizer = lax.dynamic_slice(norms.reshape(-1), (reader * rows,), (rows,))
    return (total[None], normalizer)


def solution(mesh):
    return jax.shard_map(
        on_device,
        mesh=mesh,
        in_specs=(
            P(("parts", "blk", "reader"), "sub"),
            P(("parts", "blk", "reader"), None),
            P(("parts", "reader"), "blk", "sub"),
            P(("parts", "sub")),
        ),
        out_specs=(P(("parts", "reader"), "blk", "sub"), P(("parts", "blk", "reader"))),
        check_vma=False,
    )
```

```python
from functools import partial

import jax
import jax.numpy as jnp
from jax import lax
from jax.experimental import pallas as pl
from jax.experimental.pallas import tpu as pltpu
from jax.sharding import PartitionSpec as P

SCORE_VMEM = 20 * 1024 * 1024
SUMS_VMEM = 12 * 1024 * 1024
STEP = 1024
VMEM_SPEC = pl.BlockSpec(memory_space=pltpu.VMEM)
ANY_SPEC = pl.BlockSpec(memory_space=pl.ANY)
SIDES = [(0, 1), (1, 0), (2, 3), (3, 2)]
MIDDLE = [(1, 2), (2, 1)]


def swap_bits(block, axis, bits):
    return lax.ppermute(block, axis, [(i, i ^ bits) for i in range(lax.axis_size(axis))])


def swap_gather(block, axis, bit):
    held = {0: block}
    while bit:
        for k in list(held):
            held[k ^ bit] = swap_bits(held[k], axis, bit)
        bit //= 2
    return [held[k] for k in range(len(held))]


def add_rounded(one, other):
    return (one.astype(jnp.float32) + other.astype(jnp.float32)).astype(jnp.bfloat16)


def staged_gather(block, images, noise, near_bits, far_bit):
    cut = block.shape[1] // 16 * 9
    cuts = [block[:, :cut], block[:, cut:]]
    crossed = swap_bits(images, "reader", far_bit)
    near = swap_gather(images, "reader", near_bits)
    firsts = [
        lax.optimization_barrier(
            (lax.ppermute(one, "blk", SIDES), lax.ppermute(one, "blk", MIDDLE))
        )
        for one in cuts
    ]
    early = stage(
        [[[one] for one in cuts], [[side] for side, _ in firsts]], near, noise
    )
    far_parts, end_parts = [], []
    for side, across in firsts:
        far = lax.ppermute(across, "blk", SIDES)
        side, *_ = lax.optimization_barrier((side, *near))
        across_far = lax.ppermute(side, "blk", MIDDLE)
        far, across_far = lax.optimization_barrier((far, across_far))
        end = lax.ppermute(across_far, "blk", SIDES)
        far_parts.append([far, across_far])
        end_parts.append([end, across])
    weighted, penalty, staged_near, noise = early
    ends = [parts[0] for parts in end_parts]
    crossed, *_ = lax.optimization_barrier((crossed, *ends, *early))
    far = swap_gather(crossed, "reader", near_bits)
    staged = stage_rest([far_parts, end_parts], staged_near, crossed, weighted, penalty, noise)
    return staged, far[1:]


def plain_gather(block, images, noise, near_bits, far_bit):
    near = swap_gather(images, "reader", near_bits)
    far = swap_gather(swap_bits(images, "reader", far_bit), "reader", near_bits)
    line = [[[one]] for one in line_gather(block, "blk")]
    weighted, penalty, near, noise = stage(line[:2], near, noise)
    staged = stage_rest(line[2:], near, far[0], weighted, penalty, noise)
    return staged, far[1:]


def line_gather(block, axis):
    size, member = lax.axis_size(axis), lax.axis_index(axis)
    ahead, behind = [block], [block]
    for s in range(1, size):
        ahead.append(lax.ppermute(ahead[-1], axis, [(i, i + 1) for i in range(s - 1, size - 1)]))
        behind.append(lax.ppermute(behind[-1], axis, [(i, i - 1) for i in range(1, size - s + 1)]))
    blocks = [block]
    for s in range(1, size):
        blocks.append(jnp.where(member >= s, ahead[s], behind[size - s]))
    return blocks


def pair_scatter(pieces, axis):
    member = lax.axis_index(axis)
    is_end = (member == 0) | (member == 3)
    for_far_end = [lax.ppermute(parts[3], axis, SIDES) for parts in pieces]
    *second, for_far_end[0] = lax.optimization_barrier(
        [parts[2] for parts in pieces] + for_far_end[:1]
    )
    for_far_middle = [lax.ppermute(part, axis, SIDES) for part in second]
    totals = []
    for parts, part, end, middle in zip(pieces, second, for_far_end, for_far_middle):
        across_end = lax.ppermute(add_rounded(part, end), axis, MIDDLE)
        across_middle = lax.ppermute(add_rounded(parts[3], middle), axis, MIDDLE)
        near = jnp.where(is_end, parts[1], add_rounded(parts[1], across_end))
        from_side = lax.ppermute(near, axis, SIDES)
        total = parts[0].astype(jnp.float32) + from_side.astype(jnp.float32)
        totals.append(total + jnp.where(is_end, 0.0, across_middle.astype(jnp.float32)))
    return beside(totals)


def beside_kernel(count, *refs):
    out_ref, sems = refs[count:]
    copies, stop = [], out_ref.shape[1]
    for i, ref in enumerate(refs[:count]):
        start = stop - ref.shape[1]
        copies.append(pltpu.make_async_copy(ref, out_ref.at[:, start:stop], sems.at[i]))
        copies[-1].start()
        stop = start
    for copy in copies:
        copy.wait()


def beside(pieces):
    width = sum(piece.shape[1] for piece in pieces)
    return pl.pallas_call(
        partial(beside_kernel, len(pieces)),
        out_shape=jax.ShapeDtypeStruct((pieces[0].shape[0], width), pieces[0].dtype),
        in_specs=[VMEM_SPEC] * len(pieces),
        out_specs=ANY_SPEC,
        scratch_shapes=[pltpu.SemaphoreType.DMA((len(pieces),))],
        compiler_params=pltpu.CompilerParams(vmem_limit_bytes=SUMS_VMEM),
        name="beside",
    )(*pieces[::-1])


def line_scatter(pieces, axis):
    return jnp.concatenate([line_sum(parts, axis) for parts in pieces], axis=1)


def line_sum(parts, axis):
    size = lax.axis_size(axis)
    up = down = None
    for s in range(1, size):
        send_up, send_down = parts[s], parts[size - s]
        if s > 1:
            send_up = add_rounded(send_up, up)
            send_down = add_rounded(send_down, down)
        up = lax.ppermute(send_up, axis, [(i, i + 1) for i in range(0, s) if i + 1 < size])
        down = lax.ppermute(send_down, axis, [(i, i - 1) for i in range(size - s, size) if i > 0])
    total = parts[0].astype(jnp.float32)
    if size > 1:
        total = total + up.astype(jnp.float32) + down.astype(jnp.float32)
    return total


def column_lse(scores):
    peak = jnp.max(scores, axis=0, keepdims=True)
    total = jnp.sum(jnp.exp(scores - peak), axis=0, keepdims=True)
    return peak + jnp.log(total)


def at_end():
    member = lax.axis_index("blk")
    return (member == 0) | (member == lax.axis_size("blk") - 1)


def either(refs, act):
    if len(refs) == 1:
        act(refs[0])
        return
    is_end = at_end()

    @pl.when(is_end)
    def _():
        act(refs[0])

    @pl.when(jnp.logical_not(is_end))
    def _():
        act(refs[1])


def weigh_blocks(groups, noise_ref, weighted_ref, penalty_ref, block_ref, sems, first):
    count = block_ref.shape[1]
    parts = []
    for s, group in enumerate(groups):
        start = 0
        for refs in group:
            stop = start + refs[0].shape[1]
            parts.append((s, slice(start, stop), refs))
            start = stop

    def part_copy(i, ref):
        s, columns, _ = parts[i]
        return pltpu.make_async_copy(ref, block_ref.at[s, :, columns], sems.at[i])

    for i, (_, _, refs) in enumerate(parts):
        either(refs, lambda ref, i=i: part_copy(i, ref).start())
    for s in range(len(groups)):
        rows = slice((first + s) * count, (first + s + 1) * count)
        penalty = jnp.zeros((count, 1), jnp.float32)
        for i, (t, columns, refs) in enumerate(parts):
            if t != s:
                continue
            part_copy(i, refs[0]).wait()
            for start in range(columns.start, columns.stop, STEP):
                piece = slice(start, min(start + STEP, columns.stop))
                block = block_ref[s, :, piece].astype(jnp.float32)
                scaled = block * noise_ref[:, piece]
                weighted_ref[rows, piece] = scaled.astype(jnp.bfloat16)
                penalty = penalty + 0.5 * jnp.sum(scaled * block, axis=1, keepdims=True)
        penalty_ref[rows, :] = penalty


def take_blocks(refs, counts):
    return [[[refs.pop(0) for _ in range(n)] for n in group] for group in counts]


def block_counts(blocks):
    return [[len(part) for part in group] for group in blocks]


def flat(blocks):
    return [one for group in blocks for part in group for one in part]


def stage_kernel(near_count, counts, *refs):
    refs = list(refs)
    near_refs = [refs.pop(0) for _ in range(near_count)]
    groups = take_blocks(refs, counts)
    noise_ref, weighted_ref, penalty_ref, near_ref, noise_out_ref, block_ref, near_sems, sems = refs
    rows = near_refs[0].shape[0]
    copies = []
    for k, ref in enumerate(near_refs):
        copy = pltpu.make_async_copy(ref, near_ref.at[pl.ds(k * rows, rows), :], near_sems.at[k])
        copy.start()
        copies.append(copy)
    noise_out_ref[...] = noise_ref[...]
    weigh_blocks(groups, noise_ref, weighted_ref, penalty_ref, block_ref, sems, 0)
    for copy in copies:
        copy.wait()


def stage(blocks, near, noise):
    count = blocks[0][0][0].shape[0]
    parts = sum(len(group) for group in blocks)
    width = noise.shape[1]
    refs = len(blocks) * count
    moved = [*near, *flat(blocks)]
    return pl.pallas_call(
        partial(stage_kernel, len(near), block_counts(blocks)),
        out_shape=(
            jax.ShapeDtypeStruct((refs, width), jnp.bfloat16),
            jax.ShapeDtypeStruct((refs, 1), jnp.float32),
            jax.ShapeDtypeStruct((len(near) * near[0].shape[0], width), jnp.bfloat16),
            jax.ShapeDtypeStruct((1, width), jnp.float32),
        ),
        in_specs=[ANY_SPEC] * len(moved) + [VMEM_SPEC],
        out_specs=(VMEM_SPEC,) * 4,
        scratch_shapes=[
            pltpu.VMEM((len(blocks), count, width), jnp.bfloat16),
            pltpu.SemaphoreType.DMA((len(near),)),
            pltpu.SemaphoreType.DMA((parts,)),
        ],
        compiler_params=pltpu.CompilerParams(vmem_limit_bytes=SCORE_VMEM),
        cost_estimate=pl.CostEstimate(
            flops=8 * refs * width, bytes_accessed=12_000_000, transcendentals=0
        ),
        name="stage",
    )(*moved, noise)


def place_images(k, source, all_ref, sem):
    rows = source.shape[0]
    row = pl.multiple_of((lax.axis_index("reader") ^ k) * rows, 16)
    return pltpu.make_async_copy(source, all_ref.at[pl.ds(row, rows), :], sem), pl.ds(row, rows)


def stage_rest_kernel(readers, counts, *refs):
    refs = list(refs)
    groups = take_blocks(refs, counts)
    near_ref, far_ref, early_ref, early_penalty_ref, noise_ref = [refs.pop(0) for _ in range(5)]
    turned_ref, penalty_ref, all_ref, product_ref = refs[:4]
    weighted_ref, block_ref, sems, image_sems = refs[4:]
    rows = far_ref.shape[0]
    half = readers // 2
    sources = [near_ref.at[pl.ds(k * rows, rows), :] for k in range(half)] + [far_ref]
    placed = [place_images(k, one, all_ref, image_sems.at[k]) for k, one in enumerate(sources)]
    for copy, _ in placed:
        copy.start()
    done = early_ref.shape[0]
    weighted_ref[:done, :] = early_ref[...]
    penalty_ref[:done, :] = early_penalty_ref[...]
    first = done // block_ref.shape[1]
    weigh_blocks(groups, noise_ref, weighted_ref, penalty_ref, block_ref, sems, first)
    width = weighted_ref.shape[1]
    for start in range(0, width, STEP):
        piece = slice(start, min(start + STEP, width))
        turned_ref[piece, :] = weighted_ref[:, piece].T
    products = jnp.dot(near_ref[...], turned_ref[...], preferred_element_type=jnp.float32)
    for k in range(half):
        product_ref[placed[k][1], :] = products[k * rows : (k + 1) * rows]
    product_ref[placed[half][1], :] = jnp.dot(
        far_ref[...], turned_ref[...], preferred_element_type=jnp.float32
    )
    for copy, _ in placed:
        copy.wait()


def stage_rest(blocks, near, crossed, weighted, penalty, noise):
    count = blocks[0][0][0].shape[0]
    parts = sum(len(group) for group in blocks)
    width = noise.shape[1]
    refs = len(blocks) * count + weighted.shape[0]
    slots = 2 * near.shape[0]
    readers = slots // crossed.shape[0]
    moved = flat(blocks)
    return pl.pallas_call(
        partial(stage_rest_kernel, readers, block_counts(blocks)),
        out_shape=(
            jax.ShapeDtypeStruct((width, refs), jnp.bfloat16),
            jax.ShapeDtypeStruct((refs, 1), jnp.float32),
            jax.ShapeDtypeStruct((slots, width), jnp.bfloat16),
            jax.ShapeDtypeStruct((slots, refs), jnp.float32),
        ),
        in_specs=[ANY_SPEC] * len(moved) + [VMEM_SPEC] * 5,
        out_specs=(VMEM_SPEC,) * 4,
        scratch_shapes=[
            pltpu.VMEM((refs, width), jnp.bfloat16),
            pltpu.VMEM((len(blocks), count, width), jnp.bfloat16),
            pltpu.SemaphoreType.DMA((parts,)),
            pltpu.SemaphoreType.DMA((readers // 2 + 1,)),
        ],
        compiler_params=pltpu.CompilerParams(vmem_limit_bytes=SCORE_VMEM),
        cost_estimate=pl.CostEstimate(
            flops=8 * refs * width, bytes_accessed=12_000_000, transcendentals=0
        ),
        name="stage_rest",
    )(*moved, near, crossed, weighted, penalty, noise)


def write_packet(packet_ref, scores, route_ref):
    top, rows = route_ref.shape
    packet_ref[0:1, :] = column_lse(scores)
    packet_ref[1:2, :] = jnp.zeros((1, packet_ref.shape[1]), jnp.float32)
    for t in range(top):
        packet_ref[1:2, t * rows : (t + 1) * rows] = route_ref[t : t + 1, :].astype(jnp.float32)


def score_kernel(readers, finish, *refs):
    refs = list(refs)
    half = readers // 2
    far_refs = [refs.pop(0) for _ in range(half - 1)]
    turned_ref, penalty_ref, _, product_ref, route_ref = refs[:5]
    score_ref, packet_ref, all_ref, sum_ref, image_sems = refs[5:]
    placed = [
        place_images(half + 1 + i, ref, all_ref, image_sems.at[i])
        for i, ref in enumerate(far_refs)
    ]
    for copy, _ in placed:
        copy.start()
    sum_ref[...] = product_ref[...]
    for (_, place), ref in zip(placed, far_refs):
        sum_ref[place, :] = jnp.dot(
            ref[...], turned_ref[...], preferred_element_type=jnp.float32
        )
    scores = sum_ref[...].T - penalty_ref[...]
    score_ref[...] = scores
    if finish:
        write_packet(packet_ref, scores, route_ref)
    for copy, _ in placed:
        copy.wait()


def all_scores(staged, far, routes, finish):
    turned, penalty, images, products = staged
    width, refs = turned.shape
    slots, rows = images.shape[0], far[0].shape[0]
    return pl.pallas_call(
        partial(score_kernel, slots // rows, finish),
        out_shape=(
            jax.ShapeDtypeStruct((refs, slots), jnp.float32),
            jax.ShapeDtypeStruct((2, slots), jnp.float32),
            jax.ShapeDtypeStruct((slots, width), jnp.bfloat16),
        ),
        in_specs=[VMEM_SPEC] * (len(far) + 5),
        out_specs=(VMEM_SPEC,) * 3,
        scratch_shapes=[
            pltpu.VMEM((slots, refs), jnp.float32),
            pltpu.SemaphoreType.DMA((len(far),)),
        ],
        input_output_aliases={len(far) + 2: 2},
        compiler_params=pltpu.CompilerParams(vmem_limit_bytes=SCORE_VMEM),
        cost_estimate=pl.CostEstimate(
            flops=2 * refs * slots * width,
            bytes_accessed=2 * (slots + refs) * width,
            transcendentals=0,
        ),
        name="scores",
    )(*far, turned, penalty, images, products, routes)


def packet_kernel(score_ref, route_ref, packet_ref):
    write_packet(packet_ref, score_ref[...], route_ref)


def make_packet(scores, routes):
    return pl.pallas_call(
        packet_kernel,
        out_shape=jax.ShapeDtypeStruct((2, scores.shape[1]), jnp.float32),
        name="packet",
    )(scores, routes)


def write_routes(packets, rows, route_ref):
    reader = lax.axis_index("reader")
    readers = len(packets)
    for t in range(route_ref.shape[0]):
        routes = [ref[1:2, t * rows : (t + 1) * rows] for ref in packets]
        bit = 1
        while bit < readers:
            flip = (reader & bit) > 0
            routes = [jnp.where(flip, routes[k ^ bit], one) for k, one in enumerate(routes)]
            bit *= 2
        for j, route in enumerate(routes):
            route_ref[t : t + 1, j * rows : (j + 1) * rows] = route


def emit_sums(posterior, all_ref, piece, out_refs):
    sums = jnp.dot(posterior, all_ref[:, piece], preferred_element_type=jnp.float32)
    count = sums.shape[0] // len(out_refs)
    for s, out_ref in enumerate(out_refs):
        out_ref[...] = sums[s * count : (s + 1) * count].astype(out_ref.dtype)


def first_sums_kernel(readers, piece, all_ref, score_ref, *refs):
    refs = list(refs)
    packets = [refs.pop(0) for _ in range(readers)]
    route_ref = refs.pop()
    norm_ref, post_ref, *out_refs = refs
    write_routes(packets, packets[0].shape[1] // readers, route_ref)
    routes = route_ref[...]
    kept, mine = [], None
    for k, packet in enumerate(packets):
        group = (lax.axis_index("reader") ^ k).astype(jnp.float32)
        hits = jnp.where(routes == group, 1.0, 0.0)
        named = jnp.max(hits, axis=0, keepdims=True) > 0.0
        kept.append(jnp.where(named, packet[0:1, :], -jnp.inf))
        mine = named if k == 0 else mine
    highest = kept[0]
    for value in kept[1:]:
        highest = jnp.maximum(highest, value)
    spread = jnp.exp(kept[0] - highest)
    for value in kept[1:]:
        spread = spread + jnp.exp(value - highest)
    norm = highest + jnp.log(spread)
    norm_ref[...] = norm
    exponent = jnp.where(mine, score_ref[...] - norm, -jnp.inf)
    posterior = jnp.exp(exponent).astype(jnp.bfloat16)
    post_ref[...] = posterior
    emit_sums(posterior, all_ref, piece, out_refs)


def later_sums_kernel(piece, all_ref, post_ref, *out_refs):
    emit_sums(post_ref[...], all_ref, piece, out_refs)


def group_sums(kernel, piece, members, all_images, operands, extra, scratch=()):
    refs, slots = operands[0].shape
    width = piece.stop - piece.start
    block = jax.ShapeDtypeStruct((refs // members, width), jnp.bfloat16)
    outs = pl.pallas_call(
        kernel,
        out_shape=tuple(extra) + (block,) * members,
        in_specs=[VMEM_SPEC] * (1 + len(operands)),
        out_specs=(VMEM_SPEC,) * (len(extra) + members),
        scratch_shapes=scratch,
        compiler_params=pltpu.CompilerParams(vmem_limit_bytes=SUMS_VMEM),
        cost_estimate=pl.CostEstimate(
            flops=2 * refs * slots * width,
            bytes_accessed=2 * slots * width,
            transcendentals=0,
        ),
        name="sums",
    )(all_images, *operands)
    return outs[: len(extra)], outs[len(extra) :]


def on_device(images, routes, projections, noise_weights):
    readers = lax.axis_size("reader")
    members = lax.axis_size("blk")
    reader = lax.axis_index("reader")
    rows, width = images.shape
    noise = noise_weights.reshape(1, width)

    gather = staged_gather if members == 4 and rows % 32 == 0 and readers > 1 else plain_gather
    staged, far = gather(projections[0], images, noise, readers // 4, readers // 2)
    split = lax.axis_size("sub") > 1
    scores, mine, all_images = all_scores(staged, far, routes.T, not split)
    if split:
        scores = lax.psum(scores, "sub")
        mine = make_packet(scores, routes.T)
    packets = [mine] + [swap_bits(mine, "reader", k) for k in range(1, readers)]
    pieces = [slice(0, width // 2), slice(width // 2, width)]
    extra = (
        jax.ShapeDtypeStruct((1, scores.shape[1]), jnp.float32),
        jax.ShapeDtypeStruct(scores.shape, jnp.bfloat16),
    )
    (norms, posterior), first = group_sums(
        partial(first_sums_kernel, readers, pieces[0]),
        pieces[0],
        members,
        all_images,
        (scores, *packets),
        extra,
        (pltpu.VMEM((routes.shape[1], scores.shape[1]), jnp.float32),),
    )
    _, last = group_sums(
        partial(later_sums_kernel, pieces[1]), pieces[1], members, all_images, (posterior,), ()
    )
    parts = [first, last]
    scatter = pair_scatter if members == 4 else line_scatter
    total = scatter(parts, "blk")
    normalizer = lax.dynamic_slice(norms.reshape(-1), (reader * rows,), (rows,))
    return (total[None], normalizer)


def solution(mesh):
    return jax.shard_map(
        on_device,
        mesh=mesh,
        in_specs=(
            P(("parts", "blk", "reader"), "sub"),
            P(("parts", "blk", "reader"), None),
            P(("parts", "reader"), "blk", "sub"),
            P(("parts", "sub")),
        ),
        out_specs=(P(("parts", "reader"), "blk", "sub"), P(("parts", "blk", "reader"))),
        check_vma=False,
    )
```

```python
from functools import partial

import jax
import jax.numpy as jnp
from jax import lax
from jax.experimental import pallas as pl
from jax.experimental.pallas import tpu as pltpu
from jax.sharding import PartitionSpec as P

SCORE_VMEM = 20 * 1024 * 1024
SUMS_VMEM = 12 * 1024 * 1024
STEP = 1024
VMEM_SPEC = pl.BlockSpec(memory_space=pltpu.VMEM)
ANY_SPEC = pl.BlockSpec(memory_space=pl.ANY)
SIDES = [(0, 1), (1, 0), (2, 3), (3, 2)]
MIDDLE = [(1, 2), (2, 1)]


def swap_bits(block, axis, bits):
    return lax.ppermute(block, axis, [(i, i ^ bits) for i in range(lax.axis_size(axis))])


def swap_gather(block, axis, bit):
    held = {0: block}
    while bit:
        for k in list(held):
            held[k ^ bit] = swap_bits(held[k], axis, bit)
        bit //= 2
    return [held[k] for k in range(len(held))]


def add_rounded(one, other):
    return (one.astype(jnp.float32) + other.astype(jnp.float32)).astype(jnp.bfloat16)


def staged_gather(block, images, noise, near_bits, far_bit):
    cut = block.shape[1] // 16 * 9
    cuts = [block[:, :cut], block[:, cut:]]
    crossed = swap_bits(images, "reader", far_bit)
    near = swap_gather(images, "reader", near_bits)
    firsts = [
        lax.optimization_barrier(
            (lax.ppermute(one, "blk", SIDES), lax.ppermute(one, "blk", MIDDLE))
        )
        for one in cuts
    ]
    early = stage(
        [[[one] for one in cuts], [[side] for side, _ in firsts]], near, noise
    )
    far_parts, end_parts = [], []
    for side, across in firsts:
        far = lax.ppermute(across, "blk", SIDES)
        side, *_ = lax.optimization_barrier((side, *near))
        across_far = lax.ppermute(side, "blk", MIDDLE)
        far, across_far = lax.optimization_barrier((far, across_far))
        end = lax.ppermute(across_far, "blk", SIDES)
        far_parts.append([far, across_far])
        end_parts.append([end, across])
    weighted, penalty, staged_near, noise = early
    ends = [parts[0] for parts in end_parts]
    crossed, *_ = lax.optimization_barrier((crossed, *ends, *early))
    far = swap_gather(crossed, "reader", near_bits)
    staged = stage_rest([far_parts, end_parts], staged_near, crossed, weighted, penalty, noise)
    return staged, far[1:]


def plain_gather(block, images, noise, near_bits, far_bit):
    near = swap_gather(images, "reader", near_bits)
    far = swap_gather(swap_bits(images, "reader", far_bit), "reader", near_bits)
    line = [[[one]] for one in line_gather(block, "blk")]
    weighted, penalty, near, noise = stage(line[:2], near, noise)
    staged = stage_rest(line[2:], near, far[0], weighted, penalty, noise)
    return staged, far[1:]


def line_gather(block, axis):
    size, member = lax.axis_size(axis), lax.axis_index(axis)
    ahead, behind = [block], [block]
    for s in range(1, size):
        ahead.append(lax.ppermute(ahead[-1], axis, [(i, i + 1) for i in range(s - 1, size - 1)]))
        behind.append(lax.ppermute(behind[-1], axis, [(i, i - 1) for i in range(1, size - s + 1)]))
    blocks = [block]
    for s in range(1, size):
        blocks.append(jnp.where(member >= s, ahead[s], behind[size - s]))
    return blocks


def pair_scatter(pieces, axis):
    member = lax.axis_index(axis)
    is_end = (member == 0) | (member == 3)
    for_far_end = [lax.ppermute(parts[3], axis, SIDES) for parts in pieces]
    *second, for_far_end[0] = lax.optimization_barrier(
        [parts[2] for parts in pieces] + for_far_end[:1]
    )
    for_far_middle = [lax.ppermute(part, axis, SIDES) for part in second]
    totals = []
    for parts, part, end, middle in zip(pieces, second, for_far_end, for_far_middle):
        across_end = lax.ppermute(add_rounded(part, end), axis, MIDDLE)
        across_middle = lax.ppermute(add_rounded(parts[3], middle), axis, MIDDLE)
        near = jnp.where(is_end, parts[1], add_rounded(parts[1], across_end))
        from_side = lax.ppermute(near, axis, SIDES)
        total = parts[0].astype(jnp.float32) + from_side.astype(jnp.float32)
        totals.append(total + jnp.where(is_end, 0.0, across_middle.astype(jnp.float32)))
    return beside(totals)


def beside_kernel(count, *refs):
    out_ref, sems = refs[count:]
    copies, stop = [], out_ref.shape[1]
    for i, ref in enumerate(refs[:count]):
        start = stop - ref.shape[1]
        copies.append(pltpu.make_async_copy(ref, out_ref.at[:, start:stop], sems.at[i]))
        copies[-1].start()
        stop = start
    for copy in copies:
        copy.wait()


def beside(pieces):
    width = sum(piece.shape[1] for piece in pieces)
    return pl.pallas_call(
        partial(beside_kernel, len(pieces)),
        out_shape=jax.ShapeDtypeStruct((pieces[0].shape[0], width), pieces[0].dtype),
        in_specs=[VMEM_SPEC] * len(pieces),
        out_specs=ANY_SPEC,
        scratch_shapes=[pltpu.SemaphoreType.DMA((len(pieces),))],
        compiler_params=pltpu.CompilerParams(vmem_limit_bytes=SUMS_VMEM),
        name="beside",
    )(*pieces[::-1])


def line_scatter(pieces, axis):
    return jnp.concatenate([line_sum(parts, axis) for parts in pieces], axis=1)


def line_sum(parts, axis):
    size = lax.axis_size(axis)
    up = down = None
    for s in range(1, size):
        send_up, send_down = parts[s], parts[size - s]
        if s > 1:
            send_up = add_rounded(send_up, up)
            send_down = add_rounded(send_down, down)
        up = lax.ppermute(send_up, axis, [(i, i + 1) for i in range(0, s) if i + 1 < size])
        down = lax.ppermute(send_down, axis, [(i, i - 1) for i in range(size - s, size) if i > 0])
    total = parts[0].astype(jnp.float32)
    if size > 1:
        total = total + up.astype(jnp.float32) + down.astype(jnp.float32)
    return total


def at_end():
    member = lax.axis_index("blk")
    return (member == 0) | (member == lax.axis_size("blk") - 1)


def either(refs, act):
    if len(refs) == 1:
        act(refs[0])
        return
    is_end = at_end()

    @pl.when(is_end)
    def _():
        act(refs[0])

    @pl.when(jnp.logical_not(is_end))
    def _():
        act(refs[1])


def weigh_blocks(groups, noise_ref, weighted_ref, penalty_ref, block_ref, sems, first):
    count = block_ref.shape[1]
    parts = []
    for s, group in enumerate(groups):
        start = 0
        for refs in group:
            stop = start + refs[0].shape[1]
            parts.append((s, slice(start, stop), refs))
            start = stop

    def part_copy(i, ref):
        s, columns, _ = parts[i]
        return pltpu.make_async_copy(ref, block_ref.at[s, :, columns], sems.at[i])

    for i, (_, _, refs) in enumerate(parts):
        either(refs, lambda ref, i=i: part_copy(i, ref).start())
    for s in range(len(groups)):
        rows = slice((first + s) * count, (first + s + 1) * count)
        penalty = jnp.zeros((count, 1), jnp.float32)
        for i, (t, columns, refs) in enumerate(parts):
            if t != s:
                continue
            part_copy(i, refs[0]).wait()
            for start in range(columns.start, columns.stop, STEP):
                piece = slice(start, min(start + STEP, columns.stop))
                block = block_ref[s, :, piece].astype(jnp.float32)
                scaled = block * noise_ref[:, piece]
                weighted_ref[rows, piece] = scaled.astype(jnp.bfloat16)
                penalty = penalty + 0.5 * jnp.sum(scaled * block, axis=1, keepdims=True)
        penalty_ref[rows, :] = penalty


def take_blocks(refs, counts):
    return [[[refs.pop(0) for _ in range(n)] for n in group] for group in counts]


def block_counts(blocks):
    return [[len(part) for part in group] for group in blocks]


def flat(blocks):
    return [one for group in blocks for part in group for one in part]


def stage_kernel(near_count, counts, *refs):
    refs = list(refs)
    near_refs = [refs.pop(0) for _ in range(near_count)]
    groups = take_blocks(refs, counts)
    noise_ref, weighted_ref, penalty_ref, near_ref, noise_out_ref, block_ref, near_sems, sems = refs
    rows = near_refs[0].shape[0]
    copies = []
    for k, ref in enumerate(near_refs):
        copy = pltpu.make_async_copy(ref, near_ref.at[pl.ds(k * rows, rows), :], near_sems.at[k])
        copy.start()
        copies.append(copy)
    noise_out_ref[...] = noise_ref[...]
    weigh_blocks(groups, noise_ref, weighted_ref, penalty_ref, block_ref, sems, 0)
    for copy in copies:
        copy.wait()


def stage(blocks, near, noise):
    count = blocks[0][0][0].shape[0]
    parts = sum(len(group) for group in blocks)
    width = noise.shape[1]
    refs = len(blocks) * count
    moved = [*near, *flat(blocks)]
    return pl.pallas_call(
        partial(stage_kernel, len(near), block_counts(blocks)),
        out_shape=(
            jax.ShapeDtypeStruct((refs, width), jnp.bfloat16),
            jax.ShapeDtypeStruct((refs, 1), jnp.float32),
            jax.ShapeDtypeStruct((len(near) * near[0].shape[0], width), jnp.bfloat16),
            jax.ShapeDtypeStruct((1, width), jnp.float32),
        ),
        in_specs=[ANY_SPEC] * len(moved) + [VMEM_SPEC],
        out_specs=(VMEM_SPEC,) * 4,
        scratch_shapes=[
            pltpu.VMEM((len(blocks), count, width), jnp.bfloat16),
            pltpu.SemaphoreType.DMA((len(near),)),
            pltpu.SemaphoreType.DMA((parts,)),
        ],
        compiler_params=pltpu.CompilerParams(vmem_limit_bytes=SCORE_VMEM),
        cost_estimate=pl.CostEstimate(
            flops=8 * refs * width, bytes_accessed=12_000_000, transcendentals=0
        ),
        name="stage",
    )(*moved, noise)


def place_images(k, source, all_ref, sem):
    rows = source.shape[0]
    row = pl.multiple_of((lax.axis_index("reader") ^ k) * rows, 16)
    return pltpu.make_async_copy(source, all_ref.at[pl.ds(row, rows), :], sem), pl.ds(row, rows)


def stage_rest_kernel(readers, counts, *refs):
    refs = list(refs)
    groups = take_blocks(refs, counts)
    near_ref, far_ref, early_ref, early_penalty_ref, noise_ref = [refs.pop(0) for _ in range(5)]
    turned_ref, penalty_ref, all_ref, product_ref = refs[:4]
    weighted_ref, block_ref, sems, image_sems = refs[4:]
    rows = far_ref.shape[0]
    half = readers // 2
    sources = [near_ref.at[pl.ds(k * rows, rows), :] for k in range(half)] + [far_ref]
    placed = [place_images(k, one, all_ref, image_sems.at[k]) for k, one in enumerate(sources)]
    for copy, _ in placed:
        copy.start()
    done = early_ref.shape[0]
    weighted_ref[:done, :] = early_ref[...]
    penalty_ref[:done, :] = early_penalty_ref[...]
    first = done // block_ref.shape[1]
    weigh_blocks(groups, noise_ref, weighted_ref, penalty_ref, block_ref, sems, first)
    width = weighted_ref.shape[1]
    for start in range(0, width, STEP):
        piece = slice(start, min(start + STEP, width))
        turned_ref[piece, :] = weighted_ref[:, piece].T
    products = jnp.dot(near_ref[...], turned_ref[...], preferred_element_type=jnp.float32)
    for k in range(half):
        product_ref[placed[k][1], :] = products[k * rows : (k + 1) * rows]
    product_ref[placed[half][1], :] = jnp.dot(
        far_ref[...], turned_ref[...], preferred_element_type=jnp.float32
    )
    for copy, _ in placed:
        copy.wait()


def stage_rest(blocks, near, crossed, weighted, penalty, noise):
    count = blocks[0][0][0].shape[0]
    parts = sum(len(group) for group in blocks)
    width = noise.shape[1]
    refs = len(blocks) * count + weighted.shape[0]
    slots = 2 * near.shape[0]
    readers = slots // crossed.shape[0]
    moved = flat(blocks)
    return pl.pallas_call(
        partial(stage_rest_kernel, readers, block_counts(blocks)),
        out_shape=(
            jax.ShapeDtypeStruct((width, refs), jnp.bfloat16),
            jax.ShapeDtypeStruct((refs, 1), jnp.float32),
            jax.ShapeDtypeStruct((slots, width), jnp.bfloat16),
            jax.ShapeDtypeStruct((slots, refs), jnp.float32),
        ),
        in_specs=[ANY_SPEC] * len(moved) + [VMEM_SPEC] * 5,
        out_specs=(VMEM_SPEC,) * 4,
        scratch_shapes=[
            pltpu.VMEM((refs, width), jnp.bfloat16),
            pltpu.VMEM((len(blocks), count, width), jnp.bfloat16),
            pltpu.SemaphoreType.DMA((parts,)),
            pltpu.SemaphoreType.DMA((readers // 2 + 1,)),
        ],
        compiler_params=pltpu.CompilerParams(vmem_limit_bytes=SCORE_VMEM),
        cost_estimate=pl.CostEstimate(
            flops=8 * refs * width, bytes_accessed=12_000_000, transcendentals=0
        ),
        name="stage_rest",
    )(*moved, near, crossed, weighted, penalty, noise)


def write_packet(packet_ref, scores, route_ref):
    top, rows = route_ref.shape
    peak = jnp.max(scores, axis=0, keepdims=True)
    packet_ref[0:1, :] = peak
    packet_ref[1:2, :] = jnp.sum(jnp.exp(scores - peak), axis=0, keepdims=True)
    packet_ref[2:3, :] = jnp.zeros((1, packet_ref.shape[1]), jnp.float32)
    for t in range(top):
        packet_ref[2:3, t * rows : (t + 1) * rows] = route_ref[t : t + 1, :].astype(jnp.float32)


def score_kernel(readers, finish, *refs):
    refs = list(refs)
    half = readers // 2
    far_refs = [refs.pop(0) for _ in range(half - 1)]
    turned_ref, penalty_ref, _, product_ref, route_ref = refs[:5]
    score_ref, packet_ref, all_ref, sum_ref, image_sems = refs[5:]
    placed = [
        place_images(half + 1 + i, ref, all_ref, image_sems.at[i])
        for i, ref in enumerate(far_refs)
    ]
    for copy, _ in placed:
        copy.start()
    sum_ref[...] = product_ref[...]
    for (_, place), ref in zip(placed, far_refs):
        sum_ref[place, :] = jnp.dot(
            ref[...], turned_ref[...], preferred_element_type=jnp.float32
        )
    scores = sum_ref[...].T - penalty_ref[...]
    score_ref[...] = scores
    if finish:
        write_packet(packet_ref, scores, route_ref)
    for copy, _ in placed:
        copy.wait()


def all_scores(staged, far, routes, finish):
    turned, penalty, images, products = staged
    width, refs = turned.shape
    slots, rows = images.shape[0], far[0].shape[0]
    return pl.pallas_call(
        partial(score_kernel, slots // rows, finish),
        out_shape=(
            jax.ShapeDtypeStruct((refs, slots), jnp.float32),
            jax.ShapeDtypeStruct((3, slots), jnp.float32),
            jax.ShapeDtypeStruct((slots, width), jnp.bfloat16),
        ),
        in_specs=[VMEM_SPEC] * (len(far) + 5),
        out_specs=(VMEM_SPEC,) * 3,
        scratch_shapes=[
            pltpu.VMEM((slots, refs), jnp.float32),
            pltpu.SemaphoreType.DMA((len(far),)),
        ],
        input_output_aliases={len(far) + 2: 2},
        compiler_params=pltpu.CompilerParams(vmem_limit_bytes=SCORE_VMEM),
        cost_estimate=pl.CostEstimate(
            flops=2 * refs * slots * width,
            bytes_accessed=2 * (slots + refs) * width,
            transcendentals=0,
        ),
        name="scores",
    )(*far, turned, penalty, images, products, routes)


def packet_kernel(score_ref, route_ref, packet_ref):
    write_packet(packet_ref, score_ref[...], route_ref)


def make_packet(scores, routes):
    return pl.pallas_call(
        packet_kernel,
        out_shape=jax.ShapeDtypeStruct((3, scores.shape[1]), jnp.float32),
        name="packet",
    )(scores, routes)


def write_routes(packets, rows, route_ref):
    reader = lax.axis_index("reader")
    readers = len(packets)
    for t in range(route_ref.shape[0]):
        routes = [ref[2:3, t * rows : (t + 1) * rows] for ref in packets]
        bit = 1
        while bit < readers:
            flip = (reader & bit) > 0
            routes = [jnp.where(flip, routes[k ^ bit], one) for k, one in enumerate(routes)]
            bit *= 2
        for j, route in enumerate(routes):
            route_ref[t : t + 1, j * rows : (j + 1) * rows] = route


def emit_sums(posterior, all_ref, piece, out_refs):
    sums = jnp.dot(posterior, all_ref[:, piece], preferred_element_type=jnp.float32)
    count = sums.shape[0] // len(out_refs)
    for s, out_ref in enumerate(out_refs):
        out_ref[...] = sums[s * count : (s + 1) * count].astype(out_ref.dtype)


def first_sums_kernel(readers, piece, all_ref, score_ref, *refs):
    refs = list(refs)
    packets = [refs.pop(0) for _ in range(readers)]
    route_ref = refs.pop()
    norm_ref, post_ref, *out_refs = refs
    write_routes(packets, packets[0].shape[1] // readers, route_ref)
    routes = route_ref[...]
    kept, mine = [], None
    for k, packet in enumerate(packets):
        group = (lax.axis_index("reader") ^ k).astype(jnp.float32)
        hits = jnp.where(routes == group, 1.0, 0.0)
        named = jnp.max(hits, axis=0, keepdims=True) > 0.0
        kept.append(jnp.where(named, packet[0:1, :], -jnp.inf))
        mine = named if k == 0 else mine
    highest = kept[0]
    for value in kept[1:]:
        highest = jnp.maximum(highest, value)
    spread = packets[0][1:2, :] * jnp.exp(kept[0] - highest)
    for packet, value in zip(packets[1:], kept[1:]):
        spread = spread + packet[1:2, :] * jnp.exp(value - highest)
    norm = highest + jnp.log(spread)
    norm_ref[...] = norm
    exponent = jnp.where(mine, score_ref[...] - norm, -jnp.inf)
    posterior = jnp.exp(exponent).astype(jnp.bfloat16)
    post_ref[...] = posterior
    emit_sums(posterior, all_ref, piece, out_refs)


def later_sums_kernel(piece, all_ref, post_ref, *out_refs):
    emit_sums(post_ref[...], all_ref, piece, out_refs)


def group_sums(kernel, piece, members, all_images, operands, extra, scratch=()):
    refs, slots = operands[0].shape
    width = piece.stop - piece.start
    block = jax.ShapeDtypeStruct((refs // members, width), jnp.bfloat16)
    outs = pl.pallas_call(
        kernel,
        out_shape=tuple(extra) + (block,) * members,
        in_specs=[VMEM_SPEC] * (1 + len(operands)),
        out_specs=(VMEM_SPEC,) * (len(extra) + members),
        scratch_shapes=scratch,
        compiler_params=pltpu.CompilerParams(vmem_limit_bytes=SUMS_VMEM),
        cost_estimate=pl.CostEstimate(
            flops=2 * refs * slots * width,
            bytes_accessed=2 * slots * width,
            transcendentals=0,
        ),
        name="sums",
    )(all_images, *operands)
    return outs[: len(extra)], outs[len(extra) :]


def on_device(images, routes, projections, noise_weights):
    readers = lax.axis_size("reader")
    members = lax.axis_size("blk")
    reader = lax.axis_index("reader")
    rows, width = images.shape
    noise = noise_weights.reshape(1, width)

    gather = staged_gather if members == 4 and rows % 32 == 0 and readers > 1 else plain_gather
    staged, far = gather(projections[0], images, noise, readers // 4, readers // 2)
    split = lax.axis_size("sub") > 1
    scores, mine, all_images = all_scores(staged, far, routes.T, not split)
    if split:
        scores = lax.psum(scores, "sub")
        mine = make_packet(scores, routes.T)
    packets = [mine] + [swap_bits(mine, "reader", k) for k in range(1, readers)]
    pieces = [slice(0, width // 2), slice(width // 2, width)]
    extra = (
        jax.ShapeDtypeStruct((1, scores.shape[1]), jnp.float32),
        jax.ShapeDtypeStruct(scores.shape, jnp.bfloat16),
    )
    (norms, posterior), first = group_sums(
        partial(first_sums_kernel, readers, pieces[0]),
        pieces[0],
        members,
        all_images,
        (scores, *packets),
        extra,
        (pltpu.VMEM((routes.shape[1], scores.shape[1]), jnp.float32),),
    )
    _, last = group_sums(
        partial(later_sums_kernel, pieces[1]), pieces[1], members, all_images, (posterior,), ()
    )
    parts = [first, last]
    scatter = pair_scatter if members == 4 else line_scatter
    total = scatter(parts, "blk")
    normalizer = lax.dynamic_slice(norms.reshape(-1), (reader * rows,), (rows,))
    return (total[None], normalizer)


def solution(mesh):
    return jax.shard_map(
        on_device,
        mesh=mesh,
        in_specs=(
            P(("parts", "blk", "reader"), "sub"),
            P(("parts", "blk", "reader"), None),
            P(("parts", "reader"), "blk", "sub"),
            P(("parts", "sub")),
        ),
        out_specs=(P(("parts", "reader"), "blk", "sub"), P(("parts", "blk", "reader"))),
        check_vma=False,
    )
```

```python
from functools import partial

import jax
import jax.numpy as jnp
from jax import lax
from jax.experimental import pallas as pl
from jax.experimental.pallas import tpu as pltpu
from jax.sharding import PartitionSpec as P

SCORE_VMEM = 20 * 1024 * 1024
SUMS_VMEM = 12 * 1024 * 1024
STEP = 1024
VMEM_SPEC = pl.BlockSpec(memory_space=pltpu.VMEM)
ANY_SPEC = pl.BlockSpec(memory_space=pl.ANY)
SIDES = [(0, 1), (1, 0), (2, 3), (3, 2)]
MIDDLE = [(1, 2), (2, 1)]


def swap_bits(block, axis, bits):
    return lax.ppermute(block, axis, [(i, i ^ bits) for i in range(lax.axis_size(axis))])


def swap_gather(block, axis, bit):
    held = {0: block}
    while bit:
        for k in list(held):
            held[k ^ bit] = swap_bits(held[k], axis, bit)
        bit //= 2
    return [held[k] for k in range(len(held))]


def add_rounded(one, other):
    return (one.astype(jnp.float32) + other.astype(jnp.float32)).astype(jnp.bfloat16)


def staged_gather(block, images, noise, near_bits, far_bit):
    cut = block.shape[1] // 16 * 9
    cuts = [block[:, :cut], block[:, cut:]]
    crossed = swap_bits(images, "reader", far_bit)
    near = swap_gather(images, "reader", near_bits)
    firsts = [
        lax.optimization_barrier(
            (lax.ppermute(one, "blk", SIDES), lax.ppermute(one, "blk", MIDDLE))
        )
        for one in cuts
    ]
    early = stage(
        [[[one] for one in cuts], [[side] for side, _ in firsts]], near, noise
    )
    far_parts, end_parts = [], []
    for side, across in firsts:
        far = lax.ppermute(across, "blk", SIDES)
        side, *_ = lax.optimization_barrier((side, *near))
        across_far = lax.ppermute(side, "blk", MIDDLE)
        far, across_far = lax.optimization_barrier((far, across_far))
        end = lax.ppermute(across_far, "blk", SIDES)
        far_parts.append([far, across_far])
        end_parts.append([end, across])
    weighted, penalty, staged_near, noise = early
    ends = [parts[0] for parts in end_parts]
    crossed, *_ = lax.optimization_barrier((crossed, *ends, *early))
    far = swap_gather(crossed, "reader", near_bits)
    staged = stage_rest([far_parts, end_parts], staged_near, crossed, weighted, penalty, noise)
    return staged, far[1:]


def plain_gather(block, images, noise, near_bits, far_bit):
    near = swap_gather(images, "reader", near_bits)
    far = swap_gather(swap_bits(images, "reader", far_bit), "reader", near_bits)
    line = [[[one]] for one in line_gather(block, "blk")]
    weighted, penalty, near, noise = stage(line[:2], near, noise)
    staged = stage_rest(line[2:], near, far[0], weighted, penalty, noise)
    return staged, far[1:]


def line_gather(block, axis):
    size, member = lax.axis_size(axis), lax.axis_index(axis)
    ahead, behind = [block], [block]
    for s in range(1, size):
        ahead.append(lax.ppermute(ahead[-1], axis, [(i, i + 1) for i in range(s - 1, size - 1)]))
        behind.append(lax.ppermute(behind[-1], axis, [(i, i - 1) for i in range(1, size - s + 1)]))
    blocks = [block]
    for s in range(1, size):
        blocks.append(jnp.where(member >= s, ahead[s], behind[size - s]))
    return blocks


def pair_scatter(pieces, axis):
    member = lax.axis_index(axis)
    is_end = (member == 0) | (member == 3)
    for_far_end = [lax.ppermute(parts[3], axis, SIDES) for parts in pieces]
    *second, for_far_end[0] = lax.optimization_barrier(
        [parts[2] for parts in pieces] + for_far_end[:1]
    )
    for_far_middle = [lax.ppermute(part, axis, SIDES) for part in second]
    totals = []
    for parts, part, end, middle in zip(pieces, second, for_far_end, for_far_middle):
        across_end = lax.ppermute(add_rounded(part, end), axis, MIDDLE)
        across_middle = lax.ppermute(add_rounded(parts[3], middle), axis, MIDDLE)
        near = jnp.where(is_end, parts[1], add_rounded(parts[1], across_end))
        from_side = lax.ppermute(near, axis, SIDES)
        total = parts[0].astype(jnp.float32) + from_side.astype(jnp.float32)
        totals.append(total + jnp.where(is_end, 0.0, across_middle.astype(jnp.float32)))
    return beside(totals)


def put_kernel(start, piece_ref, *refs):
    out_ref, sem = refs[-2:]
    width = piece_ref.shape[1]
    copy = pltpu.make_async_copy(piece_ref, out_ref.at[:, start : start + width], sem)
    copy.start()
    copy.wait()


def put(piece, start, width, out=None):
    operands = [piece] if out is None else [piece, out]
    return pl.pallas_call(
        partial(put_kernel, start),
        out_shape=jax.ShapeDtypeStruct((piece.shape[0], width), piece.dtype),
        in_specs=[VMEM_SPEC, ANY_SPEC][: len(operands)],
        out_specs=ANY_SPEC,
        scratch_shapes=[pltpu.SemaphoreType.DMA],
        input_output_aliases={} if out is None else {1: 0},
        compiler_params=pltpu.CompilerParams(vmem_limit_bytes=SUMS_VMEM),
        name="put",
    )(*operands)


def beside(pieces):
    width = sum(piece.shape[1] for piece in pieces)
    out, start = None, 0
    for piece in pieces:
        out = put(piece, start, width, out)
        start += piece.shape[1]
    return out


def line_scatter(pieces, axis):
    return jnp.concatenate([line_sum(parts, axis) for parts in pieces], axis=1)


def line_sum(parts, axis):
    size = lax.axis_size(axis)
    up = down = None
    for s in range(1, size):
        send_up, send_down = parts[s], parts[size - s]
        if s > 1:
            send_up = add_rounded(send_up, up)
            send_down = add_rounded(send_down, down)
        up = lax.ppermute(send_up, axis, [(i, i + 1) for i in range(0, s) if i + 1 < size])
        down = lax.ppermute(send_down, axis, [(i, i - 1) for i in range(size - s, size) if i > 0])
    total = parts[0].astype(jnp.float32)
    if size > 1:
        total = total + up.astype(jnp.float32) + down.astype(jnp.float32)
    return total


def at_end():
    member = lax.axis_index("blk")
    return (member == 0) | (member == lax.axis_size("blk") - 1)


def either(refs, act):
    if len(refs) == 1:
        act(refs[0])
        return
    is_end = at_end()

    @pl.when(is_end)
    def _():
        act(refs[0])

    @pl.when(jnp.logical_not(is_end))
    def _():
        act(refs[1])


def weigh_blocks(groups, noise_ref, weighted_ref, penalty_ref, block_ref, sems, first):
    count = block_ref.shape[1]
    parts = []
    for s, group in enumerate(groups):
        start = 0
        for refs in group:
            stop = start + refs[0].shape[1]
            parts.append((s, slice(start, stop), refs))
            start = stop

    def part_copy(i, ref):
        s, columns, _ = parts[i]
        return pltpu.make_async_copy(ref, block_ref.at[s, :, columns], sems.at[i])

    for i, (_, _, refs) in enumerate(parts):
        either(refs, lambda ref, i=i: part_copy(i, ref).start())
    for s in range(len(groups)):
        rows = slice((first + s) * count, (first + s + 1) * count)
        penalty = jnp.zeros((count, 1), jnp.float32)
        for i, (t, columns, refs) in enumerate(parts):
            if t != s:
                continue
            part_copy(i, refs[0]).wait()
            for start in range(columns.start, columns.stop, STEP):
                piece = slice(start, min(start + STEP, columns.stop))
                block = block_ref[s, :, piece].astype(jnp.float32)
                scaled = block * noise_ref[:, piece]
                weighted_ref[rows, piece] = scaled.astype(jnp.bfloat16)
                penalty = penalty + 0.5 * jnp.sum(scaled * block, axis=1, keepdims=True)
        penalty_ref[rows, :] = penalty


def take_blocks(refs, counts):
    return [[[refs.pop(0) for _ in range(n)] for n in group] for group in counts]


def block_counts(blocks):
    return [[len(part) for part in group] for group in blocks]


def flat(blocks):
    return [one for group in blocks for part in group for one in part]


def stage_kernel(near_count, counts, *refs):
    refs = list(refs)
    near_refs = [refs.pop(0) for _ in range(near_count)]
    groups = take_blocks(refs, counts)
    noise_ref, weighted_ref, penalty_ref, near_ref, noise_out_ref, block_ref, near_sems, sems = refs
    rows = near_refs[0].shape[0]
    copies = []
    for k, ref in enumerate(near_refs):
        copy = pltpu.make_async_copy(ref, near_ref.at[pl.ds(k * rows, rows), :], near_sems.at[k])
        copy.start()
        copies.append(copy)
    noise_out_ref[...] = noise_ref[...]
    weigh_blocks(groups, noise_ref, weighted_ref, penalty_ref, block_ref, sems, 0)
    for copy in copies:
        copy.wait()


def stage(blocks, near, noise):
    count = blocks[0][0][0].shape[0]
    parts = sum(len(group) for group in blocks)
    width = noise.shape[1]
    refs = len(blocks) * count
    moved = [*near, *flat(blocks)]
    return pl.pallas_call(
        partial(stage_kernel, len(near), block_counts(blocks)),
        out_shape=(
            jax.ShapeDtypeStruct((refs, width), jnp.bfloat16),
            jax.ShapeDtypeStruct((refs, 1), jnp.float32),
            jax.ShapeDtypeStruct((len(near) * near[0].shape[0], width), jnp.bfloat16),
            jax.ShapeDtypeStruct((1, width), jnp.float32),
        ),
        in_specs=[ANY_SPEC] * len(moved) + [VMEM_SPEC],
        out_specs=(VMEM_SPEC,) * 4,
        scratch_shapes=[
            pltpu.VMEM((len(blocks), count, width), jnp.bfloat16),
            pltpu.SemaphoreType.DMA((len(near),)),
            pltpu.SemaphoreType.DMA((parts,)),
        ],
        compiler_params=pltpu.CompilerParams(vmem_limit_bytes=SCORE_VMEM),
        cost_estimate=pl.CostEstimate(
            flops=8 * refs * width, bytes_accessed=12_000_000, transcendentals=0
        ),
        name="stage",
    )(*moved, noise)


def place_images(k, source, all_ref, sem):
    rows = source.shape[0]
    row = pl.multiple_of((lax.axis_index("reader") ^ k) * rows, 16)
    return pltpu.make_async_copy(source, all_ref.at[pl.ds(row, rows), :], sem), pl.ds(row, rows)


def stage_rest_kernel(readers, counts, *refs):
    refs = list(refs)
    groups = take_blocks(refs, counts)
    near_ref, far_ref, early_ref, early_penalty_ref, noise_ref = [refs.pop(0) for _ in range(5)]
    turned_ref, penalty_ref, all_ref, product_ref = refs[:4]
    weighted_ref, block_ref, sems, image_sems = refs[4:]
    rows = far_ref.shape[0]
    half = readers // 2
    sources = [near_ref.at[pl.ds(k * rows, rows), :] for k in range(half)] + [far_ref]
    placed = [place_images(k, one, all_ref, image_sems.at[k]) for k, one in enumerate(sources)]
    for copy, _ in placed:
        copy.start()
    done = early_ref.shape[0]
    weighted_ref[:done, :] = early_ref[...]
    penalty_ref[:done, :] = early_penalty_ref[...]
    first = done // block_ref.shape[1]
    weigh_blocks(groups, noise_ref, weighted_ref, penalty_ref, block_ref, sems, first)
    width = weighted_ref.shape[1]
    for start in range(0, width, STEP):
        piece = slice(start, min(start + STEP, width))
        turned_ref[piece, :] = weighted_ref[:, piece].T
    products = jnp.dot(near_ref[...], turned_ref[...], preferred_element_type=jnp.float32)
    for k in range(half):
        product_ref[placed[k][1], :] = products[k * rows : (k + 1) * rows]
    product_ref[placed[half][1], :] = jnp.dot(
        far_ref[...], turned_ref[...], preferred_element_type=jnp.float32
    )
    for copy, _ in placed:
        copy.wait()


def stage_rest(blocks, near, crossed, weighted, penalty, noise):
    count = blocks[0][0][0].shape[0]
    parts = sum(len(group) for group in blocks)
    width = noise.shape[1]
    refs = len(blocks) * count + weighted.shape[0]
    slots = 2 * near.shape[0]
    readers = slots // crossed.shape[0]
    moved = flat(blocks)
    return pl.pallas_call(
        partial(stage_rest_kernel, readers, block_counts(blocks)),
        out_shape=(
            jax.ShapeDtypeStruct((width, refs), jnp.bfloat16),
            jax.ShapeDtypeStruct((refs, 1), jnp.float32),
            jax.ShapeDtypeStruct((slots, width), jnp.bfloat16),
            jax.ShapeDtypeStruct((slots, refs), jnp.float32),
        ),
        in_specs=[ANY_SPEC] * len(moved) + [VMEM_SPEC] * 5,
        out_specs=(VMEM_SPEC,) * 4,
        scratch_shapes=[
            pltpu.VMEM((refs, width), jnp.bfloat16),
            pltpu.VMEM((len(blocks), count, width), jnp.bfloat16),
            pltpu.SemaphoreType.DMA((parts,)),
            pltpu.SemaphoreType.DMA((readers // 2 + 1,)),
        ],
        compiler_params=pltpu.CompilerParams(vmem_limit_bytes=SCORE_VMEM),
        cost_estimate=pl.CostEstimate(
            flops=8 * refs * width, bytes_accessed=12_000_000, transcendentals=0
        ),
        name="stage_rest",
    )(*moved, near, crossed, weighted, penalty, noise)


def write_packet(packet_ref, scores, route_ref):
    top, rows = route_ref.shape
    peak = jnp.max(scores, axis=0, keepdims=True)
    packet_ref[0:1, :] = peak
    packet_ref[1:2, :] = jnp.sum(jnp.exp(scores - peak), axis=0, keepdims=True)
    packet_ref[2:3, :] = jnp.zeros((1, packet_ref.shape[1]), jnp.float32)
    for t in range(top):
        packet_ref[2:3, t * rows : (t + 1) * rows] = route_ref[t : t + 1, :].astype(jnp.float32)


def score_kernel(readers, finish, *refs):
    refs = list(refs)
    half = readers // 2
    far_refs = [refs.pop(0) for _ in range(half - 1)]
    turned_ref, penalty_ref, _, product_ref, route_ref = refs[:5]
    score_ref, packet_ref, all_ref, sum_ref, image_sems = refs[5:]
    placed = [
        place_images(half + 1 + i, ref, all_ref, image_sems.at[i])
        for i, ref in enumerate(far_refs)
    ]
    for copy, _ in placed:
        copy.start()
    sum_ref[...] = product_ref[...]
    for (_, place), ref in zip(placed, far_refs):
        sum_ref[place, :] = jnp.dot(
            ref[...], turned_ref[...], preferred_element_type=jnp.float32
        )
    scores = sum_ref[...].T - penalty_ref[...]
    score_ref[...] = scores
    if finish:
        write_packet(packet_ref, scores, route_ref)
    for copy, _ in placed:
        copy.wait()


def all_scores(staged, far, routes, finish):
    turned, penalty, images, products = staged
    width, refs = turned.shape
    slots, rows = images.shape[0], far[0].shape[0]
    return pl.pallas_call(
        partial(score_kernel, slots // rows, finish),
        out_shape=(
            jax.ShapeDtypeStruct((refs, slots), jnp.float32),
            jax.ShapeDtypeStruct((3, slots), jnp.float32),
            jax.ShapeDtypeStruct((slots, width), jnp.bfloat16),
        ),
        in_specs=[VMEM_SPEC] * (len(far) + 5),
        out_specs=(VMEM_SPEC,) * 3,
        scratch_shapes=[
            pltpu.VMEM((slots, refs), jnp.float32),
            pltpu.SemaphoreType.DMA((len(far),)),
        ],
        input_output_aliases={len(far) + 2: 2},
        compiler_params=pltpu.CompilerParams(vmem_limit_bytes=SCORE_VMEM),
        cost_estimate=pl.CostEstimate(
            flops=2 * refs * slots * width,
            bytes_accessed=2 * (slots + refs) * width,
            transcendentals=0,
        ),
        name="scores",
    )(*far, turned, penalty, images, products, routes)


def packet_kernel(score_ref, route_ref, packet_ref):
    write_packet(packet_ref, score_ref[...], route_ref)


def make_packet(scores, routes):
    return pl.pallas_call(
        packet_kernel,
        out_shape=jax.ShapeDtypeStruct((3, scores.shape[1]), jnp.float32),
        name="packet",
    )(scores, routes)


def write_routes(packets, rows, route_ref):
    reader = lax.axis_index("reader")
    readers = len(packets)
    for t in range(route_ref.shape[0]):
        routes = [ref[2:3, t * rows : (t + 1) * rows] for ref in packets]
        bit = 1
        while bit < readers:
            flip = (reader & bit) > 0
            routes = [jnp.where(flip, routes[k ^ bit], one) for k, one in enumerate(routes)]
            bit *= 2
        for j, route in enumerate(routes):
            route_ref[t : t + 1, j * rows : (j + 1) * rows] = route


def emit_sums(posterior, all_ref, piece, out_refs):
    sums = jnp.dot(posterior, all_ref[:, piece], preferred_element_type=jnp.float32)
    count = sums.shape[0] // len(out_refs)
    for s, out_ref in enumerate(out_refs):
        out_ref[...] = sums[s * count : (s + 1) * count].astype(out_ref.dtype)


def first_sums_kernel(readers, piece, all_ref, score_ref, *refs):
    refs = list(refs)
    packets = [refs.pop(0) for _ in range(readers)]
    route_ref = refs.pop()
    norm_ref, post_ref, *out_refs = refs
    write_routes(packets, packets[0].shape[1] // readers, route_ref)
    routes = route_ref[...]
    kept, mine = [], None
    for k, packet in enumerate(packets):
        group = (lax.axis_index("reader") ^ k).astype(jnp.float32)
        hits = jnp.where(routes == group, 1.0, 0.0)
        named = jnp.max(hits, axis=0, keepdims=True) > 0.0
        kept.append(jnp.where(named, packet[0:1, :], -jnp.inf))
        mine = named if k == 0 else mine
    highest = kept[0]
    for value in kept[1:]:
        highest = jnp.maximum(highest, value)
    spread = packets[0][1:2, :] * jnp.exp(kept[0] - highest)
    for packet, value in zip(packets[1:], kept[1:]):
        spread = spread + packet[1:2, :] * jnp.exp(value - highest)
    norm = highest + jnp.log(spread)
    norm_ref[...] = norm
    exponent = jnp.where(mine, score_ref[...] - norm, -jnp.inf)
    posterior = jnp.exp(exponent).astype(jnp.bfloat16)
    post_ref[...] = posterior
    emit_sums(posterior, all_ref, piece, out_refs)


def later_sums_kernel(piece, all_ref, post_ref, *out_refs):
    emit_sums(post_ref[...], all_ref, piece, out_refs)


def group_sums(kernel, piece, members, all_images, operands, extra, scratch=()):
    refs, slots = operands[0].shape
    width = piece.stop - piece.start
    block = jax.ShapeDtypeStruct((refs // members, width), jnp.bfloat16)
    outs = pl.pallas_call(
        kernel,
        out_shape=tuple(extra) + (block,) * members,
        in_specs=[VMEM_SPEC] * (1 + len(operands)),
        out_specs=(VMEM_SPEC,) * (len(extra) + members),
        scratch_shapes=scratch,
        compiler_params=pltpu.CompilerParams(vmem_limit_bytes=SUMS_VMEM),
        cost_estimate=pl.CostEstimate(
            flops=2 * refs * slots * width,
            bytes_accessed=2 * slots * width,
            transcendentals=0,
        ),
        name="sums",
    )(all_images, *operands)
    return outs[: len(extra)], outs[len(extra) :]


def on_device(images, routes, projections, noise_weights):
    readers = lax.axis_size("reader")
    members = lax.axis_size("blk")
    reader = lax.axis_index("reader")
    rows, width = images.shape
    noise = noise_weights.reshape(1, width)

    gather = staged_gather if members == 4 and rows % 32 == 0 and readers > 1 else plain_gather
    staged, far = gather(projections[0], images, noise, readers // 4, readers // 2)
    split = lax.axis_size("sub") > 1
    scores, mine, all_images = all_scores(staged, far, routes.T, not split)
    if split:
        scores = lax.psum(scores, "sub")
        mine = make_packet(scores, routes.T)
    packets = [mine] + [swap_bits(mine, "reader", k) for k in range(1, readers)]
    pieces = [slice(0, width // 2), slice(width // 2, width)]
    extra = (
        jax.ShapeDtypeStruct((1, scores.shape[1]), jnp.float32),
        jax.ShapeDtypeStruct(scores.shape, jnp.bfloat16),
    )
    (norms, posterior), first = group_sums(
        partial(first_sums_kernel, readers, pieces[0]),
        pieces[0],
        members,
        all_images,
        (scores, *packets),
        extra,
        (pltpu.VMEM((routes.shape[1], scores.shape[1]), jnp.float32),),
    )
    _, last = group_sums(
        partial(later_sums_kernel, pieces[1]), pieces[1], members, all_images, (posterior,), ()
    )
    parts = [first, last]
    scatter = pair_scatter if members == 4 else line_scatter
    total = scatter(parts, "blk")
    normalizer = lax.dynamic_slice(norms.reshape(-1), (reader * rows,), (rows,))
    return (total[None], normalizer)


def solution(mesh):
    return jax.shard_map(
        on_device,
        mesh=mesh,
        in_specs=(
            P(("parts", "blk", "reader"), "sub"),
            P(("parts", "blk", "reader"), None),
            P(("parts", "reader"), "blk", "sub"),
            P(("parts", "sub")),
        ),
        out_specs=(P(("parts", "reader"), "blk", "sub"), P(("parts", "blk", "reader"))),
        check_vma=False,
    )
```

```python
from functools import partial

import jax
import jax.numpy as jnp
from jax import lax
from jax.experimental import pallas as pl
from jax.experimental.pallas import tpu as pltpu
from jax.sharding import PartitionSpec as P

SCORE_VMEM = 20 * 1024 * 1024
SUMS_VMEM = 12 * 1024 * 1024
STEP = 1024
VMEM_SPEC = pl.BlockSpec(memory_space=pltpu.VMEM)
ANY_SPEC = pl.BlockSpec(memory_space=pl.ANY)
SIDES = [(0, 1), (1, 0), (2, 3), (3, 2)]
MIDDLE = [(1, 2), (2, 1)]


def swap_bits(block, axis, bits):
    return lax.ppermute(block, axis, [(i, i ^ bits) for i in range(lax.axis_size(axis))])


def swap_gather(block, axis, bit):
    held = {0: block}
    while bit:
        for k in list(held):
            held[k ^ bit] = swap_bits(held[k], axis, bit)
        bit //= 2
    return [held[k] for k in range(len(held))]


def add_rounded(one, other):
    return (one.astype(jnp.float32) + other.astype(jnp.float32)).astype(jnp.bfloat16)


def staged_gather(block, images, noise, near_bits, far_bit):
    cut = block.shape[1] // 32 * 17
    cuts = [block[:, :cut], block[:, cut:]]
    crossed = swap_bits(images, "reader", far_bit)
    near = swap_gather(images, "reader", near_bits)
    firsts = [
        lax.optimization_barrier(
            (lax.ppermute(one, "blk", SIDES), lax.ppermute(one, "blk", MIDDLE))
        )
        for one in cuts
    ]
    early = stage(
        [[[one] for one in cuts], [[side] for side, _ in firsts]], near, noise
    )
    far_parts, end_parts = [], []
    for side, across in firsts:
        far = lax.ppermute(across, "blk", SIDES)
        side, *_ = lax.optimization_barrier((side, *near))
        across_far = lax.ppermute(side, "blk", MIDDLE)
        far, across_far = lax.optimization_barrier((far, across_far))
        end = lax.ppermute(across_far, "blk", SIDES)
        far_parts.append([far, across_far])
        end_parts.append([end, across])
    weighted, penalty, staged_near, noise = early
    ends = [parts[0] for parts in end_parts]
    crossed, *_ = lax.optimization_barrier((crossed, *ends, *early))
    far = swap_gather(crossed, "reader", near_bits)
    staged = stage_rest([far_parts, end_parts], staged_near, crossed, weighted, penalty, noise)
    return staged, far[1:]


def plain_gather(block, images, noise, near_bits, far_bit):
    near = swap_gather(images, "reader", near_bits)
    far = swap_gather(swap_bits(images, "reader", far_bit), "reader", near_bits)
    line = [[[one]] for one in line_gather(block, "blk")]
    weighted, penalty, near, noise = stage(line[:2], near, noise)
    staged = stage_rest(line[2:], near, far[0], weighted, penalty, noise)
    return staged, far[1:]


def line_gather(block, axis):
    size, member = lax.axis_size(axis), lax.axis_index(axis)
    ahead, behind = [block], [block]
    for s in range(1, size):
        ahead.append(lax.ppermute(ahead[-1], axis, [(i, i + 1) for i in range(s - 1, size - 1)]))
        behind.append(lax.ppermute(behind[-1], axis, [(i, i - 1) for i in range(1, size - s + 1)]))
    blocks = [block]
    for s in range(1, size):
        blocks.append(jnp.where(member >= s, ahead[s], behind[size - s]))
    return blocks


def pair_scatter(pieces, axis):
    member = lax.axis_index(axis)
    is_end = (member == 0) | (member == 3)
    for_far_end = [lax.ppermute(parts[3], axis, SIDES) for parts in pieces]
    *second, for_far_end[0] = lax.optimization_barrier(
        [parts[2] for parts in pieces] + for_far_end[:1]
    )
    for_far_middle = [lax.ppermute(part, axis, SIDES) for part in second]
    totals = []
    for parts, part, end, middle in zip(pieces, second, for_far_end, for_far_middle):
        across_end = lax.ppermute(add_rounded(part, end), axis, MIDDLE)
        across_middle = lax.ppermute(add_rounded(parts[3], middle), axis, MIDDLE)
        near = jnp.where(is_end, parts[1], add_rounded(parts[1], across_end))
        from_side = lax.ppermute(near, axis, SIDES)
        total = parts[0].astype(jnp.float32) + from_side.astype(jnp.float32)
        totals.append(total + jnp.where(is_end, 0.0, across_middle.astype(jnp.float32)))
    return beside(totals)


def put_kernel(start, piece_ref, *refs):
    out_ref, sem = refs[-2:]
    width = piece_ref.shape[1]
    copy = pltpu.make_async_copy(piece_ref, out_ref.at[:, start : start + width], sem)
    copy.start()
    copy.wait()


def put(piece, start, width, out=None):
    operands = [piece] if out is None else [piece, out]
    return pl.pallas_call(
        partial(put_kernel, start),
        out_shape=jax.ShapeDtypeStruct((piece.shape[0], width), piece.dtype),
        in_specs=[VMEM_SPEC, ANY_SPEC][: len(operands)],
        out_specs=ANY_SPEC,
        scratch_shapes=[pltpu.SemaphoreType.DMA],
        input_output_aliases={} if out is None else {1: 0},
        compiler_params=pltpu.CompilerParams(vmem_limit_bytes=SUMS_VMEM),
        name="put",
    )(*operands)


def beside(pieces):
    width = sum(piece.shape[1] for piece in pieces)
    out, start = None, 0
    for piece in pieces:
        out = put(piece, start, width, out)
        start += piece.shape[1]
    return out


def line_scatter(pieces, axis):
    return jnp.concatenate([line_sum(parts, axis) for parts in pieces], axis=1)


def line_sum(parts, axis):
    size = lax.axis_size(axis)
    up = down = None
    for s in range(1, size):
        send_up, send_down = parts[s], parts[size - s]
        if s > 1:
            send_up = add_rounded(send_up, up)
            send_down = add_rounded(send_down, down)
        up = lax.ppermute(send_up, axis, [(i, i + 1) for i in range(0, s) if i + 1 < size])
        down = lax.ppermute(send_down, axis, [(i, i - 1) for i in range(size - s, size) if i > 0])
    total = parts[0].astype(jnp.float32)
    if size > 1:
        total = total + up.astype(jnp.float32) + down.astype(jnp.float32)
    return total


def at_end():
    member = lax.axis_index("blk")
    return (member == 0) | (member == lax.axis_size("blk") - 1)


def either(refs, act):
    if len(refs) == 1:
        act(refs[0])
        return
    is_end = at_end()

    @pl.when(is_end)
    def _():
        act(refs[0])

    @pl.when(jnp.logical_not(is_end))
    def _():
        act(refs[1])


def weigh_blocks(groups, noise_ref, weighted_ref, penalty_ref, block_ref, sems, first):
    count = block_ref.shape[1]
    parts = []
    for s, group in enumerate(groups):
        start = 0
        for refs in group:
            stop = start + refs[0].shape[1]
            parts.append((s, slice(start, stop), refs))
            start = stop

    def part_copy(i, ref):
        s, columns, _ = parts[i]
        return pltpu.make_async_copy(ref, block_ref.at[s, :, columns], sems.at[i])

    for i, (_, _, refs) in enumerate(parts):
        either(refs, lambda ref, i=i: part_copy(i, ref).start())
    for s in range(len(groups)):
        rows = slice((first + s) * count, (first + s + 1) * count)
        penalty = jnp.zeros((count, 1), jnp.float32)
        for i, (t, columns, refs) in enumerate(parts):
            if t != s:
                continue
            part_copy(i, refs[0]).wait()
            for start in range(columns.start, columns.stop, STEP):
                piece = slice(start, min(start + STEP, columns.stop))
                block = block_ref[s, :, piece].astype(jnp.float32)
                scaled = block * noise_ref[:, piece]
                weighted_ref[rows, piece] = scaled.astype(jnp.bfloat16)
                penalty = penalty + 0.5 * jnp.sum(scaled * block, axis=1, keepdims=True)
        penalty_ref[rows, :] = penalty


def take_blocks(refs, counts):
    return [[[refs.pop(0) for _ in range(n)] for n in group] for group in counts]


def block_counts(blocks):
    return [[len(part) for part in group] for group in blocks]


def flat(blocks):
    return [one for group in blocks for part in group for one in part]


def stage_kernel(near_count, counts, *refs):
    refs = list(refs)
    near_refs = [refs.pop(0) for _ in range(near_count)]
    groups = take_blocks(refs, counts)
    noise_ref, weighted_ref, penalty_ref, near_ref, noise_out_ref, block_ref, near_sems, sems = refs
    rows = near_refs[0].shape[0]
    copies = []
    for k, ref in enumerate(near_refs):
        copy = pltpu.make_async_copy(ref, near_ref.at[pl.ds(k * rows, rows), :], near_sems.at[k])
        copy.start()
        copies.append(copy)
    noise_out_ref[...] = noise_ref[...]
    weigh_blocks(groups, noise_ref, weighted_ref, penalty_ref, block_ref, sems, 0)
    for copy in copies:
        copy.wait()


def stage(blocks, near, noise):
    count = blocks[0][0][0].shape[0]
    parts = sum(len(group) for group in blocks)
    width = noise.shape[1]
    refs = len(blocks) * count
    moved = [*near, *flat(blocks)]
    return pl.pallas_call(
        partial(stage_kernel, len(near), block_counts(blocks)),
        out_shape=(
            jax.ShapeDtypeStruct((refs, width), jnp.bfloat16),
            jax.ShapeDtypeStruct((refs, 1), jnp.float32),
            jax.ShapeDtypeStruct((len(near) * near[0].shape[0], width), jnp.bfloat16),
            jax.ShapeDtypeStruct((1, width), jnp.float32),
        ),
        in_specs=[ANY_SPEC] * len(moved) + [VMEM_SPEC],
        out_specs=(VMEM_SPEC,) * 4,
        scratch_shapes=[
            pltpu.VMEM((len(blocks), count, width), jnp.bfloat16),
            pltpu.SemaphoreType.DMA((len(near),)),
            pltpu.SemaphoreType.DMA((parts,)),
        ],
        compiler_params=pltpu.CompilerParams(vmem_limit_bytes=SCORE_VMEM),
        cost_estimate=pl.CostEstimate(
            flops=8 * refs * width, bytes_accessed=12_000_000, transcendentals=0
        ),
        name="stage",
    )(*moved, noise)


def place_images(k, source, all_ref, sem):
    rows = source.shape[0]
    row = pl.multiple_of((lax.axis_index("reader") ^ k) * rows, 16)
    return pltpu.make_async_copy(source, all_ref.at[pl.ds(row, rows), :], sem), pl.ds(row, rows)


def stage_rest_kernel(readers, counts, *refs):
    refs = list(refs)
    groups = take_blocks(refs, counts)
    near_ref, far_ref, early_ref, early_penalty_ref, noise_ref = [refs.pop(0) for _ in range(5)]
    turned_ref, penalty_ref, all_ref, product_ref = refs[:4]
    weighted_ref, block_ref, sems, image_sems = refs[4:]
    rows = far_ref.shape[0]
    half = readers // 2
    sources = [near_ref.at[pl.ds(k * rows, rows), :] for k in range(half)] + [far_ref]
    placed = [place_images(k, one, all_ref, image_sems.at[k]) for k, one in enumerate(sources)]
    for copy, _ in placed:
        copy.start()
    done = early_ref.shape[0]
    weighted_ref[:done, :] = early_ref[...]
    penalty_ref[:done, :] = early_penalty_ref[...]
    first = done // block_ref.shape[1]
    weigh_blocks(groups, noise_ref, weighted_ref, penalty_ref, block_ref, sems, first)
    width = weighted_ref.shape[1]
    for start in range(0, width, STEP):
        piece = slice(start, min(start + STEP, width))
        turned_ref[piece, :] = weighted_ref[:, piece].T
    products = jnp.dot(near_ref[...], turned_ref[...], preferred_element_type=jnp.float32)
    for k in range(half):
        product_ref[placed[k][1], :] = products[k * rows : (k + 1) * rows]
    product_ref[placed[half][1], :] = jnp.dot(
        far_ref[...], turned_ref[...], preferred_element_type=jnp.float32
    )
    for copy, _ in placed:
        copy.wait()


def stage_rest(blocks, near, crossed, weighted, penalty, noise):
    count = blocks[0][0][0].shape[0]
    parts = sum(len(group) for group in blocks)
    width = noise.shape[1]
    refs = len(blocks) * count + weighted.shape[0]
    slots = 2 * near.shape[0]
    readers = slots // crossed.shape[0]
    moved = flat(blocks)
    return pl.pallas_call(
        partial(stage_rest_kernel, readers, block_counts(blocks)),
        out_shape=(
            jax.ShapeDtypeStruct((width, refs), jnp.bfloat16),
            jax.ShapeDtypeStruct((refs, 1), jnp.float32),
            jax.ShapeDtypeStruct((slots, width), jnp.bfloat16),
            jax.ShapeDtypeStruct((slots, refs), jnp.float32),
        ),
        in_specs=[ANY_SPEC] * len(moved) + [VMEM_SPEC] * 5,
        out_specs=(VMEM_SPEC,) * 4,
        scratch_shapes=[
            pltpu.VMEM((refs, width), jnp.bfloat16),
            pltpu.VMEM((len(blocks), count, width), jnp.bfloat16),
            pltpu.SemaphoreType.DMA((parts,)),
            pltpu.SemaphoreType.DMA((readers // 2 + 1,)),
        ],
        compiler_params=pltpu.CompilerParams(vmem_limit_bytes=SCORE_VMEM),
        cost_estimate=pl.CostEstimate(
            flops=8 * refs * width, bytes_accessed=12_000_000, transcendentals=0
        ),
        name="stage_rest",
    )(*moved, near, crossed, weighted, penalty, noise)


def write_packet(packet_ref, scores, route_ref):
    top, rows = route_ref.shape
    peak = jnp.max(scores, axis=0, keepdims=True)
    packet_ref[0:1, :] = peak
    packet_ref[1:2, :] = jnp.sum(jnp.exp(scores - peak), axis=0, keepdims=True)
    packet_ref[2:3, :] = jnp.zeros((1, packet_ref.shape[1]), jnp.float32)
    for t in range(top):
        packet_ref[2:3, t * rows : (t + 1) * rows] = route_ref[t : t + 1, :].astype(jnp.float32)


def score_kernel(readers, finish, *refs):
    refs = list(refs)
    half = readers // 2
    far_refs = [refs.pop(0) for _ in range(half - 1)]
    turned_ref, penalty_ref, _, product_ref, route_ref = refs[:5]
    score_ref, packet_ref, all_ref, sum_ref, image_sems = refs[5:]
    placed = [
        place_images(half + 1 + i, ref, all_ref, image_sems.at[i])
        for i, ref in enumerate(far_refs)
    ]
    for copy, _ in placed:
        copy.start()
    sum_ref[...] = product_ref[...]
    for (_, place), ref in zip(placed, far_refs):
        sum_ref[place, :] = jnp.dot(
            ref[...], turned_ref[...], preferred_element_type=jnp.float32
        )
    scores = sum_ref[...].T - penalty_ref[...]
    score_ref[...] = scores
    if finish:
        write_packet(packet_ref, scores, route_ref)
    for copy, _ in placed:
        copy.wait()


def all_scores(staged, far, routes, finish):
    turned, penalty, images, products = staged
    width, refs = turned.shape
    slots, rows = images.shape[0], far[0].shape[0]
    return pl.pallas_call(
        partial(score_kernel, slots // rows, finish),
        out_shape=(
            jax.ShapeDtypeStruct((refs, slots), jnp.float32),
            jax.ShapeDtypeStruct((3, slots), jnp.float32),
            jax.ShapeDtypeStruct((slots, width), jnp.bfloat16),
        ),
        in_specs=[VMEM_SPEC] * (len(far) + 5),
        out_specs=(VMEM_SPEC,) * 3,
        scratch_shapes=[
            pltpu.VMEM((slots, refs), jnp.float32),
            pltpu.SemaphoreType.DMA((len(far),)),
        ],
        input_output_aliases={len(far) + 2: 2},
        compiler_params=pltpu.CompilerParams(vmem_limit_bytes=SCORE_VMEM),
        cost_estimate=pl.CostEstimate(
            flops=2 * refs * slots * width,
            bytes_accessed=2 * (slots + refs) * width,
            transcendentals=0,
        ),
        name="scores",
    )(*far, turned, penalty, images, products, routes)


def packet_kernel(score_ref, route_ref, packet_ref):
    write_packet(packet_ref, score_ref[...], route_ref)


def make_packet(scores, routes):
    return pl.pallas_call(
        packet_kernel,
        out_shape=jax.ShapeDtypeStruct((3, scores.shape[1]), jnp.float32),
        name="packet",
    )(scores, routes)


def write_routes(packets, rows, route_ref):
    reader = lax.axis_index("reader")
    readers = len(packets)
    for t in range(route_ref.shape[0]):
        routes = [ref[2:3, t * rows : (t + 1) * rows] for ref in packets]
        bit = 1
        while bit < readers:
            flip = (reader & bit) > 0
            routes = [jnp.where(flip, routes[k ^ bit], one) for k, one in enumerate(routes)]
            bit *= 2
        for j, route in enumerate(routes):
            route_ref[t : t + 1, j * rows : (j + 1) * rows] = route


def emit_sums(posterior, all_ref, piece, out_refs):
    sums = jnp.dot(posterior, all_ref[:, piece], preferred_element_type=jnp.float32)
    count = sums.shape[0] // len(out_refs)
    for s, out_ref in enumerate(out_refs):
        out_ref[...] = sums[s * count : (s + 1) * count].astype(out_ref.dtype)


def first_sums_kernel(readers, piece, all_ref, score_ref, *refs):
    refs = list(refs)
    packets = [refs.pop(0) for _ in range(readers)]
    route_ref = refs.pop()
    norm_ref, post_ref, *out_refs = refs
    write_routes(packets, packets[0].shape[1] // readers, route_ref)
    routes = route_ref[...]
    kept, mine = [], None
    for k, packet in enumerate(packets):
        group = (lax.axis_index("reader") ^ k).astype(jnp.float32)
        hits = jnp.where(routes == group, 1.0, 0.0)
        named = jnp.max(hits, axis=0, keepdims=True) > 0.0
        kept.append(jnp.where(named, packet[0:1, :], -jnp.inf))
        mine = named if k == 0 else mine
    highest = kept[0]
    for value in kept[1:]:
        highest = jnp.maximum(highest, value)
    spread = packets[0][1:2, :] * jnp.exp(kept[0] - highest)
    for packet, value in zip(packets[1:], kept[1:]):
        spread = spread + packet[1:2, :] * jnp.exp(value - highest)
    norm = highest + jnp.log(spread)
    norm_ref[...] = norm
    exponent = jnp.where(mine, score_ref[...] - norm, -jnp.inf)
    posterior = jnp.exp(exponent).astype(jnp.bfloat16)
    post_ref[...] = posterior
    emit_sums(posterior, all_ref, piece, out_refs)


def later_sums_kernel(piece, all_ref, post_ref, *out_refs):
    emit_sums(post_ref[...], all_ref, piece, out_refs)


def group_sums(kernel, piece, members, all_images, operands, extra, scratch=()):
    refs, slots = operands[0].shape
    width = piece.stop - piece.start
    block = jax.ShapeDtypeStruct((refs // members, width), jnp.bfloat16)
    outs = pl.pallas_call(
        kernel,
        out_shape=tuple(extra) + (block,) * members,
        in_specs=[VMEM_SPEC] * (1 + len(operands)),
        out_specs=(VMEM_SPEC,) * (len(extra) + members),
        scratch_shapes=scratch,
        compiler_params=pltpu.CompilerParams(vmem_limit_bytes=SUMS_VMEM),
        cost_estimate=pl.CostEstimate(
            flops=2 * refs * slots * width,
            bytes_accessed=2 * slots * width,
            transcendentals=0,
        ),
        name="sums",
    )(all_images, *operands)
    return outs[: len(extra)], outs[len(extra) :]


def on_device(images, routes, projections, noise_weights):
    readers = lax.axis_size("reader")
    members = lax.axis_size("blk")
    reader = lax.axis_index("reader")
    rows, width = images.shape
    noise = noise_weights.reshape(1, width)

    gather = staged_gather if members == 4 and rows % 32 == 0 and readers > 1 else plain_gather
    staged, far = gather(projections[0], images, noise, readers // 4, readers // 2)
    split = lax.axis_size("sub") > 1
    scores, mine, all_images = all_scores(staged, far, routes.T, not split)
    if split:
        scores = lax.psum(scores, "sub")
        mine = make_packet(scores, routes.T)
    packets = [mine] + [swap_bits(mine, "reader", k) for k in range(1, readers)]
    pieces = [slice(0, width // 2), slice(width // 2, width)]
    extra = (
        jax.ShapeDtypeStruct((1, scores.shape[1]), jnp.float32),
        jax.ShapeDtypeStruct(scores.shape, jnp.bfloat16),
    )
    (norms, posterior), first = group_sums(
        partial(first_sums_kernel, readers, pieces[0]),
        pieces[0],
        members,
        all_images,
        (scores, *packets),
        extra,
        (pltpu.VMEM((routes.shape[1], scores.shape[1]), jnp.float32),),
    )
    _, last = group_sums(
        partial(later_sums_kernel, pieces[1]), pieces[1], members, all_images, (posterior,), ()
    )
    parts = [first, last]
    scatter = pair_scatter if members == 4 else line_scatter
    total = scatter(parts, "blk")
    normalizer = lax.dynamic_slice(norms.reshape(-1), (reader * rows,), (rows,))
    return (total[None], normalizer)


def solution(mesh):
    return jax.shard_map(
        on_device,
        mesh=mesh,
        in_specs=(
            P(("parts", "blk", "reader"), "sub"),
            P(("parts", "blk", "reader"), None),
            P(("parts", "reader"), "blk", "sub"),
            P(("parts", "sub")),
        ),
        out_specs=(P(("parts", "reader"), "blk", "sub"), P(("parts", "blk", "reader"))),
        check_vma=False,
    )
```

```python
from functools import partial

import jax
import jax.numpy as jnp
from jax import lax
from jax.experimental import pallas as pl
from jax.experimental.pallas import tpu as pltpu
from jax.sharding import PartitionSpec as P

SCORE_VMEM = 20 * 1024 * 1024
SUMS_VMEM = 12 * 1024 * 1024
STEP = 1024
VMEM_SPEC = pl.BlockSpec(memory_space=pltpu.VMEM)
ANY_SPEC = pl.BlockSpec(memory_space=pl.ANY)
SIDES = [(0, 1), (1, 0), (2, 3), (3, 2)]
MIDDLE = [(1, 2), (2, 1)]


def swap_bits(block, axis, bits):
    return lax.ppermute(block, axis, [(i, i ^ bits) for i in range(lax.axis_size(axis))])


def swap_gather(block, axis, bit):
    held = {0: block}
    while bit:
        for k in list(held):
            held[k ^ bit] = swap_bits(held[k], axis, bit)
        bit //= 2
    return [held[k] for k in range(len(held))]


def add_rounded(one, other):
    return (one.astype(jnp.float32) + other.astype(jnp.float32)).astype(jnp.bfloat16)


def staged_gather(block, images, noise, near_bits, far_bit):
    cut = block.shape[1] // 16 * 9
    cuts = [block[:, :cut], block[:, cut:]]
    crossed = swap_bits(images, "reader", far_bit)
    near = swap_gather(images, "reader", near_bits)
    firsts = [(lax.ppermute(one, "blk", SIDES), lax.ppermute(one, "blk", MIDDLE)) for one in cuts]
    firsts[0] = lax.optimization_barrier(firsts[0])
    early = stage(
        [[[one] for one in cuts], [[side] for side, _ in firsts]], near, noise
    )
    far_parts, end_parts = [], []
    for side, across in firsts:
        far = lax.ppermute(across, "blk", SIDES)
        side, *_ = lax.optimization_barrier((side, *near))
        across_far = lax.ppermute(side, "blk", MIDDLE)
        far, across_far = lax.optimization_barrier((far, across_far))
        end = lax.ppermute(across_far, "blk", SIDES)
        far_parts.append([far, across_far])
        end_parts.append([end, across])
    weighted, penalty, staged_near, noise = early
    ends = [parts[0] for parts in end_parts]
    crossed, *_ = lax.optimization_barrier((crossed, *ends, *early))
    far = swap_gather(crossed, "reader", near_bits)
    staged = stage_rest([far_parts, end_parts], staged_near, crossed, weighted, penalty, noise)
    return staged, far[1:]


def plain_gather(block, images, noise, near_bits, far_bit):
    near = swap_gather(images, "reader", near_bits)
    far = swap_gather(swap_bits(images, "reader", far_bit), "reader", near_bits)
    line = [[[one]] for one in line_gather(block, "blk")]
    weighted, penalty, near, noise = stage(line[:2], near, noise)
    staged = stage_rest(line[2:], near, far[0], weighted, penalty, noise)
    return staged, far[1:]


def line_gather(block, axis):
    size, member = lax.axis_size(axis), lax.axis_index(axis)
    ahead, behind = [block], [block]
    for s in range(1, size):
        ahead.append(lax.ppermute(ahead[-1], axis, [(i, i + 1) for i in range(s - 1, size - 1)]))
        behind.append(lax.ppermute(behind[-1], axis, [(i, i - 1) for i in range(1, size - s + 1)]))
    blocks = [block]
    for s in range(1, size):
        blocks.append(jnp.where(member >= s, ahead[s], behind[size - s]))
    return blocks


def pair_scatter(pieces, axis):
    member = lax.axis_index(axis)
    is_end = (member == 0) | (member == 3)
    for_far_end = [lax.ppermute(parts[3], axis, SIDES) for parts in pieces]
    *second, for_far_end[0] = lax.optimization_barrier(
        [parts[2] for parts in pieces] + for_far_end[:1]
    )
    for_far_middle = [lax.ppermute(part, axis, SIDES) for part in second]
    totals = []
    for parts, part, end, middle in zip(pieces, second, for_far_end, for_far_middle):
        across_end = lax.ppermute(add_rounded(part, end), axis, MIDDLE)
        across_middle = lax.ppermute(add_rounded(parts[3], middle), axis, MIDDLE)
        near = jnp.where(is_end, parts[1], add_rounded(parts[1], across_end))
        from_side = lax.ppermute(near, axis, SIDES)
        total = parts[0].astype(jnp.float32) + from_side.astype(jnp.float32)
        totals.append(total + jnp.where(is_end, 0.0, across_middle.astype(jnp.float32)))
    return beside(totals)


def put_kernel(start, piece_ref, *refs):
    out_ref, sem = refs[-2:]
    width = piece_ref.shape[1]
    copy = pltpu.make_async_copy(piece_ref, out_ref.at[:, start : start + width], sem)
    copy.start()
    copy.wait()


def put(piece, start, width, out=None):
    operands = [piece] if out is None else [piece, out]
    return pl.pallas_call(
        partial(put_kernel, start),
        out_shape=jax.ShapeDtypeStruct((piece.shape[0], width), piece.dtype),
        in_specs=[VMEM_SPEC, ANY_SPEC][: len(operands)],
        out_specs=ANY_SPEC,
        scratch_shapes=[pltpu.SemaphoreType.DMA],
        input_output_aliases={} if out is None else {1: 0},
        compiler_params=pltpu.CompilerParams(vmem_limit_bytes=SUMS_VMEM),
        name="put",
    )(*operands)


def beside(pieces):
    width = sum(piece.shape[1] for piece in pieces)
    out, start = None, 0
    for piece in pieces:
        out = put(piece, start, width, out)
        start += piece.shape[1]
    return out


def line_scatter(pieces, axis):
    return jnp.concatenate([line_sum(parts, axis) for parts in pieces], axis=1)


def line_sum(parts, axis):
    size = lax.axis_size(axis)
    up = down = None
    for s in range(1, size):
        send_up, send_down = parts[s], parts[size - s]
        if s > 1:
            send_up = add_rounded(send_up, up)
            send_down = add_rounded(send_down, down)
        up = lax.ppermute(send_up, axis, [(i, i + 1) for i in range(0, s) if i + 1 < size])
        down = lax.ppermute(send_down, axis, [(i, i - 1) for i in range(size - s, size) if i > 0])
    total = parts[0].astype(jnp.float32)
    if size > 1:
        total = total + up.astype(jnp.float32) + down.astype(jnp.float32)
    return total


def at_end():
    member = lax.axis_index("blk")
    return (member == 0) | (member == lax.axis_size("blk") - 1)


def either(refs, act):
    if len(refs) == 1:
        act(refs[0])
        return
    is_end = at_end()

    @pl.when(is_end)
    def _():
        act(refs[0])

    @pl.when(jnp.logical_not(is_end))
    def _():
        act(refs[1])


def weigh_blocks(groups, noise_ref, weighted_ref, penalty_ref, block_ref, sems, first):
    count = block_ref.shape[1]
    parts = []
    for s, group in enumerate(groups):
        start = 0
        for refs in group:
            stop = start + refs[0].shape[1]
            parts.append((s, slice(start, stop), refs))
            start = stop

    def part_copy(i, ref):
        s, columns, _ = parts[i]
        return pltpu.make_async_copy(ref, block_ref.at[s, :, columns], sems.at[i])

    for i, (_, _, refs) in enumerate(parts):
        either(refs, lambda ref, i=i: part_copy(i, ref).start())
    for s in range(len(groups)):
        rows = slice((first + s) * count, (first + s + 1) * count)
        penalty = jnp.zeros((count, 1), jnp.float32)
        for i, (t, columns, refs) in enumerate(parts):
            if t != s:
                continue
            part_copy(i, refs[0]).wait()
            for start in range(columns.start, columns.stop, STEP):
                piece = slice(start, min(start + STEP, columns.stop))
                block = block_ref[s, :, piece].astype(jnp.float32)
                scaled = block * noise_ref[:, piece]
                weighted_ref[rows, piece] = scaled.astype(jnp.bfloat16)
                penalty = penalty + 0.5 * jnp.sum(scaled * block, axis=1, keepdims=True)
        penalty_ref[rows, :] = penalty


def take_blocks(refs, counts):
    return [[[refs.pop(0) for _ in range(n)] for n in group] for group in counts]


def block_counts(blocks):
    return [[len(part) for part in group] for group in blocks]


def flat(blocks):
    return [one for group in blocks for part in group for one in part]


def stage_kernel(near_count, counts, *refs):
    refs = list(refs)
    near_refs = [refs.pop(0) for _ in range(near_count)]
    groups = take_blocks(refs, counts)
    noise_ref, weighted_ref, penalty_ref, near_ref, noise_out_ref, block_ref, near_sems, sems = refs
    rows = near_refs[0].shape[0]
    copies = []
    for k, ref in enumerate(near_refs):
        copy = pltpu.make_async_copy(ref, near_ref.at[pl.ds(k * rows, rows), :], near_sems.at[k])
        copy.start()
        copies.append(copy)
    noise_out_ref[...] = noise_ref[...]
    weigh_blocks(groups, noise_ref, weighted_ref, penalty_ref, block_ref, sems, 0)
    for copy in copies:
        copy.wait()


def stage(blocks, near, noise):
    count = blocks[0][0][0].shape[0]
    parts = sum(len(group) for group in blocks)
    width = noise.shape[1]
    refs = len(blocks) * count
    moved = [*near, *flat(blocks)]
    return pl.pallas_call(
        partial(stage_kernel, len(near), block_counts(blocks)),
        out_shape=(
            jax.ShapeDtypeStruct((refs, width), jnp.bfloat16),
            jax.ShapeDtypeStruct((refs, 1), jnp.float32),
            jax.ShapeDtypeStruct((len(near) * near[0].shape[0], width), jnp.bfloat16),
            jax.ShapeDtypeStruct((1, width), jnp.float32),
        ),
        in_specs=[ANY_SPEC] * len(moved) + [VMEM_SPEC],
        out_specs=(VMEM_SPEC,) * 4,
        scratch_shapes=[
            pltpu.VMEM((len(blocks), count, width), jnp.bfloat16),
            pltpu.SemaphoreType.DMA((len(near),)),
            pltpu.SemaphoreType.DMA((parts,)),
        ],
        compiler_params=pltpu.CompilerParams(vmem_limit_bytes=SCORE_VMEM),
        cost_estimate=pl.CostEstimate(
            flops=8 * refs * width, bytes_accessed=12_000_000, transcendentals=0
        ),
        name="stage",
    )(*moved, noise)


def place_images(k, source, all_ref, sem):
    rows = source.shape[0]
    row = pl.multiple_of((lax.axis_index("reader") ^ k) * rows, 16)
    return pltpu.make_async_copy(source, all_ref.at[pl.ds(row, rows), :], sem), pl.ds(row, rows)


def stage_rest_kernel(readers, counts, *refs):
    refs = list(refs)
    groups = take_blocks(refs, counts)
    near_ref, far_ref, early_ref, early_penalty_ref, noise_ref = [refs.pop(0) for _ in range(5)]
    turned_ref, penalty_ref, all_ref, product_ref = refs[:4]
    weighted_ref, block_ref, sems, image_sems = refs[4:]
    rows = far_ref.shape[0]
    half = readers // 2
    sources = [near_ref.at[pl.ds(k * rows, rows), :] for k in range(half)] + [far_ref]
    placed = [place_images(k, one, all_ref, image_sems.at[k]) for k, one in enumerate(sources)]
    for copy, _ in placed:
        copy.start()
    done = early_ref.shape[0]
    weighted_ref[:done, :] = early_ref[...]
    penalty_ref[:done, :] = early_penalty_ref[...]
    first = done // block_ref.shape[1]
    weigh_blocks(groups, noise_ref, weighted_ref, penalty_ref, block_ref, sems, first)
    width = weighted_ref.shape[1]
    for start in range(0, width, STEP):
        piece = slice(start, min(start + STEP, width))
        turned_ref[piece, :] = weighted_ref[:, piece].T
    products = jnp.dot(near_ref[...], turned_ref[...], preferred_element_type=jnp.float32)
    for k in range(half):
        product_ref[placed[k][1], :] = products[k * rows : (k + 1) * rows]
    product_ref[placed[half][1], :] = jnp.dot(
        far_ref[...], turned_ref[...], preferred_element_type=jnp.float32
    )
    for copy, _ in placed:
        copy.wait()


def stage_rest(blocks, near, crossed, weighted, penalty, noise):
    count = blocks[0][0][0].shape[0]
    parts = sum(len(group) for group in blocks)
    width = noise.shape[1]
    refs = len(blocks) * count + weighted.shape[0]
    slots = 2 * near.shape[0]
    readers = slots // crossed.shape[0]
    moved = flat(blocks)
    return pl.pallas_call(
        partial(stage_rest_kernel, readers, block_counts(blocks)),
        out_shape=(
            jax.ShapeDtypeStruct((width, refs), jnp.bfloat16),
            jax.ShapeDtypeStruct((refs, 1), jnp.float32),
            jax.ShapeDtypeStruct((slots, width), jnp.bfloat16),
            jax.ShapeDtypeStruct((slots, refs), jnp.float32),
        ),
        in_specs=[ANY_SPEC] * len(moved) + [VMEM_SPEC] * 5,
        out_specs=(VMEM_SPEC,) * 4,
        scratch_shapes=[
            pltpu.VMEM((refs, width), jnp.bfloat16),
            pltpu.VMEM((len(blocks), count, width), jnp.bfloat16),
            pltpu.SemaphoreType.DMA((parts,)),
            pltpu.SemaphoreType.DMA((readers // 2 + 1,)),
        ],
        compiler_params=pltpu.CompilerParams(vmem_limit_bytes=SCORE_VMEM),
        cost_estimate=pl.CostEstimate(
            flops=8 * refs * width, bytes_accessed=12_000_000, transcendentals=0
        ),
        name="stage_rest",
    )(*moved, near, crossed, weighted, penalty, noise)


def write_packet(packet_ref, scores, route_ref):
    top, rows = route_ref.shape
    peak = jnp.max(scores, axis=0, keepdims=True)
    packet_ref[0:1, :] = peak
    packet_ref[1:2, :] = jnp.sum(jnp.exp(scores - peak), axis=0, keepdims=True)
    packet_ref[2:3, :] = jnp.zeros((1, packet_ref.shape[1]), jnp.float32)
    for t in range(top):
        packet_ref[2:3, t * rows : (t + 1) * rows] = route_ref[t : t + 1, :].astype(jnp.float32)


def score_kernel(readers, finish, *refs):
    refs = list(refs)
    half = readers // 2
    far_refs = [refs.pop(0) for _ in range(half - 1)]
    turned_ref, penalty_ref, _, product_ref, route_ref = refs[:5]
    score_ref, packet_ref, all_ref, sum_ref, image_sems = refs[5:]
    placed = [
        place_images(half + 1 + i, ref, all_ref, image_sems.at[i])
        for i, ref in enumerate(far_refs)
    ]
    for copy, _ in placed:
        copy.start()
    sum_ref[...] = product_ref[...]
    for (_, place), ref in zip(placed, far_refs):
        sum_ref[place, :] = jnp.dot(
            ref[...], turned_ref[...], preferred_element_type=jnp.float32
        )
    scores = sum_ref[...].T - penalty_ref[...]
    score_ref[...] = scores
    if finish:
        write_packet(packet_ref, scores, route_ref)
    for copy, _ in placed:
        copy.wait()


def all_scores(staged, far, routes, finish):
    turned, penalty, images, products = staged
    width, refs = turned.shape
    slots, rows = images.shape[0], far[0].shape[0]
    return pl.pallas_call(
        partial(score_kernel, slots // rows, finish),
        out_shape=(
            jax.ShapeDtypeStruct((refs, slots), jnp.float32),
            jax.ShapeDtypeStruct((3, slots), jnp.float32),
            jax.ShapeDtypeStruct((slots, width), jnp.bfloat16),
        ),
        in_specs=[VMEM_SPEC] * (len(far) + 5),
        out_specs=(VMEM_SPEC,) * 3,
        scratch_shapes=[
            pltpu.VMEM((slots, refs), jnp.float32),
            pltpu.SemaphoreType.DMA((len(far),)),
        ],
        input_output_aliases={len(far) + 2: 2},
        compiler_params=pltpu.CompilerParams(vmem_limit_bytes=SCORE_VMEM),
        cost_estimate=pl.CostEstimate(
            flops=2 * refs * slots * width,
            bytes_accessed=2 * (slots + refs) * width,
            transcendentals=0,
        ),
        name="scores",
    )(*far, turned, penalty, images, products, routes)


def packet_kernel(score_ref, route_ref, packet_ref):
    write_packet(packet_ref, score_ref[...], route_ref)


def make_packet(scores, routes):
    return pl.pallas_call(
        packet_kernel,
        out_shape=jax.ShapeDtypeStruct((3, scores.shape[1]), jnp.float32),
        name="packet",
    )(scores, routes)


def write_routes(packets, rows, route_ref):
    reader = lax.axis_index("reader")
    readers = len(packets)
    for t in range(route_ref.shape[0]):
        routes = [ref[2:3, t * rows : (t + 1) * rows] for ref in packets]
        bit = 1
        while bit < readers:
            flip = (reader & bit) > 0
            routes = [jnp.where(flip, routes[k ^ bit], one) for k, one in enumerate(routes)]
            bit *= 2
        for j, route in enumerate(routes):
            route_ref[t : t + 1, j * rows : (j + 1) * rows] = route


def emit_sums(posterior, all_ref, piece, out_refs):
    sums = jnp.dot(posterior, all_ref[:, piece], preferred_element_type=jnp.float32)
    count = sums.shape[0] // len(out_refs)
    for s, out_ref in enumerate(out_refs):
        out_ref[...] = sums[s * count : (s + 1) * count].astype(out_ref.dtype)


def first_sums_kernel(readers, piece, all_ref, score_ref, *refs):
    refs = list(refs)
    packets = [refs.pop(0) for _ in range(readers)]
    route_ref = refs.pop()
    norm_ref, post_ref, *out_refs = refs
    write_routes(packets, packets[0].shape[1] // readers, route_ref)
    routes = route_ref[...]
    kept, mine = [], None
    for k, packet in enumerate(packets):
        group = (lax.axis_index("reader") ^ k).astype(jnp.float32)
        hits = jnp.where(routes == group, 1.0, 0.0)
        named = jnp.max(hits, axis=0, keepdims=True) > 0.0
        kept.append(jnp.where(named, packet[0:1, :], -jnp.inf))
        mine = named if k == 0 else mine
    highest = kept[0]
    for value in kept[1:]:
        highest = jnp.maximum(highest, value)
    spread = packets[0][1:2, :] * jnp.exp(kept[0] - highest)
    for packet, value in zip(packets[1:], kept[1:]):
        spread = spread + packet[1:2, :] * jnp.exp(value - highest)
    norm = highest + jnp.log(spread)
    norm_ref[...] = norm
    exponent = jnp.where(mine, score_ref[...] - norm, -jnp.inf)
    posterior = jnp.exp(exponent).astype(jnp.bfloat16)
    post_ref[...] = posterior
    emit_sums(posterior, all_ref, piece, out_refs)


def later_sums_kernel(piece, all_ref, post_ref, *out_refs):
    emit_sums(post_ref[...], all_ref, piece, out_refs)


def group_sums(kernel, piece, members, all_images, operands, extra, scratch=()):
    refs, slots = operands[0].shape
    width = piece.stop - piece.start
    block = jax.ShapeDtypeStruct((refs // members, width), jnp.bfloat16)
    outs = pl.pallas_call(
        kernel,
        out_shape=tuple(extra) + (block,) * members,
        in_specs=[VMEM_SPEC] * (1 + len(operands)),
        out_specs=(VMEM_SPEC,) * (len(extra) + members),
        scratch_shapes=scratch,
        compiler_params=pltpu.CompilerParams(vmem_limit_bytes=SUMS_VMEM),
        cost_estimate=pl.CostEstimate(
            flops=2 * refs * slots * width,
            bytes_accessed=2 * slots * width,
            transcendentals=0,
        ),
        name="sums",
    )(all_images, *operands)
    return outs[: len(extra)], outs[len(extra) :]


def on_device(images, routes, projections, noise_weights):
    readers = lax.axis_size("reader")
    members = lax.axis_size("blk")
    reader = lax.axis_index("reader")
    rows, width = images.shape
    noise = noise_weights.reshape(1, width)

    gather = staged_gather if members == 4 and rows % 32 == 0 and readers > 1 else plain_gather
    staged, far = gather(projections[0], images, noise, readers // 4, readers // 2)
    split = lax.axis_size("sub") > 1
    scores, mine, all_images = all_scores(staged, far, routes.T, not split)
    if split:
        scores = lax.psum(scores, "sub")
        mine = make_packet(scores, routes.T)
    packets = [mine] + [swap_bits(mine, "reader", k) for k in range(1, readers)]
    pieces = [slice(0, width // 2), slice(width // 2, width)]
    extra = (
        jax.ShapeDtypeStruct((1, scores.shape[1]), jnp.float32),
        jax.ShapeDtypeStruct(scores.shape, jnp.bfloat16),
    )
    (norms, posterior), first = group_sums(
        partial(first_sums_kernel, readers, pieces[0]),
        pieces[0],
        members,
        all_images,
        (scores, *packets),
        extra,
        (pltpu.VMEM((routes.shape[1], scores.shape[1]), jnp.float32),),
    )
    _, last = group_sums(
        partial(later_sums_kernel, pieces[1]), pieces[1], members, all_images, (posterior,), ()
    )
    parts = [first, last]
    scatter = pair_scatter if members == 4 else line_scatter
    total = scatter(parts, "blk")
    normalizer = lax.dynamic_slice(norms.reshape(-1), (reader * rows,), (rows,))
    return (total[None], normalizer)


def solution(mesh):
    return jax.shard_map(
        on_device,
        mesh=mesh,
        in_specs=(
            P(("parts", "blk", "reader"), "sub"),
            P(("parts", "blk", "reader"), None),
            P(("parts", "reader"), "blk", "sub"),
            P(("parts", "sub")),
        ),
        out_specs=(P(("parts", "reader"), "blk", "sub"), P(("parts", "blk", "reader"))),
        check_vma=False,
    )
```

```python
from functools import partial

import jax
import jax.numpy as jnp
from jax import lax
from jax.experimental import pallas as pl
from jax.experimental.pallas import tpu as pltpu
from jax.sharding import PartitionSpec as P

SCORE_VMEM = 20 * 1024 * 1024
SUMS_VMEM = 9 * 1024 * 1024
STEP = 1024
VMEM_SPEC = pl.BlockSpec(memory_space=pltpu.VMEM)
ANY_SPEC = pl.BlockSpec(memory_space=pl.ANY)
SIDES = [(0, 1), (1, 0), (2, 3), (3, 2)]
MIDDLE = [(1, 2), (2, 1)]


def swap_bits(block, axis, bits):
    return lax.ppermute(block, axis, [(i, i ^ bits) for i in range(lax.axis_size(axis))])


def swap_gather(block, axis, bit):
    held = {0: block}
    while bit:
        for k in list(held):
            held[k ^ bit] = swap_bits(held[k], axis, bit)
        bit //= 2
    return [held[k] for k in range(len(held))]


def add_rounded(one, other):
    return (one.astype(jnp.float32) + other.astype(jnp.float32)).astype(jnp.bfloat16)


def staged_gather(block, images, noise, near_bits, far_bit):
    cut = block.shape[1] // 16 * 9
    cuts = [block[:, :cut], block[:, cut:]]
    crossed = swap_bits(images, "reader", far_bit)
    near = swap_gather(images, "reader", near_bits)
    firsts = [
        lax.optimization_barrier(
            (lax.ppermute(one, "blk", SIDES), lax.ppermute(one, "blk", MIDDLE))
        )
        for one in cuts
    ]
    early = stage(
        [[[one] for one in cuts], [[side] for side, _ in firsts]], near, noise
    )
    far_parts, end_parts = [], []
    for side, across in firsts:
        far = lax.ppermute(across, "blk", SIDES)
        side, *_ = lax.optimization_barrier((side, *near))
        across_far = lax.ppermute(side, "blk", MIDDLE)
        far, across_far = lax.optimization_barrier((far, across_far))
        end = lax.ppermute(across_far, "blk", SIDES)
        far_parts.append([far, across_far])
        end_parts.append([end, across])
    weighted, penalty, staged_near, noise = early
    ends = [parts[0] for parts in end_parts]
    crossed, *_ = lax.optimization_barrier((crossed, *ends, *early))
    far = swap_gather(crossed, "reader", near_bits)
    staged = stage_rest([far_parts, end_parts], staged_near, crossed, weighted, penalty, noise)
    return staged, far[1:]


def plain_gather(block, images, noise, near_bits, far_bit):
    near = swap_gather(images, "reader", near_bits)
    far = swap_gather(swap_bits(images, "reader", far_bit), "reader", near_bits)
    line = [[[one]] for one in line_gather(block, "blk")]
    weighted, penalty, near, noise = stage(line[:2], near, noise)
    staged = stage_rest(line[2:], near, far[0], weighted, penalty, noise)
    return staged, far[1:]


def line_gather(block, axis):
    size, member = lax.axis_size(axis), lax.axis_index(axis)
    ahead, behind = [block], [block]
    for s in range(1, size):
        ahead.append(lax.ppermute(ahead[-1], axis, [(i, i + 1) for i in range(s - 1, size - 1)]))
        behind.append(lax.ppermute(behind[-1], axis, [(i, i - 1) for i in range(1, size - s + 1)]))
    blocks = [block]
    for s in range(1, size):
        blocks.append(jnp.where(member >= s, ahead[s], behind[size - s]))
    return blocks


def pair_scatter(pieces, axis):
    member = lax.axis_index(axis)
    is_end = (member == 0) | (member == 3)
    for_far_end = [lax.ppermute(parts[3], axis, SIDES) for parts in pieces]
    *second, for_far_end[0] = lax.optimization_barrier(
        [parts[2] for parts in pieces] + for_far_end[:1]
    )
    for_far_middle = [lax.ppermute(part, axis, SIDES) for part in second]
    totals = []
    for parts, part, end, middle in zip(pieces, second, for_far_end, for_far_middle):
        across_end = lax.ppermute(add_rounded(part, end), axis, MIDDLE)
        across_middle = lax.ppermute(add_rounded(parts[3], middle), axis, MIDDLE)
        near = jnp.where(is_end, parts[1], add_rounded(parts[1], across_end))
        from_side = lax.ppermute(near, axis, SIDES)
        total = parts[0].astype(jnp.float32) + from_side.astype(jnp.float32)
        totals.append(total + jnp.where(is_end, 0.0, across_middle.astype(jnp.float32)))
    return beside(totals)


def put_kernel(start, piece_ref, *refs):
    out_ref, sem = refs[-2:]
    width = piece_ref.shape[1]
    copy = pltpu.make_async_copy(piece_ref, out_ref.at[:, start : start + width], sem)
    copy.start()
    copy.wait()


def put(piece, start, width, out=None):
    operands = [piece] if out is None else [piece, out]
    return pl.pallas_call(
        partial(put_kernel, start),
        out_shape=jax.ShapeDtypeStruct((piece.shape[0], width), piece.dtype),
        in_specs=[VMEM_SPEC, ANY_SPEC][: len(operands)],
        out_specs=ANY_SPEC,
        scratch_shapes=[pltpu.SemaphoreType.DMA],
        input_output_aliases={} if out is None else {1: 0},
        compiler_params=pltpu.CompilerParams(vmem_limit_bytes=SUMS_VMEM),
        name="put",
    )(*operands)


def beside(pieces):
    width = sum(piece.shape[1] for piece in pieces)
    out, start = None, 0
    for piece in pieces:
        out = put(piece, start, width, out)
        start += piece.shape[1]
    return out


def line_scatter(pieces, axis):
    return jnp.concatenate([line_sum(parts, axis) for parts in pieces], axis=1)


def line_sum(parts, axis):
    size = lax.axis_size(axis)
    up = down = None
    for s in range(1, size):
        send_up, send_down = parts[s], parts[size - s]
        if s > 1:
            send_up = add_rounded(send_up, up)
            send_down = add_rounded(send_down, down)
        up = lax.ppermute(send_up, axis, [(i, i + 1) for i in range(0, s) if i + 1 < size])
        down = lax.ppermute(send_down, axis, [(i, i - 1) for i in range(size - s, size) if i > 0])
    total = parts[0].astype(jnp.float32)
    if size > 1:
        total = total + up.astype(jnp.float32) + down.astype(jnp.float32)
    return total


def at_end():
    member = lax.axis_index("blk")
    return (member == 0) | (member == lax.axis_size("blk") - 1)


def either(refs, act):
    if len(refs) == 1:
        act(refs[0])
        return
    is_end = at_end()

    @pl.when(is_end)
    def _():
        act(refs[0])

    @pl.when(jnp.logical_not(is_end))
    def _():
        act(refs[1])


def weigh_blocks(groups, noise_ref, weighted_ref, penalty_ref, block_ref, sems, first):
    count = block_ref.shape[1]
    parts = []
    for s, group in enumerate(groups):
        start = 0
        for refs in group:
            stop = start + refs[0].shape[1]
            parts.append((s, slice(start, stop), refs))
            start = stop

    def part_copy(i, ref):
        s, columns, _ = parts[i]
        return pltpu.make_async_copy(ref, block_ref.at[s, :, columns], sems.at[i])

    for i, (_, _, refs) in enumerate(parts):
        either(refs, lambda ref, i=i: part_copy(i, ref).start())
    for s in range(len(groups)):
        rows = slice((first + s) * count, (first + s + 1) * count)
        penalty = jnp.zeros((count, 1), jnp.float32)
        for i, (t, columns, refs) in enumerate(parts):
            if t != s:
                continue
            part_copy(i, refs[0]).wait()
            for start in range(columns.start, columns.stop, STEP):
                piece = slice(start, min(start + STEP, columns.stop))
                block = block_ref[s, :, piece].astype(jnp.float32)
                scaled = block * noise_ref[:, piece]
                weighted_ref[rows, piece] = scaled.astype(jnp.bfloat16)
                penalty = penalty + 0.5 * jnp.sum(scaled * block, axis=1, keepdims=True)
        penalty_ref[rows, :] = penalty


def take_blocks(refs, counts):
    return [[[refs.pop(0) for _ in range(n)] for n in group] for group in counts]


def block_counts(blocks):
    return [[len(part) for part in group] for group in blocks]


def flat(blocks):
    return [one for group in blocks for part in group for one in part]


def stage_kernel(near_count, counts, *refs):
    refs = list(refs)
    near_refs = [refs.pop(0) for _ in range(near_count)]
    groups = take_blocks(refs, counts)
    noise_ref, weighted_ref, penalty_ref, near_ref, noise_out_ref, block_ref, near_sems, sems = refs
    rows = near_refs[0].shape[0]
    copies = []
    for k, ref in enumerate(near_refs):
        copy = pltpu.make_async_copy(ref, near_ref.at[pl.ds(k * rows, rows), :], near_sems.at[k])
        copy.start()
        copies.append(copy)
    noise_out_ref[...] = noise_ref[...]
    weigh_blocks(groups, noise_ref, weighted_ref, penalty_ref, block_ref, sems, 0)
    for copy in copies:
        copy.wait()


def stage(blocks, near, noise):
    count = blocks[0][0][0].shape[0]
    parts = sum(len(group) for group in blocks)
    width = noise.shape[1]
    refs = len(blocks) * count
    moved = [*near, *flat(blocks)]
    return pl.pallas_call(
        partial(stage_kernel, len(near), block_counts(blocks)),
        out_shape=(
            jax.ShapeDtypeStruct((refs, width), jnp.bfloat16),
            jax.ShapeDtypeStruct((refs, 1), jnp.float32),
            jax.ShapeDtypeStruct((len(near) * near[0].shape[0], width), jnp.bfloat16),
            jax.ShapeDtypeStruct((1, width), jnp.float32),
        ),
        in_specs=[ANY_SPEC] * len(moved) + [VMEM_SPEC],
        out_specs=(VMEM_SPEC,) * 4,
        scratch_shapes=[
            pltpu.VMEM((len(blocks), count, width), jnp.bfloat16),
            pltpu.SemaphoreType.DMA((len(near),)),
            pltpu.SemaphoreType.DMA((parts,)),
        ],
        compiler_params=pltpu.CompilerParams(vmem_limit_bytes=SCORE_VMEM),
        cost_estimate=pl.CostEstimate(
            flops=8 * refs * width, bytes_accessed=12_000_000, transcendentals=0
        ),
        name="stage",
    )(*moved, noise)


def place_images(k, source, all_ref, sem):
    rows = source.shape[0]
    row = pl.multiple_of((lax.axis_index("reader") ^ k) * rows, 16)
    return pltpu.make_async_copy(source, all_ref.at[pl.ds(row, rows), :], sem), pl.ds(row, rows)


def stage_rest_kernel(readers, counts, *refs):
    refs = list(refs)
    groups = take_blocks(refs, counts)
    near_ref, far_ref, early_ref, early_penalty_ref, noise_ref = [refs.pop(0) for _ in range(5)]
    turned_ref, penalty_ref, all_ref, product_ref = refs[:4]
    weighted_ref, block_ref, sems, image_sems = refs[4:]
    rows = far_ref.shape[0]
    half = readers // 2
    sources = [near_ref.at[pl.ds(k * rows, rows), :] for k in range(half)] + [far_ref]
    placed = [place_images(k, one, all_ref, image_sems.at[k]) for k, one in enumerate(sources)]
    for copy, _ in placed:
        copy.start()
    done = early_ref.shape[0]
    weighted_ref[:done, :] = early_ref[...]
    penalty_ref[:done, :] = early_penalty_ref[...]
    first = done // block_ref.shape[1]
    weigh_blocks(groups, noise_ref, weighted_ref, penalty_ref, block_ref, sems, first)
    width = weighted_ref.shape[1]
    for start in range(0, width, STEP):
        piece = slice(start, min(start + STEP, width))
        turned_ref[piece, :] = weighted_ref[:, piece].T
    products = jnp.dot(near_ref[...], turned_ref[...], preferred_element_type=jnp.float32)
    for k in range(half):
        product_ref[placed[k][1], :] = products[k * rows : (k + 1) * rows]
    product_ref[placed[half][1], :] = jnp.dot(
        far_ref[...], turned_ref[...], preferred_element_type=jnp.float32
    )
    for copy, _ in placed:
        copy.wait()


def stage_rest(blocks, near, crossed, weighted, penalty, noise):
    count = blocks[0][0][0].shape[0]
    parts = sum(len(group) for group in blocks)
    width = noise.shape[1]
    refs = len(blocks) * count + weighted.shape[0]
    slots = 2 * near.shape[0]
    readers = slots // crossed.shape[0]
    moved = flat(blocks)
    return pl.pallas_call(
        partial(stage_rest_kernel, readers, block_counts(blocks)),
        out_shape=(
            jax.ShapeDtypeStruct((width, refs), jnp.bfloat16),
            jax.ShapeDtypeStruct((refs, 1), jnp.float32),
            jax.ShapeDtypeStruct((slots, width), jnp.bfloat16),
            jax.ShapeDtypeStruct((slots, refs), jnp.float32),
        ),
        in_specs=[ANY_SPEC] * len(moved) + [VMEM_SPEC] * 5,
        out_specs=(VMEM_SPEC,) * 4,
        scratch_shapes=[
            pltpu.VMEM((refs, width), jnp.bfloat16),
            pltpu.VMEM((len(blocks), count, width), jnp.bfloat16),
            pltpu.SemaphoreType.DMA((parts,)),
            pltpu.SemaphoreType.DMA((readers // 2 + 1,)),
        ],
        compiler_params=pltpu.CompilerParams(vmem_limit_bytes=SCORE_VMEM),
        cost_estimate=pl.CostEstimate(
            flops=8 * refs * width, bytes_accessed=12_000_000, transcendentals=0
        ),
        name="stage_rest",
    )(*moved, near, crossed, weighted, penalty, noise)


def write_packet(packet_ref, scores, route_ref):
    top, rows = route_ref.shape
    peak = jnp.max(scores, axis=0, keepdims=True)
    packet_ref[0:1, :] = peak
    packet_ref[1:2, :] = jnp.sum(jnp.exp(scores - peak), axis=0, keepdims=True)
    packet_ref[2:3, :] = jnp.zeros((1, packet_ref.shape[1]), jnp.float32)
    for t in range(top):
        packet_ref[2:3, t * rows : (t + 1) * rows] = route_ref[t : t + 1, :].astype(jnp.float32)


def score_kernel(readers, finish, *refs):
    refs = list(refs)
    half = readers // 2
    far_refs = [refs.pop(0) for _ in range(half - 1)]
    turned_ref, penalty_ref, _, product_ref, route_ref = refs[:5]
    score_ref, packet_ref, all_ref, sum_ref, image_sems = refs[5:]
    placed = [
        place_images(half + 1 + i, ref, all_ref, image_sems.at[i])
        for i, ref in enumerate(far_refs)
    ]
    for copy, _ in placed:
        copy.start()
    sum_ref[...] = product_ref[...]
    for (_, place), ref in zip(placed, far_refs):
        sum_ref[place, :] = jnp.dot(
            ref[...], turned_ref[...], preferred_element_type=jnp.float32
        )
    scores = sum_ref[...].T - penalty_ref[...]
    score_ref[...] = scores
    if finish:
        write_packet(packet_ref, scores, route_ref)
    for copy, _ in placed:
        copy.wait()


def all_scores(staged, far, routes, finish):
    turned, penalty, images, products = staged
    width, refs = turned.shape
    slots, rows = images.shape[0], far[0].shape[0]
    return pl.pallas_call(
        partial(score_kernel, slots // rows, finish),
        out_shape=(
            jax.ShapeDtypeStruct((refs, slots), jnp.float32),
            jax.ShapeDtypeStruct((3, slots), jnp.float32),
            jax.ShapeDtypeStruct((slots, width), jnp.bfloat16),
        ),
        in_specs=[VMEM_SPEC] * (len(far) + 5),
        out_specs=(VMEM_SPEC,) * 3,
        scratch_shapes=[
            pltpu.VMEM((slots, refs), jnp.float32),
            pltpu.SemaphoreType.DMA((len(far),)),
        ],
        input_output_aliases={len(far) + 2: 2},
        compiler_params=pltpu.CompilerParams(vmem_limit_bytes=SCORE_VMEM),
        cost_estimate=pl.CostEstimate(
            flops=2 * refs * slots * width,
            bytes_accessed=2 * (slots + refs) * width,
            transcendentals=0,
        ),
        name="scores",
    )(*far, turned, penalty, images, products, routes)


def packet_kernel(score_ref, route_ref, packet_ref):
    write_packet(packet_ref, score_ref[...], route_ref)


def make_packet(scores, routes):
    return pl.pallas_call(
        packet_kernel,
        out_shape=jax.ShapeDtypeStruct((3, scores.shape[1]), jnp.float32),
        name="packet",
    )(scores, routes)


def write_routes(packets, rows, route_ref):
    reader = lax.axis_index("reader")
    readers = len(packets)
    for t in range(route_ref.shape[0]):
        routes = [ref[2:3, t * rows : (t + 1) * rows] for ref in packets]
        bit = 1
        while bit < readers:
            flip = (reader & bit) > 0
            routes = [jnp.where(flip, routes[k ^ bit], one) for k, one in enumerate(routes)]
            bit *= 2
        for j, route in enumerate(routes):
            route_ref[t : t + 1, j * rows : (j + 1) * rows] = route


def emit_sums(posterior, all_ref, piece, out_refs):
    sums = jnp.dot(posterior, all_ref[:, piece], preferred_element_type=jnp.float32)
    count = sums.shape[0] // len(out_refs)
    for s, out_ref in enumerate(out_refs):
        out_ref[...] = sums[s * count : (s + 1) * count].astype(out_ref.dtype)


def first_sums_kernel(readers, piece, all_ref, score_ref, *refs):
    refs = list(refs)
    packets = [refs.pop(0) for _ in range(readers)]
    route_ref = refs.pop()
    norm_ref, post_ref, *out_refs = refs
    write_routes(packets, packets[0].shape[1] // readers, route_ref)
    routes = route_ref[...]
    kept, mine = [], None
    for k, packet in enumerate(packets):
        group = (lax.axis_index("reader") ^ k).astype(jnp.float32)
        hits = jnp.where(routes == group, 1.0, 0.0)
        named = jnp.max(hits, axis=0, keepdims=True) > 0.0
        kept.append(jnp.where(named, packet[0:1, :], -jnp.inf))
        mine = named if k == 0 else mine
    highest = kept[0]
    for value in kept[1:]:
        highest = jnp.maximum(highest, value)
    spread = packets[0][1:2, :] * jnp.exp(kept[0] - highest)
    for packet, value in zip(packets[1:], kept[1:]):
        spread = spread + packet[1:2, :] * jnp.exp(value - highest)
    norm = highest + jnp.log(spread)
    norm_ref[...] = norm
    exponent = jnp.where(mine, score_ref[...] - norm, -jnp.inf)
    posterior = jnp.exp(exponent).astype(jnp.bfloat16)
    post_ref[...] = posterior
    emit_sums(posterior, all_ref, piece, out_refs)


def later_sums_kernel(piece, all_ref, post_ref, *out_refs):
    emit_sums(post_ref[...], all_ref, piece, out_refs)


def group_sums(kernel, piece, members, all_images, operands, extra, scratch=()):
    refs, slots = operands[0].shape
    width = piece.stop - piece.start
    block = jax.ShapeDtypeStruct((refs // members, width), jnp.bfloat16)
    outs = pl.pallas_call(
        kernel,
        out_shape=tuple(extra) + (block,) * members,
        in_specs=[VMEM_SPEC] * (1 + len(operands)),
        out_specs=(VMEM_SPEC,) * (len(extra) + members),
        scratch_shapes=scratch,
        compiler_params=pltpu.CompilerParams(vmem_limit_bytes=SUMS_VMEM),
        cost_estimate=pl.CostEstimate(
            flops=2 * refs * slots * width,
            bytes_accessed=2 * slots * width,
            transcendentals=0,
        ),
        name="sums",
    )(all_images, *operands)
    return outs[: len(extra)], outs[len(extra) :]


def on_device(images, routes, projections, noise_weights):
    readers = lax.axis_size("reader")
    members = lax.axis_size("blk")
    reader = lax.axis_index("reader")
    rows, width = images.shape
    noise = noise_weights.reshape(1, width)

    gather = staged_gather if members == 4 and rows % 32 == 0 and readers > 1 else plain_gather
    staged, far = gather(projections[0], images, noise, readers // 4, readers // 2)
    split = lax.axis_size("sub") > 1
    scores, mine, all_images = all_scores(staged, far, routes.T, not split)
    if split:
        scores = lax.psum(scores, "sub")
        mine = make_packet(scores, routes.T)
    packets = [mine] + [swap_bits(mine, "reader", k) for k in range(1, readers)]
    pieces = [slice(0, width // 2), slice(width // 2, width)]
    extra = (
        jax.ShapeDtypeStruct((1, scores.shape[1]), jnp.float32),
        jax.ShapeDtypeStruct(scores.shape, jnp.bfloat16),
    )
    (norms, posterior), first = group_sums(
        partial(first_sums_kernel, readers, pieces[0]),
        pieces[0],
        members,
        all_images,
        (scores, *packets),
        extra,
        (pltpu.VMEM((routes.shape[1], scores.shape[1]), jnp.float32),),
    )
    _, last = group_sums(
        partial(later_sums_kernel, pieces[1]), pieces[1], members, all_images, (posterior,), ()
    )
    parts = [first, last]
    scatter = pair_scatter if members == 4 else line_scatter
    total = scatter(parts, "blk")
    normalizer = lax.dynamic_slice(norms.reshape(-1), (reader * rows,), (rows,))
    return (total[None], normalizer)


def solution(mesh):
    return jax.shard_map(
        on_device,
        mesh=mesh,
        in_specs=(
            P(("parts", "blk", "reader"), "sub"),
            P(("parts", "blk", "reader"), None),
            P(("parts", "reader"), "blk", "sub"),
            P(("parts", "sub")),
        ),
        out_specs=(P(("parts", "reader"), "blk", "sub"), P(("parts", "blk", "reader"))),
        check_vma=False,
    )
```
